32 devices in a mesh: gx: 16 (over z, x, core), gy: 2 (over y).
Axes of the slice: x: 2, y: 2, z: 4, core: 2. Of those that a mesh axis runs over, the one named last changes fastest.
Arguments:
- iterate: float32 [32, 384, 256], P(None, 'gx', 'gy'), may hold values from -6 to 6
- source: float32 [32, 384, 256], P(None, 'gx', 'gy'), may hold values from -8 to 8
- conduct: float32 [32, 384, 256], P(None, 'gx', 'gy'), may hold values from 0.2 to 5
Outputs:
- updated: float32 [32, 384, 256], P(None, 'gx', 'gy')
The draws below stay inside these ranges and needn't reach their ends.
All inputs are finite; a program needn't handle non-finite values.
Results may differ from the reference program's by a relative error of at most 0.000041.
Values sent between devices are 32-bit elements; how exact they have to be, the bound alone decides.
No kernel may reach another device: no remote copies, remote signals or barrier semaphores. Data moves between devices by JAX's collectives and lax.ppermute only.
A program may use at most 64 MiB of HBM per device.

```python
import math
import jax
import jax.numpy as jnp

NZ = 32
SWEEPS = 3
COARSE_SWEEPS = 4
COARSEN = 8
NX = 384
NY = 256


def shard_levels(stream_key, extent, cuts, low, top_value):
    factor_of = 1.0
    for position, blocks in cuts:
        steps = jax.random.uniform(jax.random.fold_in(jax.random.fold_in(stream_key, 6), position), (blocks,), jnp.float32, low / len(cuts), top_value / len(cuts))
        factor_of = factor_of * jnp.repeat(jnp.exp(steps), extent[position] // blocks).reshape((-1,) + (1,) * (len(extent) - 1 - position))
    return factor_of


def centred(rng, shape, deviation, reach, shards=(), held_as=jnp.bfloat16):
    values = deviation * jax.random.normal(rng, shape, jnp.float32)
    if shards:
        values = values * shard_levels(rng, shape, shards, -0.22, 0.18)
    return jnp.clip(values, -reach, reach).astype(held_as)


def setup_inputs(seed: int = 0) -> dict:
    key_list = jax.random.split(jax.random.key(seed), 4)
    return {
        "iterate": centred(key_list[0], (NZ, NX, NY), 1.0, 6.0, ((1, 16), (2, 2)), jnp.float32),
        "source": centred(key_list[1], (NZ, NX, NY), 1.0, 8.0, ((1, 16), (2, 2)), jnp.float32),
        "conduct": jnp.clip(jnp.exp(math.log(5.0) - 3.218876 * jax.random.uniform(key_list[2], (NZ, NX, NY), jnp.float32) ** shard_levels(key_list[2], (NZ, NX, NY), ((1, 16), (2, 2)), -0.2, 0.2)), 0.2, 5.0),
    }


SHIFT = 0.1
LMIN = 0.3
LMAX = 2.0
OMEGA = 0.8


def neighbours(values):
    return [jnp.roll(values, 1, 0), jnp.roll(values, -1, 0), jnp.roll(values, 1, 1), jnp.roll(values, -1, 1), jnp.roll(values, 1, 2), jnp.roll(values, -1, 2)]


def operate(field, cond, factor):
    summed = jnp.zeros_like(field)
    for near_v, near_c in zip(neighbours(field), neighbours(cond)):
        summed = summed + 0.5 * (cond + near_c) * (field - near_v)
    return SHIFT * field + factor * summed


def diagonal(cond, factor):
    summed = jnp.zeros_like(cond)
    for near_c in neighbours(cond):
        summed = summed + 0.5 * (cond + near_c)
    return SHIFT + factor * summed


def restrict(values):
    depth, width_x, width_y = values.shape
    blocks = values.reshape(depth // COARSEN, COARSEN, width_x // COARSEN, COARSEN, width_y // COARSEN, COARSEN)
    return jnp.mean(blocks, axis=(1, 3, 5))


def prolong(values):
    depth, width_x, width_y = values.shape
    spread = jnp.broadcast_to(values[:, None, :, None, :, None], (depth, COARSEN, width_x, COARSEN, width_y, COARSEN))
    return spread.reshape(depth * COARSEN, width_x * COARSEN, width_y * COARSEN)


def reference(iterate, source, conduct):
    theta = (LMAX + LMIN) / 2.0
    delta = (LMAX - LMIN) / 2.0
    sigma = theta / delta
    rho_now = 1.0 / sigma
    residual = source - operate(iterate, conduct, 1.0)
    diag_fine = diagonal(conduct, 1.0)
    correction = jnp.zeros_like(residual)
    remainder = residual
    direction = residual / (theta * diag_fine)
    for sweep_index in range(SWEEPS):
        image = operate(direction, conduct, 1.0)
        correction = correction + direction
        remainder = remainder - image
        rho_next = 1.0 / (2.0 * sigma - rho_now)
        direction = rho_next * rho_now * direction + (2.0 * rho_next / delta) * remainder / diag_fine
        rho_now = rho_next
    correction = correction + direction
    coarse_rhs = restrict(residual)
    coarse_cond = restrict(conduct)
    diag_coarse = diagonal(coarse_cond, 1.0 / 64.0)
    coarse = OMEGA * coarse_rhs / diag_coarse
    for sweep_index in range(COARSE_SWEEPS - 1):
        coarse = coarse + OMEGA * (coarse_rhs - operate(coarse, coarse_cond, 1.0 / 64.0)) / diag_coarse
    return iterate + correction + prolong(coarse)
```

```python
import functools

import jax
import jax.numpy as jnp
from jax import lax
from jax.experimental import pallas as pl
from jax.experimental.pallas import tpu as pltpu
from jax.sharding import PartitionSpec as P

SWEEPS = 3
COARSE_SWEEPS = 4
COARSEN = 8

SHIFT = 0.1
LMIN = 0.3
LMAX = 2.0
OMEGA = 0.8

THETA = (LMAX + LMIN) / 2.0
DELTA = (LMAX - LMIN) / 2.0
SIGMA = THETA / DELTA

RIM = SWEEPS + 1
SUB = 8
LANES = 128
GROUP = 4 * RIM
INNER = RIM

f32 = jnp.float32
VMEM = pl.BlockSpec(memory_space=pltpu.VMEM)


def steps():
    rho, listed = 1.0 / SIGMA, []
    for _ in range(SWEEPS):
        nxt = 1.0 / (2.0 * SIGMA - rho)
        listed.append((nxt * rho, 2.0 * nxt / DELTA))
        rho = nxt
    return listed


def iota(shape, dim):
    return lax.broadcasted_iota(jnp.int32, shape, dim)


def rolled(x, by, dim):
    size = x.shape[dim]
    return pltpu.roll(x, by % size if isinstance(by, int) else by, dim)


def is_even():
    return lax.axis_index("gx") % 2 == 0


def split_z(nz):
    return nz // (LANES // GROUP)


def compact(rows, place):
    shift = 1
    while shift < COARSEN:
        rows = rows + rolled(rows, -shift, 1)
        shift *= 2
    lane = iota(rows.shape, 1)
    width = LANES // COARSEN
    spread = 2 * width
    source = jnp.clip((lane % spread - INNER) * COARSEN, 0, LANES - 1)
    return jnp.where(lane // spread == place, jnp.take_along_axis(rows, source, axis=1), 0.0)


def block_rows(values):
    sub = iota((SUB, LANES), 0)
    out = jnp.zeros((SUB, LANES), f32)
    for block in range(values.shape[0] // COARSEN):
        tile = values[block * COARSEN : (block + 1) * COARSEN]
        out = jnp.where(sub == block, jnp.sum(tile, axis=0, keepdims=True), out)
    return out


def pack_kernel(u_ref, s_ref, c_ref, p1_ref, p2_ref, e_ref, h1_ref, h2_ref):
    nz, nx, _ = u_ref.shape
    half, zs = nz // 2, split_z(nz)
    even = is_even()
    sub = iota((SUB, LANES), 0)
    lane = iota((nx, LANES), 1)
    low = sub < RIM
    per = half + zs // 2

    def send(index, first_a, first_b, last_a, last_b, small):
        first = jnp.where(low, first_a, rolled(first_b, RIM, 0))
        last = jnp.where(low, rolled(last_b, RIM, 0), last_a)
        one, two = jnp.where(even, last, first), jnp.where(even, first, last)
        p1_ref[index] = one
        p2_ref[index] = two
        if small is not None:
            h1_ref[small] = one
            h2_ref[small] = two

    for a, ref in enumerate((u_ref, c_ref, s_ref)):
        for z in range(half):
            send(
                a * per + z, ref[z, :SUB], ref[z + half, :SUB], ref[z, nx - SUB :], ref[z + half, nx - SUB :], None
            )
        strips = []
        for zi in range(zs):
            strip = jnp.zeros((nx, LANES), f32)
            for g in range(nz // zs):
                strip = jnp.where(lane // GROUP == g, rolled(ref[g * zs + zi], g * GROUP + RIM, 1), strip)
            strip = jnp.where(lane % GROUP < 2 * RIM, strip, rolled(strip, 2 * RIM, 1))
            e_ref[a * zs + zi] = strip
            strips.append(strip)
        for zi in range(zs // 2):
            one, two = strips[zi], strips[zi + zs // 2]
            send(a * per + half + zi, one[:SUB], two[:SUB], one[nx - SUB :], two[nx - SUB :], a * (zs // 2) + zi)
    cond = jnp.zeros((SUB, LANES), f32)
    for Z in range(nz // COARSEN):
        total = c_ref[Z * COARSEN]
        for z in range(1, COARSEN):
            total = total + c_ref[Z * COARSEN + z]
        cond = cond + compact(block_rows(total), Z)
    cond = cond * (1.0 / COARSEN**3)
    p1_ref[3 * per] = cond
    p2_ref[3 * per] = cond
    h1_ref[3 * (zs // 2)] = cond
    h2_ref[3 * (zs // 2)] = cond
    e_ref[3 * zs, :SUB] = cond
    for row in range(SUB, nx, SUB):
        e_ref[3 * zs, row : row + SUB] = cond


def pack(u, s, c):
    nz, nx, ny = u.shape
    zs = split_z(nz)
    per = nz // 2 + zs // 2
    big = jax.ShapeDtypeStruct((3 * per + 1, SUB, LANES), f32)
    small = jax.ShapeDtypeStruct((3 * (zs // 2) + 1, SUB, LANES), f32)
    strip = jax.ShapeDtypeStruct((3 * zs + 1, nx, LANES), f32)
    return pl.pallas_call(
        pack_kernel,
        out_shape=(big, big, strip, small, small),
        in_specs=[VMEM] * 3,
        out_specs=(VMEM,) * 5,
        name="pack",
    )(u, s, c)


def local_kernel(u_ref, s_ref, c_ref, o_ref):
    nz, nx, _ = u_ref.shape
    row, lane = iota((nx, LANES), 0), iota((nx, LANES), 1)

    def up(z):
        after = (z + 1) % nz
        return 0.5 * (c_ref[z] + c_ref[after]) * (u_ref[z] - u_ref[after])

    out = jnp.zeros((SUB, LANES), f32)
    for Z in range(nz // COARSEN):
        plain = along_x = along_y = jnp.zeros((nx, LANES), f32)
        for z in range(Z * COARSEN, (Z + 1) * COARSEN):
            u, c = u_ref[z], c_ref[z]
            plain = plain + (s_ref[z] - SHIFT * u)
            along_x = along_x + (c + rolled(c, -1, 0)) * (u - rolled(u, -1, 0))
            along_y = along_y + (c + rolled(c, -1, 1)) * (u - rolled(u, -1, 1))
        along_x = jnp.where(row == nx - 1, 0.0, 0.5 * along_x)
        along_y = jnp.where(lane == LANES - 1, 0.0, 0.5 * along_y)
        plain = plain - along_x + rolled(along_x, 1, 0) - along_y + rolled(along_y, 1, 1)
        plain = plain - up((Z + 1) * COARSEN - 1) + up((Z * COARSEN - 1) % nz)
        out = out + compact(block_rows(plain), Z)
    o_ref[...] = out


def local(u, s, c):
    return pl.pallas_call(
        local_kernel,
        out_shape=jax.ShapeDtypeStruct((SUB, LANES), f32),
        in_specs=[VMEM] * 3,
        out_specs=VMEM,
        cost_estimate=pl.CostEstimate(flops=20 * u.size, bytes_accessed=12 * u.size, transcendentals=0),
        name="local_part",
    )(u, s, c)


def faces_kernel(part_ref, p1_ref, p2_ref, r1_ref, r2_ref, e_ref, el_ref, er_ref, o_ref, *, nz, nx):
    half, zs = nz // 2, split_z(nz)
    per = half + zs // 2
    even = is_even()
    sub, lane = iota((SUB, LANES), 0), iota((SUB, LANES), 1)
    spread = 2 * (LANES // COARSEN)
    width = LANES // COARSEN
    rows = nx // COARSEN
    total = part_ref[...]

    for group in range(half // COARSEN):
        right = left = jnp.zeros((SUB, LANES), f32)
        for z in range(group * COARSEN, (group + 1) * COARSEN):
            def pick(a):
                one, two = p1_ref[a * per + z], p2_ref[a * per + z]
                near, far = r1_ref[a * per + z], r2_ref[a * per + z]
                last, first = jnp.where(even, one, two), jnp.where(even, two, one)
                after, before = jnp.where(even, near, far), jnp.where(even, far, near)
                return rolled(last, 1, 0), first, after, rolled(before, 1, 0)

            u_last, u_first, u_after, u_before = pick(0)
            c_last, c_first, c_after, c_before = pick(1)
            right = right + (c_last + c_after) * (u_last - u_after)
            left = left + (c_before + c_first) * (u_before - u_first)
        right, left = 0.5 * right, 0.5 * left
        for Z, at in ((group, 0), (group + half // COARSEN, RIM)):
            flux = compact(
                jnp.where(sub == 0, left[at : at + 1], 0.0) - jnp.where(sub == rows - 1, right[at : at + 1], 0.0), Z
            )
            total = total + flux

    wide = iota((nx, LANES), 1) % GROUP

    def strip(a, zi):
        at = a * zs + zi
        return jnp.where(wide < RIM, el_ref[at], jnp.where(wide < 3 * RIM, e_ref[at], er_ref[at]))

    flux = jnp.zeros((nx, LANES), f32)
    for zi in range(zs):
        u, c = strip(0, zi), strip(1, zi)
        flux = flux + (c + rolled(c, -1, 1)) * (u - rolled(u, -1, 1))
    flux = block_rows(0.5 * flux)
    flux = flux + rolled(flux, -GROUP, 1)
    place = lane % spread
    total = total + jnp.where(place == INNER, rolled(flux, INNER - (RIM - 1), 1), 0.0)
    total = total - jnp.where(place == INNER + width - 1, rolled(flux, INNER + width - 1 - (3 * RIM - 1), 1), 0.0)

    own = e_ref[3 * zs, :SUB]
    near, far = r1_ref[3 * per], r2_ref[3 * per]
    right, left = jnp.where(even, near, far), jnp.where(even, far, near)
    y_left, y_right = el_ref[3 * zs, :SUB], er_ref[3 * zs, :SUB]
    up = jnp.where(sub == rows - 1, rolled(right, rows - 1, 0), rolled(own, -1, 0))
    down = jnp.where(sub == 0, rolled(left, -(rows - 1), 0), rolled(own, 1, 0))
    fore = jnp.where(place == INNER + width - 1, rolled(y_right, width - 1, 1), rolled(own, -1, 1))
    back = jnp.where(place == INNER, rolled(y_left, 1 - width, 1), rolled(own, 1, 1))
    around = up + down + fore + back + rolled(own, spread, 1) + rolled(own, -spread, 1)
    diag = SHIFT + (0.5 / COARSEN**2) * (6.0 * own + around)
    weight = OMEGA / diag
    o_ref[0] = weight * (total * (1.0 / COARSEN**3))
    o_ref[1] = weight
    o_ref[2] = own


def faces(part, p1, p2, r1, r2, e, el, er, nz, nx):
    return pl.pallas_call(
        functools.partial(faces_kernel, nz=nz, nx=nx),
        out_shape=jax.ShapeDtypeStruct((3, SUB, LANES), f32),
        in_specs=[VMEM] * 8,
        out_specs=VMEM,
        name="faces",
    )(part, p1, p2, r1, r2, e, el, er)


def fine_kernel(
    u_ref, s_ref, c_ref, r1_ref, r2_ref, e_ref, el_ref, er_ref, d1l_ref, d1r_ref, d2l_ref, d2r_ref,
    o_ref,
    uh, ch, sh, cx, cy, cz, inv, q, va, vb, wu, wc, w0, w1, w2,
):
    nz, nx, _ = u_ref.shape
    half, zs = nz // 2, split_z(nz)
    groups = nz // zs
    per = half + zs // 2
    ext = nx + SUB
    even = is_even()
    low = iota((SUB, LANES), 0) < RIM
    table = steps()

    def halo(near, far):
        after, before = jnp.where(even, near, far), jnp.where(even, far, near)
        return jnp.where(low, after, before), rolled(jnp.where(low, before, after), RIM, 0)

    for a, ref in enumerate((uh, ch, sh)):

        @pl.loop(0, half)
        def _(z, a=a, ref=ref):
            first, second = halo(r1_ref[a * per + z], r2_ref[a * per + z])
            ref[z] = first
            ref[z + half] = second

    wide = iota((nx, LANES), 1) % GROUP
    thin = iota((SUB, LANES), 1) % GROUP
    long = iota((ext, LANES), 1) % GROUP

    def join(left, own, right, place):
        return jnp.where(place < RIM, left, jnp.where(place < 3 * RIM, own, right))

    def strips_of(a):
        rims = [None] * zs
        for zi in range(zs // 2):
            at, small = a * per + half + zi, a * (zs // 2) + zi
            near = join(d1l_ref[small], r1_ref[at], d1r_ref[small], thin)
            far = join(d2l_ref[small], r2_ref[at], d2r_ref[small], thin)
            rims[zi], rims[zi + zs // 2] = halo(near, far)
        listed = []
        for zi in range(zs):
            at = a * zs + zi
            listed.append(jnp.concatenate([join(el_ref[at], e_ref[at], er_ref[at], wide), rims[zi]], axis=0))
        return listed

    def z_up(x):
        return x[1:] + [rolled(x[0], -GROUP, 1)]

    def z_down(x):
        return [rolled(x[-1], GROUP, 1)] + x[:-1]

    def window(left, right):
        return jnp.where(long == RIM - 1, left, rolled(right, -(2 * RIM + 2), 1))

    us, cs, ss = strips_of(0), strips_of(1), strips_of(2)
    for zi in range(zs):
        wu[zi] = window(us[zi], us[zi])
        wc[zi] = window(cs[zi], cs[zi])
    cxs = [0.5 * (c + rolled(c, -1, 0)) for c in cs]
    cys = [0.5 * (c + rolled(c, -1, 1)) for c in cs]
    czs = [0.5 * (c + d) for c, d in zip(cs, z_up(cs))]
    czds = z_down(czs)
    invs, qs, vs = [], [], []
    u_up, u_down = z_up(us), z_down(us)
    for zi in range(zs):
        u = us[zi]
        cxl, cyl = rolled(cxs[zi], 1, 0), rolled(cys[zi], 1, 1)
        diag = SHIFT + (cxs[zi] + cxl) + (cys[zi] + cyl) + (czs[zi] + czds[zi])
        near = cxs[zi] * rolled(u, -1, 0) + cxl * rolled(u, 1, 0) + cys[zi] * rolled(u, -1, 1)
        near = near + cyl * rolled(u, 1, 1) + czs[zi] * u_up[zi] + czds[zi] * u_down[zi]
        invs.append(1.0 / diag)
        qs.append((ss[zi] - diag * u + near) * invs[zi])
        vs.append(qs[zi] * (1.0 / THETA))
    for k, w in enumerate((w0, w1, w2)):
        prod = [cys[zi] * vs[zi] for zi in range(zs)]
        for zi in range(zs):
            w[zi] = window(prod[zi], vs[zi])
        if k == SWEEPS - 1:
            break
        keep, lift = table[k]
        v_up, v_down = z_up(vs), z_down(vs)
        fresh = []
        for zi in range(zs):
            v = vs[zi]
            near = cxs[zi] * rolled(v, -1, 0) + rolled(cxs[zi] * v, 1, 0)
            near = near + cys[zi] * rolled(v, -1, 1) + rolled(prod[zi], 1, 1)
            near = near + czs[zi] * v_up[zi] + czds[zi] * v_down[zi]
            qs[zi] = qs[zi] - v + near * invs[zi]
            fresh.append(keep * v + lift * qs[zi])
        vs = fresh

    lane = iota((ext, LANES), 1)
    first_lane, last_lane = lane == 0, lane == LANES - 1

    def whole(ref, rim, z):
        return jnp.concatenate([ref[z], rim[z]], axis=0)

    def turn(w, zi, g):
        return pltpu.roll(w[zi], (2 * LANES - (RIM - 1) - g * GROUP) % LANES, 1)

    @pl.loop(0, groups)
    def _(g):
        for zi in range(zs):
            z = g * zs + zi
            above, below = (z + 1) % nz, (z + nz - 1) % nz
            u, c, s = whole(u_ref, uh, z), whole(c_ref, ch, z), whole(s_ref, sh, z)
            u_up, u_down = whole(u_ref, uh, above), whole(u_ref, uh, below)
            c_up, c_down = whole(c_ref, ch, above), whole(c_ref, ch, below)
            edge_u, edge_c = turn(wu, zi, g), turn(wc, zi, g)
            gx = 0.5 * (c + rolled(c, -1, 0))
            gxl = rolled(gx, 1, 0)
            gy = 0.5 * (c + jnp.where(last_lane, edge_c, rolled(c, -1, 1)))
            gyl = 0.5 * (c + jnp.where(first_lane, edge_c, rolled(c, 1, 1)))
            gz = 0.5 * (c + c_up)
            gzl = 0.5 * (c + c_down)
            diag = SHIFT + (gx + gxl) + (gy + gyl) + (gz + gzl)
            near = gx * rolled(u, -1, 0) + gxl * rolled(u, 1, 0)
            near = near + gy * jnp.where(last_lane, edge_u, rolled(u, -1, 1))
            near = near + gyl * jnp.where(first_lane, edge_u, rolled(u, 1, 1))
            near = near + gz * u_up + gzl * u_down
            inverse = 1.0 / diag
            scaled = (s - diag * u + near) * inverse
            v = scaled * (1.0 / THETA)
            cx[z] = gx
            cy[z] = gy
            cz[z] = gz
            inv[z] = inverse
            q[z] = scaled
            va[z] = v
            o_ref[z] = (u + v)[:nx]

    for k, w in enumerate((w0, w1, w2)):
        old, new = (va, vb) if k % 2 == 0 else (vb, va)
        keep, lift = table[k]

        @pl.loop(0, groups)
        def _(g, w=w, old=old, new=new, keep=keep, lift=lift, final=k == SWEEPS - 1):
            for zi in range(zs):
                z = g * zs + zi
                above, below = (z + 1) % nz, (z + nz - 1) % nz
                v, gx, gy = old[z], cx[z], cy[z]
                edge = turn(w, zi, g)
                near = gx * rolled(v, -1, 0) + rolled(gx * v, 1, 0)
                near = near + gy * jnp.where(last_lane, edge, rolled(v, -1, 1))
                near = near + jnp.where(first_lane, edge, rolled(gy * v, 1, 1))
                near = near + cz[z] * old[above] + cz[below] * old[below]
                scaled = q[z] - v + near * inv[z]
                fresh = keep * v + lift * scaled
                if not final:
                    q[z] = scaled
                    new[z] = fresh
                o_ref[z] = o_ref[z] + fresh[:nx]


def fine(u, s, c, r1, r2, e, el, er, d1l, d1r, d2l, d2r):
    nz, nx, ny = u.shape
    zs = split_z(nz)
    ext = nx + SUB
    full = pltpu.VMEM((nz, ext, LANES), f32)
    rim = pltpu.VMEM((nz, SUB, LANES), f32)
    strip = pltpu.VMEM((zs, ext, LANES), f32)
    return pl.pallas_call(
        fine_kernel,
        out_shape=jax.ShapeDtypeStruct(u.shape, f32),
        in_specs=[VMEM] * 12,
        out_specs=VMEM,
        scratch_shapes=[rim] * 3 + [full] * 7 + [strip] * 5,
        compiler_params=pltpu.CompilerParams(vmem_limit_bytes=32 * 1024 * 1024),
        cost_estimate=pl.CostEstimate(flops=150 * u.size, bytes_accessed=20 * u.size, transcendentals=0),
        name="fine",
    )(u, s, c, r1, r2, e, el, er, d1l, d1r, d2l, d2r)


def finish_kernel(x_ref, m_ref, r1_ref, r2_ref, yl_ref, yr_ref, d1l_ref, d1r_ref, d2l_ref, d2r_ref, o_ref, scr):
    nz, nx, _ = x_ref.shape
    rows = nx // COARSEN
    width = LANES // COARSEN
    spread = 2 * width
    even = is_even()
    lane = iota((SUB, LANES), 1)
    place = lane % spread

    def join(left, own, right):
        return jnp.where(
            place < INNER,
            rolled(left, -width, 1),
            jnp.where(place < INNER + width, own, rolled(right, width, 1)),
        )

    fields = []
    for a in range(3):
        own = join(yl_ref[a], m_ref[a], yr_ref[a])
        near = join(d1l_ref[a], r1_ref[a], d1r_ref[a])
        far = join(d2l_ref[a], r2_ref[a], d2r_ref[a])
        right, left = jnp.where(even, near, far), jnp.where(even, far, near)
        scr[a] = jnp.ones((2 * SUB, LANES), f32)
        scr[a, 0:rows] = left[:rows]
        scr[a, rows : 2 * rows] = own[:rows]
        scr[a, 2 * rows : 3 * rows] = right[:rows]
        fields.append(scr[a])
    start, weight, cond = fields
    half = 0.5 / COARSEN**2
    gx = half * (cond + rolled(cond, -1, 0))
    gy = half * (cond + rolled(cond, -1, 1))
    gz = half * (cond + rolled(cond, -spread, 1))
    v = start
    for _ in range(COARSE_SWEEPS - 1):
        fx = gx * (v - rolled(v, -1, 0))
        fy = gy * (v - rolled(v, -1, 1))
        fz = gz * (v - rolled(v, -spread, 1))
        image = SHIFT * v + (fx - rolled(fx, 1, 0)) + (fy - rolled(fy, 1, 1)) + (fz - rolled(fz, spread, 1))
        v = v + start - weight * image
    top = v[:SUB]
    for Z in range(nz // COARSEN):
        spread_out = jnp.take_along_axis(top, Z * spread + INNER + lane // COARSEN, axis=1)
        for X in range(rows):
            value = jnp.broadcast_to(spread_out[rows + X : rows + X + 1], (COARSEN, LANES))
            for z in range(Z * COARSEN, (Z + 1) * COARSEN):
                at = slice(X * COARSEN, (X + 1) * COARSEN)
                o_ref[z, at] = x_ref[z, at] + value


def finish(x, *messages):
    return pl.pallas_call(
        finish_kernel,
        out_shape=jax.ShapeDtypeStruct(x.shape, f32),
        in_specs=[VMEM] * (1 + len(messages)),
        out_specs=VMEM,
        scratch_shapes=[pltpu.VMEM((3, 2 * SUB, LANES), f32)],
        name="finish",
    )(x, *messages)


def moves():
    size_x, size_y = lax.axis_size("gx"), lax.axis_size("gy")

    def send(x, go):
        pairs = []
        for i in range(size_x):
            for j in range(size_y):
                k, l = go(i, j)
                pairs.append((i * size_y + j, (k % size_x) * size_y + l % size_y))
        return lax.ppermute(x, ("gx", "gy"), pairs)

    def one(i):
        return i + 1 if i % 2 == 0 else i - 1

    def two(i):
        return i - 1 if i % 2 == 0 else i + 1

    def stay(i):
        return i

    def straight(x, along):
        return send(x, lambda i, j: (along(i), j))

    def across(x, along):
        left = send(x, lambda i, j: (along(i), j + 1))
        if size_y == 2:
            return left, left
        return left, send(x, lambda i, j: (along(i), j - 1))

    return one, two, stay, straight, across


def body(iterate, source, conduct):
    nz, nx, ny = iterate.shape
    one, two, stay, straight, across = moves()
    p1, p2, e, h1, h2 = pack(iterate, source, conduct)
    r2 = straight(p2, two)
    d2l, d2r = across(h2, two)
    el, er = across(e, stay)
    r1 = straight(p1, one)
    d1l, d1r = across(h1, one)
    part = local(iterate, source, conduct)
    m = faces(part, p1, p2, r1, r2, e, el, er, nz, nx)
    x = fine(iterate, source, conduct, r1, r2, e, el, er, d1l, d1r, d2l, d2r)
    m2 = straight(m, two)
    c2l, c2r = across(m, two)
    ml, mr = across(m, stay)
    m1 = straight(m, one)
    c1l, c1r = across(m, one)
    return finish(x, m, m1, m2, ml, mr, c1l, c1r, c2l, c2r)


def solution(mesh):
    spec = P(None, "gx", "gy")
    return jax.shard_map(body, mesh=mesh, in_specs=(spec,) * 3, out_specs=spec, check_vma=False)
```

```python
import functools

import jax
import jax.numpy as jnp
from jax import lax
from jax.experimental import pallas as pl
from jax.experimental.pallas import tpu as pltpu
from jax.sharding import PartitionSpec as P

SWEEPS = 3
COARSE_SWEEPS = 4
COARSEN = 8

SHIFT = 0.1
LMIN = 0.3
LMAX = 2.0
OMEGA = 0.8

THETA = (LMAX + LMIN) / 2.0
DELTA = (LMAX - LMIN) / 2.0
SIGMA = THETA / DELTA

RIM = SWEEPS + 1
SUB = 8
LANES = 128
GROUP = 4 * RIM
INNER = RIM

f32 = jnp.float32
VMEM = pl.BlockSpec(memory_space=pltpu.VMEM)
SMALL = pltpu.CompilerParams(vmem_limit_bytes=12 * 1024 * 1024)


def steps():
    rho, listed = 1.0 / SIGMA, []
    for _ in range(SWEEPS):
        nxt = 1.0 / (2.0 * SIGMA - rho)
        listed.append((nxt * rho, 2.0 * nxt / DELTA))
        rho = nxt
    return listed


def iota(shape, dim):
    return lax.broadcasted_iota(jnp.int32, shape, dim)


def rolled(x, by, dim):
    size = x.shape[dim]
    return pltpu.roll(x, by % size if isinstance(by, int) else by, dim)


def is_even():
    return lax.axis_index("gx") % 2 == 0


def split_z(nz):
    return nz // (LANES // GROUP)


def compact(rows, place):
    shift = 1
    while shift < COARSEN:
        rows = rows + rolled(rows, -shift, 1)
        shift *= 2
    lane = iota(rows.shape, 1)
    width = LANES // COARSEN
    spread = 2 * width
    source = jnp.clip((lane % spread - INNER) * COARSEN, 0, LANES - 1)
    return jnp.where(lane // spread == place, jnp.take_along_axis(rows, source, axis=1), 0.0)


def block_rows(values):
    sub = iota((SUB, LANES), 0)
    out = jnp.zeros((SUB, LANES), f32)
    for block in range(values.shape[0] // COARSEN):
        tile = values[block * COARSEN : (block + 1) * COARSEN]
        out = jnp.where(sub == block, jnp.sum(tile, axis=0, keepdims=True), out)
    return out


def pack_kernel(u_ref, s_ref, c_ref, p1_ref, p2_ref, e_ref, h1_ref, h2_ref):
    nz, nx, _ = u_ref.shape
    half, zs = nz // 2, split_z(nz)
    even = is_even()
    sub = iota((SUB, LANES), 0)
    lane = iota((nx, LANES), 1)
    low = sub < RIM
    per = half + zs // 2

    def send(index, first_a, first_b, last_a, last_b, small):
        first = jnp.where(low, first_a, rolled(first_b, RIM, 0))
        last = jnp.where(low, rolled(last_b, RIM, 0), last_a)
        one, two = jnp.where(even, last, first), jnp.where(even, first, last)
        p1_ref[index] = one
        p2_ref[index] = two
        if small is not None:
            h1_ref[small] = one
            h2_ref[small] = two

    for a, ref in enumerate((u_ref, c_ref, s_ref)):
        for z in range(half):
            send(
                a * per + z, ref[z, :SUB], ref[z + half, :SUB], ref[z, nx - SUB :], ref[z + half, nx - SUB :], None
            )
        strips = []
        for zi in range(zs):
            strip = jnp.zeros((nx, LANES), f32)
            for g in range(nz // zs):
                strip = jnp.where(lane // GROUP == g, rolled(ref[g * zs + zi], g * GROUP + RIM, 1), strip)
            strip = jnp.where(lane % GROUP < 2 * RIM, strip, rolled(strip, 2 * RIM, 1))
            e_ref[a * zs + zi] = strip
            strips.append(strip)
        for zi in range(zs // 2):
            one, two = strips[zi], strips[zi + zs // 2]
            send(a * per + half + zi, one[:SUB], two[:SUB], one[nx - SUB :], two[nx - SUB :], a * (zs // 2) + zi)
    cond = jnp.zeros((SUB, LANES), f32)
    for Z in range(nz // COARSEN):
        total = c_ref[Z * COARSEN]
        for z in range(1, COARSEN):
            total = total + c_ref[Z * COARSEN + z]
        cond = cond + compact(block_rows(total), Z)
    cond = cond * (1.0 / COARSEN**3)
    p1_ref[3 * per] = cond
    p2_ref[3 * per] = cond
    h1_ref[3 * (zs // 2)] = cond
    h2_ref[3 * (zs // 2)] = cond
    e_ref[3 * zs, :SUB] = cond
    for row in range(SUB, nx, SUB):
        e_ref[3 * zs, row : row + SUB] = cond


def pack(u, s, c):
    nz, nx, ny = u.shape
    zs = split_z(nz)
    per = nz // 2 + zs // 2
    big = jax.ShapeDtypeStruct((3 * per + 1, SUB, LANES), f32)
    small = jax.ShapeDtypeStruct((3 * (zs // 2) + 1, SUB, LANES), f32)
    strip = jax.ShapeDtypeStruct((3 * zs + 1, nx, LANES), f32)
    return pl.pallas_call(
        pack_kernel,
        out_shape=(big, big, strip, small, small),
        in_specs=[VMEM] * 3,
        out_specs=(VMEM,) * 5,
        compiler_params=SMALL,
        name="pack",
    )(u, s, c)


def local_kernel(u_ref, s_ref, c_ref, o_ref):
    nz, nx, _ = u_ref.shape
    row, lane = iota((nx, LANES), 0), iota((nx, LANES), 1)

    def up(z):
        after = (z + 1) % nz
        return 0.5 * (c_ref[z] + c_ref[after]) * (u_ref[z] - u_ref[after])

    out = jnp.zeros((SUB, LANES), f32)
    for Z in range(nz // COARSEN):
        plain = along_x = along_y = jnp.zeros((nx, LANES), f32)
        for z in range(Z * COARSEN, (Z + 1) * COARSEN):
            u, c = u_ref[z], c_ref[z]
            plain = plain + (s_ref[z] - SHIFT * u)
            along_x = along_x + (c + rolled(c, -1, 0)) * (u - rolled(u, -1, 0))
            along_y = along_y + (c + rolled(c, -1, 1)) * (u - rolled(u, -1, 1))
        along_x = jnp.where(row == nx - 1, 0.0, 0.5 * along_x)
        along_y = jnp.where(lane == LANES - 1, 0.0, 0.5 * along_y)
        plain = plain - along_x + rolled(along_x, 1, 0) - along_y + rolled(along_y, 1, 1)
        plain = plain - up((Z + 1) * COARSEN - 1) + up((Z * COARSEN - 1) % nz)
        out = out + compact(block_rows(plain), Z)
    o_ref[...] = out


def local(u, s, c):
    return pl.pallas_call(
        local_kernel,
        out_shape=jax.ShapeDtypeStruct((SUB, LANES), f32),
        in_specs=[VMEM] * 3,
        out_specs=VMEM,
        cost_estimate=pl.CostEstimate(flops=20 * u.size, bytes_accessed=12 * u.size, transcendentals=0),
        compiler_params=SMALL,
        name="local_part",
    )(u, s, c)


def faces_kernel(part_ref, p1_ref, p2_ref, r1_ref, r2_ref, e_ref, el_ref, er_ref, o_ref, *, nz, nx):
    half, zs = nz // 2, split_z(nz)
    per = half + zs // 2
    even = is_even()
    sub, lane = iota((SUB, LANES), 0), iota((SUB, LANES), 1)
    spread = 2 * (LANES // COARSEN)
    width = LANES // COARSEN
    rows = nx // COARSEN
    total = part_ref[...]

    for group in range(half // COARSEN):
        right = left = jnp.zeros((SUB, LANES), f32)
        for z in range(group * COARSEN, (group + 1) * COARSEN):
            def pick(a):
                one, two = p1_ref[a * per + z], p2_ref[a * per + z]
                near, far = r1_ref[a * per + z], r2_ref[a * per + z]
                last, first = jnp.where(even, one, two), jnp.where(even, two, one)
                after, before = jnp.where(even, near, far), jnp.where(even, far, near)
                return rolled(last, 1, 0), first, after, rolled(before, 1, 0)

            u_last, u_first, u_after, u_before = pick(0)
            c_last, c_first, c_after, c_before = pick(1)
            right = right + (c_last + c_after) * (u_last - u_after)
            left = left + (c_before + c_first) * (u_before - u_first)
        right, left = 0.5 * right, 0.5 * left
        for Z, at in ((group, 0), (group + half // COARSEN, RIM)):
            flux = compact(
                jnp.where(sub == 0, left[at : at + 1], 0.0) - jnp.where(sub == rows - 1, right[at : at + 1], 0.0), Z
            )
            total = total + flux

    wide = iota((nx, LANES), 1) % GROUP

    def strip(a, zi):
        at = a * zs + zi
        return jnp.where(wide < RIM, el_ref[at], jnp.where(wide < 3 * RIM, e_ref[at], er_ref[at]))

    flux = jnp.zeros((nx, LANES), f32)
    for zi in range(zs):
        u, c = strip(0, zi), strip(1, zi)
        flux = flux + (c + rolled(c, -1, 1)) * (u - rolled(u, -1, 1))
    flux = block_rows(0.5 * flux)
    flux = flux + rolled(flux, -GROUP, 1)
    place = lane % spread
    total = total + jnp.where(place == INNER, rolled(flux, INNER - (RIM - 1), 1), 0.0)
    total = total - jnp.where(place == INNER + width - 1, rolled(flux, INNER + width - 1 - (3 * RIM - 1), 1), 0.0)

    own = e_ref[3 * zs, :SUB]
    near, far = r1_ref[3 * per], r2_ref[3 * per]
    right, left = jnp.where(even, near, far), jnp.where(even, far, near)
    y_left, y_right = el_ref[3 * zs, :SUB], er_ref[3 * zs, :SUB]
    up = jnp.where(sub == rows - 1, rolled(right, rows - 1, 0), rolled(own, -1, 0))
    down = jnp.where(sub == 0, rolled(left, -(rows - 1), 0), rolled(own, 1, 0))
    fore = jnp.where(place == INNER + width - 1, rolled(y_right, width - 1, 1), rolled(own, -1, 1))
    back = jnp.where(place == INNER, rolled(y_left, 1 - width, 1), rolled(own, 1, 1))
    around = up + down + fore + back + rolled(own, spread, 1) + rolled(own, -spread, 1)
    diag = SHIFT + (0.5 / COARSEN**2) * (6.0 * own + around)
    weight = OMEGA / diag
    o_ref[0] = weight * (total * (1.0 / COARSEN**3))
    o_ref[1] = weight
    o_ref[2] = own


def faces(part, p1, p2, r1, r2, e, el, er, nz, nx):
    return pl.pallas_call(
        functools.partial(faces_kernel, nz=nz, nx=nx),
        out_shape=jax.ShapeDtypeStruct((3, SUB, LANES), f32),
        in_specs=[VMEM] * 8,
        out_specs=VMEM,
        compiler_params=SMALL,
        name="faces",
    )(part, p1, p2, r1, r2, e, el, er)


def fine_kernel(
    u_ref, s_ref, c_ref, r1_ref, r2_ref, e_ref, el_ref, er_ref, d1l_ref, d1r_ref, d2l_ref, d2r_ref,
    o_ref,
    uh, ch, sh, cx, cy, cz, inv, q, va, vb, wu, wc, w0, w1, w2,
):
    nz, nx, _ = u_ref.shape
    half, zs = nz // 2, split_z(nz)
    groups = nz // zs
    per = half + zs // 2
    ext = nx + SUB
    even = is_even()
    low = iota((SUB, LANES), 0) < RIM
    table = steps()

    def halo(near, far):
        after, before = jnp.where(even, near, far), jnp.where(even, far, near)
        return jnp.where(low, after, before), rolled(jnp.where(low, before, after), RIM, 0)

    for a, ref in enumerate((uh, ch, sh)):

        @pl.loop(0, half)
        def _(z, a=a, ref=ref):
            first, second = halo(r1_ref[a * per + z], r2_ref[a * per + z])
            ref[z] = first
            ref[z + half] = second

    wide = iota((nx, LANES), 1) % GROUP
    thin = iota((SUB, LANES), 1) % GROUP
    long = iota((ext, LANES), 1) % GROUP

    def join(left, own, right, place):
        return jnp.where(place < RIM, left, jnp.where(place < 3 * RIM, own, right))

    def strips_of(a):
        rims = [None] * zs
        for zi in range(zs // 2):
            at, small = a * per + half + zi, a * (zs // 2) + zi
            near = join(d1l_ref[small], r1_ref[at], d1r_ref[small], thin)
            far = join(d2l_ref[small], r2_ref[at], d2r_ref[small], thin)
            rims[zi], rims[zi + zs // 2] = halo(near, far)
        listed = []
        for zi in range(zs):
            at = a * zs + zi
            listed.append(jnp.concatenate([join(el_ref[at], e_ref[at], er_ref[at], wide), rims[zi]], axis=0))
        return listed

    def z_up(x):
        return x[1:] + [rolled(x[0], -GROUP, 1)]

    def z_down(x):
        return [rolled(x[-1], GROUP, 1)] + x[:-1]

    def window(left, right):
        return jnp.where(long == RIM - 1, left, rolled(right, -(2 * RIM + 2), 1))

    us, cs, ss = strips_of(0), strips_of(1), strips_of(2)
    for zi in range(zs):
        wu[zi] = window(us[zi], us[zi])
        wc[zi] = window(cs[zi], cs[zi])
    cxs = [0.5 * (c + rolled(c, -1, 0)) for c in cs]
    cys = [0.5 * (c + rolled(c, -1, 1)) for c in cs]
    czs = [0.5 * (c + d) for c, d in zip(cs, z_up(cs))]
    czds = z_down(czs)
    invs, qs, vs = [], [], []
    u_up, u_down = z_up(us), z_down(us)
    for zi in range(zs):
        u = us[zi]
        cxl, cyl = rolled(cxs[zi], 1, 0), rolled(cys[zi], 1, 1)
        diag = SHIFT + (cxs[zi] + cxl) + (cys[zi] + cyl) + (czs[zi] + czds[zi])
        near = cxs[zi] * rolled(u, -1, 0) + cxl * rolled(u, 1, 0) + cys[zi] * rolled(u, -1, 1)
        near = near + cyl * rolled(u, 1, 1) + czs[zi] * u_up[zi] + czds[zi] * u_down[zi]
        invs.append(1.0 / diag)
        qs.append((ss[zi] - diag * u + near) * invs[zi])
        vs.append(qs[zi] * (1.0 / THETA))
    for k, w in enumerate((w0, w1, w2)):
        prod = [cys[zi] * vs[zi] for zi in range(zs)]
        for zi in range(zs):
            w[zi] = window(prod[zi], vs[zi])
        if k == SWEEPS - 1:
            break
        keep, lift = table[k]
        v_up, v_down = z_up(vs), z_down(vs)
        fresh = []
        for zi in range(zs):
            v = vs[zi]
            near = cxs[zi] * rolled(v, -1, 0) + rolled(cxs[zi] * v, 1, 0)
            near = near + cys[zi] * rolled(v, -1, 1) + rolled(prod[zi], 1, 1)
            near = near + czs[zi] * v_up[zi] + czds[zi] * v_down[zi]
            qs[zi] = qs[zi] - v + near * invs[zi]
            fresh.append(keep * v + lift * qs[zi])
        vs = fresh

    lane = iota((ext, LANES), 1)
    first_lane, last_lane = lane == 0, lane == LANES - 1

    def whole(ref, rim, z):
        return jnp.concatenate([ref[z], rim[z]], axis=0)

    def turn(w, zi, g):
        return pltpu.roll(w[zi], (2 * LANES - (RIM - 1) - g * GROUP) % LANES, 1)

    @pl.loop(0, groups)
    def _(g):
        for zi in range(zs):
            z = g * zs + zi
            above, below = (z + 1) % nz, (z + nz - 1) % nz
            u, c, s = whole(u_ref, uh, z), whole(c_ref, ch, z), whole(s_ref, sh, z)
            u_up, u_down = whole(u_ref, uh, above), whole(u_ref, uh, below)
            c_up, c_down = whole(c_ref, ch, above), whole(c_ref, ch, below)
            edge_u, edge_c = turn(wu, zi, g), turn(wc, zi, g)
            gx = 0.5 * (c + rolled(c, -1, 0))
            gxl = rolled(gx, 1, 0)
            gy = 0.5 * (c + jnp.where(last_lane, edge_c, rolled(c, -1, 1)))
            gyl = 0.5 * (c + jnp.where(first_lane, edge_c, rolled(c, 1, 1)))
            gz = 0.5 * (c + c_up)
            gzl = 0.5 * (c + c_down)
            diag = SHIFT + (gx + gxl) + (gy + gyl) + (gz + gzl)
            near = gx * rolled(u, -1, 0) + gxl * rolled(u, 1, 0)
            near = near + gy * jnp.where(last_lane, edge_u, rolled(u, -1, 1))
            near = near + gyl * jnp.where(first_lane, edge_u, rolled(u, 1, 1))
            near = near + gz * u_up + gzl * u_down
            inverse = 1.0 / diag
            scaled = (s - diag * u + near) * inverse
            v = scaled * (1.0 / THETA)
            cx[z] = gx
            cy[z] = gy
            cz[z] = gz
            inv[z] = inverse
            q[z] = scaled
            va[z] = v
            o_ref[z] = (u + v)[:nx]

    for k, w in enumerate((w0, w1, w2)):
        old, new = (va, vb) if k % 2 == 0 else (vb, va)
        keep, lift = table[k]

        @pl.loop(0, groups)
        def _(g, w=w, old=old, new=new, keep=keep, lift=lift, final=k == SWEEPS - 1):
            for zi in range(zs):
                z = g * zs + zi
                above, below = (z + 1) % nz, (z + nz - 1) % nz
                v, gx, gy = old[z], cx[z], cy[z]
                edge = turn(w, zi, g)
                near = gx * rolled(v, -1, 0) + rolled(gx * v, 1, 0)
                near = near + gy * jnp.where(last_lane, edge, rolled(v, -1, 1))
                near = near + jnp.where(first_lane, edge, rolled(gy * v, 1, 1))
                near = near + cz[z] * old[above] + cz[below] * old[below]
                scaled = q[z] - v + near * inv[z]
                fresh = keep * v + lift * scaled
                if not final:
                    q[z] = scaled
                    new[z] = fresh
                o_ref[z] = o_ref[z] + fresh[:nx]


def fine(u, s, c, r1, r2, e, el, er, d1l, d1r, d2l, d2r):
    nz, nx, ny = u.shape
    zs = split_z(nz)
    ext = nx + SUB
    full = pltpu.VMEM((nz, ext, LANES), f32)
    rim = pltpu.VMEM((nz, SUB, LANES), f32)
    strip = pltpu.VMEM((zs, ext, LANES), f32)
    return pl.pallas_call(
        fine_kernel,
        out_shape=jax.ShapeDtypeStruct(u.shape, f32),
        in_specs=[VMEM] * 12,
        out_specs=VMEM,
        scratch_shapes=[rim] * 3 + [full] * 7 + [strip] * 5,
        compiler_params=SMALL,
        cost_estimate=pl.CostEstimate(flops=150 * u.size, bytes_accessed=20 * u.size, transcendentals=0),
        name="fine",
    )(u, s, c, r1, r2, e, el, er, d1l, d1r, d2l, d2r)


def finish_kernel(x_ref, m_ref, r1_ref, r2_ref, yl_ref, yr_ref, d1l_ref, d1r_ref, d2l_ref, d2r_ref, o_ref, scr):
    nz, nx, _ = x_ref.shape
    rows = nx // COARSEN
    width = LANES // COARSEN
    spread = 2 * width
    even = is_even()
    lane = iota((SUB, LANES), 1)
    place = lane % spread

    def join(left, own, right):
        return jnp.where(
            place < INNER,
            rolled(left, -width, 1),
            jnp.where(place < INNER + width, own, rolled(right, width, 1)),
        )

    fields = []
    for a in range(3):
        own = join(yl_ref[a], m_ref[a], yr_ref[a])
        near = join(d1l_ref[a], r1_ref[a], d1r_ref[a])
        far = join(d2l_ref[a], r2_ref[a], d2r_ref[a])
        right, left = jnp.where(even, near, far), jnp.where(even, far, near)
        scr[a] = jnp.ones((2 * SUB, LANES), f32)
        scr[a, 0:rows] = left[:rows]
        scr[a, rows : 2 * rows] = own[:rows]
        scr[a, 2 * rows : 3 * rows] = right[:rows]
        fields.append(scr[a])
    start, weight, cond = fields
    half = 0.5 / COARSEN**2
    gx = half * (cond + rolled(cond, -1, 0))
    gy = half * (cond + rolled(cond, -1, 1))
    gz = half * (cond + rolled(cond, -spread, 1))
    v = start
    for _ in range(COARSE_SWEEPS - 1):
        fx = gx * (v - rolled(v, -1, 0))
        fy = gy * (v - rolled(v, -1, 1))
        fz = gz * (v - rolled(v, -spread, 1))
        image = SHIFT * v + (fx - rolled(fx, 1, 0)) + (fy - rolled(fy, 1, 1)) + (fz - rolled(fz, spread, 1))
        v = v + start - weight * image
    top = v[:SUB]
    for Z in range(nz // COARSEN):
        spread_out = jnp.take_along_axis(top, Z * spread + INNER + lane // COARSEN, axis=1)
        for X in range(rows):
            value = jnp.broadcast_to(spread_out[rows + X : rows + X + 1], (COARSEN, LANES))
            for z in range(Z * COARSEN, (Z + 1) * COARSEN):
                at = slice(X * COARSEN, (X + 1) * COARSEN)
                o_ref[z, at] = x_ref[z, at] + value


def finish(x, *messages):
    return pl.pallas_call(
        finish_kernel,
        out_shape=jax.ShapeDtypeStruct(x.shape, f32),
        in_specs=[VMEM] * (1 + len(messages)),
        out_specs=VMEM,
        scratch_shapes=[pltpu.VMEM((3, 2 * SUB, LANES), f32)],
        compiler_params=SMALL,
        name="finish",
    )(x, *messages)


def moves():
    size_x, size_y = lax.axis_size("gx"), lax.axis_size("gy")

    def send(x, go):
        pairs = []
        for i in range(size_x):
            for j in range(size_y):
                k, l = go(i, j)
                pairs.append((i * size_y + j, (k % size_x) * size_y + l % size_y))
        return lax.ppermute(x, ("gx", "gy"), pairs)

    def one(i):
        return i + 1 if i % 2 == 0 else i - 1

    def two(i):
        return i - 1 if i % 2 == 0 else i + 1

    def stay(i):
        return i

    def straight(x, along):
        return send(x, lambda i, j: (along(i), j))

    def across(x, along):
        left = send(x, lambda i, j: (along(i), j + 1))
        if size_y == 2:
            return left, left
        return left, send(x, lambda i, j: (along(i), j - 1))

    return one, two, stay, straight, across


def body(iterate, source, conduct):
    nz, nx, ny = iterate.shape
    one, two, stay, straight, across = moves()
    p1, p2, e, h1, h2 = pack(iterate, source, conduct)
    r2 = straight(p2, two)
    d2l, d2r = across(h2, two)
    el, er = across(e, stay)
    r1 = straight(p1, one)
    d1l, d1r = across(h1, one)
    part = local(iterate, source, conduct)
    m = faces(part, p1, p2, r1, r2, e, el, er, nz, nx)
    x = fine(iterate, source, conduct, r1, r2, e, el, er, d1l, d1r, d2l, d2r)
    m2 = straight(m, two)
    c2l, c2r = across(m, two)
    ml, mr = across(m, stay)
    m1 = straight(m, one)
    c1l, c1r = across(m, one)
    return finish(x, m, m1, m2, ml, mr, c1l, c1r, c2l, c2r)


def solution(mesh):
    spec = P(None, "gx", "gy")
    return jax.shard_map(body, mesh=mesh, in_specs=(spec,) * 3, out_specs=spec, check_vma=False)
```

```python
import functools

import jax
import jax.numpy as jnp
from jax import lax
from jax.experimental import pallas as pl
from jax.experimental.pallas import tpu as pltpu
from jax.sharding import PartitionSpec as P

SWEEPS = 3
COARSE_SWEEPS = 4
COARSEN = 8

SHIFT = 0.1
LMIN = 0.3
LMAX = 2.0
OMEGA = 0.8

THETA = (LMAX + LMIN) / 2.0
DELTA = (LMAX - LMIN) / 2.0
SIGMA = THETA / DELTA

RIM = SWEEPS + 1
SUB = 8
LANES = 128
HALF = LANES // 2
GROUP = 4 * RIM
ZS = LANES // GROUP
WIDTH = LANES // COARSEN
SPREAD = 2 * WIDTH
REACH = (COARSE_SWEEPS - 1) * COARSEN
CELLS = COARSEN**3

f32 = jnp.float32
VMEM = pl.BlockSpec(memory_space=pltpu.VMEM)
SMALL = pltpu.CompilerParams(vmem_limit_bytes=12 * 1024 * 1024)


def steps():
    rho, listed = 1.0 / SIGMA, []
    for _ in range(SWEEPS):
        nxt = 1.0 / (2.0 * SIGMA - rho)
        listed.append((nxt * rho, 2.0 * nxt / DELTA))
        rho = nxt
    return listed


def iota(shape, dim):
    return lax.broadcasted_iota(jnp.int32, shape, dim)


def rolled(x, by, dim):
    return pltpu.roll(x, by % x.shape[dim], dim)


def is_even():
    return lax.axis_index("gx") % 2 == 0


def tiles(count):
    return jax.ShapeDtypeStruct((count * SUB, LANES), f32)


def tile(ref, index):
    return ref[index * SUB : (index + 1) * SUB]


def picked(ref, start, stride):
    return ref[pl.ds(start, SUB, stride=stride), :]


def lane_sums(rows):
    shift = 1
    while shift < COARSEN:
        rows = rows + rolled(rows, -shift, 1)
        shift *= 2
    return rows


def compact(rows, place):
    lane = iota(rows.shape, 1)
    column = lane % SPREAD - RIM
    source = jnp.clip(column * COARSEN, 0, LANES - 1)
    here = (lane // SPREAD == place) & (column >= 0) & (column < WIDTH)
    return jnp.where(here, jnp.take_along_axis(lane_sums(rows), source, axis=1), 0.0)


def block_rows(values):
    sub = iota((SUB, LANES), 0)
    out = jnp.zeros((SUB, LANES), f32)
    for block in range(values.shape[0] // COARSEN):
        part = values[block * COARSEN : (block + 1) * COARSEN]
        out = jnp.where(sub == block, jnp.sum(part, axis=0, keepdims=True), out)
    return out


def all_rows(values):
    return jnp.sum(values, axis=0, keepdims=True)


def pack_kernel(u_hbm, s_hbm, c_hbm, q_ref, a1_ref, a2_ref, r_ref, own_ref, u_ref, s_ref, c_ref, sems, *, nz, nx):
    pieces = sems.shape[1]
    size = nz * nx // pieces
    copies = []
    for k, (source, target) in enumerate(((c_hbm, c_ref), (u_hbm, u_ref), (s_hbm, s_ref))):
        for piece in range(pieces):
            at = pl.ds(piece * size, size)
            copies.append(pltpu.make_async_copy(source.at[at], target.at[at], sems.at[k, piece]))
    for copy in copies:
        copy.start()
    for copy in copies:
        copy.wait()

    even = is_even()
    sub, lane = iota((SUB, LANES), 0), iota((SUB, LANES), 1)
    low = sub < RIM
    row, wide = iota((nx, LANES), 0), iota((nx, LANES), 1)

    def plane(ref, z):
        return ref[z % nz * nx : (z % nz + 1) * nx]

    def up(z):
        return 0.5 * (plane(c_ref, z) + plane(c_ref, z + 1)) * (plane(u_ref, z) - plane(u_ref, z + 1))

    coarse = jnp.zeros((SUB, LANES), f32)
    below = up(nz - 1)
    for Z in range(nz // COARSEN):
        sum_r = sum_c = jnp.zeros((nx, LANES), f32)
        for z in range(Z * COARSEN, (Z + 1) * COARSEN):
            u, c = plane(u_ref, z), plane(c_ref, z)
            above = up(z)
            fx = 0.5 * (c + rolled(c, -1, 0)) * (u - rolled(u, -1, 0))
            fy = 0.5 * (c + rolled(c, -1, 1)) * (u - rolled(u, -1, 1))
            fx = jnp.where(row == nx - 1, 0.0, fx)
            fy = jnp.where(wide == LANES - 1, 0.0, fy)
            r = plane(s_ref, z) - SHIFT * u - (fx - rolled(fx, 1, 0)) - (fy - rolled(fy, 1, 1)) - (above - below)
            below = above
            r_ref[z * nx : (z + 1) * nx] = r
            sum_r = sum_r + r
            sum_c = sum_c + c
            u0, u2, c0, c2 = u[:SUB], u[nx - SUB :], c[:SUB], c[nx - SUB :]
            first = jnp.where(low, c0, jnp.where(sub == SUB - 1, rolled(u0, -1, 0), rolled(r[:SUB], RIM, 0)))
            last = jnp.where(low, jnp.where(sub == 0, rolled(u2, 1, 0), rolled(r[nx - SUB :], RIM, 0)), c2)
            a1_ref[z * SUB : (z + 1) * SUB] = jnp.where(even, last, first)
            a2_ref[z * SUB : (z + 1) * SUB] = jnp.where(even, first, last)
        coarse = coarse + compact(block_rows(sum_r) + rolled(block_rows(sum_c), RIM, 0), Z)
    coarse = coarse * (1.0 / CELLS)

    zs = nz // ZS
    half = zs // 2
    for a, ref in enumerate((u_ref, c_ref, r_ref)):
        for pair in range(half):
            strip = jnp.zeros((nx, LANES), f32)
            for g in range(ZS):
                for second in range(2):
                    at = 2 * g + second
                    moved = rolled(plane(ref, g * zs + pair + second * half), at * 2 * RIM + RIM, 1)
                    strip = jnp.where(wide // (2 * RIM) == at, moved, strip)
            q_ref[(a * half + pair) * nx : (a * half + pair + 1) * nx] = strip

    base = 3 * half * nx
    for a, ref in enumerate((u_ref, c_ref)):
        for Z in range(nz // SUB):
            at = Z * SUB * nx
            first, last = picked(ref, at, nx), picked(ref, at + nx - 1, nx)
            spot = a * nz + Z * SUB
            own_ref[spot : spot + SUB] = first
            own_ref[2 * nz + spot : 2 * nz + spot + SUB] = last
            q_ref[base + spot : base + spot + SUB] = jnp.where(
                lane < HALF, rolled(first, REACH, 1), rolled(last, REACH + HALF, 1)
            )
    q_ref[base + 2 * nz : base + 2 * nz + SUB] = coarse
    a1_ref[nz * SUB :] = coarse


def pack(u, s, c, nz, nx):
    half = nz // ZS // 2
    pieces = 4
    return pl.pallas_call(
        functools.partial(pack_kernel, nz=nz, nx=nx),
        out_shape=(
            tiles(3 * half * nx // SUB + 2 * nz // SUB + 1),
            tiles(nz + 1),
            tiles(nz),
            jax.ShapeDtypeStruct(u.shape, f32),
            tiles(4 * nz // SUB),
        ),
        in_specs=[pl.BlockSpec(memory_space=pltpu.HBM)] * 3,
        out_specs=(VMEM,) * 5,
        scratch_shapes=[pltpu.VMEM(u.shape, f32)] * 3 + [pltpu.SemaphoreType.DMA((3, pieces))],
        compiler_params=SMALL,
        name="pack",
    )(u, s, c)


def facing(own_ref, a, z, nz, last):
    first, second = own_ref[a * nz + z : a * nz + z + SUB], own_ref[(2 + a) * nz + z : (2 + a) * nz + z + SUB]
    return jnp.where(last, second, first)


def opposite(rows_ref, a, z, after):
    first = picked(rows_ref, z * SUB, SUB)
    last = picked(rows_ref, z * SUB + SUB - 1, SUB)
    return jnp.where(after, last, first) if a == 0 else jnp.where(after, first, last)


def flux_between(own_ref, rows_ref, z, nz, after):
    u = facing(own_ref, 0, z, nz, after) - opposite(rows_ref, 0, z, after)
    c = facing(own_ref, 1, z, nz, after) + opposite(rows_ref, 1, z, after)
    return all_rows(0.5 * c * u)


def join_kernel(q_ref, ql_ref, qr_ref, a1_ref, own_ref, b1_ref, b2_ref, strip_ref, *, nz, nx):
    zs = nz // ZS
    half = zs // 2
    even = is_even()
    sub, lane = iota((SUB, LANES), 0), iota((SUB, LANES), 1)
    low = sub < RIM
    spot = iota((nx, LANES), 1) % GROUP
    joined = []
    for a in range(3):
        group = [None] * zs
        for pair in range(half):
            at = slice((a * half + pair) * nx, (a * half + pair + 1) * nx)
            left, own, right = ql_ref[at], q_ref[at], qr_ref[at]
            moved = rolled(jnp.where(spot < RIM, own, right), 2 * RIM, 1)
            one = jnp.where(spot < 2 * RIM, jnp.where(spot < RIM, left, own), moved)
            moved = rolled(jnp.where(spot < 3 * RIM, left, own), -2 * RIM, 1)
            two = jnp.where(spot < 2 * RIM, moved, jnp.where(spot < 3 * RIM, own, right))
            group[pair], group[pair + half] = one, two
            first = jnp.where(low, one[:SUB], rolled(two[:SUB], RIM, 0))
            last = jnp.where(low, rolled(two[nx - SUB :], RIM, 0), one[nx - SUB :])
            to = slice((a * half + pair) * SUB, (a * half + pair + 1) * SUB)
            b1_ref[to] = jnp.where(even, last, first)
            b2_ref[to] = jnp.where(even, first, last)
        for zi in range(zs):
            strip_ref[(a * zs + zi) * nx : (a * zs + zi + 1) * nx] = group[zi]
        joined.append(group)

    source, target = 3 * half * nx, 3 * half * SUB
    for index in range(2 * nz // SUB):
        at = slice(source + index * SUB, source + (index + 1) * SUB)
        both = jnp.where(lane % HALF < REACH, ql_ref[at], qr_ref[at])
        to = slice(target + index * SUB, target + (index + 1) * SUB)
        b1_ref[to] = both
        b2_ref[to] = both

    at = slice(source + 2 * nz, source + 2 * nz + SUB)
    place = lane % SPREAD
    window = jnp.where(
        place < RIM,
        rolled(ql_ref[at], -WIDTH, 1),
        jnp.where(place < RIM + WIDTH, q_ref[at], rolled(qr_ref[at], WIDTH, 1)),
    )
    flux = jnp.zeros((nx, LANES), f32)
    for u, c in zip(joined[0], joined[1]):
        flux = flux + (c + rolled(c, -1, 1)) * (u - rolled(u, -1, 1))
    flux = block_rows((0.5 / CELLS) * flux)
    flux = flux + rolled(flux, -GROUP, 1)
    near, far = RIM - 1, 3 * RIM - 1
    change = jnp.where(place == RIM - 1, -rolled(flux, RIM - 1 - near, 1), 0.0)
    change = jnp.where(place == RIM, rolled(flux, RIM - near, 1), change)
    change = jnp.where(place == RIM + WIDTH - 1, -rolled(flux, RIM + WIDTH - 1 - far, 1), change)
    change = jnp.where(place == RIM + WIDTH, rolled(flux, RIM + WIDTH - far, 1), change)
    rows = nx // COARSEN
    nearest = jnp.where(even, rows - 1, 0)
    for Z in range(nz // COARSEN):
        across = flux_between(own_ref, a1_ref, Z * COARSEN, nz, even) * (1.0 / CELLS)
        change = change - compact(jnp.where(sub == nearest, across, 0.0), Z)
    mate = a1_ref[nz * SUB :]
    mate = jnp.where(even, rolled(mate, rows - RIM, 0), rolled(mate, 1 - RIM, 0))
    cond = jnp.where(sub == rows, mate, rolled(window, -RIM, 0))
    to = target + 2 * nz
    for ref in (b1_ref, b2_ref):
        ref[to : to + SUB] = window + change
        ref[to + SUB : to + 2 * SUB] = cond


def join(q, ql, qr, a1, own, nz, nx):
    zs = nz // ZS
    message = tiles(3 * (zs // 2) + 2 * nz // SUB + 2)
    return pl.pallas_call(
        functools.partial(join_kernel, nz=nz, nx=nx),
        out_shape=(message, message, jax.ShapeDtypeStruct((3 * zs * nx, LANES), f32)),
        in_specs=[VMEM] * 5,
        out_specs=(VMEM,) * 3,
        compiler_params=SMALL,
        name="join",
    )(q, ql, qr, a1, own)


def faces_kernel(own_ref, b_ref, r1_ref, r2_ref, a2_ref, o_ref, *, nz, nx):
    half = nz // ZS // 2
    even = is_even()
    sub, lane = iota((SUB, LANES), 0), iota((SUB, LANES), 1)
    place = lane % SPREAD
    rows = nx // COARSEN
    base = 3 * half * SUB

    outer = REACH // COARSEN
    is_left, is_right = (place >= RIM - outer) & (place < RIM), (place >= RIM + WIDTH) & (place < RIM + WIDTH + outer)
    is_own = (place >= RIM) & (place < RIM + WIDTH)
    source = jnp.where(is_left, place - (RIM - outer), place - (RIM + WIDTH - outer))
    source = jnp.where(sub == 0, place - RIM, source) * COARSEN
    source = jnp.clip(source, 0, LANES - 1)
    valid = ((sub == 0) & is_own) | ((sub > 0) & (is_left | is_right))

    def outside(r_ref, Z, upper):
        def at(ref, a):
            start = base + a * nz + Z * COARSEN
            return ref[start : start + SUB]

        u = at(b_ref, 0) - rolled(at(r_ref, 0), HALF, 1)
        c = at(b_ref, 1) + rolled(at(r_ref, 1), HALF, 1)
        flux = all_rows(0.5 * c * u)
        return jnp.where(upper, rolled(flux, HALF, 1), flux)

    flux = jnp.zeros((SUB, LANES), f32)
    for Z in range(nz // COARSEN):
        one = flux_between(own_ref, a2_ref, Z * COARSEN, nz, jnp.logical_not(even))
        two = outside(r2_ref, Z, jnp.logical_not(even))
        three = outside(r1_ref, Z, even)
        sums = lane_sums(jnp.where(sub == 0, one, jnp.where(sub == 1, two, jnp.where(sub == 2, three, 0.0))))
        here = valid & (lane // SPREAD == Z)
        flux = flux + jnp.where(here, jnp.take_along_axis(sums, source, axis=1), 0.0)
    flux = flux * (1.0 / CELLS)
    far, mate = flux[0:1] + flux[1:2], flux[2:3]

    def stacked(own, other):
        before, after = jnp.where(even, other, own), jnp.where(even, own, other)
        return jnp.where(sub <= rows, rolled(before, 1, 0), rolled(after, rows + 1, 0))

    at = base + 2 * nz
    rhs = stacked(b_ref[at : at + SUB], r2_ref[at : at + SUB])
    sign = jnp.where(even, 1.0, -1.0)
    rhs = rhs + jnp.where(sub == rows, sign * far, jnp.where(sub == rows + 1, -sign * far, 0.0))
    rhs = rhs - jnp.where(sub == jnp.where(even, 2 * rows, 1), mate, 0.0)

    at = at + SUB
    near_c, far_c = r1_ref[at : at + SUB], r2_ref[at : at + SUB]
    cond = stacked(b_ref[at : at + SUB], far_c)
    before = jnp.where(even, rolled(far_c, -rows, 0), rolled(near_c, 1 - rows, 0))
    after = jnp.where(even, rolled(near_c, 2 * rows + 1, 0), rolled(far_c, rows + 1, 0))
    cond = jnp.where(sub == 0, before, jnp.where(sub == 2 * rows + 1, after, cond))
    around = rolled(cond, -1, 0) + rolled(cond, 1, 0) + rolled(cond, -1, 1) + rolled(cond, 1, 1)
    around = around + rolled(cond, -SPREAD, 1) + rolled(cond, SPREAD, 1)
    weight = OMEGA / (SHIFT + (0.5 / COARSEN**2) * (6.0 * cond + around))
    o_ref[0:SUB] = weight * rhs
    o_ref[SUB : 2 * SUB] = weight
    o_ref[2 * SUB :] = cond


def faces(own, b, r1, r2, a2, nz, nx):
    return pl.pallas_call(
        functools.partial(faces_kernel, nz=nz, nx=nx),
        out_shape=tiles(3),
        in_specs=[VMEM] * 5,
        out_specs=VMEM,
        compiler_params=SMALL,
        name="faces",
    )(own, b, r1, r2, a2)


def fine_kernel(
    u_ref, c_ref, r_ref, a1_ref, a2_ref, b1_ref, b2_ref, strip_ref,
    o_ref,
    ch, rh, cx, cy, cz, inv, q, va, vb, acc, wr, w0, w1, w2,
    *, nz, nx,
):
    zs = nz // ZS
    half = zs // 2
    ext = nx + SUB
    even = is_even()
    sub = iota((SUB, LANES), 0)
    low, end = sub < RIM, sub == SUB - 1
    table = steps()

    def sides(one, two):
        return jnp.where(even, one, two), jnp.where(even, two, one)

    for z in range(nz):
        after, before = sides(tile(a1_ref, z), tile(a2_ref, z))
        tile_at = slice(z * SUB, (z + 1) * SUB)
        ch[tile_at] = jnp.where(low, after, before)
        rh[tile_at] = rolled(jnp.where(low, before, after), RIM, 0)

    row, spot = iota((ext, LANES), 0), iota((ext, LANES), 1) % GROUP

    def strips_of(a):
        rims = [None] * zs
        for pair in range(half):
            after, before = sides(tile(b1_ref, a * half + pair), tile(b2_ref, a * half + pair))
            rims[pair] = jnp.where(low, after, before)
            rims[pair + half] = rolled(jnp.where(low, before, after), RIM, 0)
        return [
            jnp.concatenate([strip_ref[(a * zs + zi) * nx : (a * zs + zi + 1) * nx], rims[zi]], axis=0)
            for zi in range(zs)
        ]

    def z_up(x):
        return x[1:] + [rolled(x[0], -GROUP, 1)]

    def z_down(x):
        return [rolled(x[-1], GROUP, 1)] + x[:-1]

    us, cs, rs = strips_of(0), strips_of(1), strips_of(2)
    cxs = [0.5 * (c + rolled(c, -1, 0)) for c in cs]
    cys = [0.5 * (c + rolled(c, -1, 1)) for c in cs]
    czs = [0.5 * (c + d) for c, d in zip(cs, z_up(cs))]
    czds = z_down(czs)
    invs, qs, vs = [], [], []
    for zi in range(zs):
        u = us[zi]
        fx = jnp.where((row == nx - 1) | (row == ext - 1), cxs[zi] * (u - rolled(u, -1, 0)), 0.0)
        fy = jnp.where((spot == RIM - 1) | (spot == 3 * RIM - 1), cys[zi] * (u - rolled(u, -1, 1)), 0.0)
        r = rs[zi] - (fx - rolled(fx, 1, 0)) - (fy - rolled(fy, 1, 1))
        wr[zi * ext : (zi + 1) * ext] = jnp.where(spot == RIM, r, rolled(r, -2 * RIM, 1))
        diag = SHIFT + (cxs[zi] + rolled(cxs[zi], 1, 0)) + (cys[zi] + rolled(cys[zi], 1, 1)) + (czs[zi] + czds[zi])
        invs.append(1.0 / diag)
        qs.append(r * invs[zi])
        vs.append(qs[zi] * (1.0 / THETA))
    for k, w in enumerate((w0, w1, w2)):
        prod = [cys[zi] * vs[zi] for zi in range(zs)]
        for zi in range(zs):
            w[zi * ext : (zi + 1) * ext] = jnp.where(spot == RIM - 1, prod[zi], rolled(vs[zi], -(2 * RIM + 2), 1))
        if k == SWEEPS - 1:
            break
        keep, lift = table[k]
        v_up, v_down = z_up(vs), z_down(vs)
        fresh = []
        for zi in range(zs):
            v = vs[zi]
            near = cxs[zi] * rolled(v, -1, 0) + rolled(cxs[zi] * v, 1, 0)
            near = near + cys[zi] * rolled(v, -1, 1) + rolled(prod[zi], 1, 1)
            near = near + czs[zi] * v_up[zi] + czds[zi] * v_down[zi]
            qs[zi] = qs[zi] - v + near * invs[zi]
            fresh.append(keep * v + lift * qs[zi])
        vs = fresh

    wc = [jnp.where(spot == RIM - 1, c, rolled(c, -(2 * RIM + 2), 1)) for c in cs]

    lane = iota((ext, LANES), 1)
    first_lane, last_lane = lane == 0, lane == LANES - 1
    both_lanes = first_lane | last_lane

    def own(ref, z):
        return ref[z % nz * nx : (z % nz + 1) * nx]

    def long(ref, z):
        return ref[z % nz * ext : (z % nz + 1) * ext]

    def whole(z):
        return jnp.concatenate([own(c_ref, z), tile(ch, z % nz)], axis=0)

    def beside(w, z, column):
        return rolled(w, -column - z // zs * GROUP, 1)

    below = 0.5 * (whole(nz - 1) + whole(0))
    for z in range(nz):
        at = slice(z * ext, (z + 1) * ext)
        c = whole(z)
        edge = beside(wc[z % zs], z, RIM - 1)
        gx = 0.5 * (c + rolled(c, -1, 0))
        gy = 0.5 * (c + jnp.where(last_lane, edge, rolled(c, -1, 1)))
        gyl = 0.5 * (c + jnp.where(first_lane, edge, rolled(c, 1, 1)))
        above = 0.5 * (c + whole(z + 1))
        diag = SHIFT + (gx + rolled(gx, 1, 0)) + (gy + gyl) + (above + below)
        inverse = 1.0 / diag
        r, rim = own(r_ref, z), tile(rh, z)
        u_first, u_last = own(u_ref, z)[:SUB], own(u_ref, z)[nx - SUB :]
        u_rim = jnp.where(sub == 0, rolled(rim, 1 - RIM, 0), rolled(rim, RIM - 1, 0))
        fa = jnp.where(end, gx[nx - SUB : nx] * (u_last - rolled(u_rim, -1, 0)), 0.0)
        fb = jnp.where(end, gx[nx:] * (u_rim - rolled(u_first, -1, 0)), 0.0)
        r = jnp.concatenate(
            [
                r[:SUB] + rolled(fb, 1, 0),
                r[SUB : nx - SUB],
                r[nx - SUB :] - fa,
                rim + rolled(fa, 1, 0) - fb,
            ],
            axis=0,
        )
        zi = z % zs
        r = jnp.where(both_lanes, beside(wr[zi * ext : (zi + 1) * ext], z, RIM), r)
        scaled = r * inverse
        v = scaled * (1.0 / THETA)
        cx[at] = gx
        cy[at] = gy
        cz[at] = above
        inv[at] = inverse
        q[at] = scaled
        va[at] = v
        acc[z * nx : (z + 1) * nx] = v[:nx]
        below = above

    for k, w in enumerate((w0, w1, w2)):
        old, new = (va, vb) if k % 2 == 0 else (vb, va)
        keep, lift = table[k]
        for z in range(nz):
            at = slice(z * ext, (z + 1) * ext)
            zi = z % zs
            v, gx, gy = old[at], cx[at], cy[at]
            edge = beside(w[zi * ext : (zi + 1) * ext], z, RIM - 1)
            near = gx * rolled(v, -1, 0) + rolled(gx * v, 1, 0)
            near = near + gy * jnp.where(last_lane, edge, rolled(v, -1, 1))
            near = near + jnp.where(first_lane, edge, rolled(gy * v, 1, 1))
            near = near + cz[at] * long(old, z + 1) + long(cz, z - 1) * long(old, z - 1)
            scaled = q[at] - v + near * inv[at]
            fresh = keep * v + lift * scaled
            here = slice(z * nx, (z + 1) * nx)
            if k < SWEEPS - 1:
                q[at] = scaled
                new[at] = fresh
                acc[here] = acc[here] + fresh[:nx]
            else:
                o_ref[here] = own(u_ref, z) + (acc[here] + fresh[:nx])


def fine(u, c, r, a1, a2, b1, b2, strips, nz, nx):
    zs = nz // ZS
    ext = nx + SUB
    rim = pltpu.VMEM((nz * SUB, LANES), f32)
    full = pltpu.VMEM((nz * ext, LANES), f32)
    strip = pltpu.VMEM((zs * ext, LANES), f32)
    return pl.pallas_call(
        functools.partial(fine_kernel, nz=nz, nx=nx),
        out_shape=jax.ShapeDtypeStruct(u.shape, f32),
        in_specs=[VMEM] * 8,
        out_specs=VMEM,
        scratch_shapes=[rim] * 2 + [full] * 7 + [pltpu.VMEM(u.shape, f32)] + [strip] * 4,
        compiler_params=SMALL,
        cost_estimate=pl.CostEstimate(flops=150 * u.size, bytes_accessed=20 * u.size, transcendentals=0),
        name="fine",
    )(u, c, r, a1, a2, b1, b2, strips)


def finish_kernel(x_ref, m_ref, r_ref, o_ref, *, nz, nx):
    rows = nx // COARSEN
    even = is_even()
    sub, lane = iota((SUB, LANES), 0), iota((SUB, LANES), 1)
    beyond = sub == jnp.where(even, 2 * rows + 1, 0)
    fields = []
    for a in range(3):
        mine, mate = tile(m_ref, a), tile(r_ref, a)
        mate = jnp.where(even, rolled(mate, 2 * rows, 0), rolled(mate, -2 * rows, 0))
        fields.append(jnp.concatenate([jnp.where(beyond, mate, mine), mate], axis=0))
    start, weight, cond = fields
    scale = 0.5 / COARSEN**2
    gx = scale * (cond + rolled(cond, -1, 0))
    gy = scale * (cond + rolled(cond, -1, 1))
    gz = scale * (cond + rolled(cond, -SPREAD, 1))
    v = start
    for _ in range(COARSE_SWEEPS - 1):
        fx = gx * (v - rolled(v, -1, 0))
        fy = gy * (v - rolled(v, -1, 1))
        fz = gz * (v - rolled(v, -SPREAD, 1))
        image = SHIFT * v + (fx - rolled(fx, 1, 0)) + (fy - rolled(fy, 1, 1)) + (fz - rolled(fz, SPREAD, 1))
        v = v + start - weight * image
    top = v[:SUB]
    top = jnp.where(even, rolled(top, -rows - 1, 0), rolled(top, -1, 0))
    for Z in range(nz // COARSEN):
        spread = jnp.take_along_axis(top, Z * SPREAD + RIM + lane // COARSEN, axis=1)
        for X in range(rows):
            value = jnp.broadcast_to(spread[X : X + 1], (COARSEN, LANES))
            for z in range(Z * COARSEN, (Z + 1) * COARSEN):
                at = slice(z * nx + X * COARSEN, z * nx + (X + 1) * COARSEN)
                o_ref[at] = x_ref[at] + value


def finish(x, m, r, nz, nx):
    return pl.pallas_call(
        functools.partial(finish_kernel, nz=nz, nx=nx),
        out_shape=jax.ShapeDtypeStruct(x.shape, f32),
        in_specs=[VMEM] * 3,
        out_specs=VMEM,
        compiler_params=SMALL,
        name="finish",
    )(x, m, r)


def moves():
    size_x, size_y = lax.axis_size("gx"), lax.axis_size("gy")

    def send(x, go):
        pairs = []
        for i in range(size_x):
            for j in range(size_y):
                k, l = go(i, j)
                pairs.append((i * size_y + j, (k % size_x) * size_y + l % size_y))
        return lax.ppermute(x, ("gx", "gy"), pairs)

    def mate(x):
        return send(x, lambda i, j: (i + 1 if i % 2 == 0 else i - 1, j))

    def far(x):
        return send(x, lambda i, j: (i - 1 if i % 2 == 0 else i + 1, j))

    def sides(x):
        left = send(x, lambda i, j: (i, j + 1))
        if size_y == 2:
            return left, left
        return left, send(x, lambda i, j: (i, j - 1))

    return mate, far, sides


def body(iterate, source, conduct):
    nz, nx, ny = iterate.shape
    if nz != ZS * 4 or ny != LANES or nx != 3 * SUB or lax.axis_size("gx") % 2:
        raise ValueError("shapes")
    mate, far, sides = moves()
    u, s, c = (x.reshape(nz * nx, ny) for x in (iterate, source, conduct))
    q, a1, a2, r, own = pack(u, s, c, nz, nx)
    ql, qr = sides(q)
    ra1 = mate(a1)
    ra2 = far(a2)
    b1, b2, strips = join(q, ql, qr, ra1, own, nz, nx)
    rb2 = far(b2)
    rb1 = mate(b1)
    m = faces(own, b1, rb1, rb2, ra2, nz, nx)
    rm = mate(m)
    x = fine(u, c, r, ra1, ra2, rb1, rb2, strips, nz, nx)
    return finish(x, m, rm, nz, nx).reshape(nz, nx, ny)


def solution(mesh):
    spec = P(None, "gx", "gy")
    return jax.shard_map(body, mesh=mesh, in_specs=(spec,) * 3, out_specs=spec, check_vma=False)
```

```python
import functools

import jax
import jax.numpy as jnp
from jax import lax
from jax.experimental import pallas as pl
from jax.experimental.pallas import tpu as pltpu
from jax.sharding import PartitionSpec as P

SWEEPS = 3
COARSE_SWEEPS = 4
COARSEN = 8

SHIFT = 0.1
LMIN = 0.3
LMAX = 2.0
OMEGA = 0.8

THETA = (LMAX + LMIN) / 2.0
DELTA = (LMAX - LMIN) / 2.0
SIGMA = THETA / DELTA

RIM = SWEEPS + 1
SUB = 8
LANES = 128
HALF = LANES // 2
GROUP = 4 * RIM
ZS = LANES // GROUP
WIDTH = LANES // COARSEN
SPREAD = 2 * WIDTH
REACH = (COARSE_SWEEPS - 1) * COARSEN
CELLS = COARSEN**3

f32 = jnp.float32
VMEM = pl.BlockSpec(memory_space=pltpu.VMEM)
SMALL = pltpu.CompilerParams(vmem_limit_bytes=12 * 1024 * 1024)


def steps():
    rho, listed = 1.0 / SIGMA, []
    for _ in range(SWEEPS):
        nxt = 1.0 / (2.0 * SIGMA - rho)
        listed.append((nxt * rho, 2.0 * nxt / DELTA))
        rho = nxt
    return listed


def iota(shape, dim):
    return lax.broadcasted_iota(jnp.int32, shape, dim)


def part(index, size):
    return lax.shift_right_logical(index, size.bit_length() - 1), lax.bitwise_and(index, size - 1)


def rolled(x, by, dim):
    return pltpu.roll(x, by % x.shape[dim], dim)


def is_even():
    return lax.axis_index("gx") % 2 == 0


def tiles(count):
    return jax.ShapeDtypeStruct((count * SUB, LANES), f32)


def tile(ref, index):
    return ref[index * SUB : (index + 1) * SUB]


def picked(ref, start, stride):
    return ref[pl.ds(start, SUB, stride=stride), :]


def lane_sums(rows):
    shift = 1
    while shift < COARSEN:
        rows = rows + rolled(rows, -shift, 1)
        shift *= 2
    return rows


def compact(rows, place):
    plane, column = part(iota(rows.shape, 1), SPREAD)
    column = column - RIM
    source = jnp.clip(column * COARSEN, 0, LANES - 1)
    here = (plane == place) & (column >= 0) & (column < WIDTH)
    return jnp.where(here, jnp.take_along_axis(lane_sums(rows), source, axis=1), 0.0)


def section(run):
    pl.when(lax.axis_index("gx") >= 0)(run)


def block_rows(values):
    sub = iota((SUB, LANES), 0)
    out = jnp.zeros((SUB, LANES), f32)
    for block in range(values.shape[0] // COARSEN):
        part = values[block * COARSEN : (block + 1) * COARSEN]
        out = jnp.where(sub == block, jnp.sum(part, axis=0, keepdims=True), out)
    return out


def all_rows(values):
    return jnp.sum(values, axis=0, keepdims=True)


def pack_kernel(u_hbm, s_hbm, c_hbm, q_ref, f1_ref, a1_ref, a2_ref, r_ref, own_ref, u_ref, s_ref, c_ref, sems, *, nz, nx):
    pieces = sems.shape[1]
    size = nz * nx // pieces
    copies = []
    for k, (source, target) in enumerate(((c_hbm, c_ref), (u_hbm, u_ref), (s_hbm, s_ref))):
        for piece in range(pieces):
            at = pl.ds(piece * size, size)
            copies.append(pltpu.make_async_copy(source.at[at], target.at[at], sems.at[k, piece]))
    for copy in copies:
        copy.start()
    for copy in copies:
        copy.wait()

    even = is_even()
    sub, lane = iota((SUB, LANES), 0), iota((SUB, LANES), 1)
    low = sub < RIM
    row, wide = iota((nx, LANES), 0), iota((nx, LANES), 1)
    slot = part(wide, 2 * RIM)[0]

    def plane(ref, z):
        return ref[z % nz * nx : (z % nz + 1) * nx]

    def up(z):
        return 0.5 * (plane(c_ref, z) + plane(c_ref, z + 1)) * (plane(u_ref, z) - plane(u_ref, z + 1))

    coarse = jnp.zeros((SUB, LANES), f32)
    below = up(nz - 1)
    for Z in range(nz // COARSEN):
        sum_r = sum_c = jnp.zeros((nx, LANES), f32)
        for z in range(Z * COARSEN, (Z + 1) * COARSEN):
            u, c = plane(u_ref, z), plane(c_ref, z)
            above = up(z)
            fx = 0.5 * (c + rolled(c, -1, 0)) * (u - rolled(u, -1, 0))
            fy = 0.5 * (c + rolled(c, -1, 1)) * (u - rolled(u, -1, 1))
            fx = jnp.where(row == nx - 1, 0.0, fx)
            fy = jnp.where(wide == LANES - 1, 0.0, fy)
            r = plane(s_ref, z) - SHIFT * u - (fx - rolled(fx, 1, 0)) - (fy - rolled(fy, 1, 1)) - (above - below)
            below = above
            r_ref[z * nx : (z + 1) * nx] = r
            sum_r = sum_r + r
            sum_c = sum_c + c
            u0, u2, c0, c2 = u[:SUB], u[nx - SUB :], c[:SUB], c[nx - SUB :]
            first = jnp.where(low, c0, jnp.where(sub == SUB - 1, rolled(u0, -1, 0), rolled(r[:SUB], RIM, 0)))
            last = jnp.where(low, jnp.where(sub == 0, rolled(u2, 1, 0), rolled(r[nx - SUB :], RIM, 0)), c2)
            a1_ref[z * SUB : (z + 1) * SUB] = jnp.where(even, last, first)
            a2_ref[z * SUB : (z + 1) * SUB] = jnp.where(even, first, last)
        coarse = coarse + compact(block_rows(sum_r) + rolled(block_rows(sum_c), RIM, 0), Z)
    coarse = coarse * (1.0 / CELLS)

    zs = nz // ZS
    half = zs // 2
    def strips():
        for a, ref in enumerate((u_ref, c_ref, r_ref)):
            for pair in range(half):
                strip = jnp.zeros((nx, LANES), f32)
                for g in range(ZS):
                    for second in range(2):
                        at = 2 * g + second
                        moved = rolled(plane(ref, g * zs + pair + second * half), at * 2 * RIM + RIM, 1)
                        strip = jnp.where(slot == at, moved, strip)
                q_ref[(a * half + pair) * nx : (a * half + pair + 1) * nx] = strip

    section(strips)

    base = 3 * half * nx
    for a, ref in enumerate((u_ref, c_ref)):
        for Z in range(nz // SUB):
            at = Z * SUB * nx
            first, last = picked(ref, at, nx), picked(ref, at + nx - 1, nx)
            spot = a * nz + Z * SUB
            own_ref[spot : spot + SUB] = first
            own_ref[2 * nz + spot : 2 * nz + spot + SUB] = last
            f1_ref[spot : spot + SUB] = jnp.where(even, last, first)
            q_ref[base + spot : base + spot + SUB] = jnp.where(
                lane < HALF, rolled(first, REACH, 1), rolled(last, REACH + HALF, 1)
            )
    q_ref[base + 2 * nz : base + 2 * nz + SUB] = coarse
    f1_ref[2 * nz :] = coarse


def pack(u, s, c, nz, nx):
    half = nz // ZS // 2
    pieces = 4
    return pl.pallas_call(
        functools.partial(pack_kernel, nz=nz, nx=nx),
        out_shape=(
            tiles(3 * half * nx // SUB + 2 * nz // SUB + 1),
            tiles(2 * nz // SUB + 1),
            tiles(nz),
            tiles(nz),
            jax.ShapeDtypeStruct(u.shape, f32),
            tiles(4 * nz // SUB),
        ),
        in_specs=[pl.BlockSpec(memory_space=pltpu.HBM)] * 3,
        out_specs=(VMEM,) * 6,
        scratch_shapes=[pltpu.VMEM(u.shape, f32)] * 3 + [pltpu.SemaphoreType.DMA((3, pieces))],
        compiler_params=SMALL,
        name="pack",
    )(*(pltpu.with_memory_space_constraint(x, pltpu.HBM) for x in (u, s, c)))


def facing(own_ref, a, z, nz, last):
    first, second = own_ref[a * nz + z : a * nz + z + SUB], own_ref[(2 + a) * nz + z : (2 + a) * nz + z + SUB]
    return jnp.where(last, second, first)


def opposite(rows_ref, a, z, after):
    first = picked(rows_ref, z * SUB, SUB)
    last = picked(rows_ref, z * SUB + SUB - 1, SUB)
    return jnp.where(after, last, first) if a == 0 else jnp.where(after, first, last)


def join_kernel(q_ref, ql_ref, qr_ref, f1_ref, own_ref, b1_ref, b2_ref, strip_ref, *, nz, nx):
    zs = nz // ZS
    half = zs // 2
    even = is_even()
    sub, lane = iota((SUB, LANES), 0), iota((SUB, LANES), 1)
    low = sub < RIM
    spot = part(iota((nx, LANES), 1), GROUP)[1]
    joined = []
    for a in range(3):
        group = [None] * zs
        for pair in range(half):
            at = slice((a * half + pair) * nx, (a * half + pair + 1) * nx)
            left, own, right = ql_ref[at], q_ref[at], qr_ref[at]
            moved = rolled(jnp.where(spot < RIM, own, right), 2 * RIM, 1)
            one = jnp.where(spot < 2 * RIM, jnp.where(spot < RIM, left, own), moved)
            moved = rolled(jnp.where(spot < 3 * RIM, left, own), -2 * RIM, 1)
            two = jnp.where(spot < 2 * RIM, moved, jnp.where(spot < 3 * RIM, own, right))
            group[pair], group[pair + half] = one, two
            first = jnp.where(low, one[:SUB], rolled(two[:SUB], RIM, 0))
            last = jnp.where(low, rolled(two[nx - SUB :], RIM, 0), one[nx - SUB :])
            to = slice((a * half + pair) * SUB, (a * half + pair + 1) * SUB)
            b1_ref[to] = jnp.where(even, last, first)
            b2_ref[to] = jnp.where(even, first, last)
        for zi in range(zs):
            strip_ref[(a * zs + zi) * nx : (a * zs + zi + 1) * nx] = group[zi]
        joined.append(group)

    source, target = 3 * half * nx, 3 * half * SUB
    for index in range(2 * nz // SUB):
        at = slice(source + index * SUB, source + (index + 1) * SUB)
        both = jnp.where(part(lane, HALF)[1] < REACH, ql_ref[at], qr_ref[at])
        to = slice(target + index * SUB, target + (index + 1) * SUB)
        b1_ref[to] = both
        b2_ref[to] = both

    at = slice(source + 2 * nz, source + 2 * nz + SUB)
    place = part(lane, SPREAD)[1]
    window = jnp.where(
        place < RIM,
        rolled(ql_ref[at], -WIDTH, 1),
        jnp.where(place < RIM + WIDTH, q_ref[at], rolled(qr_ref[at], WIDTH, 1)),
    )
    flux = jnp.zeros((nx, LANES), f32)
    for u, c in zip(joined[0], joined[1]):
        flux = flux + (c + rolled(c, -1, 1)) * (u - rolled(u, -1, 1))
    flux = block_rows((0.5 / CELLS) * flux)
    flux = flux + rolled(flux, -GROUP, 1)
    near, far = RIM - 1, 3 * RIM - 1
    change = jnp.where(place == RIM - 1, -rolled(flux, RIM - 1 - near, 1), 0.0)
    change = jnp.where(place == RIM, rolled(flux, RIM - near, 1), change)
    change = jnp.where(place == RIM + WIDTH - 1, -rolled(flux, RIM + WIDTH - 1 - far, 1), change)
    change = jnp.where(place == RIM + WIDTH, rolled(flux, RIM + WIDTH - far, 1), change)
    rows = nx // COARSEN
    nearest = jnp.where(even, rows - 1, 0)
    for Z in range(nz // COARSEN):
        u, c = facing(own_ref, 0, Z * SUB, nz, even) - tile(f1_ref, Z), facing(own_ref, 1, Z * SUB, nz, even)
        across = all_rows((0.5 / CELLS) * (c + tile(f1_ref, nz // SUB + Z)) * u)
        change = change - compact(jnp.where(sub == nearest, across, 0.0), Z)
    mate = f1_ref[2 * nz :]
    mate = jnp.where(even, rolled(mate, rows - RIM, 0), rolled(mate, 1 - RIM, 0))
    cond = jnp.where(sub == rows, mate, rolled(window, -RIM, 0))
    to = target + 2 * nz
    for ref in (b1_ref, b2_ref):
        ref[to : to + SUB] = cond
    b2_ref[to + SUB : to + 2 * SUB] = window + change


def join(q, ql, qr, f1, own, nz, nx):
    zs = nz // ZS
    size = 3 * (zs // 2) + 2 * nz // SUB + 1
    return pl.pallas_call(
        functools.partial(join_kernel, nz=nz, nx=nx),
        out_shape=(tiles(size), tiles(size + 1), jax.ShapeDtypeStruct((3 * zs * nx, LANES), f32)),
        in_specs=[VMEM] * 5,
        out_specs=(VMEM,) * 3,
        compiler_params=SMALL,
        name="join",
    )(q, ql, qr, f1, own)


def faces_kernel(own_ref, b_ref, r2_ref, r1_ref, a2_ref, after_ref, o_ref, *, nz, nx):
    del after_ref
    half = nz // ZS // 2
    even = is_even()
    sub, lane = iota((SUB, LANES), 0), iota((SUB, LANES), 1)
    plane, place = part(lane, SPREAD)
    rows = nx // COARSEN
    base = 3 * half * SUB

    outer = REACH // COARSEN
    is_left, is_right = (place >= RIM - outer) & (place < RIM), (place >= RIM + WIDTH) & (place < RIM + WIDTH + outer)
    is_own = (place >= RIM) & (place < RIM + WIDTH)
    source = jnp.where(is_left, place - (RIM - outer), place - (RIM + WIDTH - outer))
    source = jnp.where(sub == 0, place - RIM, source) * COARSEN
    source = jnp.clip(source, 0, LANES - 1)
    valid = ((sub == 0) & is_own) | ((sub > 0) & (is_left | is_right))

    def outside(r_ref, Z, upper):
        def at(ref, a):
            start = base + a * nz + Z * COARSEN
            return ref[start : start + SUB]

        u = at(b_ref, 0) - rolled(at(r_ref, 0), HALF, 1)
        c = at(b_ref, 1) + rolled(at(r_ref, 1), HALF, 1)
        flux = all_rows(0.5 * c * u)
        return jnp.where(upper, rolled(flux, HALF, 1), flux)

    flux = jnp.zeros((SUB, LANES), f32)
    for Z in range(nz // COARSEN):
        after = jnp.logical_not(even)
        u = facing(own_ref, 0, Z * SUB, nz, after) - opposite(a2_ref, 0, Z * SUB, after)
        c = facing(own_ref, 1, Z * SUB, nz, after) + opposite(a2_ref, 1, Z * SUB, after)
        one = all_rows(0.5 * c * u)
        two = outside(r2_ref, Z, jnp.logical_not(even))
        three = outside(r1_ref, Z, even)
        sums = lane_sums(jnp.where(sub == 0, one, jnp.where(sub == 1, two, jnp.where(sub == 2, three, 0.0))))
        here = valid & (plane == Z)
        flux = flux + jnp.where(here, jnp.take_along_axis(sums, source, axis=1), 0.0)
    flux = flux * (1.0 / CELLS)
    far, mate = flux[0:1] + flux[1:2], flux[2:3]

    def stacked(own, other):
        before, after = jnp.where(even, other, own), jnp.where(even, own, other)
        return jnp.where(sub <= rows, rolled(before, 1, 0), rolled(after, rows + 1, 0))

    at = base + 2 * nz + SUB
    rhs = stacked(b_ref[at : at + SUB], r2_ref[at : at + SUB])
    sign = jnp.where(even, 1.0, -1.0)
    rhs = rhs + jnp.where(sub == rows, sign * far, jnp.where(sub == rows + 1, -sign * far, 0.0))
    rhs = rhs - jnp.where(sub == jnp.where(even, 2 * rows, 1), mate, 0.0)

    at = at - SUB
    near_c, far_c = r1_ref[at : at + SUB], r2_ref[at : at + SUB]
    cond = stacked(b_ref[at : at + SUB], far_c)
    before = jnp.where(even, rolled(far_c, -rows, 0), rolled(near_c, 1 - rows, 0))
    after = jnp.where(even, rolled(near_c, 2 * rows + 1, 0), rolled(far_c, rows + 1, 0))
    cond = jnp.where(sub == 0, before, jnp.where(sub == 2 * rows + 1, after, cond))
    around = rolled(cond, -1, 0) + rolled(cond, 1, 0) + rolled(cond, -1, 1) + rolled(cond, 1, 1)
    around = around + rolled(cond, -SPREAD, 1) + rolled(cond, SPREAD, 1)
    weight = OMEGA / (SHIFT + (0.5 / COARSEN**2) * (6.0 * cond + around))
    o_ref[0:SUB] = weight * rhs
    o_ref[SUB : 2 * SUB] = weight
    o_ref[2 * SUB :] = cond


def faces(own, b, r2, r1, a2, after, nz, nx):
    return pl.pallas_call(
        functools.partial(faces_kernel, nz=nz, nx=nx),
        out_shape=tiles(3),
        in_specs=[VMEM] * 5 + [pl.BlockSpec(memory_space=pl.ANY)],
        out_specs=VMEM,
        compiler_params=SMALL,
        name="faces",
    )(own, b, r2, r1, a2, after)


def sides(even, one, two):
    return jnp.where(even, one, two), jnp.where(even, two, one)


def rim_of(even, low, one, two):
    after, before = sides(even, one, two)
    return jnp.where(low, after, before), rolled(jnp.where(low, before, after), RIM, 0)


def rim_faces(sub, face, rim_face, u_first, u_last, rim):
    u_rim = jnp.where(sub == 0, rolled(rim, 1 - RIM, 0), rolled(rim, RIM - 1, 0))
    end = sub == SUB - 1
    after = jnp.where(end, face * (u_last - rolled(u_rim, -1, 0)), 0.0)
    before = jnp.where(end, rim_face * (u_rim - rolled(u_first, -1, 0)), 0.0)
    return after, before


def beside(w, z, zs, column):
    return rolled(w, -column - z // zs * GROUP, 1)


def window(spot, left, right, column):
    return jnp.where(spot == RIM - 1, left, rolled(right, RIM - 2 - column, 1))


def begin_kernel(
    strip_ref, a1_ref, a2_ref, u_ref, c_ref, r_ref, cx_ref, cy_ref, cz_ref, inv_ref, q_ref, v_ref, ch, *, nz, nx
):
    zs = nz // ZS
    even = is_even()
    sub = iota((SUB, LANES), 0)
    low = sub < RIM
    spot = part(iota((nx, LANES), 1), GROUP)[1]
    lane = iota((nx, LANES), 1)
    first_lane, last_lane = lane == 0, lane == LANES - 1
    rims = []
    for z in range(nz):
        cond, rim = rim_of(even, low, tile(a1_ref, z), tile(a2_ref, z))
        ch[z * SUB : (z + 1) * SUB] = cond
        rims.append(rim)

    def strip(a, zi):
        return strip_ref[(a * zs + zi) * nx : (a * zs + zi + 1) * nx]

    edge_c, edge_f = [], []
    for zi in range(zs):
        u, c = strip(0, zi), strip(1, zi)
        flux = 0.5 * (c + rolled(c, -1, 1)) * (u - rolled(u, -1, 1))
        edge_c.append(window(spot, c, c, 3 * RIM))
        edge_f.append(window(spot, flux, flux, 3 * RIM - 1))

    def own(ref, z):
        return ref[z % nz * nx : (z % nz + 1) * nx]

    below = 0.5 * (own(c_ref, -1) + own(c_ref, 0))
    for z in range(nz):
        at = slice(z * nx, (z + 1) * nx)
        u, c = own(u_ref, z), own(c_ref, z)
        whole = jnp.concatenate([c, tile(ch, z)], axis=0)
        gx = 0.5 * (whole + rolled(whole, -1, 0))
        gxl = rolled(gx, 1, 0)[:nx]
        edge = beside(edge_c[z % zs], z, zs, RIM - 1)
        gy = 0.5 * (c + jnp.where(last_lane, edge, rolled(c, -1, 1)))
        gyl = 0.5 * (c + jnp.where(first_lane, edge, rolled(c, 1, 1)))
        above = 0.5 * (c + own(c_ref, z + 1))
        inverse = 1.0 / (SHIFT + (gx[:nx] + gxl) + (gy + gyl) + (above + below))
        after, before = rim_faces(sub, gx[nx - SUB : nx], gx[nx:], u[:SUB], u[nx - SUB :], rims[z])
        r = own(r_ref, z)
        r = jnp.concatenate([r[:SUB] + rolled(before, 1, 0), r[SUB : nx - SUB], r[nx - SUB :] - after], axis=0)
        edge = beside(edge_f[z % zs], z, zs, RIM - 1)
        r = r + jnp.where(first_lane, edge, jnp.where(last_lane, -edge, 0.0))
        scaled = r * inverse
        cx_ref[at] = gx[:nx]
        cy_ref[at] = gy
        cz_ref[at] = above
        inv_ref[at] = inverse
        q_ref[at] = scaled
        v_ref[at] = scaled * (1.0 / THETA)
        below = above


def begin(strips, a1, a2, u, c, r, nz, nx):
    return pl.pallas_call(
        functools.partial(begin_kernel, nz=nz, nx=nx),
        out_shape=(jax.ShapeDtypeStruct(u.shape, f32),) * 6,
        in_specs=[VMEM] * 6,
        out_specs=(VMEM,) * 6,
        scratch_shapes=[pltpu.VMEM((nz * SUB, LANES), f32)],
        compiler_params=SMALL,
        cost_estimate=pl.CostEstimate(flops=40 * u.size, bytes_accessed=40 * u.size, transcendentals=0),
        name="begin",
    )(strips, a1, a2, u, c, r)


def fine_kernel(
    strip_ref, b2_ref, b1_ref, a1_ref, a2_ref, u_ref, c_ref, cx_ref, cy_ref, cz_ref, inv_ref, q_ref, v_ref,
    o_ref,
    ch, cxh, cyh, czh, invh, qh, vh, q, va, vb, acc, wr, w0, w1, w2,
    *, nz, nx,
):
    zs = nz // ZS
    half = zs // 2
    ext = nx + SUB
    even = is_even()
    sub = iota((SUB, LANES), 0)
    low, end = sub < RIM, sub == SUB - 1
    table = steps()

    rims = []
    for z in range(nz):
        cond, rim = rim_of(even, low, tile(a1_ref, z), tile(a2_ref, z))
        ch[z * SUB : (z + 1) * SUB] = cond
        rims.append(rim)

    row, spot = iota((ext, LANES), 0), part(iota((ext, LANES), 1), GROUP)[1]

    def strips_of(a):
        ends = [None] * zs
        for pair in range(half):
            index = a * half + pair
            ends[pair], ends[pair + half] = rim_of(even, low, tile(b1_ref, index), tile(b2_ref, index))
        return [
            jnp.concatenate([strip_ref[(a * zs + zi) * nx : (a * zs + zi + 1) * nx], ends[zi]], axis=0)
            for zi in range(zs)
        ]

    def z_up(x):
        return x[1:] + [rolled(x[0], -GROUP, 1)]

    def z_down(x):
        return [rolled(x[-1], GROUP, 1)] + x[:-1]

    us, cs, rs = strips_of(0), strips_of(1), strips_of(2)
    cxs = [0.5 * (c + rolled(c, -1, 0)) for c in cs]
    cys = [0.5 * (c + rolled(c, -1, 1)) for c in cs]
    czs = [0.5 * (c + d) for c, d in zip(cs, z_up(cs))]
    czds = z_down(czs)
    invs, qs, vs = [], [], []
    for zi in range(zs):
        u = us[zi]
        fx = jnp.where((row == nx - 1) | (row == ext - 1), cxs[zi] * (u - rolled(u, -1, 0)), 0.0)
        fy = jnp.where((spot == RIM - 1) | (spot == 3 * RIM - 1), cys[zi] * (u - rolled(u, -1, 1)), 0.0)
        r = rs[zi] - (fx - rolled(fx, 1, 0)) - (fy - rolled(fy, 1, 1))
        wr[zi * SUB : (zi + 1) * SUB] = jnp.where(spot == RIM, r, rolled(r, -2 * RIM, 1))[nx:]
        diag = SHIFT + (cxs[zi] + rolled(cxs[zi], 1, 0)) + (cys[zi] + rolled(cys[zi], 1, 1)) + (czs[zi] + czds[zi])
        invs.append(1.0 / diag)
        qs.append(r * invs[zi])
        vs.append(qs[zi] * (1.0 / THETA))
    for k, w in enumerate((w0, w1, w2)):
        prod = [cys[zi] * vs[zi] for zi in range(zs)]
        for zi in range(zs):
            w[zi * ext : (zi + 1) * ext] = window(spot, prod[zi], vs[zi], 3 * RIM)
        if k == SWEEPS - 1:
            break
        keep, lift = table[k]
        v_up, v_down = z_up(vs), z_down(vs)
        fresh = []
        for zi in range(zs):
            v = vs[zi]
            near = cxs[zi] * rolled(v, -1, 0) + rolled(cxs[zi] * v, 1, 0)
            near = near + cys[zi] * rolled(v, -1, 1) + rolled(prod[zi], 1, 1)
            near = near + czs[zi] * v_up[zi] + czds[zi] * v_down[zi]
            qs[zi] = qs[zi] - v + near * invs[zi]
            fresh.append(keep * v + lift * qs[zi])
        vs = fresh
    edge_c = [window(spot, c, c, 3 * RIM)[nx:] for c in cs]

    lane = iota((SUB, LANES), 1)
    first_lane, last_lane = lane == 0, lane == LANES - 1

    def own(ref, z):
        return ref[z % nz * nx : (z % nz + 1) * nx]

    def rim_at(ref, z):
        return tile(ref, z % nz)

    below = 0.5 * (rim_at(ch, -1) + rim_at(ch, 0))
    for z in range(nz):
        at = slice(z * SUB, (z + 1) * SUB)
        u, c = own(u_ref, z), tile(ch, z)
        zi = z % zs
        face = own(cx_ref, z)[nx - SUB :]
        gx = 0.5 * (c + jnp.where(end, rolled(own(c_ref, z)[:SUB], -1, 0), rolled(c, -1, 0)))
        gxl = jnp.where(sub == 0, rolled(face, 1, 0), rolled(gx, 1, 0))
        edge = beside(edge_c[zi], z, zs, RIM - 1)
        gy = 0.5 * (c + jnp.where(last_lane, edge, rolled(c, -1, 1)))
        gyl = 0.5 * (c + jnp.where(first_lane, edge, rolled(c, 1, 1)))
        above = 0.5 * (c + rim_at(ch, z + 1))
        inverse = 1.0 / (SHIFT + (gx + gxl) + (gy + gyl) + (above + below))
        after, before = rim_faces(sub, face, gx, u[:SUB], u[nx - SUB :], rims[z])
        r = rims[z] + rolled(after, 1, 0) - before
        r = jnp.where(first_lane | last_lane, beside(wr[zi * SUB : (zi + 1) * SUB], z, zs, RIM), r)
        scaled = r * inverse
        cxh[at] = gx
        cyh[at] = gy
        czh[at] = above
        invh[at] = inverse
        qh[at] = scaled
        vh[at] = scaled * (1.0 / THETA)
        below = above

    lane = iota((ext, LANES), 1)
    first_lane, last_lane = lane == 0, lane == LANES - 1

    def whole(ref, rim, z):
        return jnp.concatenate([own(ref, z), rim_at(rim, z)], axis=0)

    def long(ref, z):
        return ref[z % nz * ext : (z % nz + 1) * ext]

    for k, w in enumerate((w0, w1, w2)):
        old, new = (va, vb) if k % 2 else (vb, va)
        keep, lift = table[k]

        def at_z(z, k=k, old=old):
            return whole(v_ref, vh, z) if k == 0 else long(old, z)

        for z in range(nz):
            at, here = slice(z * ext, (z + 1) * ext), slice(z * nx, (z + 1) * nx)
            zi = z % zs
            v, gx, gy = at_z(z), whole(cx_ref, cxh, z), whole(cy_ref, cyh, z)
            edge = beside(w[zi * ext : (zi + 1) * ext], z, zs, RIM - 1)
            near = gx * rolled(v, -1, 0) + rolled(gx * v, 1, 0)
            near = near + gy * jnp.where(last_lane, edge, rolled(v, -1, 1))
            near = near + jnp.where(first_lane, edge, rolled(gy * v, 1, 1))
            near = near + whole(cz_ref, czh, z) * at_z(z + 1) + whole(cz_ref, czh, z - 1) * at_z(z - 1)
            scaled = (whole(q_ref, qh, z) if k == 0 else q[at]) - v + near * whole(inv_ref, invh, z)
            fresh = keep * v + lift * scaled
            total = (v[:nx] if k == 0 else acc[here]) + fresh[:nx]
            if k < SWEEPS - 1:
                q[at] = scaled
                new[at] = fresh
                acc[here] = total
            else:
                o_ref[here] = own(u_ref, z) + total


def fine(strips, b2, b1, a1, a2, u, c, begun, nz, nx):
    zs = nz // ZS
    ext = nx + SUB
    rim = pltpu.VMEM((nz * SUB, LANES), f32)
    full = pltpu.VMEM((nz * ext, LANES), f32)
    strip = pltpu.VMEM((zs * ext, LANES), f32)
    return pl.pallas_call(
        functools.partial(fine_kernel, nz=nz, nx=nx),
        out_shape=jax.ShapeDtypeStruct(u.shape, f32),
        in_specs=[VMEM] * 13,
        out_specs=VMEM,
        scratch_shapes=[rim] * 7 + [full] * 3 + [pltpu.VMEM(u.shape, f32), pltpu.VMEM((zs * SUB, LANES), f32)] + [strip] * 3,
        compiler_params=SMALL,
        cost_estimate=pl.CostEstimate(flops=100 * u.size, bytes_accessed=40 * u.size, transcendentals=0),
        name="fine",
    )(strips, b2, b1, a1, a2, u, c, *begun)


def finish_kernel(x_ref, m_ref, r_ref, o_ref, *, nz, nx):
    rows = nx // COARSEN
    even = is_even()
    sub, lane = iota((SUB, LANES), 0), iota((SUB, LANES), 1)
    beyond = sub == jnp.where(even, 2 * rows + 1, 0)
    fields = []
    for a in range(3):
        mine, mate = tile(m_ref, a), tile(r_ref, a)
        mate = jnp.where(even, rolled(mate, 2 * rows, 0), rolled(mate, -2 * rows, 0))
        fields.append(jnp.concatenate([jnp.where(beyond, mate, mine), mate], axis=0))
    start, weight, cond = fields
    scale = 0.5 / COARSEN**2
    gx = scale * (cond + rolled(cond, -1, 0))
    gy = scale * (cond + rolled(cond, -1, 1))
    gz = scale * (cond + rolled(cond, -SPREAD, 1))
    v = start
    for _ in range(COARSE_SWEEPS - 1):
        fx = gx * (v - rolled(v, -1, 0))
        fy = gy * (v - rolled(v, -1, 1))
        fz = gz * (v - rolled(v, -SPREAD, 1))
        image = SHIFT * v + (fx - rolled(fx, 1, 0)) + (fy - rolled(fy, 1, 1)) + (fz - rolled(fz, SPREAD, 1))
        v = v + start - weight * image
    top = v[:SUB]
    top = jnp.where(even, rolled(top, -rows - 1, 0), rolled(top, -1, 0))
    for Z in range(nz // COARSEN):
        spread = jnp.take_along_axis(top, Z * SPREAD + RIM + part(lane, COARSEN)[0], axis=1)
        for X in range(rows):
            value = jnp.broadcast_to(spread[X : X + 1], (COARSEN, LANES))
            for z in range(Z * COARSEN, (Z + 1) * COARSEN):
                at = slice(z * nx + X * COARSEN, z * nx + (X + 1) * COARSEN)
                o_ref[at] = x_ref[at] + value


def finish(x, m, r, nz, nx):
    return pl.pallas_call(
        functools.partial(finish_kernel, nz=nz, nx=nx),
        out_shape=jax.ShapeDtypeStruct(x.shape, f32),
        in_specs=[VMEM] * 3,
        out_specs=VMEM,
        compiler_params=SMALL,
        name="finish",
    )(x, m, r)


def moves():
    size_x, size_y = lax.axis_size("gx"), lax.axis_size("gy")

    def send(x, go):
        pairs = []
        for i in range(size_x):
            for j in range(size_y):
                k, l = go(i, j)
                pairs.append((i * size_y + j, (k % size_x) * size_y + l % size_y))
        return lax.ppermute(x, ("gx", "gy"), pairs)

    def mate(x):
        return send(x, lambda i, j: (i + 1 if i % 2 == 0 else i - 1, j))

    def far(x):
        return send(x, lambda i, j: (i - 1 if i % 2 == 0 else i + 1, j))

    def beside_y(x):
        left = send(x, lambda i, j: (i, j + 1))
        if size_y == 2:
            return left, left
        return left, send(x, lambda i, j: (i, j - 1))

    return mate, far, beside_y


def body(iterate, source, conduct):
    nz, nx, ny = iterate.shape
    if nz != ZS * 4 or ny != LANES or nx != 3 * SUB or lax.axis_size("gx") % 2:
        raise ValueError("shapes")
    mate, far, beside_y = moves()
    u, s, c = (x.reshape(nz * nx, ny) for x in (iterate, source, conduct))
    q, f1, a1, a2, r, own = pack(u, s, c, nz, nx)
    ql, qr = beside_y(q)
    rf1 = mate(f1)
    ra2 = far(a2)
    ra1 = mate(a1)
    b1, b2, strips = join(q, ql, qr, rf1, own, nz, nx)
    rb2 = far(b2)
    rb1 = mate(b1)
    begun = begin(strips, ra1, ra2, u, c, r, nz, nx)
    m = faces(own, b2, rb2, rb1, ra2, begun[0], nz, nx)
    rm = mate(m)
    x = fine(strips, rb2, rb1, ra1, ra2, u, c, begun, nz, nx)
    return finish(x, m, rm, nz, nx).reshape(nz, nx, ny)


def solution(mesh):
    spec = P(None, "gx", "gy")
    return jax.shard_map(body, mesh=mesh, in_specs=(spec,) * 3, out_specs=spec, check_vma=False)
```

```python
import functools

import jax
import jax.numpy as jnp
from jax import lax
from jax.experimental import pallas as pl
from jax.experimental.pallas import tpu as pltpu
from jax.sharding import PartitionSpec as P

SWEEPS = 3
COARSE_SWEEPS = 4
COARSEN = 8

SHIFT = 0.1
LMIN = 0.3
LMAX = 2.0
OMEGA = 0.8

THETA = (LMAX + LMIN) / 2.0
DELTA = (LMAX - LMIN) / 2.0
SIGMA = THETA / DELTA

RIM = SWEEPS + 1
SUB = 8
LANES = 128
HALF = LANES // 2
GROUP = 4 * RIM
ZS = LANES // GROUP
WIDTH = LANES // COARSEN
SPREAD = 2 * WIDTH
REACH = (COARSE_SWEEPS - 1) * COARSEN
CELLS = COARSEN**3

f32 = jnp.float32
VMEM = pl.BlockSpec(memory_space=pltpu.VMEM)
SMALL = pltpu.CompilerParams(vmem_limit_bytes=12 * 1024 * 1024)


def steps():
    rho, listed = 1.0 / SIGMA, []
    for _ in range(SWEEPS):
        nxt = 1.0 / (2.0 * SIGMA - rho)
        listed.append((nxt * rho, 2.0 * nxt / DELTA))
        rho = nxt
    return listed


def iota(shape, dim):
    return lax.broadcasted_iota(jnp.int32, shape, dim)


def part(index, size):
    return lax.shift_right_logical(index, size.bit_length() - 1), lax.bitwise_and(index, size - 1)


def rolled(x, by, dim):
    return pltpu.roll(x, by % x.shape[dim], dim)


def is_even():
    return lax.axis_index("gx") % 2 == 0


def tiles(count):
    return jax.ShapeDtypeStruct((count * SUB, LANES), f32)


def tile(ref, index):
    return ref[index * SUB : (index + 1) * SUB]


def picked(ref, start, stride):
    return ref[pl.ds(start, SUB, stride=stride), :]


def lane_sums(rows):
    shift = 1
    while shift < COARSEN:
        rows = rows + rolled(rows, -shift, 1)
        shift *= 2
    return rows


def compact(rows, place):
    plane, column = part(iota(rows.shape, 1), SPREAD)
    column = column - RIM
    source = jnp.clip(column * COARSEN, 0, LANES - 1)
    here = (plane == place) & (column >= 0) & (column < WIDTH)
    return jnp.where(here, jnp.take_along_axis(lane_sums(rows), source, axis=1), 0.0)


def section(run):
    pl.when(lax.axis_index("gx") >= 0)(run)


def block_rows(values):
    sub = iota((SUB, LANES), 0)
    out = jnp.zeros((SUB, LANES), f32)
    for block in range(values.shape[0] // COARSEN):
        part = values[block * COARSEN : (block + 1) * COARSEN]
        out = jnp.where(sub == block, jnp.sum(part, axis=0, keepdims=True), out)
    return out


def all_rows(values):
    return jnp.sum(values, axis=0, keepdims=True)


def pack_kernel(
    u_hbm, s_hbm, c_hbm, q_ref, f1_ref, last_ref, one_ref, two_ref, r_ref, own_ref, u_ref, s_ref, c_ref, sems, *, nz, nx
):
    pieces = sems.shape[1]
    size = nz * nx // pieces
    copies = []
    for k, (source, target) in enumerate(((c_hbm, c_ref), (u_hbm, u_ref), (s_hbm, s_ref))):
        for piece in range(pieces):
            at = pl.ds(piece * size, size)
            copies.append(pltpu.make_async_copy(source.at[at], target.at[at], sems.at[k, piece]))
    for copy in copies:
        copy.start()
    for copy in copies:
        copy.wait()

    even = is_even()
    sub, lane = iota((SUB, LANES), 0), iota((SUB, LANES), 1)
    low = sub < RIM
    row, wide = iota((nx, LANES), 0), iota((nx, LANES), 1)
    slot = part(wide, 2 * RIM)[0]

    def plane(ref, z):
        return ref[z % nz * nx : (z % nz + 1) * nx]

    def up(z):
        return 0.5 * (plane(c_ref, z) + plane(c_ref, z + 1)) * (plane(u_ref, z) - plane(u_ref, z + 1))

    coarse = jnp.zeros((SUB, LANES), f32)
    below = up(nz - 1)
    for Z in range(nz // COARSEN):
        sum_r = sum_c = jnp.zeros((nx, LANES), f32)
        for z in range(Z * COARSEN, (Z + 1) * COARSEN):
            u, c = plane(u_ref, z), plane(c_ref, z)
            above = up(z)
            fx = 0.5 * (c + rolled(c, -1, 0)) * (u - rolled(u, -1, 0))
            fy = 0.5 * (c + rolled(c, -1, 1)) * (u - rolled(u, -1, 1))
            fx = jnp.where(row == nx - 1, 0.0, fx)
            fy = jnp.where(wide == LANES - 1, 0.0, fy)
            r = plane(s_ref, z) - SHIFT * u - (fx - rolled(fx, 1, 0)) - (fy - rolled(fy, 1, 1)) - (above - below)
            below = above
            r_ref[z * nx : (z + 1) * nx] = r
            sum_r = sum_r + r
            sum_c = sum_c + c
            u0, u2, c0, c2 = u[:SUB], u[nx - SUB :], c[:SUB], c[nx - SUB :]
            first = jnp.where(low, c0, jnp.where(sub == SUB - 1, rolled(u0, -1, 0), rolled(r[:SUB], RIM, 0)))
            last = jnp.where(low, jnp.where(sub == 0, rolled(u2, 1, 0), rolled(r[nx - SUB :], RIM, 0)), c2)
            last_ref[z * SUB : (z + 1) * SUB] = last
            to = z % (nz // 2) * SUB
            (one_ref if z < nz // 2 else two_ref)[to : to + SUB] = first
        coarse = coarse + compact(block_rows(sum_r) + rolled(block_rows(sum_c), RIM, 0), Z)
    coarse = coarse * (1.0 / CELLS)

    zs = nz // ZS
    half = zs // 2
    def strips():
        for a, ref in enumerate((u_ref, c_ref, r_ref)):
            for pair in range(half):
                strip = jnp.zeros((nx, LANES), f32)
                for g in range(ZS):
                    for second in range(2):
                        at = 2 * g + second
                        moved = rolled(plane(ref, g * zs + pair + second * half), at * 2 * RIM + RIM, 1)
                        strip = jnp.where(slot == at, moved, strip)
                q_ref[(a * half + pair) * nx : (a * half + pair + 1) * nx] = strip

    section(strips)

    base = 3 * half * nx
    for a, ref in enumerate((u_ref, c_ref)):
        for Z in range(nz // SUB):
            at = Z * SUB * nx
            first, last = picked(ref, at, nx), picked(ref, at + nx - 1, nx)
            spot = a * nz + Z * SUB
            own_ref[spot : spot + SUB] = first
            own_ref[2 * nz + spot : 2 * nz + spot + SUB] = last
            f1_ref[spot : spot + SUB] = jnp.where(even, last, first)
            q_ref[base + spot : base + spot + SUB] = jnp.where(
                lane < HALF, rolled(first, REACH, 1), rolled(last, REACH + HALF, 1)
            )
    q_ref[base + 2 * nz : base + 2 * nz + SUB] = coarse
    f1_ref[2 * nz :] = coarse


def pack(u, s, c, nz, nx):
    half = nz // ZS // 2
    pieces = 4
    return pl.pallas_call(
        functools.partial(pack_kernel, nz=nz, nx=nx),
        out_shape=(
            tiles(3 * half * nx // SUB + 2 * nz // SUB + 1),
            tiles(2 * nz // SUB + 1),
            tiles(nz),
            tiles(nz // 2),
            tiles(nz // 2),
            jax.ShapeDtypeStruct(u.shape, f32),
            tiles(4 * nz // SUB),
        ),
        in_specs=[pl.BlockSpec(memory_space=pltpu.HBM)] * 3,
        out_specs=(VMEM,) * 7,
        scratch_shapes=[pltpu.VMEM(u.shape, f32)] * 3 + [pltpu.SemaphoreType.DMA((3, pieces))],
        compiler_params=SMALL,
        name="pack",
    )(*(pltpu.with_memory_space_constraint(x, pltpu.HBM) for x in (u, s, c)))


def facing(own_ref, a, z, nz, last):
    first, second = own_ref[a * nz + z : a * nz + z + SUB], own_ref[(2 + a) * nz + z : (2 + a) * nz + z + SUB]
    return jnp.where(last, second, first)


def join_kernel(q_ref, ql_ref, qr_ref, f1_ref, own_ref, b1_ref, b2_ref, strip_ref, kept_ref, *, nz, nx):
    zs = nz // ZS
    half = zs // 2
    even = is_even()
    sub, lane = iota((SUB, LANES), 0), iota((SUB, LANES), 1)
    low = sub < RIM
    spot = part(iota((nx, LANES), 1), GROUP)[1]
    joined = []
    for a in range(3):
        group = [None] * zs
        for pair in range(half):
            at = slice((a * half + pair) * nx, (a * half + pair + 1) * nx)
            left, own, right = ql_ref[at], q_ref[at], qr_ref[at]
            moved = rolled(jnp.where(spot < RIM, own, right), 2 * RIM, 1)
            one = jnp.where(spot < 2 * RIM, jnp.where(spot < RIM, left, own), moved)
            moved = rolled(jnp.where(spot < 3 * RIM, left, own), -2 * RIM, 1)
            two = jnp.where(spot < 2 * RIM, moved, jnp.where(spot < 3 * RIM, own, right))
            group[pair], group[pair + half] = one, two
            first = jnp.where(low, one[:SUB], rolled(two[:SUB], RIM, 0))
            last = jnp.where(low, rolled(two[nx - SUB :], RIM, 0), one[nx - SUB :])
            to = slice((a * half + pair) * SUB, (a * half + pair + 1) * SUB)
            b1_ref[to] = jnp.where(even, last, first)
            b2_ref[to] = jnp.where(even, first, last)
        for zi in range(zs):
            strip_ref[(a * zs + zi) * nx : (a * zs + zi + 1) * nx] = group[zi]
        joined.append(group)

    source, target = 3 * half * nx, 3 * half * SUB
    lower, outer = lane < HALF, part(lane, HALF)[1] < REACH
    for Z in range(nz // SUB):
        u, c = (
            jnp.where(outer, ql_ref[at : at + SUB], qr_ref[at : at + SUB])
            for at in (source + Z * SUB, source + nz + Z * SUB)
        )
        kept_ref[Z * SUB : (Z + 1) * SUB] = u
        kept_ref[nz + Z * SUB : nz + (Z + 1) * SUB] = c
        first, last = jnp.where(lower, u, rolled(c, HALF, 1)), jnp.where(lower, rolled(u, HALF, 1), c)
        to = slice(target + Z * SUB, target + (Z + 1) * SUB)
        b1_ref[to] = jnp.where(even, last, first)
        b2_ref[to] = jnp.where(even, first, last)

    at = slice(source + 2 * nz, source + 2 * nz + SUB)
    place = part(lane, SPREAD)[1]
    window = jnp.where(
        place < RIM,
        rolled(ql_ref[at], -WIDTH, 1),
        jnp.where(place < RIM + WIDTH, q_ref[at], rolled(qr_ref[at], WIDTH, 1)),
    )
    flux = jnp.zeros((nx, LANES), f32)
    for u, c in zip(joined[0], joined[1]):
        flux = flux + (c + rolled(c, -1, 1)) * (u - rolled(u, -1, 1))
    flux = block_rows((0.5 / CELLS) * flux)
    flux = flux + rolled(flux, -GROUP, 1)
    near, far = RIM - 1, 3 * RIM - 1
    change = jnp.where(place == RIM - 1, -rolled(flux, RIM - 1 - near, 1), 0.0)
    change = jnp.where(place == RIM, rolled(flux, RIM - near, 1), change)
    change = jnp.where(place == RIM + WIDTH - 1, -rolled(flux, RIM + WIDTH - 1 - far, 1), change)
    change = jnp.where(place == RIM + WIDTH, rolled(flux, RIM + WIDTH - far, 1), change)
    rows = nx // COARSEN
    nearest = jnp.where(even, rows - 1, 0)
    for Z in range(nz // COARSEN):
        u, c = facing(own_ref, 0, Z * SUB, nz, even) - tile(f1_ref, Z), facing(own_ref, 1, Z * SUB, nz, even)
        across = all_rows((0.5 / CELLS) * (c + tile(f1_ref, nz // SUB + Z)) * u)
        change = change - compact(jnp.where(sub == nearest, across, 0.0), Z)
    mate = f1_ref[2 * nz : 2 * nz + SUB]
    mate = jnp.where(even, rolled(mate, rows - RIM, 0), rolled(mate, 1 - RIM, 0))
    cond = jnp.where(sub == rows, mate, rolled(window, -RIM, 0))
    rhs = window + change
    kept_ref[2 * nz : 2 * nz + SUB] = cond
    kept_ref[2 * nz + SUB :] = rhs
    to = target + nz
    b1_ref[to:] = cond
    b2_ref[to : to + SUB] = cond
    b2_ref[to + SUB : to + 2 * SUB] = rhs
    to = to + 2 * SUB
    for a in range(2):
        for Z in range(nz // SUB):
            at = to + a * nz + Z * SUB
            b2_ref[at : at + SUB] = facing(own_ref, a, Z * SUB, nz, jnp.logical_not(even))


def join(q, ql, qr, f1, own, nz, nx):
    zs = nz // ZS
    size = 3 * (zs // 2) + nz // SUB + 1
    return pl.pallas_call(
        functools.partial(join_kernel, nz=nz, nx=nx),
        out_shape=(
            tiles(size),
            tiles(size + 1 + 2 * nz // SUB),
            jax.ShapeDtypeStruct((3 * zs * nx, LANES), f32),
            tiles(2 * nz // SUB + 2),
        ),
        in_specs=[VMEM] * 5,
        out_specs=(VMEM,) * 4,
        compiler_params=SMALL,
        name="join",
    )(q, ql, qr, f1, own)


def faces_kernel(own_ref, kept_ref, r2_ref, r1_ref, after_ref, o_ref, *, nz, nx):
    del after_ref
    half = nz // ZS // 2
    even = is_even()
    sub, lane = iota((SUB, LANES), 0), iota((SUB, LANES), 1)
    plane, place = part(lane, SPREAD)
    rows = nx // COARSEN
    base = 3 * half * SUB

    outer = REACH // COARSEN
    is_left, is_right = (place >= RIM - outer) & (place < RIM), (place >= RIM + WIDTH) & (place < RIM + WIDTH + outer)
    is_own = (place >= RIM) & (place < RIM + WIDTH)
    source = jnp.where(is_left, place - (RIM - outer), place - (RIM + WIDTH - outer))
    source = jnp.where(sub == 0, place - RIM, source) * COARSEN
    source = jnp.clip(source, 0, LANES - 1)
    valid = ((sub == 0) & is_own) | ((sub > 0) & (is_left | is_right))

    def outside(r_ref, Z, upper):
        def mine(at):
            tile_at = kept_ref[at + Z * SUB : at + (Z + 1) * SUB]
            return jnp.where(upper, rolled(tile_at, HALF, 1), tile_at)

        other = r_ref[base + Z * SUB : base + (Z + 1) * SUB]
        return all_rows(0.5 * (mine(nz) + rolled(other, HALF, 1)) * (mine(0) - other))

    odd = jnp.logical_not(even)
    far_rows = base + nz + 2 * SUB
    flux = jnp.zeros((SUB, LANES), f32)
    for Z in range(nz // COARSEN):
        u, c = (
            (facing(own_ref, a, Z * SUB, nz, odd), r2_ref[at : at + SUB])
            for a, at in ((0, far_rows + Z * SUB), (1, far_rows + nz + Z * SUB))
        )
        one = all_rows(0.5 * (c[0] + c[1]) * (u[0] - u[1]))
        two = outside(r2_ref, Z, odd)
        three = outside(r1_ref, Z, even)
        sums = lane_sums(jnp.where(sub == 0, one, jnp.where(sub == 1, two, jnp.where(sub == 2, three, 0.0))))
        here = valid & (plane == Z)
        flux = flux + jnp.where(here, jnp.take_along_axis(sums, source, axis=1), 0.0)
    flux = flux * (1.0 / CELLS)
    far, mate = flux[0:1] + flux[1:2], flux[2:3]

    def stacked(own, other):
        before, after = jnp.where(even, other, own), jnp.where(even, own, other)
        return jnp.where(sub <= rows, rolled(before, 1, 0), rolled(after, rows + 1, 0))

    at = base + nz + SUB
    rhs = stacked(kept_ref[2 * nz + SUB :], r2_ref[at : at + SUB])
    sign = jnp.where(even, 1.0, -1.0)
    rhs = rhs + jnp.where(sub == rows, sign * far, jnp.where(sub == rows + 1, -sign * far, 0.0))
    rhs = rhs - jnp.where(sub == jnp.where(even, 2 * rows, 1), mate, 0.0)

    at = at - SUB
    near_c, far_c = r1_ref[at : at + SUB], r2_ref[at : at + SUB]
    cond = stacked(kept_ref[2 * nz : 2 * nz + SUB], far_c)
    before = jnp.where(even, rolled(far_c, -rows, 0), rolled(near_c, 1 - rows, 0))
    after = jnp.where(even, rolled(near_c, 2 * rows + 1, 0), rolled(far_c, rows + 1, 0))
    cond = jnp.where(sub == 0, before, jnp.where(sub == 2 * rows + 1, after, cond))
    around = rolled(cond, -1, 0) + rolled(cond, 1, 0) + rolled(cond, -1, 1) + rolled(cond, 1, 1)
    around = around + rolled(cond, -SPREAD, 1) + rolled(cond, SPREAD, 1)
    weight = OMEGA / (SHIFT + (0.5 / COARSEN**2) * (6.0 * cond + around))
    o_ref[0:SUB] = weight * rhs
    o_ref[SUB : 2 * SUB] = weight
    o_ref[2 * SUB :] = cond


def faces(own, kept, r2, r1, after, nz, nx):
    return pl.pallas_call(
        functools.partial(faces_kernel, nz=nz, nx=nx),
        out_shape=tiles(3),
        in_specs=[VMEM] * 4 + [pl.BlockSpec(memory_space=pl.ANY)],
        out_specs=VMEM,
        compiler_params=SMALL,
        name="faces",
    )(own, kept, r2, r1, after)


def sides(even, one, two):
    return jnp.where(even, one, two), jnp.where(even, two, one)


def rim_of(low, after, before):
    return jnp.where(low, after, before), rolled(jnp.where(low, before, after), RIM, 0)


def rims_of(low, one_ref, two_ref, last_ref, nz):
    half = nz // 2
    for z in range(nz):
        yield rim_of(low, tile(one_ref if z < half else two_ref, z % half), tile(last_ref, z))


def rim_faces(sub, face, rim_face, u_first, u_last, rim):
    u_rim = jnp.where(sub == 0, rolled(rim, 1 - RIM, 0), rolled(rim, RIM - 1, 0))
    end = sub == SUB - 1
    after = jnp.where(end, face * (u_last - rolled(u_rim, -1, 0)), 0.0)
    before = jnp.where(end, rim_face * (u_rim - rolled(u_first, -1, 0)), 0.0)
    return after, before


def beside(w, z, zs, column):
    return rolled(w, -column - z // zs * GROUP, 1)


def window(spot, left, right, column):
    return jnp.where(spot == RIM - 1, left, rolled(right, RIM - 2 - column, 1))


def begin_kernel(
    strip_ref, u_ref, c_ref, r_ref, cx_ref, cy_ref, cz_ref, diag_ref, inv_ref, q_ref, v_ref, *, nz, nx
):
    zs = nz // ZS
    spot = part(iota((nx, LANES), 1), GROUP)[1]
    row, lane = iota((nx, LANES), 0), iota((nx, LANES), 1)
    first_lane, last_lane = lane == 0, lane == LANES - 1

    def strip(a, zi):
        return strip_ref[(a * zs + zi) * nx : (a * zs + zi + 1) * nx]

    edge_c, edge_f = [], []
    for zi in range(zs):
        u, c = strip(0, zi), strip(1, zi)
        flux = 0.5 * (c + rolled(c, -1, 1)) * (u - rolled(u, -1, 1))
        edge_c.append(window(spot, c, c, 3 * RIM))
        edge_f.append(window(spot, flux, flux, 3 * RIM - 1))

    def own(ref, z):
        return ref[z % nz * nx : (z % nz + 1) * nx]

    below = 0.5 * (own(c_ref, -1) + own(c_ref, 0))
    for z in range(nz):
        at = slice(z * nx, (z + 1) * nx)
        c = own(c_ref, z)
        gx = jnp.where(row == nx - 1, 0.0, 0.5 * (c + rolled(c, -1, 0)))
        edge = beside(edge_c[z % zs], z, zs, RIM - 1)
        gy = 0.5 * (c + jnp.where(last_lane, edge, rolled(c, -1, 1)))
        gyl = 0.5 * (c + jnp.where(first_lane, edge, rolled(c, 1, 1)))
        above = 0.5 * (c + own(c_ref, z + 1))
        diag = SHIFT + (gx + rolled(gx, 1, 0)) + (gy + gyl) + (above + below)
        edge = beside(edge_f[z % zs], z, zs, RIM - 1)
        r = own(r_ref, z) + jnp.where(first_lane, edge, jnp.where(last_lane, -edge, 0.0))
        inner = slice(SUB, nx - SUB)
        inverse = 1.0 / diag[inner]
        scaled = r[inner] * inverse
        cx_ref[at] = gx
        cy_ref[at] = gy
        cz_ref[at] = above
        diag_ref[at] = diag
        q_ref[at] = jnp.concatenate([r[:SUB], scaled, r[nx - SUB :]], axis=0)
        to = slice(z * (nx - 2 * SUB), (z + 1) * (nx - 2 * SUB))
        inv_ref[to] = inverse
        v_ref[to] = scaled * (1.0 / THETA)
        below = above


def begin(strips, u, c, r, nz, nx):
    inner = jax.ShapeDtypeStruct((nz * (nx - 2 * SUB), LANES), f32)
    return pl.pallas_call(
        functools.partial(begin_kernel, nz=nz, nx=nx),
        out_shape=(jax.ShapeDtypeStruct(u.shape, f32),) * 4 + (inner, jax.ShapeDtypeStruct(u.shape, f32), inner),
        in_specs=[VMEM] * 4,
        out_specs=(VMEM,) * 7,
        compiler_params=SMALL,
        cost_estimate=pl.CostEstimate(flops=40 * u.size, bytes_accessed=40 * u.size, transcendentals=0),
        name="begin",
    )(strips, u, c, r)


def fine_kernel(
    strip_ref, b2_ref, b1_ref, one_ref, two_ref, last_ref, u_ref, c_ref, cx_ref, cy_ref, cz_ref, diag_ref, inv_ref, q_ref, v_ref,
    o_ref,
    ch, cyh, czh, cx, inv, q, va, vb, acc, wr, w0, w1, w2,
    *, nz, nx,
):
    zs = nz // ZS
    half = zs // 2
    ext = nx + SUB
    even = is_even()
    sub = iota((SUB, LANES), 0)
    low, end = sub < RIM, sub == SUB - 1
    table = steps()

    rims = []
    for z, (cond, rim) in enumerate(rims_of(low, one_ref, two_ref, last_ref, nz)):
        ch[z * SUB : (z + 1) * SUB] = cond
        rims.append(rim)

    row, spot = iota((ext, LANES), 0), part(iota((ext, LANES), 1), GROUP)[1]

    def strips_of(a):
        ends = [None] * zs
        for pair in range(half):
            index = a * half + pair
            ends[pair], ends[pair + half] = rim_of(low, *sides(even, tile(b1_ref, index), tile(b2_ref, index)))
        return [
            jnp.concatenate([strip_ref[(a * zs + zi) * nx : (a * zs + zi + 1) * nx], ends[zi]], axis=0)
            for zi in range(zs)
        ]

    def z_up(x):
        return x[1:] + [rolled(x[0], -GROUP, 1)]

    def z_down(x):
        return [rolled(x[-1], GROUP, 1)] + x[:-1]

    us, cs, rs = strips_of(0), strips_of(1), strips_of(2)
    cxs = [0.5 * (c + rolled(c, -1, 0)) for c in cs]
    cys = [0.5 * (c + rolled(c, -1, 1)) for c in cs]
    czs = [0.5 * (c + d) for c, d in zip(cs, z_up(cs))]
    czds = z_down(czs)
    invs, qs, vs = [], [], []
    for zi in range(zs):
        u = us[zi]
        fx = jnp.where((row == nx - 1) | (row == ext - 1), cxs[zi] * (u - rolled(u, -1, 0)), 0.0)
        fy = jnp.where((spot == RIM - 1) | (spot == 3 * RIM - 1), cys[zi] * (u - rolled(u, -1, 1)), 0.0)
        r = rs[zi] - (fx - rolled(fx, 1, 0)) - (fy - rolled(fy, 1, 1))
        wr[zi * SUB : (zi + 1) * SUB] = jnp.where(spot == RIM, r, rolled(r, -2 * RIM, 1))[nx:]
        diag = SHIFT + (cxs[zi] + rolled(cxs[zi], 1, 0)) + (cys[zi] + rolled(cys[zi], 1, 1)) + (czs[zi] + czds[zi])
        invs.append(1.0 / diag)
        qs.append(r * invs[zi])
        vs.append(qs[zi] * (1.0 / THETA))
    for k, w in enumerate((w0, w1, w2)):
        prod = [cys[zi] * vs[zi] for zi in range(zs)]
        for zi in range(zs):
            w[zi * ext : (zi + 1) * ext] = window(spot, prod[zi], vs[zi], 3 * RIM)
        if k == SWEEPS - 1:
            break
        keep, lift = table[k]
        v_up, v_down = z_up(vs), z_down(vs)
        fresh = []
        for zi in range(zs):
            v = vs[zi]
            near = cxs[zi] * rolled(v, -1, 0) + rolled(cxs[zi] * v, 1, 0)
            near = near + cys[zi] * rolled(v, -1, 1) + rolled(prod[zi], 1, 1)
            near = near + czs[zi] * v_up[zi] + czds[zi] * v_down[zi]
            qs[zi] = qs[zi] - v + near * invs[zi]
            fresh.append(keep * v + lift * qs[zi])
        vs = fresh
    edge_c = [window(spot, c, c, 3 * RIM)[nx:] for c in cs]

    lane = iota((SUB, LANES), 1)
    first_lane, last_lane = lane == 0, lane == LANES - 1

    def own(ref, z):
        return ref[z % nz * nx : (z % nz + 1) * nx]

    def rim_at(ref, z):
        return tile(ref, z % nz)

    below = 0.5 * (rim_at(ch, -1) + rim_at(ch, 0))
    for z in range(nz):
        at = slice(z * SUB, (z + 1) * SUB)
        u, c = own(u_ref, z), tile(ch, z)
        c_first, c_last = own(c_ref, z)[:SUB], own(c_ref, z)[nx - SUB :]
        zi = z % zs
        face = jnp.where(end, 0.5 * (c_last + rolled(c, -1, 0)), 0.0)
        gx = 0.5 * (c + jnp.where(end, rolled(c_first, -1, 0), rolled(c, -1, 0)))
        gxl = rolled(gx, 1, 0)
        edge = beside(edge_c[zi], z, zs, RIM - 1)
        gy = 0.5 * (c + jnp.where(last_lane, edge, rolled(c, -1, 1)))
        gyl = 0.5 * (c + jnp.where(first_lane, edge, rolled(c, 1, 1)))
        above = 0.5 * (c + rim_at(ch, z + 1))
        diag = SHIFT + (gx + jnp.where(sub == 0, rolled(face, 1, 0), gxl)) + (gy + gyl) + (above + below)
        after, before = rim_faces(sub, face, gx, u[:SUB], u[nx - SUB :], rims[z])
        r = rims[z] + rolled(after, 1, 0) - before
        r = jnp.where(first_lane | last_lane, beside(wr[zi * SUB : (zi + 1) * SUB], z, zs, RIM), r)
        own_diag, own_q = own(diag_ref, z), own(q_ref, z)
        long_at = slice(z * ext, (z + 1) * ext)
        parts = []
        for this_diag, this_r in (
            (own_diag[:SUB] + jnp.where(sub == 0, gxl, 0.0), own_q[:SUB] + rolled(before, 1, 0)),
            (own_diag[nx - SUB :] + face, own_q[nx - SUB :] - after),
            (diag, r),
        ):
            inverse = 1.0 / this_diag
            scaled = this_r * inverse
            parts.append((inverse, scaled, scaled * (1.0 / THETA)))
        inner = slice(z * (nx - 2 * SUB), (z + 1) * (nx - 2 * SUB))
        middle = (inv_ref[inner], own_q[SUB : nx - SUB], v_ref[inner])
        for ref, one, two, three, four in zip((inv, q, va), parts[0], middle, parts[1], parts[2]):
            ref[long_at] = jnp.concatenate([one, two, three, four], axis=0)
        own_cx = own(cx_ref, z)
        cx[long_at] = jnp.concatenate([own_cx[: nx - SUB], own_cx[nx - SUB :] + face, gx], axis=0)
        cyh[at] = gy
        czh[at] = above
        below = above

    lane = iota((ext, LANES), 1)
    first_lane, last_lane = lane == 0, lane == LANES - 1

    def whole(ref, rim, z):
        return jnp.concatenate([own(ref, z), rim_at(rim, z)], axis=0)

    def long(ref, z):
        return ref[z % nz * ext : (z % nz + 1) * ext]

    for k, w in enumerate((w0, w1, w2)):
        old, new = (va, vb) if k % 2 == 0 else (vb, va)
        keep, lift = table[k]
        for z in range(nz):
            at, here = slice(z * ext, (z + 1) * ext), slice(z * nx, (z + 1) * nx)
            zi = z % zs
            v, gx, gy = old[at], cx[at], whole(cy_ref, cyh, z)
            edge = beside(w[zi * ext : (zi + 1) * ext], z, zs, RIM - 1)
            near = gx * rolled(v, -1, 0) + rolled(gx * v, 1, 0)
            near = near + gy * jnp.where(last_lane, edge, rolled(v, -1, 1))
            near = near + jnp.where(first_lane, edge, rolled(gy * v, 1, 1))
            near = near + whole(cz_ref, czh, z) * long(old, z + 1) + whole(cz_ref, czh, z - 1) * long(old, z - 1)
            scaled = q[at] - v + near * inv[at]
            fresh = keep * v + lift * scaled
            total = (v[:nx] if k == 0 else acc[here]) + fresh[:nx]
            if k < SWEEPS - 1:
                q[at] = scaled
                new[at] = fresh
                acc[here] = total
            else:
                o_ref[here] = own(u_ref, z) + total


def fine(strips, b2, b1, one, two, last, u, c, begun, nz, nx):
    zs = nz // ZS
    ext = nx + SUB
    rim = pltpu.VMEM((nz * SUB, LANES), f32)
    full = pltpu.VMEM((nz * ext, LANES), f32)
    strip = pltpu.VMEM((zs * ext, LANES), f32)
    return pl.pallas_call(
        functools.partial(fine_kernel, nz=nz, nx=nx),
        out_shape=jax.ShapeDtypeStruct(u.shape, f32),
        in_specs=[VMEM] * 15,
        out_specs=VMEM,
        scratch_shapes=[rim] * 3 + [full] * 5 + [pltpu.VMEM(u.shape, f32), pltpu.VMEM((zs * SUB, LANES), f32)] + [strip] * 3,
        compiler_params=SMALL,
        cost_estimate=pl.CostEstimate(flops=100 * u.size, bytes_accessed=40 * u.size, transcendentals=0),
        name="fine",
    )(strips, b2, b1, one, two, last, u, c, *begun)


def finish_kernel(x_ref, m_ref, r_ref, o_ref, *, nz, nx):
    rows = nx // COARSEN
    even = is_even()
    sub, lane = iota((SUB, LANES), 0), iota((SUB, LANES), 1)
    beyond = sub == jnp.where(even, 2 * rows + 1, 0)
    fields = []
    for a in range(3):
        mine, mate = tile(m_ref, a), tile(r_ref, a)
        mate = jnp.where(even, rolled(mate, 2 * rows, 0), rolled(mate, -2 * rows, 0))
        fields.append(jnp.concatenate([jnp.where(beyond, mate, mine), mate], axis=0))
    start, weight, cond = fields
    scale = 0.5 / COARSEN**2
    gx = scale * (cond + rolled(cond, -1, 0))
    gy = scale * (cond + rolled(cond, -1, 1))
    gz = scale * (cond + rolled(cond, -SPREAD, 1))
    v = start
    for _ in range(COARSE_SWEEPS - 1):
        fx = gx * (v - rolled(v, -1, 0))
        fy = gy * (v - rolled(v, -1, 1))
        fz = gz * (v - rolled(v, -SPREAD, 1))
        image = SHIFT * v + (fx - rolled(fx, 1, 0)) + (fy - rolled(fy, 1, 1)) + (fz - rolled(fz, SPREAD, 1))
        v = v + start - weight * image
    top = v[:SUB]
    top = jnp.where(even, rolled(top, -rows - 1, 0), rolled(top, -1, 0))
    for Z in range(nz // COARSEN):
        spread = jnp.take_along_axis(top, Z * SPREAD + RIM + part(lane, COARSEN)[0], axis=1)
        for X in range(rows):
            value = jnp.broadcast_to(spread[X : X + 1], (COARSEN, LANES))
            for z in range(Z * COARSEN, (Z + 1) * COARSEN):
                at = slice(z * nx + X * COARSEN, z * nx + (X + 1) * COARSEN)
                o_ref[at] = x_ref[at] + value


def finish(x, m, r, nz, nx):
    return pl.pallas_call(
        functools.partial(finish_kernel, nz=nz, nx=nx),
        out_shape=jax.ShapeDtypeStruct(x.shape, f32),
        in_specs=[VMEM] * 3,
        out_specs=VMEM,
        compiler_params=SMALL,
        name="finish",
    )(x, m, r)


def moves():
    size_x, size_y = lax.axis_size("gx"), lax.axis_size("gy")

    def send(x, go):
        pairs = []
        for i in range(size_x):
            for j in range(size_y):
                k, l = go(i, j)
                pairs.append((i * size_y + j, (k % size_x) * size_y + l % size_y))
        return lax.ppermute(x, ("gx", "gy"), pairs)

    def mate(x):
        return send(x, lambda i, j: (i + 1 if i % 2 == 0 else i - 1, j))

    def shift(x, by):
        return send(x, lambda i, j: (i + by, j))

    def far(x):
        return send(x, lambda i, j: (i - 1 if i % 2 == 0 else i + 1, j))

    def beside_y(x):
        left = send(x, lambda i, j: (i, j + 1))
        if size_y == 2:
            return left, left
        return left, send(x, lambda i, j: (i, j - 1))

    return mate, far, shift, beside_y


def body(iterate, source, conduct):
    nz, nx, ny = iterate.shape
    if nz != ZS * 4 or ny != LANES or nx != 3 * SUB or lax.axis_size("gx") % 2:
        raise ValueError("shapes")
    mate, far, shift, beside_y = moves()
    u, s, c = (x.reshape(nz * nx, ny) for x in (iterate, source, conduct))
    q, f1, last, one, two, r, own = pack(u, s, c, nz, nx)
    ql, qr = beside_y(q)
    rf1 = mate(f1)
    before = shift(last, 1)
    b1, b2, strips, kept = join(q, ql, qr, rf1, own, nz, nx)
    rb2 = far(b2)
    rb1 = mate(b1)
    one, two, strips = lax.optimization_barrier((one, two, strips))
    after = shift(one, -1), shift(two, -1)
    begun = begin(strips, u, c, r, nz, nx)
    m = faces(own, kept, rb2, rb1, begun[0], nz, nx)
    rm = mate(m)
    x = fine(strips, rb2, rb1, *after, before, u, c, begun, nz, nx)
    return finish(x, m, rm, nz, nx).reshape(nz, nx, ny)


def solution(mesh):
    spec = P(None, "gx", "gy")
    return jax.shard_map(body, mesh=mesh, in_specs=(spec,) * 3, out_specs=spec, check_vma=False)
```

```python
import functools

import jax
import jax.numpy as jnp
from jax import lax
from jax.experimental import pallas as pl
from jax.experimental.pallas import tpu as pltpu
from jax.sharding import PartitionSpec as P

SWEEPS = 3
COARSE_SWEEPS = 4
COARSEN = 8

SHIFT = 0.1
LMIN = 0.3
LMAX = 2.0
OMEGA = 0.8

THETA = (LMAX + LMIN) / 2.0
DELTA = (LMAX - LMIN) / 2.0
SIGMA = THETA / DELTA

RIM = SWEEPS + 1
SUB = 8
LANES = 128
HALF = LANES // 2
GROUP = 4 * RIM
ZS = LANES // GROUP
WIDTH = LANES // COARSEN
SPREAD = 2 * WIDTH
REACH = (COARSE_SWEEPS - 1) * COARSEN
CELLS = COARSEN**3

f32 = jnp.float32
VMEM = pl.BlockSpec(memory_space=pltpu.VMEM)
SMALL = pltpu.CompilerParams(vmem_limit_bytes=12 * 1024 * 1024)


def steps():
    rho, listed = 1.0 / SIGMA, []
    for _ in range(SWEEPS):
        nxt = 1.0 / (2.0 * SIGMA - rho)
        listed.append((nxt * rho, 2.0 * nxt / DELTA))
        rho = nxt
    return listed


def iota(shape, dim):
    return lax.broadcasted_iota(jnp.int32, shape, dim)


def part(index, size):
    return lax.shift_right_logical(index, size.bit_length() - 1), lax.bitwise_and(index, size - 1)


def rolled(x, by, dim):
    return pltpu.roll(x, by % x.shape[dim], dim)


def is_even():
    return lax.axis_index("gx") % 2 == 0


def tiles(count):
    return jax.ShapeDtypeStruct((count * SUB, LANES), f32)


def tile(ref, index):
    return ref[index * SUB : (index + 1) * SUB]


def picked(ref, start, stride):
    return ref[pl.ds(start, SUB, stride=stride), :]


def lane_sums(rows):
    shift = 1
    while shift < COARSEN:
        rows = rows + rolled(rows, -shift, 1)
        shift *= 2
    return rows


def compact(rows, place):
    plane, column = part(iota(rows.shape, 1), SPREAD)
    column = column - RIM
    source = jnp.clip(column * COARSEN, 0, LANES - 1)
    here = (plane == place) & (column >= 0) & (column < WIDTH)
    return jnp.where(here, jnp.take_along_axis(lane_sums(rows), source, axis=1), 0.0)


def section(run):
    pl.when(lax.axis_index("gx") >= 0)(run)


def block_rows(values):
    sub = iota((SUB, LANES), 0)
    out = jnp.zeros((SUB, LANES), f32)
    for block in range(values.shape[0] // COARSEN):
        part = values[block * COARSEN : (block + 1) * COARSEN]
        out = jnp.where(sub == block, jnp.sum(part, axis=0, keepdims=True), out)
    return out


def all_rows(values):
    return jnp.sum(values, axis=0, keepdims=True)


def pack_kernel(
    u_hbm, s_hbm, c_hbm, q_ref, f1_ref, last_ref, one_ref, two_ref, r_ref, own_ref, u_ref, s_ref, c_ref, sums_ref, sems, *, nz, nx
):
    pieces = sems.shape[1]
    size = nz * nx // pieces
    copies = []
    for k, (source, target) in enumerate(((c_hbm, c_ref), (u_hbm, u_ref), (s_hbm, s_ref))):
        for piece in range(pieces):
            at = pl.ds(piece * size, size)
            copies.append(pltpu.make_async_copy(source.at[at], target.at[at], sems.at[k, piece]))
    for copy in copies:
        copy.start()
    for copy in copies:
        copy.wait()

    even = is_even()
    sub, lane = iota((SUB, LANES), 0), iota((SUB, LANES), 1)
    low = sub < RIM
    row, wide = iota((nx, LANES), 0), iota((nx, LANES), 1)
    slot = part(wide, 2 * RIM)[0]

    def plane(ref, z):
        return ref[z % nz * nx : (z % nz + 1) * nx]

    def up(z):
        return 0.5 * (plane(c_ref, z) + plane(c_ref, z + 1)) * (plane(u_ref, z) - plane(u_ref, z + 1))

    for z in range(nz):
        u, c = plane(u_ref, z), plane(c_ref, z)
        fy = 0.5 * (c + rolled(c, -1, 1)) * (u - rolled(u, -1, 1))
        r_ref[z * nx : (z + 1) * nx] = jnp.where(wide == LANES - 1, 0.0, fy)
    below = up(nz - 1)
    for Z in range(nz // COARSEN):
        sum_r = sum_c = jnp.zeros((nx, LANES), f32)
        for z in range(Z * COARSEN, (Z + 1) * COARSEN):
            u, c = plane(u_ref, z), plane(c_ref, z)
            above = up(z)
            fx = 0.5 * (c + rolled(c, -1, 0)) * (u - rolled(u, -1, 0))
            fy = plane(r_ref, z)
            fx = jnp.where(row == nx - 1, 0.0, fx)
            r = plane(s_ref, z) - SHIFT * u - (fx - rolled(fx, 1, 0)) - (fy - rolled(fy, 1, 1)) - (above - below)
            below = above
            r_ref[z * nx : (z + 1) * nx] = r
            sum_r = sum_r + r
            sum_c = sum_c + c
            u0, u2, c0, c2 = u[:SUB], u[nx - SUB :], c[:SUB], c[nx - SUB :]
            first = jnp.where(low, c0, jnp.where(sub == SUB - 1, rolled(u0, -1, 0), rolled(r[:SUB], RIM, 0)))
            last = jnp.where(low, jnp.where(sub == 0, rolled(u2, 1, 0), rolled(r[nx - SUB :], RIM, 0)), c2)
            last_ref[z * SUB : (z + 1) * SUB] = last
            to = z % (nz // 2) * SUB
            (one_ref if z < nz // 2 else two_ref)[to : to + SUB] = first
        sums_ref[Z * nx : (Z + 1) * nx] = sum_r
        sums_ref[(Z + nz // COARSEN) * nx : (Z + nz // COARSEN + 1) * nx] = sum_c

    zs = nz // ZS
    half = zs // 2
    def strips():
        for a, ref in enumerate((u_ref, c_ref, r_ref)):
            for pair in range(half):
                strip = jnp.zeros((nx, LANES), f32)
                for g in range(ZS):
                    for second in range(2):
                        at = 2 * g + second
                        moved = rolled(plane(ref, g * zs + pair + second * half), at * 2 * RIM + RIM, 1)
                        strip = jnp.where(slot == at, moved, strip)
                q_ref[(a * half + pair) * nx : (a * half + pair + 1) * nx] = strip

    def finish():
        coarse = jnp.zeros((SUB, LANES), f32)
        planes = nz // COARSEN
        for Z in range(planes):
            sum_r, sum_c = (sums_ref[(Z + k * planes) * nx : (Z + k * planes + 1) * nx] for k in range(2))
            coarse = coarse + compact(block_rows(sum_r) + rolled(block_rows(sum_c), RIM, 0), Z)
        coarse = coarse * (1.0 / CELLS)
        strips()

        base = 3 * half * nx
        for a, ref in enumerate((u_ref, c_ref)):
            for Z in range(nz // SUB):
                at = Z * SUB * nx
                first, last = picked(ref, at, nx), picked(ref, at + nx - 1, nx)
                spot = a * nz + Z * SUB
                own_ref[spot : spot + SUB] = first
                own_ref[2 * nz + spot : 2 * nz + spot + SUB] = last
                f1_ref[spot : spot + SUB] = jnp.where(even, last, first)
                q_ref[base + spot : base + spot + SUB] = jnp.where(
                    lane < HALF, rolled(first, REACH, 1), rolled(last, REACH + HALF, 1)
                )
        q_ref[base + 2 * nz : base + 2 * nz + SUB] = coarse
        f1_ref[2 * nz :] = coarse

    section(finish)


def pack(u, s, c, nz, nx):
    half = nz // ZS // 2
    pieces = 4
    return pl.pallas_call(
        functools.partial(pack_kernel, nz=nz, nx=nx),
        out_shape=(
            tiles(3 * half * nx // SUB + 2 * nz // SUB + 1),
            tiles(2 * nz // SUB + 1),
            tiles(nz),
            tiles(nz // 2),
            tiles(nz // 2),
            jax.ShapeDtypeStruct(u.shape, f32),
            tiles(4 * nz // SUB),
        ),
        in_specs=[pl.BlockSpec(memory_space=pltpu.HBM)] * 3,
        out_specs=(VMEM,) * 7,
        scratch_shapes=[pltpu.VMEM(u.shape, f32)] * 3
        + [pltpu.VMEM((2 * nz // COARSEN * nx, LANES), f32), pltpu.SemaphoreType.DMA((3, pieces))],
        compiler_params=SMALL,
        name="pack",
    )(*(pltpu.with_memory_space_constraint(x, pltpu.HBM) for x in (u, s, c)))


def facing(own_ref, a, z, nz, last):
    first, second = own_ref[a * nz + z : a * nz + z + SUB], own_ref[(2 + a) * nz + z : (2 + a) * nz + z + SUB]
    return jnp.where(last, second, first)


def join_kernel(q_ref, ql_ref, qr_ref, f1_ref, own_ref, b1_ref, b2_ref, strip_ref, kept_ref, *, nz, nx):
    zs = nz // ZS
    half = zs // 2
    even = is_even()
    sub, lane = iota((SUB, LANES), 0), iota((SUB, LANES), 1)
    low = sub < RIM
    spot = part(iota((nx, LANES), 1), GROUP)[1]
    joined = []
    for a in range(3):
        group = [None] * zs
        for pair in range(half):
            at = slice((a * half + pair) * nx, (a * half + pair + 1) * nx)
            left, own, right = ql_ref[at], q_ref[at], qr_ref[at]
            moved = rolled(jnp.where(spot < RIM, own, right), 2 * RIM, 1)
            one = jnp.where(spot < 2 * RIM, jnp.where(spot < RIM, left, own), moved)
            moved = rolled(jnp.where(spot < 3 * RIM, left, own), -2 * RIM, 1)
            two = jnp.where(spot < 2 * RIM, moved, jnp.where(spot < 3 * RIM, own, right))
            group[pair], group[pair + half] = one, two
            first = jnp.where(low, one[:SUB], rolled(two[:SUB], RIM, 0))
            last = jnp.where(low, rolled(two[nx - SUB :], RIM, 0), one[nx - SUB :])
            to = slice((a * half + pair) * SUB, (a * half + pair + 1) * SUB)
            b1_ref[to] = jnp.where(even, last, first)
            b2_ref[to] = jnp.where(even, first, last)
        for zi in range(zs):
            strip_ref[(a * zs + zi) * nx : (a * zs + zi + 1) * nx] = group[zi]
        joined.append(group)

    source, target = 3 * half * nx, 3 * half * SUB
    lower, outer = lane < HALF, part(lane, HALF)[1] < REACH
    for Z in range(nz // SUB):
        u, c = (
            jnp.where(outer, ql_ref[at : at + SUB], qr_ref[at : at + SUB])
            for at in (source + Z * SUB, source + nz + Z * SUB)
        )
        kept_ref[Z * SUB : (Z + 1) * SUB] = u
        kept_ref[nz + Z * SUB : nz + (Z + 1) * SUB] = c
        first, last = jnp.where(lower, u, rolled(c, HALF, 1)), jnp.where(lower, rolled(u, HALF, 1), c)
        to = slice(target + Z * SUB, target + (Z + 1) * SUB)
        b1_ref[to] = jnp.where(even, last, first)
        b2_ref[to] = jnp.where(even, first, last)

    at = slice(source + 2 * nz, source + 2 * nz + SUB)
    place = part(lane, SPREAD)[1]
    window = jnp.where(
        place < RIM,
        rolled(ql_ref[at], -WIDTH, 1),
        jnp.where(place < RIM + WIDTH, q_ref[at], rolled(qr_ref[at], WIDTH, 1)),
    )
    flux = jnp.zeros((nx, LANES), f32)
    for u, c in zip(joined[0], joined[1]):
        flux = flux + (c + rolled(c, -1, 1)) * (u - rolled(u, -1, 1))
    flux = block_rows((0.5 / CELLS) * flux)
    flux = flux + rolled(flux, -GROUP, 1)
    near, far = RIM - 1, 3 * RIM - 1
    change = jnp.where(place == RIM - 1, -rolled(flux, RIM - 1 - near, 1), 0.0)
    change = jnp.where(place == RIM, rolled(flux, RIM - near, 1), change)
    change = jnp.where(place == RIM + WIDTH - 1, -rolled(flux, RIM + WIDTH - 1 - far, 1), change)
    change = jnp.where(place == RIM + WIDTH, rolled(flux, RIM + WIDTH - far, 1), change)
    rows = nx // COARSEN
    nearest = jnp.where(even, rows - 1, 0)
    for Z in range(nz // COARSEN):
        u, c = facing(own_ref, 0, Z * SUB, nz, even) - tile(f1_ref, Z), facing(own_ref, 1, Z * SUB, nz, even)
        across = all_rows((0.5 / CELLS) * (c + tile(f1_ref, nz // SUB + Z)) * u)
        change = change - compact(jnp.where(sub == nearest, across, 0.0), Z)
    mate = f1_ref[2 * nz : 2 * nz + SUB]
    mate = jnp.where(even, rolled(mate, rows - RIM, 0), rolled(mate, 1 - RIM, 0))
    cond = jnp.where(sub == rows, mate, rolled(window, -RIM, 0))
    rhs = window + change
    kept_ref[2 * nz : 2 * nz + SUB] = cond
    kept_ref[2 * nz + SUB :] = rhs
    to = target + nz
    b1_ref[to:] = cond
    b2_ref[to : to + SUB] = cond
    b2_ref[to + SUB : to + 2 * SUB] = rhs
    to = to + 2 * SUB
    for a in range(2):
        for Z in range(nz // SUB):
            at = to + a * nz + Z * SUB
            b2_ref[at : at + SUB] = facing(own_ref, a, Z * SUB, nz, jnp.logical_not(even))


def join(q, ql, qr, f1, own, nz, nx):
    zs = nz // ZS
    size = 3 * (zs // 2) + nz // SUB + 1
    return pl.pallas_call(
        functools.partial(join_kernel, nz=nz, nx=nx),
        out_shape=(
            tiles(size),
            tiles(size + 1 + 2 * nz // SUB),
            jax.ShapeDtypeStruct((3 * zs * nx, LANES), f32),
            tiles(2 * nz // SUB + 2),
        ),
        in_specs=[VMEM] * 5,
        out_specs=(VMEM,) * 4,
        compiler_params=SMALL,
        name="join",
    )(q, ql, qr, f1, own)


def faces_kernel(own_ref, kept_ref, r2_ref, r1_ref, after_ref, o_ref, *, nz, nx):
    del after_ref
    half = nz // ZS // 2
    even = is_even()
    sub, lane = iota((SUB, LANES), 0), iota((SUB, LANES), 1)
    plane, place = part(lane, SPREAD)
    rows = nx // COARSEN
    base = 3 * half * SUB

    outer = REACH // COARSEN
    is_left, is_right = (place >= RIM - outer) & (place < RIM), (place >= RIM + WIDTH) & (place < RIM + WIDTH + outer)
    is_own = (place >= RIM) & (place < RIM + WIDTH)
    source = jnp.where(is_left, place - (RIM - outer), place - (RIM + WIDTH - outer))
    source = jnp.where(sub == 0, place - RIM, source) * COARSEN
    source = jnp.clip(source, 0, LANES - 1)
    valid = ((sub == 0) & is_own) | ((sub > 0) & (is_left | is_right))

    def outside(r_ref, Z, upper):
        def mine(at):
            tile_at = kept_ref[at + Z * SUB : at + (Z + 1) * SUB]
            return jnp.where(upper, rolled(tile_at, HALF, 1), tile_at)

        other = r_ref[base + Z * SUB : base + (Z + 1) * SUB]
        return all_rows(0.5 * (mine(nz) + rolled(other, HALF, 1)) * (mine(0) - other))

    odd = jnp.logical_not(even)
    far_rows = base + nz + 2 * SUB
    flux = jnp.zeros((SUB, LANES), f32)
    for Z in range(nz // COARSEN):
        u, c = (
            (facing(own_ref, a, Z * SUB, nz, odd), r2_ref[at : at + SUB])
            for a, at in ((0, far_rows + Z * SUB), (1, far_rows + nz + Z * SUB))
        )
        one = all_rows(0.5 * (c[0] + c[1]) * (u[0] - u[1]))
        two = outside(r2_ref, Z, odd)
        three = outside(r1_ref, Z, even)
        sums = lane_sums(jnp.where(sub == 0, one, jnp.where(sub == 1, two, jnp.where(sub == 2, three, 0.0))))
        here = valid & (plane == Z)
        flux = flux + jnp.where(here, jnp.take_along_axis(sums, source, axis=1), 0.0)
    flux = flux * (1.0 / CELLS)
    far, mate = flux[0:1] + flux[1:2], flux[2:3]

    def stacked(own, other):
        before, after = jnp.where(even, other, own), jnp.where(even, own, other)
        return jnp.where(sub <= rows, rolled(before, 1, 0), rolled(after, rows + 1, 0))

    at = base + nz + SUB
    rhs = stacked(kept_ref[2 * nz + SUB :], r2_ref[at : at + SUB])
    sign = jnp.where(even, 1.0, -1.0)
    rhs = rhs + jnp.where(sub == rows, sign * far, jnp.where(sub == rows + 1, -sign * far, 0.0))
    rhs = rhs - jnp.where(sub == jnp.where(even, 2 * rows, 1), mate, 0.0)

    at = at - SUB
    near_c, far_c = r1_ref[at : at + SUB], r2_ref[at : at + SUB]
    cond = stacked(kept_ref[2 * nz : 2 * nz + SUB], far_c)
    before = jnp.where(even, rolled(far_c, -rows, 0), rolled(near_c, 1 - rows, 0))
    after = jnp.where(even, rolled(near_c, 2 * rows + 1, 0), rolled(far_c, rows + 1, 0))
    cond = jnp.where(sub == 0, before, jnp.where(sub == 2 * rows + 1, after, cond))
    around = rolled(cond, -1, 0) + rolled(cond, 1, 0) + rolled(cond, -1, 1) + rolled(cond, 1, 1)
    around = around + rolled(cond, -SPREAD, 1) + rolled(cond, SPREAD, 1)
    weight = OMEGA / (SHIFT + (0.5 / COARSEN**2) * (6.0 * cond + around))
    o_ref[0:SUB] = weight * rhs
    o_ref[SUB : 2 * SUB] = weight
    o_ref[2 * SUB :] = cond


def faces(own, kept, r2, r1, after, nz, nx):
    return pl.pallas_call(
        functools.partial(faces_kernel, nz=nz, nx=nx),
        out_shape=tiles(3),
        in_specs=[VMEM] * 4 + [pl.BlockSpec(memory_space=pl.ANY)],
        out_specs=VMEM,
        compiler_params=SMALL,
        name="faces",
    )(own, kept, r2, r1, after)


def sides(even, one, two):
    return jnp.where(even, one, two), jnp.where(even, two, one)


def rim_of(low, after, before):
    return jnp.where(low, after, before), rolled(jnp.where(low, before, after), RIM, 0)


def rims_of(low, one_ref, two_ref, last_ref, nz):
    half = nz // 2
    for z in range(nz):
        yield rim_of(low, tile(one_ref if z < half else two_ref, z % half), tile(last_ref, z))


def rim_faces(sub, face, rim_face, u_first, u_last, rim):
    u_rim = jnp.where(sub == 0, rolled(rim, 1 - RIM, 0), rolled(rim, RIM - 1, 0))
    end = sub == SUB - 1
    after = jnp.where(end, face * (u_last - rolled(u_rim, -1, 0)), 0.0)
    before = jnp.where(end, rim_face * (u_rim - rolled(u_first, -1, 0)), 0.0)
    return after, before


def beside(w, z, zs, column):
    return rolled(w, -column - z // zs * GROUP, 1)


def window(spot, left, right, column):
    return jnp.where(spot == RIM - 1, left, rolled(right, RIM - 2 - column, 1))


def begin_kernel(
    strip_ref, u_ref, c_ref, r_ref, cx_ref, cy_ref, cz_ref, diag_ref, inv_ref, q_ref, v_ref, *, nz, nx
):
    zs = nz // ZS
    spot = part(iota((nx, LANES), 1), GROUP)[1]
    row, lane = iota((nx, LANES), 0), iota((nx, LANES), 1)
    first_lane, last_lane = lane == 0, lane == LANES - 1

    def strip(a, zi):
        return strip_ref[(a * zs + zi) * nx : (a * zs + zi + 1) * nx]

    edge_c, edge_f = [], []
    for zi in range(zs):
        u, c = strip(0, zi), strip(1, zi)
        flux = 0.5 * (c + rolled(c, -1, 1)) * (u - rolled(u, -1, 1))
        edge_c.append(window(spot, c, c, 3 * RIM))
        edge_f.append(window(spot, flux, flux, 3 * RIM - 1))

    def own(ref, z):
        return ref[z % nz * nx : (z % nz + 1) * nx]

    below = 0.5 * (own(c_ref, -1) + own(c_ref, 0))
    for z in range(nz):
        at = slice(z * nx, (z + 1) * nx)
        c = own(c_ref, z)
        gx = jnp.where(row == nx - 1, 0.0, 0.5 * (c + rolled(c, -1, 0)))
        edge = beside(edge_c[z % zs], z, zs, RIM - 1)
        gy = 0.5 * (c + jnp.where(last_lane, edge, rolled(c, -1, 1)))
        gyl = 0.5 * (c + jnp.where(first_lane, edge, rolled(c, 1, 1)))
        above = 0.5 * (c + own(c_ref, z + 1))
        diag = SHIFT + (gx + rolled(gx, 1, 0)) + (gy + gyl) + (above + below)
        edge = beside(edge_f[z % zs], z, zs, RIM - 1)
        r = own(r_ref, z) + jnp.where(first_lane, edge, jnp.where(last_lane, -edge, 0.0))
        inner = slice(SUB, nx - SUB)
        inverse = 1.0 / diag[inner]
        scaled = r[inner] * inverse
        cx_ref[at] = gx
        cy_ref[at] = gy
        cz_ref[at] = above
        diag_ref[at] = diag
        q_ref[at] = jnp.concatenate([r[:SUB], scaled, r[nx - SUB :]], axis=0)
        to = slice(z * (nx - 2 * SUB), (z + 1) * (nx - 2 * SUB))
        inv_ref[to] = inverse
        v_ref[to] = scaled * (1.0 / THETA)
        below = above


def begin(strips, u, c, r, nz, nx):
    inner = jax.ShapeDtypeStruct((nz * (nx - 2 * SUB), LANES), f32)
    return pl.pallas_call(
        functools.partial(begin_kernel, nz=nz, nx=nx),
        out_shape=(jax.ShapeDtypeStruct(u.shape, f32),) * 4 + (inner, jax.ShapeDtypeStruct(u.shape, f32), inner),
        in_specs=[VMEM] * 4,
        out_specs=(VMEM,) * 7,
        compiler_params=SMALL,
        cost_estimate=pl.CostEstimate(flops=40 * u.size, bytes_accessed=40 * u.size, transcendentals=0),
        name="begin",
    )(strips, u, c, r)


def fine_kernel(
    strip_ref, b2_ref, b1_ref, one_ref, two_ref, last_ref, u_ref, c_ref, cx_ref, cy_ref, cz_ref, diag_ref, inv_ref, q_ref, v_ref,
    o_ref,
    ch, cyh, czh, cx, inv, q, va, vb, acc, wr, w0, w1, w2,
    *, nz, nx,
):
    zs = nz // ZS
    half = zs // 2
    ext = nx + SUB
    even = is_even()
    sub = iota((SUB, LANES), 0)
    low, end = sub < RIM, sub == SUB - 1
    table = steps()

    rims = []
    for z, (cond, rim) in enumerate(rims_of(low, one_ref, two_ref, last_ref, nz)):
        ch[z * SUB : (z + 1) * SUB] = cond
        rims.append(rim)

    row, spot = iota((ext, LANES), 0), part(iota((ext, LANES), 1), GROUP)[1]

    def strips_of(a):
        ends = [None] * zs
        for pair in range(half):
            index = a * half + pair
            ends[pair], ends[pair + half] = rim_of(low, *sides(even, tile(b1_ref, index), tile(b2_ref, index)))
        return [
            jnp.concatenate([strip_ref[(a * zs + zi) * nx : (a * zs + zi + 1) * nx], ends[zi]], axis=0)
            for zi in range(zs)
        ]

    def z_up(x):
        return x[1:] + [rolled(x[0], -GROUP, 1)]

    def z_down(x):
        return [rolled(x[-1], GROUP, 1)] + x[:-1]

    us, cs, rs = strips_of(0), strips_of(1), strips_of(2)
    cxs = [0.5 * (c + rolled(c, -1, 0)) for c in cs]
    cys = [0.5 * (c + rolled(c, -1, 1)) for c in cs]
    czs = [0.5 * (c + d) for c, d in zip(cs, z_up(cs))]
    czds = z_down(czs)
    invs, qs, vs = [], [], []
    for zi in range(zs):
        u = us[zi]
        fx = jnp.where((row == nx - 1) | (row == ext - 1), cxs[zi] * (u - rolled(u, -1, 0)), 0.0)
        fy = jnp.where((spot == RIM - 1) | (spot == 3 * RIM - 1), cys[zi] * (u - rolled(u, -1, 1)), 0.0)
        r = rs[zi] - (fx - rolled(fx, 1, 0)) - (fy - rolled(fy, 1, 1))
        wr[zi * SUB : (zi + 1) * SUB] = jnp.where(spot == RIM, r, rolled(r, -2 * RIM, 1))[nx:]
        diag = SHIFT + (cxs[zi] + rolled(cxs[zi], 1, 0)) + (cys[zi] + rolled(cys[zi], 1, 1)) + (czs[zi] + czds[zi])
        invs.append(1.0 / diag)
        qs.append(r * invs[zi])
        vs.append(qs[zi] * (1.0 / THETA))
    for k, w in enumerate((w0, w1, w2)):
        prod = [cys[zi] * vs[zi] for zi in range(zs)]
        for zi in range(zs):
            w[zi * ext : (zi + 1) * ext] = window(spot, prod[zi], vs[zi], 3 * RIM)
        if k == SWEEPS - 1:
            break
        keep, lift = table[k]
        v_up, v_down = z_up(vs), z_down(vs)
        fresh = []
        for zi in range(zs):
            v = vs[zi]
            near = cxs[zi] * rolled(v, -1, 0) + rolled(cxs[zi] * v, 1, 0)
            near = near + cys[zi] * rolled(v, -1, 1) + rolled(prod[zi], 1, 1)
            near = near + czs[zi] * v_up[zi] + czds[zi] * v_down[zi]
            qs[zi] = qs[zi] - v + near * invs[zi]
            fresh.append(keep * v + lift * qs[zi])
        vs = fresh
    edge_c = [window(spot, c, c, 3 * RIM)[nx:] for c in cs]

    lane = iota((SUB, LANES), 1)
    first_lane, last_lane = lane == 0, lane == LANES - 1

    def own(ref, z):
        return ref[z % nz * nx : (z % nz + 1) * nx]

    def rim_at(ref, z):
        return tile(ref, z % nz)

    below = 0.5 * (rim_at(ch, -1) + rim_at(ch, 0))
    for z in range(nz):
        at = slice(z * SUB, (z + 1) * SUB)
        u, c = own(u_ref, z), tile(ch, z)
        c_first, c_last = own(c_ref, z)[:SUB], own(c_ref, z)[nx - SUB :]
        zi = z % zs
        face = jnp.where(end, 0.5 * (c_last + rolled(c, -1, 0)), 0.0)
        gx = 0.5 * (c + jnp.where(end, rolled(c_first, -1, 0), rolled(c, -1, 0)))
        gxl = rolled(gx, 1, 0)
        edge = beside(edge_c[zi], z, zs, RIM - 1)
        gy = 0.5 * (c + jnp.where(last_lane, edge, rolled(c, -1, 1)))
        gyl = 0.5 * (c + jnp.where(first_lane, edge, rolled(c, 1, 1)))
        above = 0.5 * (c + rim_at(ch, z + 1))
        diag = SHIFT + (gx + jnp.where(sub == 0, rolled(face, 1, 0), gxl)) + (gy + gyl) + (above + below)
        after, before = rim_faces(sub, face, gx, u[:SUB], u[nx - SUB :], rims[z])
        r = rims[z] + rolled(after, 1, 0) - before
        r = jnp.where(first_lane | last_lane, beside(wr[zi * SUB : (zi + 1) * SUB], z, zs, RIM), r)
        own_diag, own_q = own(diag_ref, z), own(q_ref, z)
        long_at = slice(z * ext, (z + 1) * ext)
        parts = []
        for this_diag, this_r in (
            (own_diag[:SUB] + jnp.where(sub == 0, gxl, 0.0), own_q[:SUB] + rolled(before, 1, 0)),
            (own_diag[nx - SUB :] + face, own_q[nx - SUB :] - after),
            (diag, r),
        ):
            inverse = 1.0 / this_diag
            scaled = this_r * inverse
            parts.append((inverse, scaled, scaled * (1.0 / THETA)))
        inner = slice(z * (nx - 2 * SUB), (z + 1) * (nx - 2 * SUB))
        middle = (inv_ref[inner], own_q[SUB : nx - SUB], v_ref[inner])
        for ref, one, two, three, four in zip((inv, q, va), parts[0], middle, parts[1], parts[2]):
            ref[long_at] = jnp.concatenate([one, two, three, four], axis=0)
        own_cx = own(cx_ref, z)
        cx[long_at] = jnp.concatenate([own_cx[: nx - SUB], own_cx[nx - SUB :] + face, gx], axis=0)
        cyh[at] = gy
        czh[at] = above
        below = above

    lane = iota((ext, LANES), 1)
    first_lane, last_lane = lane == 0, lane == LANES - 1

    def whole(ref, rim, z):
        return jnp.concatenate([own(ref, z), rim_at(rim, z)], axis=0)

    def long(ref, z):
        return ref[z % nz * ext : (z % nz + 1) * ext]

    for k, w in enumerate((w0, w1, w2)):
        old, new = (va, vb) if k % 2 == 0 else (vb, va)
        keep, lift = table[k]
        for z in range(nz):
            at, here = slice(z * ext, (z + 1) * ext), slice(z * nx, (z + 1) * nx)
            zi = z % zs
            v, gx, gy = old[at], cx[at], whole(cy_ref, cyh, z)
            edge = beside(w[zi * ext : (zi + 1) * ext], z, zs, RIM - 1)
            near = gx * rolled(v, -1, 0) + rolled(gx * v, 1, 0)
            near = near + gy * jnp.where(last_lane, edge, rolled(v, -1, 1))
            near = near + jnp.where(first_lane, edge, rolled(gy * v, 1, 1))
            near = near + whole(cz_ref, czh, z) * long(old, z + 1) + whole(cz_ref, czh, z - 1) * long(old, z - 1)
            scaled = q[at] - v + near * inv[at]
            fresh = keep * v + lift * scaled
            total = (v[:nx] if k == 0 else acc[here]) + fresh[:nx]
            if k < SWEEPS - 1:
                q[at] = scaled
                new[at] = fresh
                acc[here] = total
            else:
                o_ref[here] = own(u_ref, z) + total


def fine(strips, b2, b1, one, two, last, u, c, begun, nz, nx):
    zs = nz // ZS
    ext = nx + SUB
    rim = pltpu.VMEM((nz * SUB, LANES), f32)
    full = pltpu.VMEM((nz * ext, LANES), f32)
    strip = pltpu.VMEM((zs * ext, LANES), f32)
    return pl.pallas_call(
        functools.partial(fine_kernel, nz=nz, nx=nx),
        out_shape=jax.ShapeDtypeStruct(u.shape, f32),
        in_specs=[VMEM] * 15,
        out_specs=VMEM,
        scratch_shapes=[rim] * 3 + [full] * 5 + [pltpu.VMEM(u.shape, f32), pltpu.VMEM((zs * SUB, LANES), f32)] + [strip] * 3,
        compiler_params=SMALL,
        cost_estimate=pl.CostEstimate(flops=100 * u.size, bytes_accessed=40 * u.size, transcendentals=0),
        name="fine",
    )(strips, b2, b1, one, two, last, u, c, *begun)


def finish_kernel(x_ref, m_ref, r_ref, o_ref, *, nz, nx):
    rows = nx // COARSEN
    even = is_even()
    sub, lane = iota((SUB, LANES), 0), iota((SUB, LANES), 1)
    beyond = sub == jnp.where(even, 2 * rows + 1, 0)
    fields = []
    for a in range(3):
        mine, mate = tile(m_ref, a), tile(r_ref, a)
        mate = jnp.where(even, rolled(mate, 2 * rows, 0), rolled(mate, -2 * rows, 0))
        fields.append(jnp.concatenate([jnp.where(beyond, mate, mine), mate], axis=0))
    start, weight, cond = fields
    scale = 0.5 / COARSEN**2
    turns = (-1, 0), (1, 0), (-1, 1), (1, 1), (-SPREAD, 1), (SPREAD, 1)
    shares = [scale * (cond + rolled(cond, *turn)) for turn in turns]
    keep = 1.0 - weight * (SHIFT + sum(shares))
    shares = [weight * share for share in shares]
    v = start
    for _ in range(COARSE_SWEEPS - 1):
        terms = [share * rolled(v, *turn) for share, turn in zip(shares, turns)]
        v = (start + keep * v) + ((terms[0] + terms[1]) + (terms[2] + terms[3]) + (terms[4] + terms[5]))
    top = v[:SUB]
    top = jnp.where(even, rolled(top, -rows - 1, 0), rolled(top, -1, 0))
    for Z in range(nz // COARSEN):
        spread = jnp.take_along_axis(top, Z * SPREAD + RIM + part(lane, COARSEN)[0], axis=1)
        for X in range(rows):
            value = jnp.broadcast_to(spread[X : X + 1], (COARSEN, LANES))
            for z in range(Z * COARSEN, (Z + 1) * COARSEN):
                at = slice(z * nx + X * COARSEN, z * nx + (X + 1) * COARSEN)
                o_ref[at] = x_ref[at] + value


def finish(x, m, r, nz, nx):
    return pl.pallas_call(
        functools.partial(finish_kernel, nz=nz, nx=nx),
        out_shape=jax.ShapeDtypeStruct(x.shape, f32),
        in_specs=[VMEM] * 3,
        out_specs=VMEM,
        compiler_params=SMALL,
        name="finish",
    )(x, m, r)


def moves():
    size_x, size_y = lax.axis_size("gx"), lax.axis_size("gy")

    def send(x, go):
        pairs = []
        for i in range(size_x):
            for j in range(size_y):
                k, l = go(i, j)
                pairs.append((i * size_y + j, (k % size_x) * size_y + l % size_y))
        return lax.ppermute(x, ("gx", "gy"), pairs)

    def mate(x):
        return send(x, lambda i, j: (i + 1 if i % 2 == 0 else i - 1, j))

    def shift(x, by):
        return send(x, lambda i, j: (i + by, j))

    def far(x):
        return send(x, lambda i, j: (i - 1 if i % 2 == 0 else i + 1, j))

    def beside_y(x):
        left = send(x, lambda i, j: (i, j + 1))
        if size_y == 2:
            return left, left
        return left, send(x, lambda i, j: (i, j - 1))

    return mate, far, shift, beside_y


def body(iterate, source, conduct):
    nz, nx, ny = iterate.shape
    if nz != ZS * 4 or ny != LANES or nx != 3 * SUB or lax.axis_size("gx") % 2:
        raise ValueError("shapes")
    mate, far, shift, beside_y = moves()
    u, s, c = (x.reshape(nz * nx, ny) for x in (iterate, source, conduct))
    q, f1, last, one, two, r, own = pack(u, s, c, nz, nx)
    ql, qr = beside_y(q)
    rf1 = mate(f1)
    before = shift(last, 1)
    b1, b2, strips, kept = join(q, ql, qr, rf1, own, nz, nx)
    rb2 = far(b2)
    rb1 = mate(b1)
    one, two, strips = lax.optimization_barrier((one, two, strips))
    after = shift(one, -1), shift(two, -1)
    begun = begin(strips, u, c, r, nz, nx)
    m = faces(own, kept, rb2, rb1, begun[0], nz, nx)
    rm = mate(m)
    x = fine(strips, rb2, rb1, *after, before, u, c, begun, nz, nx)
    return finish(x, m, rm, nz, nx).reshape(nz, nx, ny)


def solution(mesh):
    spec = P(None, "gx", "gy")
    return jax.shard_map(body, mesh=mesh, in_specs=(spec,) * 3, out_specs=spec, check_vma=False)
```

```python
import functools

import jax
import jax.numpy as jnp
from jax import lax
from jax.experimental import pallas as pl
from jax.experimental.pallas import tpu as pltpu
from jax.sharding import PartitionSpec as P

SWEEPS = 3
COARSE_SWEEPS = 4
COARSEN = 8

SHIFT = 0.1
LMIN = 0.3
LMAX = 2.0
OMEGA = 0.8

THETA = (LMAX + LMIN) / 2.0
DELTA = (LMAX - LMIN) / 2.0
SIGMA = THETA / DELTA

RIM = SWEEPS + 1
SUB = 8
LANES = 128
HALF = LANES // 2
GROUP = 4 * RIM
ZS = LANES // GROUP
WIDTH = LANES // COARSEN
SPREAD = 2 * WIDTH
REACH = (COARSE_SWEEPS - 1) * COARSEN
CELLS = COARSEN**3

f32 = jnp.float32
VMEM = pl.BlockSpec(memory_space=pltpu.VMEM)
SMALL = pltpu.CompilerParams(vmem_limit_bytes=12 * 1024 * 1024)


def steps():
    rho, listed = 1.0 / SIGMA, []
    for _ in range(SWEEPS):
        nxt = 1.0 / (2.0 * SIGMA - rho)
        listed.append((nxt * rho, 2.0 * nxt / DELTA))
        rho = nxt
    return listed


def iota(shape, dim):
    return lax.broadcasted_iota(jnp.int32, shape, dim)


def part(index, size):
    return lax.shift_right_logical(index, size.bit_length() - 1), lax.bitwise_and(index, size - 1)


def rolled(x, by, dim):
    return pltpu.roll(x, by % x.shape[dim], dim)


def is_even():
    return lax.axis_index("gx") % 2 == 0


def tiles(count):
    return jax.ShapeDtypeStruct((count * SUB, LANES), f32)


def tile(ref, index):
    return ref[index * SUB : (index + 1) * SUB]


def picked(ref, start, stride):
    return ref[pl.ds(start, SUB, stride=stride), :]


def gathered(rows, source):
    parts = [jnp.take_along_axis(rows, source + k, axis=1) for k in range(COARSEN)]
    while len(parts) > 1:
        parts = [a + b for a, b in zip(parts[::2], parts[1::2])]
    return parts[0]


def compact(rows, place):
    plane, column = part(iota(rows.shape, 1), SPREAD)
    column = column - RIM
    source = jnp.clip(column * COARSEN, 0, LANES - COARSEN)
    here = (plane == place) & (column >= 0) & (column < WIDTH)
    return jnp.where(here, gathered(rows, source), 0.0)


def section(run):
    pl.when(lax.axis_index("gx") >= 0)(run)


def block_rows(values):
    sub = iota((SUB, LANES), 0)
    out = jnp.zeros((SUB, LANES), f32)
    for block in range(values.shape[0] // COARSEN):
        part = values[block * COARSEN : (block + 1) * COARSEN]
        out = jnp.where(sub == block, jnp.sum(part, axis=0, keepdims=True), out)
    return out


def all_rows(values):
    return jnp.sum(values, axis=0, keepdims=True)


def pack_kernel(
    u_hbm, s_hbm, c_hbm, q_ref, f1_ref, last_ref, one_ref, two_ref, r_ref, own_ref, u_ref, s_ref, c_ref, sums_ref, sems, *, nz, nx
):
    pieces = sems.shape[1]
    size = nz * nx // pieces
    copies = []
    for k, (source, target) in enumerate(((c_hbm, c_ref), (u_hbm, u_ref), (s_hbm, s_ref))):
        for piece in range(pieces):
            at = pl.ds(piece * size, size)
            copies.append(pltpu.make_async_copy(source.at[at], target.at[at], sems.at[k, piece]))
    for copy in copies:
        copy.start()
    for copy in copies[: 2 * pieces]:
        copy.wait()

    even = is_even()
    sub, lane = iota((SUB, LANES), 0), iota((SUB, LANES), 1)
    low = sub < RIM
    row, wide = iota((nx, LANES), 0), iota((nx, LANES), 1)
    slot = part(wide, 2 * RIM)[0]

    def plane(ref, z):
        return ref[z % nz * nx : (z % nz + 1) * nx]

    def up(z):
        return 0.5 * (plane(c_ref, z) + plane(c_ref, z + 1)) * (plane(u_ref, z) - plane(u_ref, z + 1))

    for z in range(nz):
        u, c = plane(u_ref, z), plane(c_ref, z)
        fy = 0.5 * (c + rolled(c, -1, 1)) * (u - rolled(u, -1, 1))
        r_ref[z * nx : (z + 1) * nx] = jnp.where(wide == LANES - 1, 0.0, fy)
    for copy in copies[2 * pieces :]:
        copy.wait()
    below = up(nz - 1)
    for Z in range(nz // COARSEN):
        sum_r = sum_c = jnp.zeros((nx, LANES), f32)
        for z in range(Z * COARSEN, (Z + 1) * COARSEN):
            u, c = plane(u_ref, z), plane(c_ref, z)
            above = up(z)
            fx = 0.5 * (c + rolled(c, -1, 0)) * (u - rolled(u, -1, 0))
            fy = plane(r_ref, z)
            fx = jnp.where(row == nx - 1, 0.0, fx)
            r = plane(s_ref, z) - SHIFT * u - (fx - rolled(fx, 1, 0)) - (fy - rolled(fy, 1, 1)) - (above - below)
            below = above
            r_ref[z * nx : (z + 1) * nx] = r
            sum_r = sum_r + r
            sum_c = sum_c + c
            u0, u2, c0, c2 = u[:SUB], u[nx - SUB :], c[:SUB], c[nx - SUB :]
            first = jnp.where(low, c0, jnp.where(sub == SUB - 1, rolled(u0, -1, 0), rolled(r[:SUB], RIM, 0)))
            last = jnp.where(low, jnp.where(sub == 0, rolled(u2, 1, 0), rolled(r[nx - SUB :], RIM, 0)), c2)
            last_ref[z * SUB : (z + 1) * SUB] = last
            to = z % (nz // 2) * SUB
            (one_ref if z < nz // 2 else two_ref)[to : to + SUB] = first
        sums_ref[Z * nx : (Z + 1) * nx] = sum_r
        sums_ref[(Z + nz // COARSEN) * nx : (Z + nz // COARSEN + 1) * nx] = sum_c

    zs = nz // ZS
    half = zs // 2
    def strips():
        for a, ref in enumerate((u_ref, c_ref, r_ref)):
            for pair in range(half):
                strip = jnp.zeros((nx, LANES), f32)
                for g in range(ZS):
                    for second in range(2):
                        at = 2 * g + second
                        moved = rolled(plane(ref, g * zs + pair + second * half), at * 2 * RIM + RIM, 1)
                        strip = jnp.where(slot == at, moved, strip)
                q_ref[(a * half + pair) * nx : (a * half + pair + 1) * nx] = strip

    def finish():
        coarse = jnp.zeros((SUB, LANES), f32)
        planes = nz // COARSEN
        for Z in range(planes):
            sum_r, sum_c = (sums_ref[(Z + k * planes) * nx : (Z + k * planes + 1) * nx] for k in range(2))
            coarse = coarse + compact(block_rows(sum_r) + rolled(block_rows(sum_c), RIM, 0), Z)
        coarse = coarse * (1.0 / CELLS)
        strips()

        base = 3 * half * nx
        for a, ref in enumerate((u_ref, c_ref)):
            for Z in range(nz // SUB):
                at = Z * SUB * nx
                first, last = picked(ref, at, nx), picked(ref, at + nx - 1, nx)
                spot = a * nz + Z * SUB
                own_ref[spot : spot + SUB] = first
                own_ref[2 * nz + spot : 2 * nz + spot + SUB] = last
                f1_ref[spot : spot + SUB] = jnp.where(even, last, first)
                q_ref[base + spot : base + spot + SUB] = jnp.where(
                    lane < HALF, rolled(first, REACH, 1), rolled(last, REACH + HALF, 1)
                )
        q_ref[base + 2 * nz : base + 2 * nz + SUB] = coarse
        f1_ref[2 * nz :] = coarse

    section(finish)


def pack(u, s, c, nz, nx):
    half = nz // ZS // 2
    pieces = 4
    return pl.pallas_call(
        functools.partial(pack_kernel, nz=nz, nx=nx),
        out_shape=(
            tiles(3 * half * nx // SUB + 2 * nz // SUB + 1),
            tiles(2 * nz // SUB + 1),
            tiles(nz),
            tiles(nz // 2),
            tiles(nz // 2),
            jax.ShapeDtypeStruct(u.shape, f32),
            tiles(4 * nz // SUB),
        ),
        in_specs=[pl.BlockSpec(memory_space=pltpu.HBM)] * 3,
        out_specs=(VMEM,) * 7,
        scratch_shapes=[pltpu.VMEM(u.shape, f32)] * 3
        + [pltpu.VMEM((2 * nz // COARSEN * nx, LANES), f32), pltpu.SemaphoreType.DMA((3, pieces))],
        compiler_params=SMALL,
        name="pack",
    )(*(pltpu.with_memory_space_constraint(x, pltpu.HBM) for x in (u, s, c)))


def facing(own_ref, a, z, nz, last):
    first, second = own_ref[a * nz + z : a * nz + z + SUB], own_ref[(2 + a) * nz + z : (2 + a) * nz + z + SUB]
    return jnp.where(last, second, first)


def join_kernel(q_ref, ql_ref, qr_ref, f1_ref, own_ref, b1_ref, b2_ref, strip_ref, kept_ref, *, nz, nx):
    zs = nz // ZS
    half = zs // 2
    even = is_even()
    sub, lane = iota((SUB, LANES), 0), iota((SUB, LANES), 1)
    low = sub < RIM
    spot = part(iota((nx, LANES), 1), GROUP)[1]
    joined = []
    for a in range(3):
        group = [None] * zs
        for pair in range(half):
            at = slice((a * half + pair) * nx, (a * half + pair + 1) * nx)
            left, own, right = ql_ref[at], q_ref[at], qr_ref[at]
            moved = rolled(jnp.where(spot < RIM, own, right), 2 * RIM, 1)
            one = jnp.where(spot < 2 * RIM, jnp.where(spot < RIM, left, own), moved)
            moved = rolled(jnp.where(spot < 3 * RIM, left, own), -2 * RIM, 1)
            two = jnp.where(spot < 2 * RIM, moved, jnp.where(spot < 3 * RIM, own, right))
            group[pair], group[pair + half] = one, two
            first = jnp.where(low, one[:SUB], rolled(two[:SUB], RIM, 0))
            last = jnp.where(low, rolled(two[nx - SUB :], RIM, 0), one[nx - SUB :])
            to = slice((a * half + pair) * SUB, (a * half + pair + 1) * SUB)
            b1_ref[to] = jnp.where(even, last, first)
            b2_ref[to] = jnp.where(even, first, last)
        for zi in range(zs):
            strip_ref[(a * zs + zi) * nx : (a * zs + zi + 1) * nx] = group[zi]
        joined.append(group)

    source, target = 3 * half * nx, 3 * half * SUB
    lower, outer = lane < HALF, part(lane, HALF)[1] < REACH
    for Z in range(nz // SUB):
        u, c = (
            jnp.where(outer, ql_ref[at : at + SUB], qr_ref[at : at + SUB])
            for at in (source + Z * SUB, source + nz + Z * SUB)
        )
        kept_ref[Z * SUB : (Z + 1) * SUB] = u
        kept_ref[nz + Z * SUB : nz + (Z + 1) * SUB] = c
        first, last = jnp.where(lower, u, rolled(c, HALF, 1)), jnp.where(lower, rolled(u, HALF, 1), c)
        to = slice(target + Z * SUB, target + (Z + 1) * SUB)
        b1_ref[to] = jnp.where(even, last, first)
        b2_ref[to] = jnp.where(even, first, last)

    at = slice(source + 2 * nz, source + 2 * nz + SUB)
    place = part(lane, SPREAD)[1]
    window = jnp.where(
        place < RIM,
        rolled(ql_ref[at], -WIDTH, 1),
        jnp.where(place < RIM + WIDTH, q_ref[at], rolled(qr_ref[at], WIDTH, 1)),
    )
    flux = jnp.zeros((nx, LANES), f32)
    for u, c in zip(joined[0], joined[1]):
        flux = flux + (c + rolled(c, -1, 1)) * (u - rolled(u, -1, 1))
    flux = block_rows((0.5 / CELLS) * flux)
    flux = flux + rolled(flux, -GROUP, 1)
    near, far = RIM - 1, 3 * RIM - 1
    change = jnp.where(place == RIM - 1, -rolled(flux, RIM - 1 - near, 1), 0.0)
    change = jnp.where(place == RIM, rolled(flux, RIM - near, 1), change)
    change = jnp.where(place == RIM + WIDTH - 1, -rolled(flux, RIM + WIDTH - 1 - far, 1), change)
    change = jnp.where(place == RIM + WIDTH, rolled(flux, RIM + WIDTH - far, 1), change)
    rows = nx // COARSEN
    nearest = jnp.where(even, rows - 1, 0)
    for Z in range(nz // COARSEN):
        u, c = facing(own_ref, 0, Z * SUB, nz, even) - tile(f1_ref, Z), facing(own_ref, 1, Z * SUB, nz, even)
        across = all_rows((0.5 / CELLS) * (c + tile(f1_ref, nz // SUB + Z)) * u)
        change = change - compact(jnp.where(sub == nearest, across, 0.0), Z)
    mate = f1_ref[2 * nz : 2 * nz + SUB]
    mate = jnp.where(even, rolled(mate, rows - RIM, 0), rolled(mate, 1 - RIM, 0))
    cond = jnp.where(sub == rows, mate, rolled(window, -RIM, 0))
    rhs = window + change
    kept_ref[2 * nz : 2 * nz + SUB] = cond
    kept_ref[2 * nz + SUB :] = rhs
    to = target + nz
    b1_ref[to:] = cond
    b2_ref[to : to + SUB] = cond
    b2_ref[to + SUB : to + 2 * SUB] = rhs
    to = to + 2 * SUB
    for a in range(2):
        for Z in range(nz // SUB):
            at = to + a * nz + Z * SUB
            b2_ref[at : at + SUB] = facing(own_ref, a, Z * SUB, nz, jnp.logical_not(even))


def join(q, ql, qr, f1, own, nz, nx):
    zs = nz // ZS
    size = 3 * (zs // 2) + nz // SUB + 1
    return pl.pallas_call(
        functools.partial(join_kernel, nz=nz, nx=nx),
        out_shape=(
            tiles(size),
            tiles(size + 1 + 2 * nz // SUB),
            jax.ShapeDtypeStruct((3 * zs * nx, LANES), f32),
            tiles(2 * nz // SUB + 2),
        ),
        in_specs=[VMEM] * 5,
        out_specs=(VMEM,) * 4,
        compiler_params=SMALL,
        name="join",
    )(q, ql, qr, f1, own)


def faces_kernel(own_ref, kept_ref, r2_ref, r1_ref, after_ref, o_ref, *, nz, nx):
    del after_ref
    half = nz // ZS // 2
    even = is_even()
    sub, lane = iota((SUB, LANES), 0), iota((SUB, LANES), 1)
    plane, place = part(lane, SPREAD)
    rows = nx // COARSEN
    base = 3 * half * SUB

    outer = REACH // COARSEN
    is_left, is_right = (place >= RIM - outer) & (place < RIM), (place >= RIM + WIDTH) & (place < RIM + WIDTH + outer)
    is_own = (place >= RIM) & (place < RIM + WIDTH)
    source = jnp.where(is_left, place - (RIM - outer), place - (RIM + WIDTH - outer))
    source = jnp.where(sub == 0, place - RIM, source) * COARSEN
    source = jnp.clip(source, 0, LANES - COARSEN)
    valid = ((sub == 0) & is_own) | ((sub > 0) & (is_left | is_right))

    def outside(r_ref, Z, upper):
        def mine(at):
            tile_at = kept_ref[at + Z * SUB : at + (Z + 1) * SUB]
            return jnp.where(upper, rolled(tile_at, HALF, 1), tile_at)

        other = r_ref[base + Z * SUB : base + (Z + 1) * SUB]
        return all_rows(0.5 * (mine(nz) + rolled(other, HALF, 1)) * (mine(0) - other))

    odd = jnp.logical_not(even)
    far_rows = base + nz + 2 * SUB
    flux = jnp.zeros((SUB, LANES), f32)
    for Z in range(nz // COARSEN):
        u, c = (
            (facing(own_ref, a, Z * SUB, nz, odd), r2_ref[at : at + SUB])
            for a, at in ((0, far_rows + Z * SUB), (1, far_rows + nz + Z * SUB))
        )
        one = all_rows(0.5 * (c[0] + c[1]) * (u[0] - u[1]))
        two = outside(r2_ref, Z, odd)
        three = outside(r1_ref, Z, even)
        sums = jnp.where(sub == 0, one, jnp.where(sub == 1, two, jnp.where(sub == 2, three, 0.0)))
        here = valid & (plane == Z)
        flux = flux + jnp.where(here, gathered(sums, source), 0.0)
    flux = flux * (1.0 / CELLS)
    far, mate = flux[0:1] + flux[1:2], flux[2:3]

    def stacked(own, other):
        before, after = jnp.where(even, other, own), jnp.where(even, own, other)
        return jnp.where(sub <= rows, rolled(before, 1, 0), rolled(after, rows + 1, 0))

    at = base + nz + SUB
    rhs = stacked(kept_ref[2 * nz + SUB :], r2_ref[at : at + SUB])
    sign = jnp.where(even, 1.0, -1.0)
    rhs = rhs + jnp.where(sub == rows, sign * far, jnp.where(sub == rows + 1, -sign * far, 0.0))
    rhs = rhs - jnp.where(sub == jnp.where(even, 2 * rows, 1), mate, 0.0)

    at = at - SUB
    near_c, far_c = r1_ref[at : at + SUB], r2_ref[at : at + SUB]
    cond = stacked(kept_ref[2 * nz : 2 * nz + SUB], far_c)
    before = jnp.where(even, rolled(far_c, -rows, 0), rolled(near_c, 1 - rows, 0))
    after = jnp.where(even, rolled(near_c, 2 * rows + 1, 0), rolled(far_c, rows + 1, 0))
    cond = jnp.where(sub == 0, before, jnp.where(sub == 2 * rows + 1, after, cond))
    around = rolled(cond, -1, 0) + rolled(cond, 1, 0) + rolled(cond, -1, 1) + rolled(cond, 1, 1)
    around = around + rolled(cond, -SPREAD, 1) + rolled(cond, SPREAD, 1)
    weight = OMEGA / (SHIFT + (0.5 / COARSEN**2) * (6.0 * cond + around))
    o_ref[0:SUB] = weight * rhs
    o_ref[SUB : 2 * SUB] = weight
    o_ref[2 * SUB :] = cond


def faces(own, kept, r2, r1, after, nz, nx):
    return pl.pallas_call(
        functools.partial(faces_kernel, nz=nz, nx=nx),
        out_shape=tiles(3),
        in_specs=[VMEM] * 4 + [pl.BlockSpec(memory_space=pl.ANY)],
        out_specs=VMEM,
        compiler_params=SMALL,
        name="faces",
    )(own, kept, r2, r1, after)


def sides(even, one, two):
    return jnp.where(even, one, two), jnp.where(even, two, one)


def rim_of(low, after, before):
    return jnp.where(low, after, before), rolled(jnp.where(low, before, after), RIM, 0)


def rims_of(low, one_ref, two_ref, last_ref, nz):
    half = nz // 2
    for z in range(nz):
        yield rim_of(low, tile(one_ref if z < half else two_ref, z % half), tile(last_ref, z))


def rim_faces(sub, face, rim_face, u_first, u_last, rim):
    u_rim = jnp.where(sub == 0, rolled(rim, 1 - RIM, 0), rolled(rim, RIM - 1, 0))
    end = sub == SUB - 1
    after = jnp.where(end, face * (u_last - rolled(u_rim, -1, 0)), 0.0)
    before = jnp.where(end, rim_face * (u_rim - rolled(u_first, -1, 0)), 0.0)
    return after, before


def beside(w, z, zs, column):
    return rolled(w, -column - z // zs * GROUP, 1)


def window(spot, left, right, column):
    return jnp.where(spot == RIM - 1, left, rolled(right, RIM - 2 - column, 1))


def begin_kernel(
    strip_ref, u_ref, c_ref, r_ref, cx_ref, cy_ref, cz_ref, diag_ref, inv_ref, q_ref, v_ref, *, nz, nx
):
    zs = nz // ZS
    spot = part(iota((nx, LANES), 1), GROUP)[1]
    row, lane = iota((nx, LANES), 0), iota((nx, LANES), 1)
    first_lane, last_lane = lane == 0, lane == LANES - 1

    def strip(a, zi):
        return strip_ref[(a * zs + zi) * nx : (a * zs + zi + 1) * nx]

    edge_c, edge_f = [], []
    for zi in range(zs):
        u, c = strip(0, zi), strip(1, zi)
        flux = 0.5 * (c + rolled(c, -1, 1)) * (u - rolled(u, -1, 1))
        edge_c.append(window(spot, c, c, 3 * RIM))
        edge_f.append(window(spot, flux, flux, 3 * RIM - 1))

    def own(ref, z):
        return ref[z % nz * nx : (z % nz + 1) * nx]

    below = 0.5 * (own(c_ref, -1) + own(c_ref, 0))
    for z in range(nz):
        at = slice(z * nx, (z + 1) * nx)
        c = own(c_ref, z)
        gx = jnp.where(row == nx - 1, 0.0, 0.5 * (c + rolled(c, -1, 0)))
        edge = beside(edge_c[z % zs], z, zs, RIM - 1)
        gy = 0.5 * (c + jnp.where(last_lane, edge, rolled(c, -1, 1)))
        gyl = 0.5 * (c + jnp.where(first_lane, edge, rolled(c, 1, 1)))
        above = 0.5 * (c + own(c_ref, z + 1))
        diag = SHIFT + (gx + rolled(gx, 1, 0)) + (gy + gyl) + (above + below)
        edge = beside(edge_f[z % zs], z, zs, RIM - 1)
        r = own(r_ref, z) + jnp.where(first_lane, edge, jnp.where(last_lane, -edge, 0.0))
        inner = slice(SUB, nx - SUB)
        inverse = 1.0 / diag[inner]
        scaled = r[inner] * inverse
        cx_ref[at] = gx
        cy_ref[at] = gy
        cz_ref[at] = above
        diag_ref[at] = diag
        q_ref[at] = jnp.concatenate([r[:SUB], scaled, r[nx - SUB :]], axis=0)
        to = slice(z * (nx - 2 * SUB), (z + 1) * (nx - 2 * SUB))
        inv_ref[to] = inverse
        v_ref[to] = scaled * (1.0 / THETA)
        below = above


def begin(strips, u, c, r, nz, nx):
    inner = jax.ShapeDtypeStruct((nz * (nx - 2 * SUB), LANES), f32)
    return pl.pallas_call(
        functools.partial(begin_kernel, nz=nz, nx=nx),
        out_shape=(jax.ShapeDtypeStruct(u.shape, f32),) * 4 + (inner, jax.ShapeDtypeStruct(u.shape, f32), inner),
        in_specs=[VMEM] * 4,
        out_specs=(VMEM,) * 7,
        compiler_params=SMALL,
        cost_estimate=pl.CostEstimate(flops=40 * u.size, bytes_accessed=40 * u.size, transcendentals=0),
        name="begin",
    )(strips, u, c, r)


def fine_kernel(
    strip_ref, b2_ref, b1_ref, one_ref, two_ref, last_ref, u_ref, c_ref, cx_ref, cy_ref, cz_ref, diag_ref, inv_ref, q_ref, v_ref,
    cx, inv, q, va, acc, w2,
    ch, cyh, czh, vb, wr, w0, w1,
    *, nz, nx,
):
    zs = nz // ZS
    half = zs // 2
    ext = nx + SUB
    even = is_even()
    sub = iota((SUB, LANES), 0)
    low, end = sub < RIM, sub == SUB - 1
    table = steps()

    rims = []
    for z, (cond, rim) in enumerate(rims_of(low, one_ref, two_ref, last_ref, nz)):
        ch[z * SUB : (z + 1) * SUB] = cond
        rims.append(rim)

    row, spot = iota((ext, LANES), 0), part(iota((ext, LANES), 1), GROUP)[1]

    def strips_of(a):
        ends = [None] * zs
        for pair in range(half):
            index = a * half + pair
            ends[pair], ends[pair + half] = rim_of(low, *sides(even, tile(b1_ref, index), tile(b2_ref, index)))
        return [
            jnp.concatenate([strip_ref[(a * zs + zi) * nx : (a * zs + zi + 1) * nx], ends[zi]], axis=0)
            for zi in range(zs)
        ]

    def z_up(x):
        return x[1:] + [rolled(x[0], -GROUP, 1)]

    def z_down(x):
        return [rolled(x[-1], GROUP, 1)] + x[:-1]

    us, cs, rs = strips_of(0), strips_of(1), strips_of(2)
    cxs = [0.5 * (c + rolled(c, -1, 0)) for c in cs]
    cys = [0.5 * (c + rolled(c, -1, 1)) for c in cs]
    czs = [0.5 * (c + d) for c, d in zip(cs, z_up(cs))]
    czds = z_down(czs)
    invs, qs, vs = [], [], []
    for zi in range(zs):
        u = us[zi]
        fx = jnp.where((row == nx - 1) | (row == ext - 1), cxs[zi] * (u - rolled(u, -1, 0)), 0.0)
        fy = jnp.where((spot == RIM - 1) | (spot == 3 * RIM - 1), cys[zi] * (u - rolled(u, -1, 1)), 0.0)
        r = rs[zi] - (fx - rolled(fx, 1, 0)) - (fy - rolled(fy, 1, 1))
        wr[zi * SUB : (zi + 1) * SUB] = jnp.where(spot == RIM, r, rolled(r, -2 * RIM, 1))[nx:]
        diag = SHIFT + (cxs[zi] + rolled(cxs[zi], 1, 0)) + (cys[zi] + rolled(cys[zi], 1, 1)) + (czs[zi] + czds[zi])
        invs.append(1.0 / diag)
        qs.append(r * invs[zi])
        vs.append(qs[zi] * (1.0 / THETA))
    for k, w in enumerate((w0, w1, w2)):
        prod = [cys[zi] * vs[zi] for zi in range(zs)]
        for zi in range(zs):
            w[zi * ext : (zi + 1) * ext] = window(spot, prod[zi], vs[zi], 3 * RIM)
        if k == SWEEPS - 1:
            break
        keep, lift = table[k]
        v_up, v_down = z_up(vs), z_down(vs)
        fresh = []
        for zi in range(zs):
            v = vs[zi]
            near = cxs[zi] * rolled(v, -1, 0) + rolled(cxs[zi] * v, 1, 0)
            near = near + cys[zi] * rolled(v, -1, 1) + rolled(prod[zi], 1, 1)
            near = near + czs[zi] * v_up[zi] + czds[zi] * v_down[zi]
            qs[zi] = qs[zi] - v + near * invs[zi]
            fresh.append(keep * v + lift * qs[zi])
        vs = fresh
    edge_c = [window(spot, c, c, 3 * RIM)[nx:] for c in cs]

    lane = iota((SUB, LANES), 1)
    first_lane, last_lane = lane == 0, lane == LANES - 1

    def own(ref, z):
        return ref[z % nz * nx : (z % nz + 1) * nx]

    def rim_at(ref, z):
        return tile(ref, z % nz)

    below = 0.5 * (rim_at(ch, -1) + rim_at(ch, 0))
    for z in range(nz):
        at = slice(z * SUB, (z + 1) * SUB)
        u, c = own(u_ref, z), tile(ch, z)
        c_first, c_last = own(c_ref, z)[:SUB], own(c_ref, z)[nx - SUB :]
        zi = z % zs
        face = jnp.where(end, 0.5 * (c_last + rolled(c, -1, 0)), 0.0)
        gx = 0.5 * (c + jnp.where(end, rolled(c_first, -1, 0), rolled(c, -1, 0)))
        gxl = rolled(gx, 1, 0)
        edge = beside(edge_c[zi], z, zs, RIM - 1)
        gy = 0.5 * (c + jnp.where(last_lane, edge, rolled(c, -1, 1)))
        gyl = 0.5 * (c + jnp.where(first_lane, edge, rolled(c, 1, 1)))
        above = 0.5 * (c + rim_at(ch, z + 1))
        diag = SHIFT + (gx + jnp.where(sub == 0, rolled(face, 1, 0), gxl)) + (gy + gyl) + (above + below)
        after, before = rim_faces(sub, face, gx, u[:SUB], u[nx - SUB :], rims[z])
        r = rims[z] + rolled(after, 1, 0) - before
        r = jnp.where(first_lane | last_lane, beside(wr[zi * SUB : (zi + 1) * SUB], z, zs, RIM), r)
        own_diag, own_q = own(diag_ref, z), own(q_ref, z)
        long_at = slice(z * ext, (z + 1) * ext)
        parts = []
        for this_diag, this_r in (
            (own_diag[:SUB] + jnp.where(sub == 0, gxl, 0.0), own_q[:SUB] + rolled(before, 1, 0)),
            (own_diag[nx - SUB :] + face, own_q[nx - SUB :] - after),
            (diag, r),
        ):
            inverse = 1.0 / this_diag
            scaled = this_r * inverse
            parts.append((inverse, scaled, scaled * (1.0 / THETA)))
        inner = slice(z * (nx - 2 * SUB), (z + 1) * (nx - 2 * SUB))
        middle = (inv_ref[inner], own_q[SUB : nx - SUB], v_ref[inner])
        for ref, one, two, three, four in zip((inv, q, va), parts[0], middle, parts[1], parts[2]):
            ref[long_at] = jnp.concatenate([one, two, three, four], axis=0)
        own_cx = own(cx_ref, z)
        cx[long_at] = jnp.concatenate([own_cx[: nx - SUB], own_cx[nx - SUB :] + face, gx], axis=0)
        cyh[at] = gy
        czh[at] = above
        below = above

    lane = iota((ext, LANES), 1)
    first_lane, last_lane = lane == 0, lane == LANES - 1

    def whole(ref, rim, z):
        return jnp.concatenate([own(ref, z), rim_at(rim, z)], axis=0)

    def long(ref, z):
        return ref[z % nz * ext : (z % nz + 1) * ext]

    for k, w in enumerate((w0, w1)):
        old, new = (va, vb) if k % 2 == 0 else (vb, va)
        keep, lift = table[k]
        for z in range(nz):
            at, here = slice(z * ext, (z + 1) * ext), slice(z * nx, (z + 1) * nx)
            zi = z % zs
            v, gx, gy = old[at], cx[at], whole(cy_ref, cyh, z)
            edge = beside(w[zi * ext : (zi + 1) * ext], z, zs, RIM - 1)
            near = gx * rolled(v, -1, 0) + rolled(gx * v, 1, 0)
            near = near + gy * jnp.where(last_lane, edge, rolled(v, -1, 1))
            near = near + jnp.where(first_lane, edge, rolled(gy * v, 1, 1))
            near = near + whole(cz_ref, czh, z) * long(old, z + 1) + whole(cz_ref, czh, z - 1) * long(old, z - 1)
            scaled = q[at] - v + near * inv[at]
            fresh = keep * v + lift * scaled
            q[at] = scaled
            new[at] = fresh
            acc[here] = (own(u_ref, z) + v[:nx] if k == 0 else acc[here]) + fresh[:nx]


def fine(strips, b2, b1, one, two, last, u, c, begun, nz, nx):
    zs = nz // ZS
    ext = nx + SUB
    rim = pltpu.VMEM((nz * SUB, LANES), f32)
    full = jax.ShapeDtypeStruct((nz * ext, LANES), f32)
    strip = pltpu.VMEM((zs * ext, LANES), f32)
    return pl.pallas_call(
        functools.partial(fine_kernel, nz=nz, nx=nx),
        out_shape=(full,) * 4 + (jax.ShapeDtypeStruct(u.shape, f32), jax.ShapeDtypeStruct((zs * ext, LANES), f32)),
        in_specs=[VMEM] * 15,
        out_specs=(VMEM,) * 6,
        scratch_shapes=[rim] * 3 + [pltpu.VMEM((nz * ext, LANES), f32), pltpu.VMEM((zs * SUB, LANES), f32)] + [strip] * 2,
        compiler_params=SMALL,
        cost_estimate=pl.CostEstimate(flops=100 * u.size, bytes_accessed=40 * u.size, transcendentals=0),
        name="fine",
    )(strips, b2, b1, one, two, last, u, c, *begun)


def finish_kernel(
    cx_ref, inv_ref, q_ref, v_ref, sum_ref, w_ref, cy_ref, cz_ref, m_ref, r_ref, o_ref, out, sems, *, nz, nx
):
    zs = nz // ZS
    ext = nx + SUB
    rows = nx // COARSEN
    even = is_even()
    sub, lane = iota((SUB, LANES), 0), iota((SUB, LANES), 1)
    beyond = sub == jnp.where(even, 2 * rows + 1, 0)
    fields = []
    for a in range(3):
        mine, mate = tile(m_ref, a), tile(r_ref, a)
        mate = jnp.where(even, rolled(mate, 2 * rows, 0), rolled(mate, -2 * rows, 0))
        fields.append(jnp.concatenate([jnp.where(beyond, mate, mine), mate], axis=0))
    start, weight, cond = fields
    scale = 0.5 / COARSEN**2
    turns = (-1, 0), (1, 0), (-1, 1), (1, 1), (-SPREAD, 1), (SPREAD, 1)
    shares = [scale * (cond + rolled(cond, *turn)) for turn in turns]
    keep = 1.0 - weight * (SHIFT + sum(shares))
    shares = [weight * share for share in shares]
    v = start
    for _ in range(COARSE_SWEEPS - 1):
        terms = [share * rolled(v, *turn) for share, turn in zip(shares, turns)]
        v = (start + keep * v) + ((terms[0] + terms[1]) + (terms[2] + terms[3]) + (terms[4] + terms[5]))
    top = v[:SUB]
    top = jnp.where(even, rolled(top, -rows - 1, 0), rolled(top, -1, 0))

    wide = iota((nx, LANES), 1)
    first_lane, last_lane = wide == 0, wide == LANES - 1
    keep, lift = steps()[-1]

    def own(ref, z):
        return ref[z % nz * nx : (z % nz + 1) * nx]

    def long(ref, z):
        return ref[z % nz * ext : z % nz * ext + nx]

    copies = []
    size = COARSEN * nx
    for Z in range(nz // COARSEN):
        spread = jnp.take_along_axis(top, Z * SPREAD + RIM + part(lane, COARSEN)[0], axis=1)
        value = jnp.concatenate([jnp.broadcast_to(spread[X : X + 1], (COARSEN, LANES)) for X in range(rows)], axis=0)
        for z in range(Z * COARSEN, (Z + 1) * COARSEN):
            at = slice(z * ext, (z + 1) * ext)
            v, gx = v_ref[at], cx_ref[at]
            near = (gx * rolled(v, -1, 0) + rolled(gx * v, 1, 0))[:nx]
            v, gy, zi = v[:nx], own(cy_ref, z), z % zs
            edge = beside(w_ref[zi * ext : zi * ext + nx], z, zs, RIM - 1)
            near = near + gy * jnp.where(last_lane, edge, rolled(v, -1, 1))
            near = near + jnp.where(first_lane, edge, rolled(gy * v, 1, 1))
            near = near + own(cz_ref, z) * long(v_ref, z + 1) + own(cz_ref, z - 1) * long(v_ref, z - 1)
            scaled = long(q_ref, z) - v + near * long(inv_ref, z)
            here = slice(z * nx, (z + 1) * nx)
            out[here] = (own(sum_ref, z) + (keep * v + lift * scaled)) + value
        here = pl.ds(Z * size, size)
        copies.append(pltpu.make_async_copy(out.at[here], o_ref.at[here], sems.at[Z]))
        copies[-1].start()
    for copy in copies:
        copy.wait()


def finish(passed, cy, cz, m, r, nz, nx):
    shape = (nz * nx, LANES)
    return pl.pallas_call(
        functools.partial(finish_kernel, nz=nz, nx=nx),
        out_shape=jax.ShapeDtypeStruct(shape, f32),
        in_specs=[VMEM] * 10,
        out_specs=pl.BlockSpec(memory_space=pltpu.HBM),
        scratch_shapes=[pltpu.VMEM(shape, f32), pltpu.SemaphoreType.DMA((nz // COARSEN,))],
        compiler_params=SMALL,
        name="finish",
    )(*passed, cy, cz, m, r)


def moves():
    size_x, size_y = lax.axis_size("gx"), lax.axis_size("gy")

    def send(x, go):
        pairs = []
        for i in range(size_x):
            for j in range(size_y):
                k, l = go(i, j)
                pairs.append((i * size_y + j, (k % size_x) * size_y + l % size_y))
        return lax.ppermute(x, ("gx", "gy"), pairs)

    def mate(x):
        return send(x, lambda i, j: (i + 1 if i % 2 == 0 else i - 1, j))

    def shift(x, by):
        return send(x, lambda i, j: (i + by, j))

    def far(x):
        return send(x, lambda i, j: (i - 1 if i % 2 == 0 else i + 1, j))

    def beside_y(x):
        left = send(x, lambda i, j: (i, j + 1))
        if size_y == 2:
            return left, left
        return left, send(x, lambda i, j: (i, j - 1))

    return mate, far, shift, beside_y


def body(iterate, source, conduct):
    nz, nx, ny = iterate.shape
    if nz != ZS * 4 or ny != LANES or nx != 3 * SUB or lax.axis_size("gx") % 2:
        raise ValueError("shapes")
    mate, far, shift, beside_y = moves()
    u, s, c = (x.reshape(nz * nx, ny) for x in (iterate, source, conduct))
    q, f1, last, one, two, r, own = pack(u, s, c, nz, nx)
    ql, qr = beside_y(q)
    rf1 = mate(f1)
    before = shift(last, 1)
    b1, b2, strips, kept = join(q, ql, qr, rf1, own, nz, nx)
    rb2 = far(b2)
    rb1 = mate(b1)
    one, two, strips = lax.optimization_barrier((one, two, strips))
    after = shift(one, -1), shift(two, -1)
    begun = begin(strips, u, c, r, nz, nx)
    m = faces(own, kept, rb2, rb1, begun[0], nz, nx)
    rm = mate(m)
    passed = fine(strips, rb2, rb1, *after, before, u, c, begun, nz, nx)
    return finish(passed, begun[1], begun[2], m, rm, nz, nx).reshape(nz, nx, ny)


def solution(mesh):
    spec = P(None, "gx", "gy")
    return jax.shard_map(body, mesh=mesh, in_specs=(spec,) * 3, out_specs=spec, check_vma=False)
```

```python
import functools

import jax
import jax.numpy as jnp
from jax import lax
from jax.experimental import pallas as pl
from jax.experimental.pallas import tpu as pltpu
from jax.sharding import PartitionSpec as P

SWEEPS = 3
COARSE_SWEEPS = 4
COARSEN = 8

SHIFT = 0.1
LMIN = 0.3
LMAX = 2.0
OMEGA = 0.8

THETA = (LMAX + LMIN) / 2.0
DELTA = (LMAX - LMIN) / 2.0
SIGMA = THETA / DELTA

RIM = SWEEPS + 1
SUB = 8
LANES = 128
HALF = LANES // 2
GROUP = 4 * RIM
ZS = LANES // GROUP
WIDTH = LANES // COARSEN
SPREAD = 2 * WIDTH
REACH = (COARSE_SWEEPS - 1) * COARSEN
CELLS = COARSEN**3

f32 = jnp.float32
VMEM = pl.BlockSpec(memory_space=pltpu.VMEM)
SMALL = pltpu.CompilerParams(vmem_limit_bytes=12 * 1024 * 1024)


def steps():
    rho, listed = 1.0 / SIGMA, []
    for _ in range(SWEEPS):
        nxt = 1.0 / (2.0 * SIGMA - rho)
        listed.append((nxt * rho, 2.0 * nxt / DELTA))
        rho = nxt
    return listed


def iota(shape, dim):
    return lax.broadcasted_iota(jnp.int32, shape, dim)


def part(index, size):
    return lax.shift_right_logical(index, size.bit_length() - 1), lax.bitwise_and(index, size - 1)


def rolled(x, by, dim):
    return pltpu.roll(x, by % x.shape[dim], dim)


def is_even():
    return lax.axis_index("gx") % 2 == 0


def tiles(count):
    return jax.ShapeDtypeStruct((count * SUB, LANES), f32)


def tile(ref, index):
    return ref[index * SUB : (index + 1) * SUB]


def picked(ref, start, stride):
    return ref[pl.ds(start, SUB, stride=stride), :]


def gathered(rows, source):
    parts = [jnp.take_along_axis(rows, source + k, axis=1) for k in range(COARSEN)]
    while len(parts) > 1:
        parts = [a + b for a, b in zip(parts[::2], parts[1::2])]
    return parts[0]


def compact(rows, place):
    plane, column = part(iota(rows.shape, 1), SPREAD)
    column = column - RIM
    source = jnp.clip(column * COARSEN, 0, LANES - COARSEN)
    here = (plane == place) & (column >= 0) & (column < WIDTH)
    return jnp.where(here, gathered(rows, source), 0.0)


def section(run):
    pl.when(lax.axis_index("gx") >= 0)(run)


def block_rows(values):
    sub = iota((SUB, LANES), 0)
    out = jnp.zeros((SUB, LANES), f32)
    for block in range(values.shape[0] // COARSEN):
        part = values[block * COARSEN : (block + 1) * COARSEN]
        out = jnp.where(sub == block, jnp.sum(part, axis=0, keepdims=True), out)
    return out


def all_rows(values):
    return jnp.sum(values, axis=0, keepdims=True)


def pack_kernel(
    u_hbm, s_hbm, c_hbm, q_ref, f1_ref, last_ref, one_ref, two_ref, r_ref, own_ref, u_ref, s_ref, c_ref, sums_ref, sems, *, nz, nx
):
    pieces = sems.shape[1]
    size = nz * nx // pieces
    copies = []
    for k, (source, target) in enumerate(((c_hbm, c_ref), (u_hbm, u_ref), (s_hbm, s_ref))):
        for piece in range(pieces):
            at = pl.ds(piece * size, size)
            copies.append(pltpu.make_async_copy(source.at[at], target.at[at], sems.at[k, piece]))
    for copy in copies:
        copy.start()
    for copy in copies[: 2 * pieces]:
        copy.wait()

    even = is_even()
    sub, lane = iota((SUB, LANES), 0), iota((SUB, LANES), 1)
    low = sub < RIM
    row, wide = iota((nx, LANES), 0), iota((nx, LANES), 1)
    slot, spot = part(wide, 2 * RIM)

    def plane(ref, z):
        return ref[z % nz * nx : (z % nz + 1) * nx]

    def up(z):
        return 0.5 * (plane(c_ref, z) + plane(c_ref, z + 1)) * (plane(u_ref, z) - plane(u_ref, z + 1))

    for z in range(nz):
        u, c = plane(u_ref, z), plane(c_ref, z)
        fy = 0.5 * (c + rolled(c, -1, 1)) * (u - rolled(u, -1, 1))
        r_ref[z * nx : (z + 1) * nx] = jnp.where(wide == LANES - 1, 0.0, fy)
    for copy in copies[2 * pieces :]:
        copy.wait()
    below = up(nz - 1)
    for Z in range(nz // COARSEN):
        sum_r = sum_c = jnp.zeros((nx, LANES), f32)
        for z in range(Z * COARSEN, (Z + 1) * COARSEN):
            u, c = plane(u_ref, z), plane(c_ref, z)
            above = up(z)
            fx = 0.5 * (c + rolled(c, -1, 0)) * (u - rolled(u, -1, 0))
            fy = plane(r_ref, z)
            fx = jnp.where(row == nx - 1, 0.0, fx)
            r = plane(s_ref, z) - SHIFT * u - (fx - rolled(fx, 1, 0)) - (fy - rolled(fy, 1, 1)) - (above - below)
            below = above
            r_ref[z * nx : (z + 1) * nx] = r
            sum_r = sum_r + r
            sum_c = sum_c + c
            u0, u2, c0, c2 = u[:SUB], u[nx - SUB :], c[:SUB], c[nx - SUB :]
            first = jnp.where(low, c0, jnp.where(sub == SUB - 1, rolled(u0, -1, 0), rolled(r[:SUB], RIM, 0)))
            last = jnp.where(low, jnp.where(sub == 0, rolled(u2, 1, 0), rolled(r[nx - SUB :], RIM, 0)), c2)
            last_ref[z * SUB : (z + 1) * SUB] = last
            to = z % (nz // 2) * SUB
            (one_ref if z < nz // 2 else two_ref)[to : to + SUB] = first
        sums_ref[Z * nx : (Z + 1) * nx] = sum_r
        sums_ref[(Z + nz // COARSEN) * nx : (Z + nz // COARSEN + 1) * nx] = sum_c

    zs = nz // ZS
    half = zs // 2
    def strips():
        for zi in range(zs):
            strip = jnp.zeros((nx, LANES), f32)
            for g in range(ZS):
                z, at = g * zs + zi, g * GROUP + RIM
                outer = jnp.where(spot < 2, rolled(plane(u_ref, z), at + RIM + 1, 1), rolled(plane(r_ref, z), at + 2 * RIM + 1, 1))
                strip = jnp.where(slot == 2 * g + 1, outer, strip)
                strip = jnp.where(slot == 2 * g, rolled(plane(c_ref, z), at, 1), strip)
            q_ref[zi * nx : (zi + 1) * nx] = strip

    def finish():
        coarse = jnp.zeros((SUB, LANES), f32)
        planes = nz // COARSEN
        for Z in range(planes):
            sum_r, sum_c = (sums_ref[(Z + k * planes) * nx : (Z + k * planes + 1) * nx] for k in range(2))
            coarse = coarse + compact(block_rows(sum_r) + rolled(block_rows(sum_c), RIM, 0), Z)
        coarse = coarse * (1.0 / CELLS)
        strips()

        base = zs * nx + SUB
        for a, ref in enumerate((u_ref, c_ref)):
            for Z in range(nz // SUB):
                at = Z * SUB * nx
                first, last = picked(ref, at, nx), picked(ref, at + nx - 1, nx)
                to = a * nz + Z * SUB
                own_ref[to : to + SUB] = first
                own_ref[2 * nz + to : 2 * nz + to + SUB] = last
                f1_ref[to : to + SUB] = jnp.where(even, last, first)
                q_ref[base + to : base + to + SUB] = jnp.where(
                    lane < HALF, rolled(first, REACH, 1), rolled(last, REACH + HALF, 1)
                )
        q_ref[base + 2 * nz : base + 2 * nz + SUB] = coarse
        f1_ref[2 * nz :] = coarse
        corners = jnp.zeros((SUB, LANES), f32)
        group = part(lane, GROUP)[0]
        for Z in range(nz // SUB):
            at = Z * SUB * nx
            first, last = picked(u_ref, at, nx), picked(u_ref, at + nx - 1, nx)
            both = jnp.where(low, first, rolled(last, RIM, 0)), jnp.where(low, rolled(first, RIM, 0), last)
            for second in range(2):
                g = 2 * Z + second
                corners = jnp.where(group == g, rolled(both[second], g * GROUP + RIM, 1), corners)
        q_ref[zs * nx : base] = corners

    section(finish)


def pack(u, s, c, nz, nx):
    pieces = 4
    return pl.pallas_call(
        functools.partial(pack_kernel, nz=nz, nx=nx),
        out_shape=(
            tiles(nz // ZS * nx // SUB + 2 * nz // SUB + 2),
            tiles(2 * nz // SUB + 1),
            tiles(nz),
            tiles(nz // 2),
            tiles(nz // 2),
            jax.ShapeDtypeStruct(u.shape, f32),
            tiles(4 * nz // SUB),
        ),
        in_specs=[pl.BlockSpec(memory_space=pltpu.HBM)] * 3,
        out_specs=(VMEM,) * 7,
        scratch_shapes=[pltpu.VMEM(u.shape, f32)] * 3
        + [pltpu.VMEM((2 * nz // COARSEN * nx, LANES), f32), pltpu.SemaphoreType.DMA((3, pieces))],
        compiler_params=SMALL,
        name="pack",
    )(*(pltpu.with_memory_space_constraint(x, pltpu.HBM) for x in (u, s, c)))


def facing(own_ref, a, z, nz, last):
    first, second = own_ref[a * nz + z : a * nz + z + SUB], own_ref[(2 + a) * nz + z : (2 + a) * nz + z + SUB]
    return jnp.where(last, second, first)


def join_kernel(q_ref, ql_ref, qr_ref, f1_ref, own_ref, b1_ref, b2_ref, strip_ref, kept_ref, *, nz, nx):
    zs = nz // ZS
    half = zs // 2
    even = is_even()
    sub, lane = iota((SUB, LANES), 0), iota((SUB, LANES), 1)
    low = sub < RIM
    spot = part(iota((nx, LANES), 1), GROUP)[1]
    thin, row = part(lane, GROUP)[1], iota((nx, LANES), 0)

    def before(spot, left, own, right):
        moved = rolled(jnp.where(spot < RIM, own, right), 2 * RIM, 1)
        return jnp.where(spot < 2 * RIM, jnp.where(spot < RIM, left, own), moved)

    def behind(spot, left, own, right):
        lower, at = spot < 2 * RIM, 2 * RIM
        split = spot < at + 2 + SWEEPS
        residual = jnp.where(
            lower,
            rolled(jnp.where(split, left, own), -(at + 1), 1),
            rolled(jnp.where(split, own, right), -1, 1),
        )
        split = spot == at
        u = jnp.where(
            lower,
            rolled(jnp.where(split, left, own), RIM - 1 - at, 1),
            rolled(jnp.where(split, own, right), RIM - 1, 1),
        )
        return residual, u

    at = slice(zs * nx, zs * nx + SUB)
    corners = before(thin, ql_ref[at], q_ref[at], qr_ref[at])
    joined = [], [], []
    for zi in range(zs):
        at = slice(zi * nx, (zi + 1) * nx)
        parts = ql_ref[at], q_ref[at], qr_ref[at]
        residual, u = behind(spot, *parts)
        u = jnp.where(row == 0, corners[zi : zi + 1], u)
        u = jnp.where(row == nx - 1, corners[RIM + zi : RIM + zi + 1], u)
        for group, strip in zip(joined, (u, before(spot, *parts), residual)):
            group.append(strip)
    for a, group in enumerate(joined):
        for zi in range(zs):
            strip_ref[(a * zs + zi) * nx : (a * zs + zi + 1) * nx] = group[zi]
        for pair in range(half):
            one, two = group[pair], group[pair + half]
            first = jnp.where(low, one[:SUB], rolled(two[:SUB], RIM, 0))
            last = jnp.where(low, rolled(two[nx - SUB :], RIM, 0), one[nx - SUB :])
            to = slice((a * half + pair) * SUB, (a * half + pair + 1) * SUB)
            b1_ref[to] = jnp.where(even, last, first)
            b2_ref[to] = jnp.where(even, first, last)

    source, target = zs * nx + SUB, 3 * half * SUB
    lower, outer = lane < HALF, part(lane, HALF)[1] < REACH
    for Z in range(nz // SUB):
        u, c = (
            jnp.where(outer, ql_ref[at : at + SUB], qr_ref[at : at + SUB])
            for at in (source + Z * SUB, source + nz + Z * SUB)
        )
        kept_ref[Z * SUB : (Z + 1) * SUB] = u
        kept_ref[nz + Z * SUB : nz + (Z + 1) * SUB] = c
        first, last = jnp.where(lower, u, rolled(c, HALF, 1)), jnp.where(lower, rolled(u, HALF, 1), c)
        to = slice(target + Z * SUB, target + (Z + 1) * SUB)
        b1_ref[to] = jnp.where(even, last, first)
        b2_ref[to] = jnp.where(even, first, last)

    at = slice(source + 2 * nz, source + 2 * nz + SUB)
    place = part(lane, SPREAD)[1]
    window = jnp.where(
        place < RIM,
        rolled(ql_ref[at], -WIDTH, 1),
        jnp.where(place < RIM + WIDTH, q_ref[at], rolled(qr_ref[at], WIDTH, 1)),
    )
    flux = jnp.zeros((nx, LANES), f32)
    for u, c in zip(joined[0], joined[1]):
        flux = flux + (c + rolled(c, -1, 1)) * (u - rolled(u, -1, 1))
    flux = block_rows((0.5 / CELLS) * flux)
    flux = flux + rolled(flux, -GROUP, 1)
    near, far = RIM - 1, 3 * RIM - 1
    change = jnp.where(place == RIM - 1, -rolled(flux, RIM - 1 - near, 1), 0.0)
    change = jnp.where(place == RIM, rolled(flux, RIM - near, 1), change)
    change = jnp.where(place == RIM + WIDTH - 1, -rolled(flux, RIM + WIDTH - 1 - far, 1), change)
    change = jnp.where(place == RIM + WIDTH, rolled(flux, RIM + WIDTH - far, 1), change)
    rows = nx // COARSEN
    nearest = jnp.where(even, rows - 1, 0)
    for Z in range(nz // COARSEN):
        u, c = facing(own_ref, 0, Z * SUB, nz, even) - tile(f1_ref, Z), facing(own_ref, 1, Z * SUB, nz, even)
        across = all_rows((0.5 / CELLS) * (c + tile(f1_ref, nz // SUB + Z)) * u)
        change = change - compact(jnp.where(sub == nearest, across, 0.0), Z)
    mate = f1_ref[2 * nz : 2 * nz + SUB]
    mate = jnp.where(even, rolled(mate, rows - RIM, 0), rolled(mate, 1 - RIM, 0))
    cond = jnp.where(sub == rows, mate, rolled(window, -RIM, 0))
    rhs = window + change
    kept_ref[2 * nz : 2 * nz + SUB] = cond
    kept_ref[2 * nz + SUB :] = rhs
    to = target + nz
    b1_ref[to:] = cond
    b2_ref[to : to + SUB] = cond
    b2_ref[to + SUB : to + 2 * SUB] = rhs
    to = to + 2 * SUB
    for a in range(2):
        for Z in range(nz // SUB):
            at = to + a * nz + Z * SUB
            b2_ref[at : at + SUB] = facing(own_ref, a, Z * SUB, nz, jnp.logical_not(even))


def join(q, ql, qr, f1, own, nz, nx):
    zs = nz // ZS
    size = 3 * (zs // 2) + nz // SUB + 1
    return pl.pallas_call(
        functools.partial(join_kernel, nz=nz, nx=nx),
        out_shape=(
            tiles(size),
            tiles(size + 1 + 2 * nz // SUB),
            jax.ShapeDtypeStruct((3 * zs * nx, LANES), f32),
            tiles(2 * nz // SUB + 2),
        ),
        in_specs=[VMEM] * 5,
        out_specs=(VMEM,) * 4,
        compiler_params=SMALL,
        name="join",
    )(q, ql, qr, f1, own)


def faces_kernel(own_ref, kept_ref, r2_ref, r1_ref, after_ref, o_ref, *, nz, nx):
    del after_ref
    half = nz // ZS // 2
    even = is_even()
    sub, lane = iota((SUB, LANES), 0), iota((SUB, LANES), 1)
    plane, place = part(lane, SPREAD)
    rows = nx // COARSEN
    base = 3 * half * SUB

    outer = REACH // COARSEN
    is_left, is_right = (place >= RIM - outer) & (place < RIM), (place >= RIM + WIDTH) & (place < RIM + WIDTH + outer)
    is_own = (place >= RIM) & (place < RIM + WIDTH)
    source = jnp.where(is_left, place - (RIM - outer), place - (RIM + WIDTH - outer))
    source = jnp.where(sub == 0, place - RIM, source) * COARSEN
    source = jnp.clip(source, 0, LANES - COARSEN)
    valid = ((sub == 0) & is_own) | ((sub > 0) & (is_left | is_right))

    def outside(r_ref, Z, upper):
        def mine(at):
            tile_at = kept_ref[at + Z * SUB : at + (Z + 1) * SUB]
            return jnp.where(upper, rolled(tile_at, HALF, 1), tile_at)

        other = r_ref[base + Z * SUB : base + (Z + 1) * SUB]
        return all_rows(0.5 * (mine(nz) + rolled(other, HALF, 1)) * (mine(0) - other))

    odd = jnp.logical_not(even)
    far_rows = base + nz + 2 * SUB
    flux = jnp.zeros((SUB, LANES), f32)
    for Z in range(nz // COARSEN):
        u, c = (
            (facing(own_ref, a, Z * SUB, nz, odd), r2_ref[at : at + SUB])
            for a, at in ((0, far_rows + Z * SUB), (1, far_rows + nz + Z * SUB))
        )
        one = all_rows(0.5 * (c[0] + c[1]) * (u[0] - u[1]))
        two = outside(r2_ref, Z, odd)
        three = outside(r1_ref, Z, even)
        sums = jnp.where(sub == 0, one, jnp.where(sub == 1, two, jnp.where(sub == 2, three, 0.0)))
        here = valid & (plane == Z)
        flux = flux + jnp.where(here, gathered(sums, source), 0.0)
    flux = flux * (1.0 / CELLS)
    far, mate = flux[0:1] + flux[1:2], flux[2:3]

    def stacked(own, other):
        before, after = jnp.where(even, other, own), jnp.where(even, own, other)
        return jnp.where(sub <= rows, rolled(before, 1, 0), rolled(after, rows + 1, 0))

    at = base + nz + SUB
    rhs = stacked(kept_ref[2 * nz + SUB :], r2_ref[at : at + SUB])
    sign = jnp.where(even, 1.0, -1.0)
    rhs = rhs + jnp.where(sub == rows, sign * far, jnp.where(sub == rows + 1, -sign * far, 0.0))
    rhs = rhs - jnp.where(sub == jnp.where(even, 2 * rows, 1), mate, 0.0)

    at = at - SUB
    near_c, far_c = r1_ref[at : at + SUB], r2_ref[at : at + SUB]
    cond = stacked(kept_ref[2 * nz : 2 * nz + SUB], far_c)
    before = jnp.where(even, rolled(far_c, -rows, 0), rolled(near_c, 1 - rows, 0))
    after = jnp.where(even, rolled(near_c, 2 * rows + 1, 0), rolled(far_c, rows + 1, 0))
    cond = jnp.where(sub == 0, before, jnp.where(sub == 2 * rows + 1, after, cond))
    around = rolled(cond, -1, 0) + rolled(cond, 1, 0) + rolled(cond, -1, 1) + rolled(cond, 1, 1)
    around = around + rolled(cond, -SPREAD, 1) + rolled(cond, SPREAD, 1)
    weight = OMEGA / (SHIFT + (0.5 / COARSEN**2) * (6.0 * cond + around))
    o_ref[0:SUB] = weight * rhs
    o_ref[SUB : 2 * SUB] = weight
    o_ref[2 * SUB :] = cond


def faces(own, kept, r2, r1, after, nz, nx):
    return pl.pallas_call(
        functools.partial(faces_kernel, nz=nz, nx=nx),
        out_shape=tiles(3),
        in_specs=[VMEM] * 4 + [pl.BlockSpec(memory_space=pl.ANY)],
        out_specs=VMEM,
        compiler_params=SMALL,
        name="faces",
    )(own, kept, r2, r1, after)


def sides(even, one, two):
    return jnp.where(even, one, two), jnp.where(even, two, one)


def rim_of(low, after, before):
    return jnp.where(low, after, before), rolled(jnp.where(low, before, after), RIM, 0)


def rims_of(low, one_ref, two_ref, last_ref, nz):
    half = nz // 2
    for z in range(nz):
        yield rim_of(low, tile(one_ref if z < half else two_ref, z % half), tile(last_ref, z))


def rim_faces(sub, face, rim_face, u_first, u_last, rim):
    u_rim = jnp.where(sub == 0, rolled(rim, 1 - RIM, 0), rolled(rim, RIM - 1, 0))
    end = sub == SUB - 1
    after = jnp.where(end, face * (u_last - rolled(u_rim, -1, 0)), 0.0)
    before = jnp.where(end, rim_face * (u_rim - rolled(u_first, -1, 0)), 0.0)
    return after, before


def beside(w, z, zs, column):
    return rolled(w, -column - z // zs * GROUP, 1)


def window(spot, left, right, column):
    return jnp.where(spot == RIM - 1, left, rolled(right, RIM - 2 - column, 1))


def begin_kernel(
    strip_ref, u_ref, c_ref, r_ref, cx_ref, cy_ref, cz_ref, diag_ref, inv_ref, q_ref, v_ref, *, nz, nx
):
    zs = nz // ZS
    spot = part(iota((nx, LANES), 1), GROUP)[1]
    row, lane = iota((nx, LANES), 0), iota((nx, LANES), 1)
    first_lane, last_lane = lane == 0, lane == LANES - 1

    def strip(a, zi):
        return strip_ref[(a * zs + zi) * nx : (a * zs + zi + 1) * nx]

    edge_c, edge_f = [], []
    for zi in range(zs):
        u, c = strip(0, zi), strip(1, zi)
        flux = 0.5 * (c + rolled(c, -1, 1)) * (u - rolled(u, -1, 1))
        edge_c.append(window(spot, c, c, 3 * RIM))
        edge_f.append(window(spot, flux, flux, 3 * RIM - 1))

    def own(ref, z):
        return ref[z % nz * nx : (z % nz + 1) * nx]

    below = 0.5 * (own(c_ref, -1) + own(c_ref, 0))
    for z in range(nz):
        at = slice(z * nx, (z + 1) * nx)
        c = own(c_ref, z)
        gx = jnp.where(row == nx - 1, 0.0, 0.5 * (c + rolled(c, -1, 0)))
        edge = beside(edge_c[z % zs], z, zs, RIM - 1)
        gy = 0.5 * (c + jnp.where(last_lane, edge, rolled(c, -1, 1)))
        gyl = 0.5 * (c + jnp.where(first_lane, edge, rolled(c, 1, 1)))
        above = 0.5 * (c + own(c_ref, z + 1))
        diag = SHIFT + (gx + rolled(gx, 1, 0)) + (gy + gyl) + (above + below)
        edge = beside(edge_f[z % zs], z, zs, RIM - 1)
        r = own(r_ref, z) + jnp.where(first_lane, edge, jnp.where(last_lane, -edge, 0.0))
        inner = slice(SUB, nx - SUB)
        inverse = 1.0 / diag[inner]
        scaled = r[inner] * inverse
        cx_ref[at] = gx
        cy_ref[at] = gy
        cz_ref[at] = above
        diag_ref[at] = diag
        q_ref[at] = jnp.concatenate([r[:SUB], scaled, r[nx - SUB :]], axis=0)
        to = slice(z * (nx - 2 * SUB), (z + 1) * (nx - 2 * SUB))
        inv_ref[to] = inverse
        v_ref[to] = scaled * (1.0 / THETA)
        below = above


def begin(strips, u, c, r, nz, nx):
    inner = jax.ShapeDtypeStruct((nz * (nx - 2 * SUB), LANES), f32)
    return pl.pallas_call(
        functools.partial(begin_kernel, nz=nz, nx=nx),
        out_shape=(jax.ShapeDtypeStruct(u.shape, f32),) * 4 + (inner, jax.ShapeDtypeStruct(u.shape, f32), inner),
        in_specs=[VMEM] * 4,
        out_specs=(VMEM,) * 7,
        compiler_params=SMALL,
        cost_estimate=pl.CostEstimate(flops=40 * u.size, bytes_accessed=40 * u.size, transcendentals=0),
        name="begin",
    )(strips, u, c, r)


def fine_kernel(
    strip_ref, b2_ref, b1_ref, one_ref, two_ref, last_ref, u_ref, c_ref, cx_ref, cy_ref, cz_ref, diag_ref, inv_ref, q_ref, v_ref,
    cx, inv, q, va, acc, w2,
    ch, cyh, czh, vb, wr, w0, w1,
    *, nz, nx,
):
    zs = nz // ZS
    half = zs // 2
    ext = nx + SUB
    even = is_even()
    sub = iota((SUB, LANES), 0)
    low, end = sub < RIM, sub == SUB - 1
    table = steps()

    rims = []
    for z, (cond, rim) in enumerate(rims_of(low, one_ref, two_ref, last_ref, nz)):
        ch[z * SUB : (z + 1) * SUB] = cond
        rims.append(rim)

    row, spot = iota((ext, LANES), 0), part(iota((ext, LANES), 1), GROUP)[1]

    def strips_of(a):
        ends = [None] * zs
        for pair in range(half):
            index = a * half + pair
            ends[pair], ends[pair + half] = rim_of(low, *sides(even, tile(b1_ref, index), tile(b2_ref, index)))
        return [
            jnp.concatenate([strip_ref[(a * zs + zi) * nx : (a * zs + zi + 1) * nx], ends[zi]], axis=0)
            for zi in range(zs)
        ]

    def z_up(x):
        return x[1:] + [rolled(x[0], -GROUP, 1)]

    def z_down(x):
        return [rolled(x[-1], GROUP, 1)] + x[:-1]

    us, cs, rs = strips_of(0), strips_of(1), strips_of(2)
    cxs = [0.5 * (c + rolled(c, -1, 0)) for c in cs]
    cys = [0.5 * (c + rolled(c, -1, 1)) for c in cs]
    czs = [0.5 * (c + d) for c, d in zip(cs, z_up(cs))]
    czds = z_down(czs)
    invs, qs, vs = [], [], []
    for zi in range(zs):
        u = us[zi]
        fx = jnp.where((row == nx - 1) | (row == ext - 1), cxs[zi] * (u - rolled(u, -1, 0)), 0.0)
        fy = jnp.where((spot == RIM - 1) | (spot == 3 * RIM - 1), cys[zi] * (u - rolled(u, -1, 1)), 0.0)
        r = rs[zi] - (fx - rolled(fx, 1, 0)) - (fy - rolled(fy, 1, 1))
        wr[zi * SUB : (zi + 1) * SUB] = jnp.where(spot == RIM, r, rolled(r, -2 * RIM, 1))[nx:]
        diag = SHIFT + (cxs[zi] + rolled(cxs[zi], 1, 0)) + (cys[zi] + rolled(cys[zi], 1, 1)) + (czs[zi] + czds[zi])
        invs.append(1.0 / diag)
        qs.append(r * invs[zi])
        vs.append(qs[zi] * (1.0 / THETA))
    for k, w in enumerate((w0, w1, w2)):
        prod = [cys[zi] * vs[zi] for zi in range(zs)]
        for zi in range(zs):
            w[zi * ext : (zi + 1) * ext] = window(spot, prod[zi], vs[zi], 3 * RIM)
        if k == SWEEPS - 1:
            break
        keep, lift = table[k]
        v_up, v_down = z_up(vs), z_down(vs)
        fresh = []
        for zi in range(zs):
            v = vs[zi]
            near = cxs[zi] * rolled(v, -1, 0) + rolled(cxs[zi] * v, 1, 0)
            near = near + cys[zi] * rolled(v, -1, 1) + rolled(prod[zi], 1, 1)
            near = near + czs[zi] * v_up[zi] + czds[zi] * v_down[zi]
            qs[zi] = qs[zi] - v + near * invs[zi]
            fresh.append(keep * v + lift * qs[zi])
        vs = fresh
    edge_c = [window(spot, c, c, 3 * RIM)[nx:] for c in cs]

    lane = iota((SUB, LANES), 1)
    first_lane, last_lane = lane == 0, lane == LANES - 1

    def own(ref, z):
        return ref[z % nz * nx : (z % nz + 1) * nx]

    def rim_at(ref, z):
        return tile(ref, z % nz)

    below = 0.5 * (rim_at(ch, -1) + rim_at(ch, 0))
    for z in range(nz):
        at = slice(z * SUB, (z + 1) * SUB)
        u, c = own(u_ref, z), tile(ch, z)
        c_first, c_last = own(c_ref, z)[:SUB], own(c_ref, z)[nx - SUB :]
        zi = z % zs
        face = jnp.where(end, 0.5 * (c_last + rolled(c, -1, 0)), 0.0)
        gx = 0.5 * (c + jnp.where(end, rolled(c_first, -1, 0), rolled(c, -1, 0)))
        gxl = rolled(gx, 1, 0)
        edge = beside(edge_c[zi], z, zs, RIM - 1)
        gy = 0.5 * (c + jnp.where(last_lane, edge, rolled(c, -1, 1)))
        gyl = 0.5 * (c + jnp.where(first_lane, edge, rolled(c, 1, 1)))
        above = 0.5 * (c + rim_at(ch, z + 1))
        diag = SHIFT + (gx + jnp.where(sub == 0, rolled(face, 1, 0), gxl)) + (gy + gyl) + (above + below)
        after, before = rim_faces(sub, face, gx, u[:SUB], u[nx - SUB :], rims[z])
        r = rims[z] + rolled(after, 1, 0) - before
        r = jnp.where(first_lane | last_lane, beside(wr[zi * SUB : (zi + 1) * SUB], z, zs, RIM), r)
        own_diag, own_q = own(diag_ref, z), own(q_ref, z)
        long_at = slice(z * ext, (z + 1) * ext)
        parts = []
        for this_diag, this_r in (
            (own_diag[:SUB] + jnp.where(sub == 0, gxl, 0.0), own_q[:SUB] + rolled(before, 1, 0)),
            (own_diag[nx - SUB :] + face, own_q[nx - SUB :] - after),
            (diag, r),
        ):
            inverse = 1.0 / this_diag
            scaled = this_r * inverse
            parts.append((inverse, scaled, scaled * (1.0 / THETA)))
        inner = slice(z * (nx - 2 * SUB), (z + 1) * (nx - 2 * SUB))
        middle = (inv_ref[inner], own_q[SUB : nx - SUB], v_ref[inner])
        for ref, one, two, three, four in zip((inv, q, va), parts[0], middle, parts[1], parts[2]):
            ref[long_at] = jnp.concatenate([one, two, three, four], axis=0)
        own_cx = own(cx_ref, z)
        cx[long_at] = jnp.concatenate([own_cx[: nx - SUB], own_cx[nx - SUB :] + face, gx], axis=0)
        cyh[at] = gy
        czh[at] = above
        below = above

    lane = iota((ext, LANES), 1)
    first_lane, last_lane = lane == 0, lane == LANES - 1

    def whole(ref, rim, z):
        return jnp.concatenate([own(ref, z), rim_at(rim, z)], axis=0)

    def long(ref, z):
        return ref[z % nz * ext : (z % nz + 1) * ext]

    for k, w in enumerate((w0, w1)):
        old, new = (va, vb) if k % 2 == 0 else (vb, va)
        keep, lift = table[k]
        for z in range(nz):
            at, here = slice(z * ext, (z + 1) * ext), slice(z * nx, (z + 1) * nx)
            zi = z % zs
            v, gx, gy = old[at], cx[at], whole(cy_ref, cyh, z)
            edge = beside(w[zi * ext : (zi + 1) * ext], z, zs, RIM - 1)
            near = gx * rolled(v, -1, 0) + rolled(gx * v, 1, 0)
            near = near + gy * jnp.where(last_lane, edge, rolled(v, -1, 1))
            near = near + jnp.where(first_lane, edge, rolled(gy * v, 1, 1))
            near = near + whole(cz_ref, czh, z) * long(old, z + 1) + whole(cz_ref, czh, z - 1) * long(old, z - 1)
            scaled = q[at] - v + near * inv[at]
            fresh = keep * v + lift * scaled
            q[at] = scaled
            new[at] = fresh
            acc[here] = (own(u_ref, z) + v[:nx] if k == 0 else acc[here]) + fresh[:nx]


def fine(strips, b2, b1, one, two, last, u, c, begun, nz, nx):
    zs = nz // ZS
    ext = nx + SUB
    rim = pltpu.VMEM((nz * SUB, LANES), f32)
    full = jax.ShapeDtypeStruct((nz * ext, LANES), f32)
    strip = pltpu.VMEM((zs * ext, LANES), f32)
    return pl.pallas_call(
        functools.partial(fine_kernel, nz=nz, nx=nx),
        out_shape=(full,) * 4 + (jax.ShapeDtypeStruct(u.shape, f32), jax.ShapeDtypeStruct((zs * ext, LANES), f32)),
        in_specs=[VMEM] * 15,
        out_specs=(VMEM,) * 6,
        scratch_shapes=[rim] * 3 + [pltpu.VMEM((nz * ext, LANES), f32), pltpu.VMEM((zs * SUB, LANES), f32)] + [strip] * 2,
        compiler_params=SMALL,
        cost_estimate=pl.CostEstimate(flops=100 * u.size, bytes_accessed=40 * u.size, transcendentals=0),
        name="fine",
    )(strips, b2, b1, one, two, last, u, c, *begun)


def finish_kernel(
    cx_ref, inv_ref, q_ref, v_ref, sum_ref, w_ref, cy_ref, cz_ref, m_ref, r_ref, o_ref, out, sems, *, nz, nx
):
    zs = nz // ZS
    ext = nx + SUB
    rows = nx // COARSEN
    even = is_even()
    sub, lane = iota((SUB, LANES), 0), iota((SUB, LANES), 1)
    beyond = sub == jnp.where(even, 2 * rows + 1, 0)
    fields = []
    for a in range(3):
        mine, mate = tile(m_ref, a), tile(r_ref, a)
        mate = jnp.where(even, rolled(mate, 2 * rows, 0), rolled(mate, -2 * rows, 0))
        fields.append(jnp.concatenate([jnp.where(beyond, mate, mine), mate], axis=0))
    start, weight, cond = fields
    scale = 0.5 / COARSEN**2
    turns = (-1, 0), (1, 0), (-1, 1), (1, 1), (-SPREAD, 1), (SPREAD, 1)
    shares = [scale * (cond + rolled(cond, *turn)) for turn in turns]
    keep = 1.0 - weight * (SHIFT + sum(shares))
    shares = [weight * share for share in shares]
    v = start
    for _ in range(COARSE_SWEEPS - 1):
        terms = [share * rolled(v, *turn) for share, turn in zip(shares, turns)]
        v = (start + keep * v) + ((terms[0] + terms[1]) + (terms[2] + terms[3]) + (terms[4] + terms[5]))
    top = v[:SUB]
    top = jnp.where(even, rolled(top, -rows - 1, 0), rolled(top, -1, 0))

    wide = iota((nx, LANES), 1)
    first_lane, last_lane = wide == 0, wide == LANES - 1
    keep, lift = steps()[-1]

    def own(ref, z):
        return ref[z % nz * nx : (z % nz + 1) * nx]

    def long(ref, z):
        return ref[z % nz * ext : z % nz * ext + nx]

    copies = []
    size = COARSEN * nx
    for Z in range(nz // COARSEN):
        spread = jnp.take_along_axis(top, Z * SPREAD + RIM + part(lane, COARSEN)[0], axis=1)
        value = jnp.concatenate([jnp.broadcast_to(spread[X : X + 1], (COARSEN, LANES)) for X in range(rows)], axis=0)
        for z in range(Z * COARSEN, (Z + 1) * COARSEN):
            at = slice(z * ext, (z + 1) * ext)
            v, gx = v_ref[at], cx_ref[at]
            near = (gx * rolled(v, -1, 0) + rolled(gx * v, 1, 0))[:nx]
            v, gy, zi = v[:nx], own(cy_ref, z), z % zs
            edge = beside(w_ref[zi * ext : zi * ext + nx], z, zs, RIM - 1)
            near = near + gy * jnp.where(last_lane, edge, rolled(v, -1, 1))
            near = near + jnp.where(first_lane, edge, rolled(gy * v, 1, 1))
            near = near + own(cz_ref, z) * long(v_ref, z + 1) + own(cz_ref, z - 1) * long(v_ref, z - 1)
            scaled = long(q_ref, z) - v + near * long(inv_ref, z)
            here = slice(z * nx, (z + 1) * nx)
            out[here] = (own(sum_ref, z) + (keep * v + lift * scaled)) + value
        here = pl.ds(Z * size, size)
        copies.append(pltpu.make_async_copy(out.at[here], o_ref.at[here], sems.at[Z]))
        copies[-1].start()
    for copy in copies:
        copy.wait()


def finish(passed, cy, cz, m, r, nz, nx):
    shape = (nz * nx, LANES)
    return pl.pallas_call(
        functools.partial(finish_kernel, nz=nz, nx=nx),
        out_shape=jax.ShapeDtypeStruct(shape, f32),
        in_specs=[VMEM] * 10,
        out_specs=pl.BlockSpec(memory_space=pltpu.HBM),
        scratch_shapes=[pltpu.VMEM(shape, f32), pltpu.SemaphoreType.DMA((nz // COARSEN,))],
        compiler_params=SMALL,
        name="finish",
    )(*passed, cy, cz, m, r)


def moves():
    size_x, size_y = lax.axis_size("gx"), lax.axis_size("gy")

    def send(x, go):
        pairs = []
        for i in range(size_x):
            for j in range(size_y):
                k, l = go(i, j)
                pairs.append((i * size_y + j, (k % size_x) * size_y + l % size_y))
        return lax.ppermute(x, ("gx", "gy"), pairs)

    def mate(x):
        return send(x, lambda i, j: (i + 1 if i % 2 == 0 else i - 1, j))

    def shift(x, by):
        return send(x, lambda i, j: (i + by, j))

    def far(x):
        return send(x, lambda i, j: (i - 1 if i % 2 == 0 else i + 1, j))

    def beside_y(x):
        left = send(x, lambda i, j: (i, j + 1))
        if size_y == 2:
            return left, left
        return left, send(x, lambda i, j: (i, j - 1))

    return mate, far, shift, beside_y


def body(iterate, source, conduct):
    nz, nx, ny = iterate.shape
    if nz != ZS * 4 or ny != LANES or nx != 3 * SUB or lax.axis_size("gx") % 2:
        raise ValueError("shapes")
    mate, far, shift, beside_y = moves()
    u, s, c = (x.reshape(nz * nx, ny) for x in (iterate, source, conduct))
    q, f1, last, one, two, r, own = pack(u, s, c, nz, nx)
    ql, qr = beside_y(q)
    rf1 = mate(f1)
    before = shift(last, 1)
    b1, b2, strips, kept = join(q, ql, qr, rf1, own, nz, nx)
    rb2 = far(b2)
    rb1 = mate(b1)
    one, two, strips = lax.optimization_barrier((one, two, strips))
    after = shift(one, -1), shift(two, -1)
    begun = begin(strips, u, c, r, nz, nx)
    m = faces(own, kept, rb2, rb1, begun[0], nz, nx)
    rm = mate(m)
    passed = fine(strips, rb2, rb1, *after, before, u, c, begun, nz, nx)
    return finish(passed, begun[1], begun[2], m, rm, nz, nx).reshape(nz, nx, ny)


def solution(mesh):
    spec = P(None, "gx", "gy")
    return jax.shard_map(body, mesh=mesh, in_specs=(spec,) * 3, out_specs=spec, check_vma=False)
```

```python
import functools

import jax
import jax.numpy as jnp
from jax import lax
from jax.experimental import pallas as pl
from jax.experimental.pallas import tpu as pltpu
from jax.sharding import PartitionSpec as P

SWEEPS = 3
COARSE_SWEEPS = 4
COARSEN = 8

SHIFT = 0.1
LMIN = 0.3
LMAX = 2.0
OMEGA = 0.8

THETA = (LMAX + LMIN) / 2.0
DELTA = (LMAX - LMIN) / 2.0
SIGMA = THETA / DELTA

RIM = SWEEPS + 1
SUB = 8
LANES = 128
HALF = LANES // 2
GROUP = 4 * RIM
ZS = LANES // GROUP
WIDTH = LANES // COARSEN
SPREAD = 2 * WIDTH
REACH = (COARSE_SWEEPS - 1) * COARSEN
CELLS = COARSEN**3

f32 = jnp.float32
VMEM = pl.BlockSpec(memory_space=pltpu.VMEM)
SMALL = pltpu.CompilerParams(vmem_limit_bytes=12 * 1024 * 1024)


def steps():
    rho, listed = 1.0 / SIGMA, []
    for _ in range(SWEEPS):
        nxt = 1.0 / (2.0 * SIGMA - rho)
        listed.append((nxt * rho, 2.0 * nxt / DELTA))
        rho = nxt
    return listed


def iota(shape, dim):
    return lax.broadcasted_iota(jnp.int32, shape, dim)


def part(index, size):
    return lax.shift_right_logical(index, size.bit_length() - 1), lax.bitwise_and(index, size - 1)


def rolled(x, by, dim):
    return pltpu.roll(x, by % x.shape[dim], dim)


def is_even():
    return lax.axis_index("gx") % 2 == 0


def tiles(count):
    return jax.ShapeDtypeStruct((count * SUB, LANES), f32)


def tile(ref, index):
    return ref[index * SUB : (index + 1) * SUB]


def picked(ref, start, stride):
    return ref[pl.ds(start, SUB, stride=stride), :]


def gathered(rows, source):
    parts = [jnp.take_along_axis(rows, source + k, axis=1) for k in range(COARSEN)]
    while len(parts) > 1:
        parts = [a + b for a, b in zip(parts[::2], parts[1::2])]
    return parts[0]


def compact(rows, place):
    plane, column = part(iota(rows.shape, 1), SPREAD)
    column = column - RIM
    source = jnp.clip(column * COARSEN, 0, LANES - COARSEN)
    here = (plane == place) & (column >= 0) & (column < WIDTH)
    return jnp.where(here, gathered(rows, source), 0.0)


def section(run):
    pl.when(lax.axis_index("gx") >= 0)(run)


def block_rows(values):
    sub = iota((SUB, LANES), 0)
    out = jnp.zeros((SUB, LANES), f32)
    for block in range(values.shape[0] // COARSEN):
        part = values[block * COARSEN : (block + 1) * COARSEN]
        out = jnp.where(sub == block, jnp.sum(part, axis=0, keepdims=True), out)
    return out


def all_rows(values):
    return jnp.sum(values, axis=0, keepdims=True)


def pack_kernel(
    u_hbm, s_hbm, c_hbm, q_ref, f1_ref, last_ref, one_ref, two_ref, r_ref, own_ref, u_ref, s_ref, c_ref, sums_ref, sems, *, nz, nx
):
    pieces = sems.shape[1]
    size = nz * nx // pieces
    copies = []
    for k, (source, target) in enumerate(((c_hbm, c_ref), (u_hbm, u_ref), (s_hbm, s_ref))):
        for piece in range(pieces):
            at = pl.ds(piece * size, size)
            copies.append(pltpu.make_async_copy(source.at[at], target.at[at], sems.at[k, piece]))
    for copy in copies:
        copy.start()
    for copy in copies[: 2 * pieces]:
        copy.wait()

    even = is_even()
    sub, lane = iota((SUB, LANES), 0), iota((SUB, LANES), 1)
    low = sub < RIM
    row, wide = iota((nx, LANES), 0), iota((nx, LANES), 1)
    slot, spot = part(wide, 2 * RIM)

    def plane(ref, z):
        return ref[z % nz * nx : (z % nz + 1) * nx]

    def up(z):
        return 0.5 * (plane(c_ref, z) + plane(c_ref, z + 1)) * (plane(u_ref, z) - plane(u_ref, z + 1))

    for z in range(nz):
        u, c = plane(u_ref, z), plane(c_ref, z)
        fy = 0.5 * (c + rolled(c, -1, 1)) * (u - rolled(u, -1, 1))
        r_ref[z * nx : (z + 1) * nx] = jnp.where(wide == LANES - 1, 0.0, fy)
    for copy in copies[2 * pieces :]:
        copy.wait()
    below = up(nz - 1)
    for Z in range(nz // COARSEN):
        sum_r = sum_c = jnp.zeros((nx, LANES), f32)
        for z in range(Z * COARSEN, (Z + 1) * COARSEN):
            u, c = plane(u_ref, z), plane(c_ref, z)
            above = up(z)
            fx = 0.5 * (c + rolled(c, -1, 0)) * (u - rolled(u, -1, 0))
            fy = plane(r_ref, z)
            fx = jnp.where(row == nx - 1, 0.0, fx)
            r = plane(s_ref, z) - SHIFT * u - (fx - rolled(fx, 1, 0)) - (fy - rolled(fy, 1, 1)) - (above - below)
            below = above
            r_ref[z * nx : (z + 1) * nx] = r
            sum_r = sum_r + r
            sum_c = sum_c + c
            u0, u2, c0, c2 = u[:SUB], u[nx - SUB :], c[:SUB], c[nx - SUB :]
            first = jnp.where(low, c0, jnp.where(sub == SUB - 1, rolled(u0, -1, 0), rolled(r[:SUB], RIM, 0)))
            last = jnp.where(low, jnp.where(sub == 0, rolled(u2, 1, 0), rolled(r[nx - SUB :], RIM, 0)), c2)
            last_ref[z * SUB : (z + 1) * SUB] = last
            to = z % (nz // 2) * SUB
            (one_ref if z < nz // 2 else two_ref)[to : to + SUB] = first
        sums_ref[Z * nx : (Z + 1) * nx] = sum_r
        sums_ref[(Z + nz // COARSEN) * nx : (Z + nz // COARSEN + 1) * nx] = sum_c

    zs = nz // ZS
    half = zs // 2
    def strips():
        for zi in range(zs):
            strip = jnp.zeros((nx, LANES), f32)
            for g in range(ZS):
                z, at = g * zs + zi, g * GROUP + RIM
                outer = jnp.where(spot < 2, rolled(plane(u_ref, z), at + RIM + 1, 1), rolled(plane(r_ref, z), at + 2 * RIM + 1, 1))
                strip = jnp.where(slot == 2 * g + 1, outer, strip)
                strip = jnp.where(slot == 2 * g, rolled(plane(c_ref, z), at, 1), strip)
            q_ref[zi * nx : (zi + 1) * nx] = strip

    def finish():
        coarse = jnp.zeros((SUB, LANES), f32)
        planes = nz // COARSEN
        for Z in range(planes):
            sum_r, sum_c = (sums_ref[(Z + k * planes) * nx : (Z + k * planes + 1) * nx] for k in range(2))
            coarse = coarse + compact(block_rows(sum_r) + rolled(block_rows(sum_c), RIM, 0), Z)
        coarse = coarse * (1.0 / CELLS)
        strips()

        base = zs * nx + SUB
        for a, ref in enumerate((u_ref, c_ref)):
            for Z in range(nz // SUB):
                at = Z * SUB * nx
                first, last = picked(ref, at, nx), picked(ref, at + nx - 1, nx)
                to = a * nz + Z * SUB
                own_ref[to : to + SUB] = first
                own_ref[2 * nz + to : 2 * nz + to + SUB] = last
                f1_ref[to : to + SUB] = jnp.where(even, last, first)
                q_ref[base + to : base + to + SUB] = jnp.where(
                    lane < HALF, rolled(first, REACH, 1), rolled(last, REACH + HALF, 1)
                )
        q_ref[base + 2 * nz : base + 2 * nz + SUB] = coarse
        f1_ref[2 * nz :] = coarse
        corners = jnp.zeros((SUB, LANES), f32)
        group = part(lane, GROUP)[0]
        for Z in range(nz // SUB):
            at = Z * SUB * nx
            first, last = picked(u_ref, at, nx), picked(u_ref, at + nx - 1, nx)
            both = jnp.where(low, first, rolled(last, RIM, 0)), jnp.where(low, rolled(first, RIM, 0), last)
            for second in range(2):
                g = 2 * Z + second
                corners = jnp.where(group == g, rolled(both[second], g * GROUP + RIM, 1), corners)
        q_ref[zs * nx : base] = corners

    finish()


def pack(u, s, c, nz, nx):
    pieces = 1
    return pl.pallas_call(
        functools.partial(pack_kernel, nz=nz, nx=nx),
        out_shape=(
            tiles(nz // ZS * nx // SUB + 2 * nz // SUB + 2),
            tiles(2 * nz // SUB + 1),
            tiles(nz),
            tiles(nz // 2),
            tiles(nz // 2),
            jax.ShapeDtypeStruct(u.shape, f32),
            tiles(4 * nz // SUB),
        ),
        in_specs=[pl.BlockSpec(memory_space=pltpu.HBM)] * 3,
        out_specs=(VMEM,) * 7,
        scratch_shapes=[pltpu.VMEM(u.shape, f32)] * 3
        + [pltpu.VMEM((2 * nz // COARSEN * nx, LANES), f32), pltpu.SemaphoreType.DMA((3, pieces))],
        compiler_params=SMALL,
        name="pack",
    )(*(pltpu.with_memory_space_constraint(x, pltpu.HBM) for x in (u, s, c)))


def facing(own_ref, a, z, nz, last):
    first, second = own_ref[a * nz + z : a * nz + z + SUB], own_ref[(2 + a) * nz + z : (2 + a) * nz + z + SUB]
    return jnp.where(last, second, first)


def join_kernel(q_ref, ql_ref, qr_ref, f1_ref, own_ref, b1_ref, b2_ref, strip_ref, kept_ref, *, nz, nx):
    zs = nz // ZS
    half = zs // 2
    even = is_even()
    sub, lane = iota((SUB, LANES), 0), iota((SUB, LANES), 1)
    low = sub < RIM
    spot = part(iota((nx, LANES), 1), GROUP)[1]
    thin, row = part(lane, GROUP)[1], iota((nx, LANES), 0)

    def before(spot, left, own, right):
        moved = rolled(jnp.where(spot < RIM, own, right), 2 * RIM, 1)
        return jnp.where(spot < 2 * RIM, jnp.where(spot < RIM, left, own), moved)

    def behind(spot, left, own, right):
        lower, at = spot < 2 * RIM, 2 * RIM
        split = spot < at + 2 + SWEEPS
        residual = jnp.where(
            lower,
            rolled(jnp.where(split, left, own), -(at + 1), 1),
            rolled(jnp.where(split, own, right), -1, 1),
        )
        split = spot == at
        u = jnp.where(
            lower,
            rolled(jnp.where(split, left, own), RIM - 1 - at, 1),
            rolled(jnp.where(split, own, right), RIM - 1, 1),
        )
        return residual, u

    at = slice(zs * nx, zs * nx + SUB)
    corners = before(thin, ql_ref[at], q_ref[at], qr_ref[at])
    joined = [], [], []
    for zi in range(zs):
        at = slice(zi * nx, (zi + 1) * nx)
        parts = ql_ref[at], q_ref[at], qr_ref[at]
        residual, u = behind(spot, *parts)
        u = jnp.where(row == 0, corners[zi : zi + 1], u)
        u = jnp.where(row == nx - 1, corners[RIM + zi : RIM + zi + 1], u)
        for group, strip in zip(joined, (u, before(spot, *parts), residual)):
            group.append(strip)
    for a, group in enumerate(joined):
        for zi in range(zs):
            strip_ref[(a * zs + zi) * nx : (a * zs + zi + 1) * nx] = group[zi]
        for pair in range(half):
            one, two = group[pair], group[pair + half]
            first = jnp.where(low, one[:SUB], rolled(two[:SUB], RIM, 0))
            last = jnp.where(low, rolled(two[nx - SUB :], RIM, 0), one[nx - SUB :])
            to = slice((a * half + pair) * SUB, (a * half + pair + 1) * SUB)
            b1_ref[to] = jnp.where(even, last, first)
            b2_ref[to] = jnp.where(even, first, last)

    source, target = zs * nx + SUB, 3 * half * SUB
    lower, outer = lane < HALF, part(lane, HALF)[1] < REACH
    for Z in range(nz // SUB):
        u, c = (
            jnp.where(outer, ql_ref[at : at + SUB], qr_ref[at : at + SUB])
            for at in (source + Z * SUB, source + nz + Z * SUB)
        )
        kept_ref[Z * SUB : (Z + 1) * SUB] = u
        kept_ref[nz + Z * SUB : nz + (Z + 1) * SUB] = c
        first, last = jnp.where(lower, u, rolled(c, HALF, 1)), jnp.where(lower, rolled(u, HALF, 1), c)
        to = slice(target + Z * SUB, target + (Z + 1) * SUB)
        b1_ref[to] = jnp.where(even, last, first)
        b2_ref[to] = jnp.where(even, first, last)

    at = slice(source + 2 * nz, source + 2 * nz + SUB)
    place = part(lane, SPREAD)[1]
    window = jnp.where(
        place < RIM,
        rolled(ql_ref[at], -WIDTH, 1),
        jnp.where(place < RIM + WIDTH, q_ref[at], rolled(qr_ref[at], WIDTH, 1)),
    )
    flux = jnp.zeros((nx, LANES), f32)
    for u, c in zip(joined[0], joined[1]):
        flux = flux + (c + rolled(c, -1, 1)) * (u - rolled(u, -1, 1))
    flux = block_rows((0.5 / CELLS) * flux)
    flux = flux + rolled(flux, -GROUP, 1)
    near, far = RIM - 1, 3 * RIM - 1
    change = jnp.where(place == RIM - 1, -rolled(flux, RIM - 1 - near, 1), 0.0)
    change = jnp.where(place == RIM, rolled(flux, RIM - near, 1), change)
    change = jnp.where(place == RIM + WIDTH - 1, -rolled(flux, RIM + WIDTH - 1 - far, 1), change)
    change = jnp.where(place == RIM + WIDTH, rolled(flux, RIM + WIDTH - far, 1), change)
    rows = nx // COARSEN
    nearest = jnp.where(even, rows - 1, 0)
    for Z in range(nz // COARSEN):
        u, c = facing(own_ref, 0, Z * SUB, nz, even) - tile(f1_ref, Z), facing(own_ref, 1, Z * SUB, nz, even)
        across = all_rows((0.5 / CELLS) * (c + tile(f1_ref, nz // SUB + Z)) * u)
        change = change - compact(jnp.where(sub == nearest, across, 0.0), Z)
    mate = f1_ref[2 * nz : 2 * nz + SUB]
    mate = jnp.where(even, rolled(mate, rows - RIM, 0), rolled(mate, 1 - RIM, 0))
    cond = jnp.where(sub == rows, mate, rolled(window, -RIM, 0))
    rhs = window + change
    kept_ref[2 * nz : 2 * nz + SUB] = cond
    kept_ref[2 * nz + SUB :] = rhs
    to = target + nz
    b1_ref[to:] = cond
    b2_ref[to : to + SUB] = cond
    b2_ref[to + SUB : to + 2 * SUB] = rhs
    to = to + 2 * SUB
    for a in range(2):
        for Z in range(nz // SUB):
            at = to + a * nz + Z * SUB
            b2_ref[at : at + SUB] = facing(own_ref, a, Z * SUB, nz, jnp.logical_not(even))


def join(q, ql, qr, f1, own, nz, nx):
    zs = nz // ZS
    size = 3 * (zs // 2) + nz // SUB + 1
    return pl.pallas_call(
        functools.partial(join_kernel, nz=nz, nx=nx),
        out_shape=(
            tiles(size),
            tiles(size + 1 + 2 * nz // SUB),
            jax.ShapeDtypeStruct((3 * zs * nx, LANES), f32),
            tiles(2 * nz // SUB + 2),
        ),
        in_specs=[VMEM] * 5,
        out_specs=(VMEM,) * 4,
        compiler_params=SMALL,
        name="join",
    )(q, ql, qr, f1, own)


def faces_kernel(own_ref, kept_ref, r2_ref, r1_ref, after_ref, o_ref, *, nz, nx):
    del after_ref
    half = nz // ZS // 2
    even = is_even()
    sub, lane = iota((SUB, LANES), 0), iota((SUB, LANES), 1)
    plane, place = part(lane, SPREAD)
    rows = nx // COARSEN
    base = 3 * half * SUB

    outer = REACH // COARSEN
    is_left, is_right = (place >= RIM - outer) & (place < RIM), (place >= RIM + WIDTH) & (place < RIM + WIDTH + outer)
    is_own = (place >= RIM) & (place < RIM + WIDTH)
    source = jnp.where(is_left, place - (RIM - outer), place - (RIM + WIDTH - outer))
    source = jnp.where(sub == 0, place - RIM, source) * COARSEN
    source = jnp.clip(source, 0, LANES - COARSEN)
    valid = ((sub == 0) & is_own) | ((sub > 0) & (is_left | is_right))

    def outside(r_ref, Z, upper):
        def mine(at):
            tile_at = kept_ref[at + Z * SUB : at + (Z + 1) * SUB]
            return jnp.where(upper, rolled(tile_at, HALF, 1), tile_at)

        other = r_ref[base + Z * SUB : base + (Z + 1) * SUB]
        return all_rows(0.5 * (mine(nz) + rolled(other, HALF, 1)) * (mine(0) - other))

    odd = jnp.logical_not(even)
    far_rows = base + nz + 2 * SUB
    flux = jnp.zeros((SUB, LANES), f32)
    for Z in range(nz // COARSEN):
        u, c = (
            (facing(own_ref, a, Z * SUB, nz, odd), r2_ref[at : at + SUB])
            for a, at in ((0, far_rows + Z * SUB), (1, far_rows + nz + Z * SUB))
        )
        one = all_rows(0.5 * (c[0] + c[1]) * (u[0] - u[1]))
        two = outside(r2_ref, Z, odd)
        three = outside(r1_ref, Z, even)
        sums = jnp.where(sub == 0, one, jnp.where(sub == 1, two, jnp.where(sub == 2, three, 0.0)))
        here = valid & (plane == Z)
        flux = flux + jnp.where(here, gathered(sums, source), 0.0)
    flux = flux * (1.0 / CELLS)
    far, mate = flux[0:1] + flux[1:2], flux[2:3]

    def stacked(own, other):
        before, after = jnp.where(even, other, own), jnp.where(even, own, other)
        return jnp.where(sub <= rows, rolled(before, 1, 0), rolled(after, rows + 1, 0))

    at = base + nz + SUB
    rhs = stacked(kept_ref[2 * nz + SUB :], r2_ref[at : at + SUB])
    sign = jnp.where(even, 1.0, -1.0)
    rhs = rhs + jnp.where(sub == rows, sign * far, jnp.where(sub == rows + 1, -sign * far, 0.0))
    rhs = rhs - jnp.where(sub == jnp.where(even, 2 * rows, 1), mate, 0.0)

    at = at - SUB
    near_c, far_c = r1_ref[at : at + SUB], r2_ref[at : at + SUB]
    cond = stacked(kept_ref[2 * nz : 2 * nz + SUB], far_c)
    before = jnp.where(even, rolled(far_c, -rows, 0), rolled(near_c, 1 - rows, 0))
    after = jnp.where(even, rolled(near_c, 2 * rows + 1, 0), rolled(far_c, rows + 1, 0))
    cond = jnp.where(sub == 0, before, jnp.where(sub == 2 * rows + 1, after, cond))
    around = rolled(cond, -1, 0) + rolled(cond, 1, 0) + rolled(cond, -1, 1) + rolled(cond, 1, 1)
    around = around + rolled(cond, -SPREAD, 1) + rolled(cond, SPREAD, 1)
    weight = OMEGA / (SHIFT + (0.5 / COARSEN**2) * (6.0 * cond + around))
    o_ref[0:SUB] = weight * rhs
    o_ref[SUB : 2 * SUB] = weight
    o_ref[2 * SUB :] = cond


def faces(own, kept, r2, r1, after, nz, nx):
    return pl.pallas_call(
        functools.partial(faces_kernel, nz=nz, nx=nx),
        out_shape=tiles(3),
        in_specs=[VMEM] * 4 + [pl.BlockSpec(memory_space=pl.ANY)],
        out_specs=VMEM,
        compiler_params=SMALL,
        name="faces",
    )(own, kept, r2, r1, after)


def sides(even, one, two):
    return jnp.where(even, one, two), jnp.where(even, two, one)


def rim_of(low, after, before):
    return jnp.where(low, after, before), rolled(jnp.where(low, before, after), RIM, 0)


def rims_of(low, one_ref, two_ref, last_ref, nz):
    half = nz // 2
    for z in range(nz):
        yield rim_of(low, tile(one_ref if z < half else two_ref, z % half), tile(last_ref, z))


def rim_faces(sub, face, rim_face, u_first, u_last, rim):
    u_rim = jnp.where(sub == 0, rolled(rim, 1 - RIM, 0), rolled(rim, RIM - 1, 0))
    end = sub == SUB - 1
    after = jnp.where(end, face * (u_last - rolled(u_rim, -1, 0)), 0.0)
    before = jnp.where(end, rim_face * (u_rim - rolled(u_first, -1, 0)), 0.0)
    return after, before


def beside(w, z, zs, column):
    return rolled(w, -column - z // zs * GROUP, 1)


def window(spot, left, right, column):
    return jnp.where(spot == RIM - 1, left, rolled(right, RIM - 2 - column, 1))


def begin_kernel(
    strip_ref, u_ref, c_ref, r_ref, cx_ref, cy_ref, cz_ref, diag_ref, inv_ref, q_ref, v_ref, *, nz, nx
):
    zs = nz // ZS
    spot = part(iota((nx, LANES), 1), GROUP)[1]
    row, lane = iota((nx, LANES), 0), iota((nx, LANES), 1)
    first_lane, last_lane = lane == 0, lane == LANES - 1

    def strip(a, zi):
        return strip_ref[(a * zs + zi) * nx : (a * zs + zi + 1) * nx]

    edge_c, edge_f = [], []
    for zi in range(zs):
        u, c = strip(0, zi), strip(1, zi)
        flux = 0.5 * (c + rolled(c, -1, 1)) * (u - rolled(u, -1, 1))
        edge_c.append(window(spot, c, c, 3 * RIM))
        edge_f.append(window(spot, flux, flux, 3 * RIM - 1))

    def own(ref, z):
        return ref[z % nz * nx : (z % nz + 1) * nx]

    below = 0.5 * (own(c_ref, -1) + own(c_ref, 0))
    for z in range(nz):
        at = slice(z * nx, (z + 1) * nx)
        c = own(c_ref, z)
        gx = jnp.where(row == nx - 1, 0.0, 0.5 * (c + rolled(c, -1, 0)))
        edge = beside(edge_c[z % zs], z, zs, RIM - 1)
        gy = 0.5 * (c + jnp.where(last_lane, edge, rolled(c, -1, 1)))
        gyl = 0.5 * (c + jnp.where(first_lane, edge, rolled(c, 1, 1)))
        above = 0.5 * (c + own(c_ref, z + 1))
        diag = SHIFT + (gx + rolled(gx, 1, 0)) + (gy + gyl) + (above + below)
        edge = beside(edge_f[z % zs], z, zs, RIM - 1)
        r = own(r_ref, z) + jnp.where(first_lane, edge, jnp.where(last_lane, -edge, 0.0))
        inner = slice(SUB, nx - SUB)
        inverse = 1.0 / diag[inner]
        scaled = r[inner] * inverse
        cx_ref[at] = gx
        cy_ref[at] = gy
        cz_ref[at] = above
        diag_ref[at] = diag
        q_ref[at] = jnp.concatenate([r[:SUB], scaled, r[nx - SUB :]], axis=0)
        to = slice(z * (nx - 2 * SUB), (z + 1) * (nx - 2 * SUB))
        inv_ref[to] = inverse
        v_ref[to] = scaled * (1.0 / THETA)
        below = above


def begin(strips, u, c, r, nz, nx):
    inner = jax.ShapeDtypeStruct((nz * (nx - 2 * SUB), LANES), f32)
    return pl.pallas_call(
        functools.partial(begin_kernel, nz=nz, nx=nx),
        out_shape=(jax.ShapeDtypeStruct(u.shape, f32),) * 4 + (inner, jax.ShapeDtypeStruct(u.shape, f32), inner),
        in_specs=[VMEM] * 4,
        out_specs=(VMEM,) * 7,
        compiler_params=SMALL,
        cost_estimate=pl.CostEstimate(flops=40 * u.size, bytes_accessed=40 * u.size, transcendentals=0),
        name="begin",
    )(strips, u, c, r)


def fine_kernel(
    strip_ref, b2_ref, b1_ref, one_ref, two_ref, last_ref, u_ref, c_ref, cx_ref, cy_ref, cz_ref, diag_ref, inv_ref, q_ref, v_ref,
    cx, inv, q, va, acc, w2,
    ch, cyh, czh, vb, wr, w0, w1,
    *, nz, nx,
):
    zs = nz // ZS
    half = zs // 2
    ext = nx + SUB
    even = is_even()
    sub = iota((SUB, LANES), 0)
    low, end = sub < RIM, sub == SUB - 1
    table = steps()

    rims = []
    for z, (cond, rim) in enumerate(rims_of(low, one_ref, two_ref, last_ref, nz)):
        ch[z * SUB : (z + 1) * SUB] = cond
        rims.append(rim)

    row, spot = iota((ext, LANES), 0), part(iota((ext, LANES), 1), GROUP)[1]

    def strips_of(a):
        ends = [None] * zs
        for pair in range(half):
            index = a * half + pair
            ends[pair], ends[pair + half] = rim_of(low, *sides(even, tile(b1_ref, index), tile(b2_ref, index)))
        return [
            jnp.concatenate([strip_ref[(a * zs + zi) * nx : (a * zs + zi + 1) * nx], ends[zi]], axis=0)
            for zi in range(zs)
        ]

    def z_up(x):
        return x[1:] + [rolled(x[0], -GROUP, 1)]

    def z_down(x):
        return [rolled(x[-1], GROUP, 1)] + x[:-1]

    us, cs, rs = strips_of(0), strips_of(1), strips_of(2)
    cxs = [0.5 * (c + rolled(c, -1, 0)) for c in cs]
    cys = [0.5 * (c + rolled(c, -1, 1)) for c in cs]
    czs = [0.5 * (c + d) for c, d in zip(cs, z_up(cs))]
    czds = z_down(czs)
    invs, qs, vs = [], [], []
    for zi in range(zs):
        u = us[zi]
        fx = jnp.where((row == nx - 1) | (row == ext - 1), cxs[zi] * (u - rolled(u, -1, 0)), 0.0)
        fy = jnp.where((spot == RIM - 1) | (spot == 3 * RIM - 1), cys[zi] * (u - rolled(u, -1, 1)), 0.0)
        r = rs[zi] - (fx - rolled(fx, 1, 0)) - (fy - rolled(fy, 1, 1))
        wr[zi * SUB : (zi + 1) * SUB] = jnp.where(spot == RIM, r, rolled(r, -2 * RIM, 1))[nx:]
        diag = SHIFT + (cxs[zi] + rolled(cxs[zi], 1, 0)) + (cys[zi] + rolled(cys[zi], 1, 1)) + (czs[zi] + czds[zi])
        invs.append(1.0 / diag)
        qs.append(r * invs[zi])
        vs.append(qs[zi] * (1.0 / THETA))
    for k, w in enumerate((w0, w1, w2)):
        prod = [cys[zi] * vs[zi] for zi in range(zs)]
        for zi in range(zs):
            w[zi * ext : (zi + 1) * ext] = window(spot, prod[zi], vs[zi], 3 * RIM)
        if k == SWEEPS - 1:
            break
        keep, lift = table[k]
        v_up, v_down = z_up(vs), z_down(vs)
        fresh = []
        for zi in range(zs):
            v = vs[zi]
            near = cxs[zi] * rolled(v, -1, 0) + rolled(cxs[zi] * v, 1, 0)
            near = near + cys[zi] * rolled(v, -1, 1) + rolled(prod[zi], 1, 1)
            near = near + czs[zi] * v_up[zi] + czds[zi] * v_down[zi]
            qs[zi] = qs[zi] - v + near * invs[zi]
            fresh.append(keep * v + lift * qs[zi])
        vs = fresh
    edge_c = [window(spot, c, c, 3 * RIM)[nx:] for c in cs]

    lane = iota((SUB, LANES), 1)
    first_lane, last_lane = lane == 0, lane == LANES - 1

    def own(ref, z):
        return ref[z % nz * nx : (z % nz + 1) * nx]

    def rim_at(ref, z):
        return tile(ref, z % nz)

    below = 0.5 * (rim_at(ch, -1) + rim_at(ch, 0))
    for z in range(nz):
        at = slice(z * SUB, (z + 1) * SUB)
        u, c = own(u_ref, z), tile(ch, z)
        c_first, c_last = own(c_ref, z)[:SUB], own(c_ref, z)[nx - SUB :]
        zi = z % zs
        face = jnp.where(end, 0.5 * (c_last + rolled(c, -1, 0)), 0.0)
        gx = 0.5 * (c + jnp.where(end, rolled(c_first, -1, 0), rolled(c, -1, 0)))
        gxl = rolled(gx, 1, 0)
        edge = beside(edge_c[zi], z, zs, RIM - 1)
        gy = 0.5 * (c + jnp.where(last_lane, edge, rolled(c, -1, 1)))
        gyl = 0.5 * (c + jnp.where(first_lane, edge, rolled(c, 1, 1)))
        above = 0.5 * (c + rim_at(ch, z + 1))
        diag = SHIFT + (gx + jnp.where(sub == 0, rolled(face, 1, 0), gxl)) + (gy + gyl) + (above + below)
        after, before = rim_faces(sub, face, gx, u[:SUB], u[nx - SUB :], rims[z])
        r = rims[z] + rolled(after, 1, 0) - before
        r = jnp.where(first_lane | last_lane, beside(wr[zi * SUB : (zi + 1) * SUB], z, zs, RIM), r)
        own_diag, own_q = own(diag_ref, z), own(q_ref, z)
        long_at = slice(z * ext, (z + 1) * ext)
        parts = []
        for this_diag, this_r in (
            (own_diag[:SUB] + jnp.where(sub == 0, gxl, 0.0), own_q[:SUB] + rolled(before, 1, 0)),
            (own_diag[nx - SUB :] + face, own_q[nx - SUB :] - after),
            (diag, r),
        ):
            inverse = 1.0 / this_diag
            scaled = this_r * inverse
            parts.append((inverse, scaled, scaled * (1.0 / THETA)))
        inner = slice(z * (nx - 2 * SUB), (z + 1) * (nx - 2 * SUB))
        middle = (inv_ref[inner], own_q[SUB : nx - SUB], v_ref[inner])
        for ref, one, two, three, four in zip((inv, q, va), parts[0], middle, parts[1], parts[2]):
            ref[long_at] = jnp.concatenate([one, two, three, four], axis=0)
        own_cx = own(cx_ref, z)
        cx[long_at] = jnp.concatenate([own_cx[: nx - SUB], own_cx[nx - SUB :] + face, gx], axis=0)
        cyh[at] = gy
        czh[at] = above
        below = above

    lane = iota((ext, LANES), 1)
    first_lane, last_lane = lane == 0, lane == LANES - 1

    def whole(ref, rim, z):
        return jnp.concatenate([own(ref, z), rim_at(rim, z)], axis=0)

    def long(ref, z):
        return ref[z % nz * ext : (z % nz + 1) * ext]

    for k, w in enumerate((w0, w1)):
        old, new = (va, vb) if k % 2 == 0 else (vb, va)
        keep, lift = table[k]
        for z in range(nz):
            at, here = slice(z * ext, (z + 1) * ext), slice(z * nx, (z + 1) * nx)
            zi = z % zs
            v, gx, gy = old[at], cx[at], whole(cy_ref, cyh, z)
            edge = beside(w[zi * ext : (zi + 1) * ext], z, zs, RIM - 1)
            near = gx * rolled(v, -1, 0) + rolled(gx * v, 1, 0)
            near = near + gy * jnp.where(last_lane, edge, rolled(v, -1, 1))
            near = near + jnp.where(first_lane, edge, rolled(gy * v, 1, 1))
            near = near + whole(cz_ref, czh, z) * long(old, z + 1) + whole(cz_ref, czh, z - 1) * long(old, z - 1)
            scaled = q[at] - v + near * inv[at]
            fresh = keep * v + lift * scaled
            q[at] = scaled
            new[at] = fresh
            acc[here] = (own(u_ref, z) + v[:nx] if k == 0 else acc[here]) + fresh[:nx]


def fine(strips, b2, b1, one, two, last, u, c, begun, nz, nx):
    zs = nz // ZS
    ext = nx + SUB
    rim = pltpu.VMEM((nz * SUB, LANES), f32)
    full = jax.ShapeDtypeStruct((nz * ext, LANES), f32)
    strip = pltpu.VMEM((zs * ext, LANES), f32)
    return pl.pallas_call(
        functools.partial(fine_kernel, nz=nz, nx=nx),
        out_shape=(full,) * 4 + (jax.ShapeDtypeStruct(u.shape, f32), jax.ShapeDtypeStruct((zs * ext, LANES), f32)),
        in_specs=[VMEM] * 15,
        out_specs=(VMEM,) * 6,
        scratch_shapes=[rim] * 3 + [pltpu.VMEM((nz * ext, LANES), f32), pltpu.VMEM((zs * SUB, LANES), f32)] + [strip] * 2,
        compiler_params=SMALL,
        cost_estimate=pl.CostEstimate(flops=100 * u.size, bytes_accessed=40 * u.size, transcendentals=0),
        name="fine",
    )(strips, b2, b1, one, two, last, u, c, *begun)


def finish_kernel(
    cx_ref, inv_ref, q_ref, v_ref, sum_ref, w_ref, cy_ref, cz_ref, m_ref, r_ref, o_ref, out, sems, *, nz, nx
):
    zs = nz // ZS
    ext = nx + SUB
    rows = nx // COARSEN
    even = is_even()
    sub, lane = iota((SUB, LANES), 0), iota((SUB, LANES), 1)
    beyond = sub == jnp.where(even, 2 * rows + 1, 0)
    fields = []
    for a in range(3):
        mine, mate = tile(m_ref, a), tile(r_ref, a)
        mate = jnp.where(even, rolled(mate, 2 * rows, 0), rolled(mate, -2 * rows, 0))
        fields.append(jnp.concatenate([jnp.where(beyond, mate, mine), mate], axis=0))
    start, weight, cond = fields
    scale = 0.5 / COARSEN**2
    turns = (-1, 0), (1, 0), (-1, 1), (1, 1), (-SPREAD, 1), (SPREAD, 1)
    shares = [scale * (cond + rolled(cond, *turn)) for turn in turns]
    keep = 1.0 - weight * (SHIFT + sum(shares))
    shares = [weight * share for share in shares]
    v = start
    for _ in range(COARSE_SWEEPS - 1):
        terms = [share * rolled(v, *turn) for share, turn in zip(shares, turns)]
        v = (start + keep * v) + ((terms[0] + terms[1]) + (terms[2] + terms[3]) + (terms[4] + terms[5]))
    top = v[:SUB]
    top = jnp.where(even, rolled(top, -rows - 1, 0), rolled(top, -1, 0))

    wide = iota((nx, LANES), 1)
    first_lane, last_lane = wide == 0, wide == LANES - 1
    keep, lift = steps()[-1]

    def own(ref, z):
        return ref[z % nz * nx : (z % nz + 1) * nx]

    def long(ref, z):
        return ref[z % nz * ext : z % nz * ext + nx]

    copies = []
    size = COARSEN * nx
    for Z in range(nz // COARSEN):
        spread = jnp.take_along_axis(top, Z * SPREAD + RIM + part(lane, COARSEN)[0], axis=1)
        value = jnp.concatenate([jnp.broadcast_to(spread[X : X + 1], (COARSEN, LANES)) for X in range(rows)], axis=0)
        for z in range(Z * COARSEN, (Z + 1) * COARSEN):
            at = slice(z * ext, (z + 1) * ext)
            v, gx = v_ref[at], cx_ref[at]
            near = (gx * rolled(v, -1, 0) + rolled(gx * v, 1, 0))[:nx]
            v, gy, zi = v[:nx], own(cy_ref, z), z % zs
            edge = beside(w_ref[zi * ext : zi * ext + nx], z, zs, RIM - 1)
            near = near + gy * jnp.where(last_lane, edge, rolled(v, -1, 1))
            near = near + jnp.where(first_lane, edge, rolled(gy * v, 1, 1))
            near = near + own(cz_ref, z) * long(v_ref, z + 1) + own(cz_ref, z - 1) * long(v_ref, z - 1)
            scaled = long(q_ref, z) - v + near * long(inv_ref, z)
            here = slice(z * nx, (z + 1) * nx)
            out[here] = (own(sum_ref, z) + (keep * v + lift * scaled)) + value
        here = pl.ds(Z * size, size)
        copies.append(pltpu.make_async_copy(out.at[here], o_ref.at[here], sems.at[Z]))
        copies[-1].start()
    for copy in copies:
        copy.wait()


def finish(passed, cy, cz, m, r, nz, nx):
    shape = (nz * nx, LANES)
    return pl.pallas_call(
        functools.partial(finish_kernel, nz=nz, nx=nx),
        out_shape=jax.ShapeDtypeStruct(shape, f32),
        in_specs=[VMEM] * 10,
        out_specs=pl.BlockSpec(memory_space=pltpu.HBM),
        scratch_shapes=[pltpu.VMEM(shape, f32), pltpu.SemaphoreType.DMA((nz // COARSEN,))],
        compiler_params=SMALL,
        name="finish",
    )(*passed, cy, cz, m, r)


def moves():
    size_x, size_y = lax.axis_size("gx"), lax.axis_size("gy")

    def send(x, go):
        pairs = []
        for i in range(size_x):
            for j in range(size_y):
                k, l = go(i, j)
                pairs.append((i * size_y + j, (k % size_x) * size_y + l % size_y))
        return lax.ppermute(x, ("gx", "gy"), pairs)

    def mate(x):
        return send(x, lambda i, j: (i + 1 if i % 2 == 0 else i - 1, j))

    def shift(x, by):
        return send(x, lambda i, j: (i + by, j))

    def far(x):
        return send(x, lambda i, j: (i - 1 if i % 2 == 0 else i + 1, j))

    def beside_y(x):
        left = send(x, lambda i, j: (i, j + 1))
        if size_y == 2:
            return left, left
        return left, send(x, lambda i, j: (i, j - 1))

    return mate, far, shift, beside_y


def body(iterate, source, conduct):
    nz, nx, ny = iterate.shape
    if nz != ZS * 4 or ny != LANES or nx != 3 * SUB or lax.axis_size("gx") % 2:
        raise ValueError("shapes")
    mate, far, shift, beside_y = moves()
    u, s, c = (x.reshape(nz * nx, ny) for x in (iterate, source, conduct))
    q, f1, last, one, two, r, own = pack(u, s, c, nz, nx)
    ql, qr = beside_y(q)
    rf1 = mate(f1)
    before = shift(last, 1)
    b1, b2, strips, kept = join(q, ql, qr, rf1, own, nz, nx)
    rb2 = far(b2)
    rb1 = mate(b1)
    one, two, strips = lax.optimization_barrier((one, two, strips))
    after = shift(one, -1), shift(two, -1)
    begun = begin(strips, u, c, r, nz, nx)
    m = faces(own, kept, rb2, rb1, begun[0], nz, nx)
    rm = mate(m)
    passed = fine(strips, rb2, rb1, *after, before, u, c, begun, nz, nx)
    return finish(passed, begun[1], begun[2], m, rm, nz, nx).reshape(nz, nx, ny)


def solution(mesh):
    spec = P(None, "gx", "gy")
    return jax.shard_map(body, mesh=mesh, in_specs=(spec,) * 3, out_specs=spec, check_vma=False)
```

```python
import functools

import jax
import jax.numpy as jnp
from jax import lax
from jax.experimental import pallas as pl
from jax.experimental.pallas import tpu as pltpu
from jax.sharding import PartitionSpec as P

SWEEPS = 3
COARSE_SWEEPS = 4
COARSEN = 8

SHIFT = 0.1
LMIN = 0.3
LMAX = 2.0
OMEGA = 0.8

THETA = (LMAX + LMIN) / 2.0
DELTA = (LMAX - LMIN) / 2.0
SIGMA = THETA / DELTA

RIM = SWEEPS + 1
SUB = 8
LANES = 128
HALF = LANES // 2
GROUP = 4 * RIM
ZS = LANES // GROUP
WIDTH = LANES // COARSEN
SPREAD = 2 * WIDTH
REACH = (COARSE_SWEEPS - 1) * COARSEN
CELLS = COARSEN**3

f32 = jnp.float32
VMEM = pl.BlockSpec(memory_space=pltpu.VMEM)
SMALL = pltpu.CompilerParams(vmem_limit_bytes=12 * 1024 * 1024)


def steps():
    rho, listed = 1.0 / SIGMA, []
    for _ in range(SWEEPS):
        nxt = 1.0 / (2.0 * SIGMA - rho)
        listed.append((nxt * rho, 2.0 * nxt / DELTA))
        rho = nxt
    return listed


def iota(shape, dim):
    return lax.broadcasted_iota(jnp.int32, shape, dim)


def part(index, size):
    return lax.shift_right_logical(index, size.bit_length() - 1), lax.bitwise_and(index, size - 1)


def rolled(x, by, dim):
    return pltpu.roll(x, by % x.shape[dim], dim)


def is_even():
    return lax.axis_index("gx") % 2 == 0


def tiles(count):
    return jax.ShapeDtypeStruct((count * SUB, LANES), f32)


def tile(ref, index):
    return ref[index * SUB : (index + 1) * SUB]


def picked(ref, start, stride):
    return ref[pl.ds(start, SUB, stride=stride), :]


def gathered(rows, source):
    parts = [jnp.take_along_axis(rows, source + k, axis=1) for k in range(COARSEN)]
    while len(parts) > 1:
        parts = [a + b for a, b in zip(parts[::2], parts[1::2])]
    return parts[0]


def compact(rows, place):
    plane, column = part(iota(rows.shape, 1), SPREAD)
    column = column - RIM
    source = jnp.clip(column * COARSEN, 0, LANES - COARSEN)
    here = (plane == place) & (column >= 0) & (column < WIDTH)
    return jnp.where(here, gathered(rows, source), 0.0)


def block_rows(values):
    sub = iota((SUB, LANES), 0)
    out = jnp.zeros((SUB, LANES), f32)
    for block in range(values.shape[0] // COARSEN):
        part = values[block * COARSEN : (block + 1) * COARSEN]
        out = jnp.where(sub == block, jnp.sum(part, axis=0, keepdims=True), out)
    return out


def all_rows(values):
    return jnp.sum(values, axis=0, keepdims=True)


def pack_kernel(
    u_hbm, s_hbm, c_hbm, q_ref, f1_ref, last_ref, one_ref, two_ref, r_ref, own_ref, u_ref, s_ref, c_ref, sums_ref, sems, *, nz, nx
):
    pieces = sems.shape[1]
    size = nz * nx // pieces
    copies = []
    for k, (source, target) in enumerate(((c_hbm, c_ref), (u_hbm, u_ref), (s_hbm, s_ref))):
        for piece in range(pieces):
            at = pl.ds(piece * size, size)
            copies.append(pltpu.make_async_copy(source.at[at], target.at[at], sems.at[k, piece]))
    for copy in copies:
        copy.start()
    for copy in copies[: 2 * pieces]:
        copy.wait()

    even = is_even()
    sub, lane = iota((SUB, LANES), 0), iota((SUB, LANES), 1)
    low = sub < RIM
    row, wide = iota((nx, LANES), 0), iota((nx, LANES), 1)
    slot, spot = part(wide, 2 * RIM)

    def plane(ref, z):
        return ref[z % nz * nx : (z % nz + 1) * nx]

    def up(z):
        return 0.5 * (plane(c_ref, z) + plane(c_ref, z + 1)) * (plane(u_ref, z) - plane(u_ref, z + 1))

    for z in range(nz):
        u, c = plane(u_ref, z), plane(c_ref, z)
        fy = 0.5 * (c + rolled(c, -1, 1)) * (u - rolled(u, -1, 1))
        r_ref[z * nx : (z + 1) * nx] = jnp.where(wide == LANES - 1, 0.0, fy)
    for copy in copies[2 * pieces :]:
        copy.wait()
    below = up(nz - 1)
    for Z in range(nz // COARSEN):
        sum_r = sum_c = jnp.zeros((nx, LANES), f32)
        for z in range(Z * COARSEN, (Z + 1) * COARSEN):
            u, c = plane(u_ref, z), plane(c_ref, z)
            above = up(z)
            fx = 0.5 * (c + rolled(c, -1, 0)) * (u - rolled(u, -1, 0))
            fy = plane(r_ref, z)
            fx = jnp.where(row == nx - 1, 0.0, fx)
            r = plane(s_ref, z) - SHIFT * u - (fx - rolled(fx, 1, 0)) - (fy - rolled(fy, 1, 1)) - (above - below)
            below = above
            r_ref[z * nx : (z + 1) * nx] = r
            sum_r = sum_r + r
            sum_c = sum_c + c
            u0, u2, c0, c2 = u[:SUB], u[nx - SUB :], c[:SUB], c[nx - SUB :]
            first = jnp.where(low, c0, jnp.where(sub == SUB - 1, rolled(u0, -1, 0), rolled(r[:SUB], RIM, 0)))
            last = jnp.where(low, jnp.where(sub == 0, rolled(u2, 1, 0), rolled(r[nx - SUB :], RIM, 0)), c2)
            last_ref[z * SUB : (z + 1) * SUB] = last
            to = z % (nz // 2) * SUB
            (one_ref if z < nz // 2 else two_ref)[to : to + SUB] = first
        sums_ref[Z * nx : (Z + 1) * nx] = sum_r
        sums_ref[(Z + nz // COARSEN) * nx : (Z + nz // COARSEN + 1) * nx] = sum_c

    zs = nz // ZS
    half = zs // 2
    def strips():
        for zi in range(zs):
            strip = jnp.zeros((nx, LANES), f32)
            for g in range(ZS):
                z, at = g * zs + zi, g * GROUP + RIM
                outer = jnp.where(spot < 2, rolled(plane(u_ref, z), at + RIM + 1, 1), rolled(plane(r_ref, z), at + 2 * RIM + 1, 1))
                strip = jnp.where(slot == 2 * g + 1, outer, strip)
                strip = jnp.where(slot == 2 * g, rolled(plane(c_ref, z), at, 1), strip)
            q_ref[zi * nx : (zi + 1) * nx] = strip

    def finish():
        coarse = jnp.zeros((SUB, LANES), f32)
        planes = nz // COARSEN
        for Z in range(planes):
            sum_r, sum_c = (sums_ref[(Z + k * planes) * nx : (Z + k * planes + 1) * nx] for k in range(2))
            coarse = coarse + compact(block_rows(sum_r) + rolled(block_rows(sum_c), RIM, 0), Z)
        coarse = coarse * (1.0 / CELLS)
        strips()

        base = zs * nx + SUB
        for a, ref in enumerate((u_ref, c_ref)):
            for Z in range(nz // SUB):
                at = Z * SUB * nx
                first, last = picked(ref, at, nx), picked(ref, at + nx - 1, nx)
                to = a * nz + Z * SUB
                own_ref[to : to + SUB] = first
                own_ref[2 * nz + to : 2 * nz + to + SUB] = last
                f1_ref[to : to + SUB] = jnp.where(even, last, first)
                q_ref[base + to : base + to + SUB] = jnp.where(
                    lane < HALF, rolled(first, REACH, 1), rolled(last, REACH + HALF, 1)
                )
        q_ref[base + 2 * nz : base + 2 * nz + SUB] = coarse
        f1_ref[2 * nz :] = coarse
        corners = jnp.zeros((SUB, LANES), f32)
        group = part(lane, GROUP)[0]
        for Z in range(nz // SUB):
            at = Z * SUB * nx
            first, last = picked(u_ref, at, nx), picked(u_ref, at + nx - 1, nx)
            both = jnp.where(low, first, rolled(last, RIM, 0)), jnp.where(low, rolled(first, RIM, 0), last)
            for second in range(2):
                g = 2 * Z + second
                corners = jnp.where(group == g, rolled(both[second], g * GROUP + RIM, 1), corners)
        q_ref[zs * nx : base] = corners

    finish()


def pack(u, s, c, nz, nx):
    pieces = 1
    return pl.pallas_call(
        functools.partial(pack_kernel, nz=nz, nx=nx),
        out_shape=(
            tiles(nz // ZS * nx // SUB + 2 * nz // SUB + 2),
            tiles(2 * nz // SUB + 1),
            tiles(nz),
            tiles(nz // 2),
            tiles(nz // 2),
            jax.ShapeDtypeStruct(u.shape, f32),
            tiles(4 * nz // SUB),
        ),
        in_specs=[pl.BlockSpec(memory_space=pltpu.HBM)] * 3,
        out_specs=(VMEM,) * 7,
        scratch_shapes=[pltpu.VMEM(u.shape, f32)] * 3
        + [pltpu.VMEM((2 * nz // COARSEN * nx, LANES), f32), pltpu.SemaphoreType.DMA((3, pieces))],
        compiler_params=SMALL,
        name="pack",
    )(*(pltpu.with_memory_space_constraint(x, pltpu.HBM) for x in (u, s, c)))


def facing(own_ref, a, z, nz, last):
    first, second = own_ref[a * nz + z : a * nz + z + SUB], own_ref[(2 + a) * nz + z : (2 + a) * nz + z + SUB]
    return jnp.where(last, second, first)


def join_kernel(q_ref, ql_ref, qr_ref, f1_ref, own_ref, b1_ref, b2_ref, strip_ref, kept_ref, *, nz, nx):
    zs = nz // ZS
    half = zs // 2
    even = is_even()
    sub, lane = iota((SUB, LANES), 0), iota((SUB, LANES), 1)
    low = sub < RIM
    spot = part(iota((nx, LANES), 1), GROUP)[1]
    thin, row = part(lane, GROUP)[1], iota((nx, LANES), 0)

    def before(spot, left, own, right):
        moved = rolled(jnp.where(spot < RIM, own, right), 2 * RIM, 1)
        return jnp.where(spot < 2 * RIM, jnp.where(spot < RIM, left, own), moved)

    def behind(spot, left, own, right):
        lower, at = spot < 2 * RIM, 2 * RIM
        split = spot < at + 2 + SWEEPS
        residual = jnp.where(
            lower,
            rolled(jnp.where(split, left, own), -(at + 1), 1),
            rolled(jnp.where(split, own, right), -1, 1),
        )
        split = spot == at
        u = jnp.where(
            lower,
            rolled(jnp.where(split, left, own), RIM - 1 - at, 1),
            rolled(jnp.where(split, own, right), RIM - 1, 1),
        )
        return residual, u

    at = slice(zs * nx, zs * nx + SUB)
    corners = before(thin, ql_ref[at], q_ref[at], qr_ref[at])
    joined = [], [], []
    for zi in range(zs):
        at = slice(zi * nx, (zi + 1) * nx)
        parts = ql_ref[at], q_ref[at], qr_ref[at]
        residual, u = behind(spot, *parts)
        u = jnp.where(row == 0, corners[zi : zi + 1], u)
        u = jnp.where(row == nx - 1, corners[RIM + zi : RIM + zi + 1], u)
        for group, strip in zip(joined, (u, before(spot, *parts), residual)):
            group.append(strip)
    for a, group in enumerate(joined):
        for zi in range(zs):
            strip_ref[(a * zs + zi) * nx : (a * zs + zi + 1) * nx] = group[zi]
        for pair in range(half):
            one, two = group[pair], group[pair + half]
            first = jnp.where(low, one[:SUB], rolled(two[:SUB], RIM, 0))
            last = jnp.where(low, rolled(two[nx - SUB :], RIM, 0), one[nx - SUB :])
            to = slice((a * half + pair) * SUB, (a * half + pair + 1) * SUB)
            b1_ref[to] = jnp.where(even, last, first)
            b2_ref[to] = jnp.where(even, first, last)

    source, target = zs * nx + SUB, 3 * half * SUB
    lower, outer = lane < HALF, part(lane, HALF)[1] < REACH
    for Z in range(nz // SUB):
        u, c = (
            jnp.where(outer, ql_ref[at : at + SUB], qr_ref[at : at + SUB])
            for at in (source + Z * SUB, source + nz + Z * SUB)
        )
        kept_ref[Z * SUB : (Z + 1) * SUB] = u
        kept_ref[nz + Z * SUB : nz + (Z + 1) * SUB] = c
        first, last = jnp.where(lower, u, rolled(c, HALF, 1)), jnp.where(lower, rolled(u, HALF, 1), c)
        to = slice(target + Z * SUB, target + (Z + 1) * SUB)
        b1_ref[to] = jnp.where(even, last, first)
        b2_ref[to] = jnp.where(even, first, last)

    at = slice(source + 2 * nz, source + 2 * nz + SUB)
    place = part(lane, SPREAD)[1]
    window = jnp.where(
        place < RIM,
        rolled(ql_ref[at], -WIDTH, 1),
        jnp.where(place < RIM + WIDTH, q_ref[at], rolled(qr_ref[at], WIDTH, 1)),
    )
    flux = jnp.zeros((nx, LANES), f32)
    for u, c in zip(joined[0], joined[1]):
        flux = flux + (c + rolled(c, -1, 1)) * (u - rolled(u, -1, 1))
    flux = block_rows((0.5 / CELLS) * flux)
    flux = flux + rolled(flux, -GROUP, 1)
    near, far = RIM - 1, 3 * RIM - 1
    change = jnp.where(place == RIM - 1, -rolled(flux, RIM - 1 - near, 1), 0.0)
    change = jnp.where(place == RIM, rolled(flux, RIM - near, 1), change)
    change = jnp.where(place == RIM + WIDTH - 1, -rolled(flux, RIM + WIDTH - 1 - far, 1), change)
    change = jnp.where(place == RIM + WIDTH, rolled(flux, RIM + WIDTH - far, 1), change)
    rows = nx // COARSEN
    nearest = jnp.where(even, rows - 1, 0)
    for Z in range(nz // COARSEN):
        u, c = facing(own_ref, 0, Z * SUB, nz, even) - tile(f1_ref, Z), facing(own_ref, 1, Z * SUB, nz, even)
        across = all_rows((0.5 / CELLS) * (c + tile(f1_ref, nz // SUB + Z)) * u)
        change = change - compact(jnp.where(sub == nearest, across, 0.0), Z)
    mate = f1_ref[2 * nz : 2 * nz + SUB]
    mate = jnp.where(even, rolled(mate, rows - RIM, 0), rolled(mate, 1 - RIM, 0))
    cond = jnp.where(sub == rows, mate, rolled(window, -RIM, 0))
    rhs = window + change
    kept_ref[2 * nz : 2 * nz + SUB] = cond
    kept_ref[2 * nz + SUB :] = rhs
    to = target + nz
    b1_ref[to:] = cond
    b2_ref[to : to + SUB] = cond
    b2_ref[to + SUB : to + 2 * SUB] = rhs
    to = to + 2 * SUB
    for a in range(2):
        for Z in range(nz // SUB):
            at = to + a * nz + Z * SUB
            b2_ref[at : at + SUB] = facing(own_ref, a, Z * SUB, nz, jnp.logical_not(even))


def join(q, ql, qr, f1, own, nz, nx):
    zs = nz // ZS
    size = 3 * (zs // 2) + nz // SUB + 1
    return pl.pallas_call(
        functools.partial(join_kernel, nz=nz, nx=nx),
        out_shape=(
            tiles(size),
            tiles(size + 1 + 2 * nz // SUB),
            jax.ShapeDtypeStruct((3 * zs * nx, LANES), f32),
            tiles(2 * nz // SUB + 2),
        ),
        in_specs=[VMEM] * 5,
        out_specs=(VMEM,) * 4,
        compiler_params=SMALL,
        name="join",
    )(q, ql, qr, f1, own)


def faces_kernel(own_ref, kept_ref, r2_ref, r1_ref, after_ref, o_ref, *, nz, nx):
    del after_ref
    half = nz // ZS // 2
    even = is_even()
    sub, lane = iota((SUB, LANES), 0), iota((SUB, LANES), 1)
    plane, place = part(lane, SPREAD)
    rows = nx // COARSEN
    base = 3 * half * SUB

    outer = REACH // COARSEN
    is_left, is_right = (place >= RIM - outer) & (place < RIM), (place >= RIM + WIDTH) & (place < RIM + WIDTH + outer)
    is_own = (place >= RIM) & (place < RIM + WIDTH)
    source = jnp.where(is_left, place - (RIM - outer), place - (RIM + WIDTH - outer))
    source = jnp.where(sub == 0, place - RIM, source) * COARSEN
    source = jnp.clip(source, 0, LANES - COARSEN)
    valid = ((sub == 0) & is_own) | ((sub > 0) & (is_left | is_right))

    def outside(r_ref, Z, upper):
        def mine(at):
            tile_at = kept_ref[at + Z * SUB : at + (Z + 1) * SUB]
            return jnp.where(upper, rolled(tile_at, HALF, 1), tile_at)

        other = r_ref[base + Z * SUB : base + (Z + 1) * SUB]
        return all_rows(0.5 * (mine(nz) + rolled(other, HALF, 1)) * (mine(0) - other))

    odd = jnp.logical_not(even)
    far_rows = base + nz + 2 * SUB
    flux = jnp.zeros((SUB, LANES), f32)
    for Z in range(nz // COARSEN):
        u, c = (
            (facing(own_ref, a, Z * SUB, nz, odd), r2_ref[at : at + SUB])
            for a, at in ((0, far_rows + Z * SUB), (1, far_rows + nz + Z * SUB))
        )
        one = all_rows(0.5 * (c[0] + c[1]) * (u[0] - u[1]))
        two = outside(r2_ref, Z, odd)
        three = outside(r1_ref, Z, even)
        sums = jnp.where(sub == 0, one, jnp.where(sub == 1, two, jnp.where(sub == 2, three, 0.0)))
        here = valid & (plane == Z)
        flux = flux + jnp.where(here, gathered(sums, source), 0.0)
    flux = flux * (1.0 / CELLS)
    far, mate = flux[0:1] + flux[1:2], flux[2:3]

    def stacked(own, other):
        before, after = jnp.where(even, other, own), jnp.where(even, own, other)
        return jnp.where(sub <= rows, rolled(before, 1, 0), rolled(after, rows + 1, 0))

    at = base + nz + SUB
    rhs = stacked(kept_ref[2 * nz + SUB :], r2_ref[at : at + SUB])
    sign = jnp.where(even, 1.0, -1.0)
    rhs = rhs + jnp.where(sub == rows, sign * far, jnp.where(sub == rows + 1, -sign * far, 0.0))
    rhs = rhs - jnp.where(sub == jnp.where(even, 2 * rows, 1), mate, 0.0)

    at = at - SUB
    near_c, far_c = r1_ref[at : at + SUB], r2_ref[at : at + SUB]
    cond = stacked(kept_ref[2 * nz : 2 * nz + SUB], far_c)
    before = jnp.where(even, rolled(far_c, -rows, 0), rolled(near_c, 1 - rows, 0))
    after = jnp.where(even, rolled(near_c, 2 * rows + 1, 0), rolled(far_c, rows + 1, 0))
    cond = jnp.where(sub == 0, before, jnp.where(sub == 2 * rows + 1, after, cond))
    around = rolled(cond, -1, 0) + rolled(cond, 1, 0) + rolled(cond, -1, 1) + rolled(cond, 1, 1)
    around = around + rolled(cond, -SPREAD, 1) + rolled(cond, SPREAD, 1)
    weight = OMEGA / (SHIFT + (0.5 / COARSEN**2) * (6.0 * cond + around))
    o_ref[0:SUB] = weight * rhs
    o_ref[SUB : 2 * SUB] = weight
    o_ref[2 * SUB :] = cond


def faces(own, kept, r2, r1, after, nz, nx):
    return pl.pallas_call(
        functools.partial(faces_kernel, nz=nz, nx=nx),
        out_shape=tiles(3),
        in_specs=[VMEM] * 4 + [pl.BlockSpec(memory_space=pl.ANY)],
        out_specs=VMEM,
        compiler_params=SMALL,
        name="faces",
    )(own, kept, r2, r1, after)


def sides(even, one, two):
    return jnp.where(even, one, two), jnp.where(even, two, one)


def rim_of(low, after, before):
    return jnp.where(low, after, before), rolled(jnp.where(low, before, after), RIM, 0)


def rims_of(low, one_ref, two_ref, last_ref, nz):
    half = nz // 2
    for z in range(nz):
        yield rim_of(low, tile(one_ref if z < half else two_ref, z % half), tile(last_ref, z))


def rim_faces(sub, face, rim_face, u_first, u_last, rim):
    u_rim = jnp.where(sub == 0, rolled(rim, 1 - RIM, 0), rolled(rim, RIM - 1, 0))
    end = sub == SUB - 1
    after = jnp.where(end, face * (u_last - rolled(u_rim, -1, 0)), 0.0)
    before = jnp.where(end, rim_face * (u_rim - rolled(u_first, -1, 0)), 0.0)
    return after, before


def beside(w, z, zs, column):
    return rolled(w, -column - z // zs * GROUP, 1)


def window(spot, left, right, column):
    return jnp.where(spot == RIM - 1, left, rolled(right, RIM - 2 - column, 1))


def begin_kernel(
    strip_ref, u_ref, c_ref, r_ref, cx_ref, cy_ref, cz_ref, diag_ref, inv_ref, q_ref, v_ref, *, nz, nx
):
    zs = nz // ZS
    spot = part(iota((nx, LANES), 1), GROUP)[1]
    row, lane = iota((nx, LANES), 0), iota((nx, LANES), 1)
    first_lane, last_lane = lane == 0, lane == LANES - 1

    def strip(a, zi):
        return strip_ref[(a * zs + zi) * nx : (a * zs + zi + 1) * nx]

    edge_c, edge_f = [], []
    for zi in range(zs):
        u, c = strip(0, zi), strip(1, zi)
        flux = 0.5 * (c + rolled(c, -1, 1)) * (u - rolled(u, -1, 1))
        edge_c.append(window(spot, c, c, 3 * RIM))
        edge_f.append(window(spot, flux, flux, 3 * RIM - 1))

    def own(ref, z):
        return ref[z % nz * nx : (z % nz + 1) * nx]

    below = 0.5 * (own(c_ref, -1) + own(c_ref, 0))
    for z in range(nz):
        at = slice(z * nx, (z + 1) * nx)
        c = own(c_ref, z)
        gx = jnp.where(row == nx - 1, 0.0, 0.5 * (c + rolled(c, -1, 0)))
        edge = beside(edge_c[z % zs], z, zs, RIM - 1)
        gy = 0.5 * (c + jnp.where(last_lane, edge, rolled(c, -1, 1)))
        gyl = 0.5 * (c + jnp.where(first_lane, edge, rolled(c, 1, 1)))
        above = 0.5 * (c + own(c_ref, z + 1))
        diag = SHIFT + (gx + rolled(gx, 1, 0)) + (gy + gyl) + (above + below)
        edge = beside(edge_f[z % zs], z, zs, RIM - 1)
        r = own(r_ref, z) + jnp.where(first_lane, edge, jnp.where(last_lane, -edge, 0.0))
        inner = slice(SUB, nx - SUB)
        inverse = 1.0 / diag[inner]
        scaled = r[inner] * inverse
        cx_ref[at] = gx
        cy_ref[at] = gy
        cz_ref[at] = above
        diag_ref[at] = diag
        q_ref[at] = jnp.concatenate([r[:SUB], scaled, r[nx - SUB :]], axis=0)
        to = slice(z * (nx - 2 * SUB), (z + 1) * (nx - 2 * SUB))
        inv_ref[to] = inverse
        v_ref[to] = scaled * (1.0 / THETA)
        below = above


def begin(strips, u, c, r, nz, nx):
    inner = jax.ShapeDtypeStruct((nz * (nx - 2 * SUB), LANES), f32)
    return pl.pallas_call(
        functools.partial(begin_kernel, nz=nz, nx=nx),
        out_shape=(jax.ShapeDtypeStruct(u.shape, f32),) * 4 + (inner, jax.ShapeDtypeStruct(u.shape, f32), inner),
        in_specs=[VMEM] * 4,
        out_specs=(VMEM,) * 7,
        compiler_params=SMALL,
        cost_estimate=pl.CostEstimate(flops=40 * u.size, bytes_accessed=40 * u.size, transcendentals=0),
        name="begin",
    )(strips, u, c, r)


def fine_kernel(
    strip_ref, b2_ref, b1_ref, one_ref, two_ref, last_ref, u_ref, c_ref, cx_ref, cy_ref, cz_ref, diag_ref, inv_ref, q_ref, v_ref,
    cx, inv, q, va, acc, w2,
    ch, cyh, czh, vb, wr, w0, w1,
    *, nz, nx,
):
    zs = nz // ZS
    half = zs // 2
    ext = nx + SUB
    even = is_even()
    sub = iota((SUB, LANES), 0)
    low, end = sub < RIM, sub == SUB - 1
    table = steps()

    rims = []
    for z, (cond, rim) in enumerate(rims_of(low, one_ref, two_ref, last_ref, nz)):
        ch[z * SUB : (z + 1) * SUB] = cond
        rims.append(rim)

    row, spot = iota((ext, LANES), 0), part(iota((ext, LANES), 1), GROUP)[1]

    def strips_of(a):
        ends = [None] * zs
        for pair in range(half):
            index = a * half + pair
            ends[pair], ends[pair + half] = rim_of(low, *sides(even, tile(b1_ref, index), tile(b2_ref, index)))
        return [
            jnp.concatenate([strip_ref[(a * zs + zi) * nx : (a * zs + zi + 1) * nx], ends[zi]], axis=0)
            for zi in range(zs)
        ]

    def z_up(x):
        return x[1:] + [rolled(x[0], -GROUP, 1)]

    def z_down(x):
        return [rolled(x[-1], GROUP, 1)] + x[:-1]

    us, cs, rs = strips_of(0), strips_of(1), strips_of(2)
    cxs = [0.5 * (c + rolled(c, -1, 0)) for c in cs]
    cys = [0.5 * (c + rolled(c, -1, 1)) for c in cs]
    czs = [0.5 * (c + d) for c, d in zip(cs, z_up(cs))]
    czds = z_down(czs)
    invs, qs, vs = [], [], []
    for zi in range(zs):
        u = us[zi]
        fx = jnp.where((row == nx - 1) | (row == ext - 1), cxs[zi] * (u - rolled(u, -1, 0)), 0.0)
        fy = jnp.where((spot == RIM - 1) | (spot == 3 * RIM - 1), cys[zi] * (u - rolled(u, -1, 1)), 0.0)
        r = rs[zi] - (fx - rolled(fx, 1, 0)) - (fy - rolled(fy, 1, 1))
        wr[zi * SUB : (zi + 1) * SUB] = jnp.where(spot == RIM, r, rolled(r, -2 * RIM, 1))[nx:]
        diag = SHIFT + (cxs[zi] + rolled(cxs[zi], 1, 0)) + (cys[zi] + rolled(cys[zi], 1, 1)) + (czs[zi] + czds[zi])
        invs.append(1.0 / diag)
        qs.append(r * invs[zi])
        vs.append(qs[zi] * (1.0 / THETA))
    for k, w in enumerate((w0, w1, w2)):
        prod = [cys[zi] * vs[zi] for zi in range(zs)]
        for zi in range(zs):
            w[zi * ext : (zi + 1) * ext] = window(spot, prod[zi], vs[zi], 3 * RIM)
        if k == SWEEPS - 1:
            break
        keep, lift = table[k]
        v_up, v_down = z_up(vs), z_down(vs)
        fresh = []
        for zi in range(zs):
            v = vs[zi]
            near = cxs[zi] * rolled(v, -1, 0) + rolled(cxs[zi] * v, 1, 0)
            near = near + cys[zi] * rolled(v, -1, 1) + rolled(prod[zi], 1, 1)
            near = near + czs[zi] * v_up[zi] + czds[zi] * v_down[zi]
            qs[zi] = qs[zi] - v + near * invs[zi]
            fresh.append(keep * v + lift * qs[zi])
        vs = fresh
    edge_c = [window(spot, c, c, 3 * RIM)[nx:] for c in cs]

    lane = iota((SUB, LANES), 1)
    first_lane, last_lane = lane == 0, lane == LANES - 1

    def own(ref, z):
        return ref[z % nz * nx : (z % nz + 1) * nx]

    def rim_at(ref, z):
        return tile(ref, z % nz)

    below = 0.5 * (rim_at(ch, -1) + rim_at(ch, 0))
    for z in range(nz):
        at = slice(z * SUB, (z + 1) * SUB)
        u, c = own(u_ref, z), tile(ch, z)
        c_first, c_last = own(c_ref, z)[:SUB], own(c_ref, z)[nx - SUB :]
        zi = z % zs
        face = jnp.where(end, 0.5 * (c_last + rolled(c, -1, 0)), 0.0)
        gx = 0.5 * (c + jnp.where(end, rolled(c_first, -1, 0), rolled(c, -1, 0)))
        gxl = rolled(gx, 1, 0)
        edge = beside(edge_c[zi], z, zs, RIM - 1)
        gy = 0.5 * (c + jnp.where(last_lane, edge, rolled(c, -1, 1)))
        gyl = 0.5 * (c + jnp.where(first_lane, edge, rolled(c, 1, 1)))
        above = 0.5 * (c + rim_at(ch, z + 1))
        diag = SHIFT + (gx + jnp.where(sub == 0, rolled(face, 1, 0), gxl)) + (gy + gyl) + (above + below)
        after, before = rim_faces(sub, face, gx, u[:SUB], u[nx - SUB :], rims[z])
        r = rims[z] + rolled(after, 1, 0) - before
        r = jnp.where(first_lane | last_lane, beside(wr[zi * SUB : (zi + 1) * SUB], z, zs, RIM), r)
        own_diag, own_q = own(diag_ref, z), own(q_ref, z)
        long_at = slice(z * ext, (z + 1) * ext)
        parts = []
        for this_diag, this_r in (
            (own_diag[:SUB] + jnp.where(sub == 0, gxl, 0.0), own_q[:SUB] + rolled(before, 1, 0)),
            (own_diag[nx - SUB :] + face, own_q[nx - SUB :] - after),
            (diag, r),
        ):
            inverse = 1.0 / this_diag
            scaled = this_r * inverse
            parts.append((inverse, scaled, scaled * (1.0 / THETA)))
        inner = slice(z * (nx - 2 * SUB), (z + 1) * (nx - 2 * SUB))
        middle = (inv_ref[inner], own_q[SUB : nx - SUB], v_ref[inner])
        for ref, one, two, three, four in zip((inv, q, va), parts[0], middle, parts[1], parts[2]):
            ref[long_at] = jnp.concatenate([one, two, three, four], axis=0)
        own_cx = own(cx_ref, z)
        cx[long_at] = jnp.concatenate([own_cx[: nx - SUB], own_cx[nx - SUB :] + face, gx], axis=0)
        cyh[at] = gy
        czh[at] = above
        below = above

    lane = iota((ext, LANES), 1)
    first_lane, last_lane = lane == 0, lane == LANES - 1

    def whole(ref, rim, z):
        return jnp.concatenate([own(ref, z), rim_at(rim, z)], axis=0)

    def long(ref, z):
        return ref[z % nz * ext : (z % nz + 1) * ext]

    for k, w in enumerate((w0, w1)):
        old, new = (va, vb) if k % 2 == 0 else (vb, va)
        keep, lift = table[k]
        for z in range(nz):
            at, here = slice(z * ext, (z + 1) * ext), slice(z * nx, (z + 1) * nx)
            zi = z % zs
            v, gx, gy = old[at], cx[at], whole(cy_ref, cyh, z)
            edge = beside(w[zi * ext : (zi + 1) * ext], z, zs, RIM - 1)
            near = gx * rolled(v, -1, 0) + rolled(gx * v, 1, 0)
            near = near + gy * jnp.where(last_lane, edge, rolled(v, -1, 1))
            near = near + jnp.where(first_lane, edge, rolled(gy * v, 1, 1))
            near = near + whole(cz_ref, czh, z) * long(old, z + 1) + whole(cz_ref, czh, z - 1) * long(old, z - 1)
            scaled = q[at] - v + near * inv[at]
            fresh = keep * v + lift * scaled
            q[at] = scaled
            new[at] = fresh
            acc[here] = (own(u_ref, z) + v[:nx] if k == 0 else acc[here]) + fresh[:nx]


def fine(strips, b2, b1, one, two, last, u, c, begun, nz, nx):
    zs = nz // ZS
    ext = nx + SUB
    rim = pltpu.VMEM((nz * SUB, LANES), f32)
    full = jax.ShapeDtypeStruct((nz * ext, LANES), f32)
    strip = pltpu.VMEM((zs * ext, LANES), f32)
    return pl.pallas_call(
        functools.partial(fine_kernel, nz=nz, nx=nx),
        out_shape=(full,) * 4 + (jax.ShapeDtypeStruct(u.shape, f32), jax.ShapeDtypeStruct((zs * ext, LANES), f32)),
        in_specs=[VMEM] * 15,
        out_specs=(VMEM,) * 6,
        scratch_shapes=[rim] * 3 + [pltpu.VMEM((nz * ext, LANES), f32), pltpu.VMEM((zs * SUB, LANES), f32)] + [strip] * 2,
        compiler_params=SMALL,
        cost_estimate=pl.CostEstimate(flops=100 * u.size, bytes_accessed=40 * u.size, transcendentals=0),
        name="fine",
    )(strips, b2, b1, one, two, last, u, c, *begun)


def finish_kernel(
    cx_ref, inv_ref, q_ref, v_ref, sum_ref, w_ref, cy_ref, cz_ref, m_ref, r_ref, o_ref, out, sems, *, nz, nx
):
    zs = nz // ZS
    ext = nx + SUB
    rows = nx // COARSEN
    even = is_even()
    sub, lane = iota((SUB, LANES), 0), iota((SUB, LANES), 1)
    beyond = sub == jnp.where(even, 2 * rows + 1, 0)
    fields = []
    for a in range(3):
        mine, mate = tile(m_ref, a), tile(r_ref, a)
        mate = jnp.where(even, rolled(mate, 2 * rows, 0), rolled(mate, -2 * rows, 0))
        fields.append(jnp.concatenate([jnp.where(beyond, mate, mine), mate], axis=0))
    start, weight, cond = fields
    scale = 0.5 / COARSEN**2
    turns = (-1, 0), (1, 0), (-1, 1), (1, 1), (-SPREAD, 1), (SPREAD, 1)
    shares = [scale * (cond + rolled(cond, *turn)) for turn in turns]
    keep = 1.0 - weight * (SHIFT + sum(shares))
    shares = [weight * share for share in shares]
    v = start
    for _ in range(COARSE_SWEEPS - 1):
        terms = [share * rolled(v, *turn) for share, turn in zip(shares, turns)]
        v = (start + keep * v) + ((terms[0] + terms[1]) + (terms[2] + terms[3]) + (terms[4] + terms[5]))
    top = v[:SUB]
    top = jnp.where(even, rolled(top, -rows - 1, 0), rolled(top, -1, 0))

    wide = iota((nx, LANES), 1)
    first_lane, last_lane = wide == 0, wide == LANES - 1
    keep, lift = steps()[-1]

    def own(ref, z):
        return ref[z % nz * nx : (z % nz + 1) * nx]

    def long(ref, z):
        return ref[z % nz * ext : z % nz * ext + nx]

    copies = []
    size = COARSEN * nx
    for Z in range(nz // COARSEN):
        spread = jnp.take_along_axis(top, Z * SPREAD + RIM + part(lane, COARSEN)[0], axis=1)
        value = jnp.concatenate([jnp.broadcast_to(spread[X : X + 1], (COARSEN, LANES)) for X in range(rows)], axis=0)
        for z in range(Z * COARSEN, (Z + 1) * COARSEN):
            at = slice(z * ext, (z + 1) * ext)
            v, gx = v_ref[at], cx_ref[at]
            near = (gx * rolled(v, -1, 0) + rolled(gx * v, 1, 0))[:nx]
            v, gy, zi = v[:nx], own(cy_ref, z), z % zs
            edge = beside(w_ref[zi * ext : zi * ext + nx], z, zs, RIM - 1)
            near = near + gy * jnp.where(last_lane, edge, rolled(v, -1, 1))
            near = near + jnp.where(first_lane, edge, rolled(gy * v, 1, 1))
            near = near + own(cz_ref, z) * long(v_ref, z + 1) + own(cz_ref, z - 1) * long(v_ref, z - 1)
            scaled = long(q_ref, z) - v + near * long(inv_ref, z)
            here = slice(z * nx, (z + 1) * nx)
            out[here] = (own(sum_ref, z) + (keep * v + lift * scaled)) + value
        here = pl.ds(Z * size, size)
        copies.append(pltpu.make_async_copy(out.at[here], o_ref.at[here], sems.at[Z]))
        copies[-1].start()
    for copy in copies:
        copy.wait()


def finish(passed, cy, cz, m, r, nz, nx):
    shape = (nz * nx, LANES)
    return pl.pallas_call(
        functools.partial(finish_kernel, nz=nz, nx=nx),
        out_shape=jax.ShapeDtypeStruct(shape, f32),
        in_specs=[VMEM] * 10,
        out_specs=pl.BlockSpec(memory_space=pltpu.HBM),
        scratch_shapes=[pltpu.VMEM(shape, f32), pltpu.SemaphoreType.DMA((nz // COARSEN,))],
        compiler_params=SMALL,
        name="finish",
    )(*passed, cy, cz, m, r)


def moves():
    size_x, size_y = lax.axis_size("gx"), lax.axis_size("gy")

    def send(x, go):
        pairs = []
        for i in range(size_x):
            for j in range(size_y):
                k, l = go(i, j)
                pairs.append((i * size_y + j, (k % size_x) * size_y + l % size_y))
        return lax.ppermute(x, ("gx", "gy"), pairs)

    def mate(x):
        return send(x, lambda i, j: (i + 1 if i % 2 == 0 else i - 1, j))

    def shift(x, by):
        return send(x, lambda i, j: (i + by, j))

    def far(x):
        return send(x, lambda i, j: (i - 1 if i % 2 == 0 else i + 1, j))

    def beside_y(x):
        left = send(x, lambda i, j: (i, j + 1))
        if size_y == 2:
            return left, left
        return left, send(x, lambda i, j: (i, j - 1))

    return mate, far, shift, beside_y


def body(iterate, source, conduct):
    nz, nx, ny = iterate.shape
    if nz != ZS * 4 or ny != LANES or nx != 3 * SUB or lax.axis_size("gx") % 2:
        raise ValueError("shapes")
    mate, far, shift, beside_y = moves()
    u, s, c = (x.reshape(nz * nx, ny) for x in (iterate, source, conduct))
    q, f1, last, one, two, r, own = pack(u, s, c, nz, nx)
    ql, qr = beside_y(q)
    rf1 = mate(f1)
    before = shift(last, 1)
    b1, b2, strips, kept = join(q, ql, qr, rf1, own, nz, nx)
    rb2 = far(b2)
    rb1 = mate(b1)
    one, two, strips = lax.optimization_barrier((one, two, strips))
    after = shift(one, -1), shift(two, -1)
    begun = begin(strips, u, c, r, nz, nx)
    m = faces(own, kept, rb2, rb1, begun[0], nz, nx)
    rm = mate(m)
    passed = fine(strips, rb2, rb1, *after, before, u, c, begun, nz, nx)
    return finish(passed, begun[1], begun[2], m, rm, nz, nx).reshape(nz, nx, ny)


def solution(mesh):
    spec = P(None, "gx", "gy")
    return jax.shard_map(body, mesh=mesh, in_specs=(spec,) * 3, out_specs=spec, check_vma=False)
```

```python
import functools

import jax
import jax.numpy as jnp
from jax import lax
from jax.experimental import pallas as pl
from jax.experimental.pallas import tpu as pltpu
from jax.sharding import PartitionSpec as P

SWEEPS = 3
COARSE_SWEEPS = 4
COARSEN = 8

SHIFT = 0.1
LMIN = 0.3
LMAX = 2.0
OMEGA = 0.8

THETA = (LMAX + LMIN) / 2.0
DELTA = (LMAX - LMIN) / 2.0
SIGMA = THETA / DELTA

RIM = SWEEPS + 1
SUB = 8
LANES = 128
HALF = LANES // 2
GROUP = 4 * RIM
ZS = LANES // GROUP
WIDTH = LANES // COARSEN
SPREAD = 2 * WIDTH
REACH = (COARSE_SWEEPS - 1) * COARSEN
CELLS = COARSEN**3

f32 = jnp.float32
VMEM = pl.BlockSpec(memory_space=pltpu.VMEM)
SMALL = pltpu.CompilerParams(vmem_limit_bytes=12 * 1024 * 1024)


def steps():
    rho, listed = 1.0 / SIGMA, []
    for _ in range(SWEEPS):
        nxt = 1.0 / (2.0 * SIGMA - rho)
        listed.append((nxt * rho, 2.0 * nxt / DELTA))
        rho = nxt
    return listed


def iota(shape, dim):
    return lax.broadcasted_iota(jnp.int32, shape, dim)


def part(index, size):
    return lax.shift_right_logical(index, size.bit_length() - 1), lax.bitwise_and(index, size - 1)


def rolled(x, by, dim):
    return pltpu.roll(x, by % x.shape[dim], dim)


def is_even():
    return lax.axis_index("gx") % 2 == 0


def tiles(count):
    return jax.ShapeDtypeStruct((count * SUB, LANES), f32)


def tile(ref, index):
    return ref[index * SUB : (index + 1) * SUB]


def picked(ref, start, stride):
    return ref[pl.ds(start, SUB, stride=stride), :]


def gathered(rows, source):
    parts = [jnp.take_along_axis(rows, source + k, axis=1) for k in range(COARSEN)]
    while len(parts) > 1:
        parts = [a + b for a, b in zip(parts[::2], parts[1::2])]
    return parts[0]


def compact(rows, place):
    plane, column = part(iota(rows.shape, 1), SPREAD)
    column = column - RIM
    source = jnp.clip(column * COARSEN, 0, LANES - COARSEN)
    here = (plane == place) & (column >= 0) & (column < WIDTH)
    return jnp.where(here, gathered(rows, source), 0.0)


def block_rows(values):
    sub = iota((SUB, LANES), 0)
    out = jnp.zeros((SUB, LANES), f32)
    for block in range(values.shape[0] // COARSEN):
        part = values[block * COARSEN : (block + 1) * COARSEN]
        out = jnp.where(sub == block, jnp.sum(part, axis=0, keepdims=True), out)
    return out


def all_rows(values):
    return jnp.sum(values, axis=0, keepdims=True)


def pack_kernel(
    u_hbm, s_hbm, c_hbm, q_ref, f1_ref, last_ref, one_ref, two_ref, r_ref, own_ref, u_ref, s_ref, c_ref, sums_ref, sems, *, nz, nx
):
    pieces = sems.shape[1]
    size = nz * nx // pieces
    copies = []
    for k, (source, target) in enumerate(((c_hbm, c_ref), (u_hbm, u_ref), (s_hbm, s_ref))):
        for piece in range(pieces):
            at = pl.ds(piece * size, size)
            copies.append(pltpu.make_async_copy(source.at[at], target.at[at], sems.at[k, piece]))
    for copy in copies:
        copy.start()
    for copy in copies[: 2 * pieces]:
        copy.wait()

    even = is_even()
    sub, lane = iota((SUB, LANES), 0), iota((SUB, LANES), 1)
    low = sub < RIM
    row, wide = iota((nx, LANES), 0), iota((nx, LANES), 1)
    slot, spot = part(wide, 2 * RIM)

    def plane(ref, z):
        return ref[z % nz * nx : (z % nz + 1) * nx]

    def up(z):
        return 0.5 * (plane(c_ref, z) + plane(c_ref, z + 1)) * (plane(u_ref, z) - plane(u_ref, z + 1))

    for z in range(nz):
        u, c = plane(u_ref, z), plane(c_ref, z)
        fy = 0.5 * (c + rolled(c, -1, 1)) * (u - rolled(u, -1, 1))
        r_ref[z * nx : (z + 1) * nx] = jnp.where(wide == LANES - 1, 0.0, fy)
    for copy in copies[2 * pieces :]:
        copy.wait()
    below = up(nz - 1)
    for Z in range(nz // COARSEN):
        sum_r = sum_c = jnp.zeros((nx, LANES), f32)
        for z in range(Z * COARSEN, (Z + 1) * COARSEN):
            u, c = plane(u_ref, z), plane(c_ref, z)
            above = up(z)
            fx = 0.5 * (c + rolled(c, -1, 0)) * (u - rolled(u, -1, 0))
            fy = plane(r_ref, z)
            fx = jnp.where(row == nx - 1, 0.0, fx)
            r = plane(s_ref, z) - SHIFT * u - (fx - rolled(fx, 1, 0)) - (fy - rolled(fy, 1, 1)) - (above - below)
            below = above
            r_ref[z * nx : (z + 1) * nx] = r
            sum_r = sum_r + r
            sum_c = sum_c + c
            u0, u2, c0, c2 = u[:SUB], u[nx - SUB :], c[:SUB], c[nx - SUB :]
            first = jnp.where(low, c0, jnp.where(sub == SUB - 1, rolled(u0, -1, 0), rolled(r[:SUB], RIM, 0)))
            last = jnp.where(low, jnp.where(sub == 0, rolled(u2, 1, 0), rolled(r[nx - SUB :], RIM, 0)), c2)
            last_ref[z * SUB : (z + 1) * SUB] = last
            to = z % (nz // 2) * SUB
            (one_ref if z < nz // 2 else two_ref)[to : to + SUB] = first
        sums_ref[Z * nx : (Z + 1) * nx] = sum_r
        sums_ref[(Z + nz // COARSEN) * nx : (Z + nz // COARSEN + 1) * nx] = sum_c

    zs = nz // ZS
    half = zs // 2
    def strips():
        for zi in range(zs):
            strip = jnp.zeros((nx, LANES), f32)
            for g in range(ZS):
                z, at = g * zs + zi, g * GROUP + RIM
                outer = jnp.where(spot < 2, rolled(plane(u_ref, z), at + RIM + 1, 1), rolled(plane(r_ref, z), at + 2 * RIM + 1, 1))
                strip = jnp.where(slot == 2 * g + 1, outer, strip)
                strip = jnp.where(slot == 2 * g, rolled(plane(c_ref, z), at, 1), strip)
            q_ref[zi * nx : (zi + 1) * nx] = strip

    def finish():
        coarse = jnp.zeros((SUB, LANES), f32)
        planes = nz // COARSEN
        for Z in range(planes):
            sum_r, sum_c = (sums_ref[(Z + k * planes) * nx : (Z + k * planes + 1) * nx] for k in range(2))
            coarse = coarse + compact(block_rows(sum_r) + rolled(block_rows(sum_c), RIM, 0), Z)
        coarse = coarse * (1.0 / CELLS)
        strips()

        base = zs * nx + SUB
        for a, ref in enumerate((u_ref, c_ref)):
            for Z in range(nz // SUB):
                at = Z * SUB * nx
                first, last = picked(ref, at, nx), picked(ref, at + nx - 1, nx)
                to = a * nz + Z * SUB
                own_ref[to : to + SUB] = first
                own_ref[2 * nz + to : 2 * nz + to + SUB] = last
                f1_ref[to : to + SUB] = jnp.where(even, last, first)
                q_ref[base + to : base + to + SUB] = jnp.where(
                    lane < HALF, rolled(first, REACH, 1), rolled(last, REACH + HALF, 1)
                )
        q_ref[base + 2 * nz : base + 2 * nz + SUB] = coarse
        f1_ref[2 * nz :] = coarse
        corners = jnp.zeros((SUB, LANES), f32)
        group = part(lane, GROUP)[0]
        for Z in range(nz // SUB):
            at = Z * SUB * nx
            first, last = picked(u_ref, at, nx), picked(u_ref, at + nx - 1, nx)
            both = jnp.where(low, first, rolled(last, RIM, 0)), jnp.where(low, rolled(first, RIM, 0), last)
            for second in range(2):
                g = 2 * Z + second
                corners = jnp.where(group == g, rolled(both[second], g * GROUP + RIM, 1), corners)
        q_ref[zs * nx : base] = corners

    finish()


def pack(u, s, c, nz, nx):
    pieces = 1
    return pl.pallas_call(
        functools.partial(pack_kernel, nz=nz, nx=nx),
        out_shape=(
            tiles(nz // ZS * nx // SUB + 2 * nz // SUB + 2),
            tiles(2 * nz // SUB + 1),
            tiles(nz),
            tiles(nz // 2),
            tiles(nz // 2),
            jax.ShapeDtypeStruct(u.shape, f32),
            tiles(4 * nz // SUB),
        ),
        in_specs=[pl.BlockSpec(memory_space=pltpu.HBM)] * 3,
        out_specs=(VMEM,) * 7,
        scratch_shapes=[pltpu.VMEM(u.shape, f32)] * 3
        + [pltpu.VMEM((2 * nz // COARSEN * nx, LANES), f32), pltpu.SemaphoreType.DMA((3, pieces))],
        compiler_params=SMALL,
        name="pack",
    )(*(pltpu.with_memory_space_constraint(x, pltpu.HBM) for x in (u, s, c)))


def facing(own_ref, a, z, nz, last):
    first, second = own_ref[a * nz + z : a * nz + z + SUB], own_ref[(2 + a) * nz + z : (2 + a) * nz + z + SUB]
    return jnp.where(last, second, first)


def join_kernel(q_ref, ql_ref, qr_ref, f1_ref, own_ref, b1_ref, b2_ref, strip_ref, kept_ref, *, nz, nx):
    zs = nz // ZS
    half = zs // 2
    even = is_even()
    sub, lane = iota((SUB, LANES), 0), iota((SUB, LANES), 1)
    low = sub < RIM
    spot = part(iota((nx, LANES), 1), GROUP)[1]
    thin, row = part(lane, GROUP)[1], iota((nx, LANES), 0)

    def before(spot, left, own, right):
        moved = rolled(jnp.where(spot < RIM, own, right), 2 * RIM, 1)
        return jnp.where(spot < 2 * RIM, jnp.where(spot < RIM, left, own), moved)

    def behind(spot, left, own, right):
        lower, at = spot < 2 * RIM, 2 * RIM
        split = spot < at + 2 + SWEEPS
        residual = jnp.where(
            lower,
            rolled(jnp.where(split, left, own), -(at + 1), 1),
            rolled(jnp.where(split, own, right), -1, 1),
        )
        split = spot == at
        u = jnp.where(
            lower,
            rolled(jnp.where(split, left, own), RIM - 1 - at, 1),
            rolled(jnp.where(split, own, right), RIM - 1, 1),
        )
        return residual, u

    at = slice(zs * nx, zs * nx + SUB)
    corners = before(thin, ql_ref[at], q_ref[at], qr_ref[at])
    joined = [], [], []
    for zi in range(zs):
        at = slice(zi * nx, (zi + 1) * nx)
        parts = ql_ref[at], q_ref[at], qr_ref[at]
        residual, u = behind(spot, *parts)
        u = jnp.where(row == 0, corners[zi : zi + 1], u)
        u = jnp.where(row == nx - 1, corners[RIM + zi : RIM + zi + 1], u)
        for group, strip in zip(joined, (u, before(spot, *parts), residual)):
            group.append(strip)
    for a, group in enumerate(joined):
        for zi in range(zs):
            strip_ref[(a * zs + zi) * nx : (a * zs + zi + 1) * nx] = group[zi]
        for pair in range(half):
            one, two = group[pair], group[pair + half]
            first = jnp.where(low, one[:SUB], rolled(two[:SUB], RIM, 0))
            last = jnp.where(low, rolled(two[nx - SUB :], RIM, 0), one[nx - SUB :])
            to = slice((a * half + pair) * SUB, (a * half + pair + 1) * SUB)
            b1_ref[to] = jnp.where(even, last, first)
            b2_ref[to] = jnp.where(even, first, last)

    source, target = zs * nx + SUB, 3 * half * SUB
    lower, outer = lane < HALF, part(lane, HALF)[1] < REACH
    for Z in range(nz // SUB):
        u, c = (
            jnp.where(outer, ql_ref[at : at + SUB], qr_ref[at : at + SUB])
            for at in (source + Z * SUB, source + nz + Z * SUB)
        )
        kept_ref[Z * SUB : (Z + 1) * SUB] = u
        kept_ref[nz + Z * SUB : nz + (Z + 1) * SUB] = c
        first, last = jnp.where(lower, u, rolled(c, HALF, 1)), jnp.where(lower, rolled(u, HALF, 1), c)
        to = slice(target + Z * SUB, target + (Z + 1) * SUB)
        b1_ref[to] = jnp.where(even, last, first)
        b2_ref[to] = jnp.where(even, first, last)

    at = slice(source + 2 * nz, source + 2 * nz + SUB)
    place = part(lane, SPREAD)[1]
    window = jnp.where(
        place < RIM,
        rolled(ql_ref[at], -WIDTH, 1),
        jnp.where(place < RIM + WIDTH, q_ref[at], rolled(qr_ref[at], WIDTH, 1)),
    )
    flux = jnp.zeros((nx, LANES), f32)
    for u, c in zip(joined[0], joined[1]):
        flux = flux + (c + rolled(c, -1, 1)) * (u - rolled(u, -1, 1))
    flux = block_rows((0.5 / CELLS) * flux)
    plane = part(lane, SPREAD)[0] * SPREAD
    at_left, after = (place == RIM - 1) | (place == RIM), (place == RIM) | (place == RIM + WIDTH)
    at_face = at_left | (place == RIM + WIDTH - 1) | (place == RIM + WIDTH)
    face = plane + jnp.where(at_left, RIM - 1, 3 * RIM - 1)
    flux = jnp.take_along_axis(flux, face, axis=1) + jnp.take_along_axis(flux, face + GROUP, axis=1)
    change = jnp.where(at_face, jnp.where(after, flux, -flux), 0.0)
    rows = nx // COARSEN
    nearest = jnp.where(even, rows - 1, 0)
    for Z in range(nz // COARSEN):
        u, c = facing(own_ref, 0, Z * SUB, nz, even) - tile(f1_ref, Z), facing(own_ref, 1, Z * SUB, nz, even)
        across = all_rows((0.5 / CELLS) * (c + tile(f1_ref, nz // SUB + Z)) * u)
        change = change - compact(jnp.where(sub == nearest, across, 0.0), Z)
    mate = f1_ref[2 * nz : 2 * nz + SUB]
    mate = jnp.where(even, rolled(mate, rows - RIM, 0), rolled(mate, 1 - RIM, 0))
    cond = jnp.where(sub == rows, mate, rolled(window, -RIM, 0))
    coarse = jnp.where(sub < RIM, window + change, rolled(cond, RIM, 0))
    kept_ref[2 * nz :] = coarse
    to = target + nz
    b1_ref[to:] = coarse
    b2_ref[to : to + SUB] = coarse
    to = to + SUB
    for a in range(2):
        for Z in range(nz // SUB):
            at = to + a * nz + Z * SUB
            b2_ref[at : at + SUB] = facing(own_ref, a, Z * SUB, nz, jnp.logical_not(even))


def join(q, ql, qr, f1, own, nz, nx):
    zs = nz // ZS
    size = 3 * (zs // 2) + nz // SUB + 1
    return pl.pallas_call(
        functools.partial(join_kernel, nz=nz, nx=nx),
        out_shape=(
            tiles(size),
            tiles(size + 2 * nz // SUB),
            jax.ShapeDtypeStruct((3 * zs * nx, LANES), f32),
            tiles(2 * nz // SUB + 1),
        ),
        in_specs=[VMEM] * 5,
        out_specs=(VMEM,) * 4,
        compiler_params=SMALL,
        name="join",
    )(q, ql, qr, f1, own)


def faces_kernel(own_ref, kept_ref, r2_ref, r1_ref, after_ref, o_ref, *, nz, nx):
    del after_ref
    half = nz // ZS // 2
    even = is_even()
    sub, lane = iota((SUB, LANES), 0), iota((SUB, LANES), 1)
    plane, place = part(lane, SPREAD)
    rows = nx // COARSEN
    base = 3 * half * SUB

    outer = REACH // COARSEN
    is_left, is_right = (place >= RIM - outer) & (place < RIM), (place >= RIM + WIDTH) & (place < RIM + WIDTH + outer)
    is_own = (place >= RIM) & (place < RIM + WIDTH)
    source = jnp.where(is_left, place - (RIM - outer), place - (RIM + WIDTH - outer))
    source = jnp.where(sub == 0, place - RIM, source) * COARSEN
    source = jnp.clip(source, 0, LANES - COARSEN)
    valid = ((sub == 0) & is_own) | ((sub > 0) & (is_left | is_right))

    def outside(r_ref, Z, upper):
        def mine(at):
            tile_at = kept_ref[at + Z * SUB : at + (Z + 1) * SUB]
            return jnp.where(upper, rolled(tile_at, HALF, 1), tile_at)

        other = r_ref[base + Z * SUB : base + (Z + 1) * SUB]
        return all_rows(0.5 * (mine(nz) + rolled(other, HALF, 1)) * (mine(0) - other))

    odd = jnp.logical_not(even)
    far_rows = base + nz + SUB
    flux = jnp.zeros((SUB, LANES), f32)
    for Z in range(nz // COARSEN):
        u, c = (
            (facing(own_ref, a, Z * SUB, nz, odd), r2_ref[at : at + SUB])
            for a, at in ((0, far_rows + Z * SUB), (1, far_rows + nz + Z * SUB))
        )
        one = all_rows(0.5 * (c[0] + c[1]) * (u[0] - u[1]))
        two = outside(r2_ref, Z, odd)
        three = outside(r1_ref, Z, even)
        sums = jnp.where(sub == 0, one, jnp.where(sub == 1, two, jnp.where(sub == 2, three, 0.0)))
        here = valid & (plane == Z)
        flux = flux + jnp.where(here, gathered(sums, source), 0.0)
    flux = flux * (1.0 / CELLS)
    far, mate = flux[0:1] + flux[1:2], flux[2:3]

    def stacked(own, other):
        before, after = jnp.where(even, other, own), jnp.where(even, own, other)
        return jnp.where(sub <= rows, rolled(before, 1, 0), rolled(after, rows + 1, 0))

    at = base + nz
    coarse, near_c, far_c = kept_ref[2 * nz :], r1_ref[at : at + SUB], r2_ref[at : at + SUB]
    rhs = stacked(coarse, far_c)
    sign = jnp.where(even, 1.0, -1.0)
    rhs = rhs + jnp.where(sub == rows, sign * far, jnp.where(sub == rows + 1, -sign * far, 0.0))
    rhs = rhs - jnp.where(sub == jnp.where(even, 2 * rows, 1), mate, 0.0)
    coarse, near_c, far_c = (rolled(x, -RIM, 0) for x in (coarse, near_c, far_c))
    cond = stacked(coarse, far_c)
    before = jnp.where(even, rolled(far_c, -rows, 0), rolled(near_c, 1 - rows, 0))
    after = jnp.where(even, rolled(near_c, 2 * rows + 1, 0), rolled(far_c, rows + 1, 0))
    cond = jnp.where(sub == 0, before, jnp.where(sub == 2 * rows + 1, after, cond))
    around = rolled(cond, -1, 0) + rolled(cond, 1, 0) + rolled(cond, -1, 1) + rolled(cond, 1, 1)
    around = around + rolled(cond, -SPREAD, 1) + rolled(cond, SPREAD, 1)
    weight = OMEGA / (SHIFT + (0.5 / COARSEN**2) * (6.0 * cond + around))
    o_ref[0:SUB] = weight * rhs
    o_ref[SUB : 2 * SUB] = weight
    o_ref[2 * SUB :] = cond


def faces(own, kept, r2, r1, after, nz, nx):
    return pl.pallas_call(
        functools.partial(faces_kernel, nz=nz, nx=nx),
        out_shape=tiles(3),
        in_specs=[VMEM] * 4 + [pl.BlockSpec(memory_space=pl.ANY)],
        out_specs=VMEM,
        compiler_params=SMALL,
        name="faces",
    )(own, kept, r2, r1, after)


def sides(even, one, two):
    return jnp.where(even, one, two), jnp.where(even, two, one)


def rim_of(low, after, before):
    return jnp.where(low, after, before), rolled(jnp.where(low, before, after), RIM, 0)


def rims_of(low, one_ref, two_ref, last_ref, nz):
    half = nz // 2
    for z in range(nz):
        yield rim_of(low, tile(one_ref if z < half else two_ref, z % half), tile(last_ref, z))


def rim_faces(sub, face, rim_face, u_first, u_last, rim):
    u_rim = jnp.where(sub == 0, rolled(rim, 1 - RIM, 0), rolled(rim, RIM - 1, 0))
    end = sub == SUB - 1
    after = jnp.where(end, face * (u_last - rolled(u_rim, -1, 0)), 0.0)
    before = jnp.where(end, rim_face * (u_rim - rolled(u_first, -1, 0)), 0.0)
    return after, before


def beside(w, z, zs, column):
    return rolled(w, -column - z // zs * GROUP, 1)


def window(spot, left, right, column):
    return jnp.where(spot == RIM - 1, left, rolled(right, RIM - 2 - column, 1))


def begin_kernel(
    strip_ref, u_ref, c_ref, r_ref, cx_ref, cy_ref, cz_ref, diag_ref, inv_ref, q_ref, v_ref, *, nz, nx
):
    zs = nz // ZS
    spot = part(iota((nx, LANES), 1), GROUP)[1]
    row, lane = iota((nx, LANES), 0), iota((nx, LANES), 1)
    first_lane, last_lane = lane == 0, lane == LANES - 1

    def strip(a, zi):
        return strip_ref[(a * zs + zi) * nx : (a * zs + zi + 1) * nx]

    edge_c, edge_f = [], []
    for zi in range(zs):
        u, c = strip(0, zi), strip(1, zi)
        flux = 0.5 * (c + rolled(c, -1, 1)) * (u - rolled(u, -1, 1))
        edge_c.append(window(spot, c, c, 3 * RIM))
        edge_f.append(window(spot, flux, flux, 3 * RIM - 1))

    def own(ref, z):
        return ref[z % nz * nx : (z % nz + 1) * nx]

    below = 0.5 * (own(c_ref, -1) + own(c_ref, 0))
    for z in range(nz):
        at = slice(z * nx, (z + 1) * nx)
        c = own(c_ref, z)
        gx = jnp.where(row == nx - 1, 0.0, 0.5 * (c + rolled(c, -1, 0)))
        edge = beside(edge_c[z % zs], z, zs, RIM - 1)
        gy = 0.5 * (c + jnp.where(last_lane, edge, rolled(c, -1, 1)))
        gyl = 0.5 * (c + jnp.where(first_lane, edge, rolled(c, 1, 1)))
        above = 0.5 * (c + own(c_ref, z + 1))
        diag = SHIFT + (gx + rolled(gx, 1, 0)) + (gy + gyl) + (above + below)
        edge = beside(edge_f[z % zs], z, zs, RIM - 1)
        r = own(r_ref, z) + jnp.where(first_lane, edge, jnp.where(last_lane, -edge, 0.0))
        inner = slice(SUB, nx - SUB)
        inverse = 1.0 / diag[inner]
        scaled = r[inner] * inverse
        cx_ref[at] = gx
        cy_ref[at] = gy
        cz_ref[at] = above
        diag_ref[at] = diag
        q_ref[at] = jnp.concatenate([r[:SUB], scaled, r[nx - SUB :]], axis=0)
        to = slice(z * (nx - 2 * SUB), (z + 1) * (nx - 2 * SUB))
        inv_ref[to] = inverse
        v_ref[to] = scaled * (1.0 / THETA)
        below = above


def begin(strips, u, c, r, nz, nx):
    inner = jax.ShapeDtypeStruct((nz * (nx - 2 * SUB), LANES), f32)
    return pl.pallas_call(
        functools.partial(begin_kernel, nz=nz, nx=nx),
        out_shape=(jax.ShapeDtypeStruct(u.shape, f32),) * 4 + (inner, jax.ShapeDtypeStruct(u.shape, f32), inner),
        in_specs=[VMEM] * 4,
        out_specs=(VMEM,) * 7,
        compiler_params=SMALL,
        cost_estimate=pl.CostEstimate(flops=40 * u.size, bytes_accessed=40 * u.size, transcendentals=0),
        name="begin",
    )(strips, u, c, r)


def fine_kernel(
    strip_ref, b2_ref, b1_ref, one_ref, two_ref, last_ref, u_ref, c_ref, cx_ref, cy_ref, cz_ref, diag_ref, inv_ref, q_ref, v_ref,
    cx, inv, q, va, acc, w2,
    ch, cyh, czh, vb, wr, w0, w1,
    *, nz, nx,
):
    zs = nz // ZS
    half = zs // 2
    ext = nx + SUB
    even = is_even()
    sub = iota((SUB, LANES), 0)
    low, end = sub < RIM, sub == SUB - 1
    table = steps()

    rims = []
    for z, (cond, rim) in enumerate(rims_of(low, one_ref, two_ref, last_ref, nz)):
        ch[z * SUB : (z + 1) * SUB] = cond
        rims.append(rim)

    row, spot = iota((ext, LANES), 0), part(iota((ext, LANES), 1), GROUP)[1]

    def strips_of(a):
        ends = [None] * zs
        for pair in range(half):
            index = a * half + pair
            ends[pair], ends[pair + half] = rim_of(low, *sides(even, tile(b1_ref, index), tile(b2_ref, index)))
        return [
            jnp.concatenate([strip_ref[(a * zs + zi) * nx : (a * zs + zi + 1) * nx], ends[zi]], axis=0)
            for zi in range(zs)
        ]

    def z_up(x):
        return x[1:] + [rolled(x[0], -GROUP, 1)]

    def z_down(x):
        return [rolled(x[-1], GROUP, 1)] + x[:-1]

    us, cs, rs = strips_of(0), strips_of(1), strips_of(2)
    cxs = [0.5 * (c + rolled(c, -1, 0)) for c in cs]
    cys = [0.5 * (c + rolled(c, -1, 1)) for c in cs]
    czs = [0.5 * (c + d) for c, d in zip(cs, z_up(cs))]
    czds = z_down(czs)
    invs, qs, vs = [], [], []
    for zi in range(zs):
        u = us[zi]
        fx = jnp.where((row == nx - 1) | (row == ext - 1), cxs[zi] * (u - rolled(u, -1, 0)), 0.0)
        fy = jnp.where((spot == RIM - 1) | (spot == 3 * RIM - 1), cys[zi] * (u - rolled(u, -1, 1)), 0.0)
        r = rs[zi] - (fx - rolled(fx, 1, 0)) - (fy - rolled(fy, 1, 1))
        wr[zi * SUB : (zi + 1) * SUB] = jnp.where(spot == RIM, r, rolled(r, -2 * RIM, 1))[nx:]
        diag = SHIFT + (cxs[zi] + rolled(cxs[zi], 1, 0)) + (cys[zi] + rolled(cys[zi], 1, 1)) + (czs[zi] + czds[zi])
        invs.append(1.0 / diag)
        qs.append(r * invs[zi])
        vs.append(qs[zi] * (1.0 / THETA))
    for k, w in enumerate((w0, w1, w2)):
        prod = [cys[zi] * vs[zi] for zi in range(zs)]
        for zi in range(zs):
            w[zi * ext : (zi + 1) * ext] = window(spot, prod[zi], vs[zi], 3 * RIM)
        if k == SWEEPS - 1:
            break
        keep, lift = table[k]
        v_up, v_down = z_up(vs), z_down(vs)
        fresh = []
        for zi in range(zs):
            v = vs[zi]
            near = cxs[zi] * rolled(v, -1, 0) + rolled(cxs[zi] * v, 1, 0)
            near = near + cys[zi] * rolled(v, -1, 1) + rolled(prod[zi], 1, 1)
            near = near + czs[zi] * v_up[zi] + czds[zi] * v_down[zi]
            qs[zi] = qs[zi] - v + near * invs[zi]
            fresh.append(keep * v + lift * qs[zi])
        vs = fresh
    edge_c = [window(spot, c, c, 3 * RIM)[nx:] for c in cs]

    lane = iota((SUB, LANES), 1)
    first_lane, last_lane = lane == 0, lane == LANES - 1

    def own(ref, z):
        return ref[z % nz * nx : (z % nz + 1) * nx]

    def rim_at(ref, z):
        return tile(ref, z % nz)

    below = 0.5 * (rim_at(ch, -1) + rim_at(ch, 0))
    for z in range(nz):
        at = slice(z * SUB, (z + 1) * SUB)
        u, c = own(u_ref, z), tile(ch, z)
        c_first, c_last = own(c_ref, z)[:SUB], own(c_ref, z)[nx - SUB :]
        zi = z % zs
        face = jnp.where(end, 0.5 * (c_last + rolled(c, -1, 0)), 0.0)
        gx = 0.5 * (c + jnp.where(end, rolled(c_first, -1, 0), rolled(c, -1, 0)))
        gxl = rolled(gx, 1, 0)
        edge = beside(edge_c[zi], z, zs, RIM - 1)
        gy = 0.5 * (c + jnp.where(last_lane, edge, rolled(c, -1, 1)))
        gyl = 0.5 * (c + jnp.where(first_lane, edge, rolled(c, 1, 1)))
        above = 0.5 * (c + rim_at(ch, z + 1))
        diag = SHIFT + (gx + jnp.where(sub == 0, rolled(face, 1, 0), gxl)) + (gy + gyl) + (above + below)
        after, before = rim_faces(sub, face, gx, u[:SUB], u[nx - SUB :], rims[z])
        r = rims[z] + rolled(after, 1, 0) - before
        r = jnp.where(first_lane | last_lane, beside(wr[zi * SUB : (zi + 1) * SUB], z, zs, RIM), r)
        own_diag, own_q = own(diag_ref, z), own(q_ref, z)
        long_at = slice(z * ext, (z + 1) * ext)
        parts = []
        for this_diag, this_r in (
            (own_diag[:SUB] + jnp.where(sub == 0, gxl, 0.0), own_q[:SUB] + rolled(before, 1, 0)),
            (own_diag[nx - SUB :] + face, own_q[nx - SUB :] - after),
            (diag, r),
        ):
            inverse = 1.0 / this_diag
            scaled = this_r * inverse
            parts.append((inverse, scaled, scaled * (1.0 / THETA)))
        inner = slice(z * (nx - 2 * SUB), (z + 1) * (nx - 2 * SUB))
        middle = (inv_ref[inner], own_q[SUB : nx - SUB], v_ref[inner])
        for ref, one, two, three, four in zip((inv, q, va), parts[0], middle, parts[1], parts[2]):
            ref[long_at] = jnp.concatenate([one, two, three, four], axis=0)
        own_cx = own(cx_ref, z)
        cx[long_at] = jnp.concatenate([own_cx[: nx - SUB], own_cx[nx - SUB :] + face, gx], axis=0)
        cyh[at] = gy
        czh[at] = above
        below = above

    lane = iota((ext, LANES), 1)
    first_lane, last_lane = lane == 0, lane == LANES - 1

    def whole(ref, rim, z):
        return jnp.concatenate([own(ref, z), rim_at(rim, z)], axis=0)

    def long(ref, z):
        return ref[z % nz * ext : (z % nz + 1) * ext]

    for k, w in enumerate((w0, w1)):
        old, new = (va, vb) if k % 2 == 0 else (vb, va)
        keep, lift = table[k]
        for z in range(nz):
            at, here = slice(z * ext, (z + 1) * ext), slice(z * nx, (z + 1) * nx)
            zi = z % zs
            v, gx, gy = old[at], cx[at], whole(cy_ref, cyh, z)
            edge = beside(w[zi * ext : (zi + 1) * ext], z, zs, RIM - 1)
            near = gx * rolled(v, -1, 0) + rolled(gx * v, 1, 0)
            near = near + gy * jnp.where(last_lane, edge, rolled(v, -1, 1))
            near = near + jnp.where(first_lane, edge, rolled(gy * v, 1, 1))
            near = near + whole(cz_ref, czh, z) * long(old, z + 1) + whole(cz_ref, czh, z - 1) * long(old, z - 1)
            scaled = q[at] - v + near * inv[at]
            fresh = keep * v + lift * scaled
            q[at] = scaled
            new[at] = fresh
            acc[here] = (own(u_ref, z) + v[:nx] if k == 0 else acc[here]) + fresh[:nx]


def fine(strips, b2, b1, one, two, last, u, c, begun, nz, nx):
    zs = nz // ZS
    ext = nx + SUB
    rim = pltpu.VMEM((nz * SUB, LANES), f32)
    full = jax.ShapeDtypeStruct((nz * ext, LANES), f32)
    strip = pltpu.VMEM((zs * ext, LANES), f32)
    return pl.pallas_call(
        functools.partial(fine_kernel, nz=nz, nx=nx),
        out_shape=(full,) * 4 + (jax.ShapeDtypeStruct(u.shape, f32), jax.ShapeDtypeStruct((zs * ext, LANES), f32)),
        in_specs=[VMEM] * 15,
        out_specs=(VMEM,) * 6,
        scratch_shapes=[rim] * 3 + [pltpu.VMEM((nz * ext, LANES), f32), pltpu.VMEM((zs * SUB, LANES), f32)] + [strip] * 2,
        compiler_params=SMALL,
        cost_estimate=pl.CostEstimate(flops=100 * u.size, bytes_accessed=40 * u.size, transcendentals=0),
        name="fine",
    )(strips, b2, b1, one, two, last, u, c, *begun)


def finish_kernel(
    cx_ref, inv_ref, q_ref, v_ref, sum_ref, w_ref, cy_ref, cz_ref, m_ref, r_ref, o_ref, out, sems, *, nz, nx
):
    zs = nz // ZS
    ext = nx + SUB
    rows = nx // COARSEN
    even = is_even()
    sub, lane = iota((SUB, LANES), 0), iota((SUB, LANES), 1)
    beyond = sub == jnp.where(even, 2 * rows + 1, 0)
    fields = []
    for a in range(3):
        mine, mate = tile(m_ref, a), tile(r_ref, a)
        mate = jnp.where(even, rolled(mate, 2 * rows, 0), rolled(mate, -2 * rows, 0))
        fields.append(jnp.concatenate([jnp.where(beyond, mate, mine), mate], axis=0))
    start, weight, cond = fields
    scale = 0.5 / COARSEN**2
    turns = (-1, 0), (1, 0), (-1, 1), (1, 1), (-SPREAD, 1), (SPREAD, 1)
    shares = [scale * (cond + rolled(cond, *turn)) for turn in turns]
    keep = 1.0 - weight * (SHIFT + sum(shares))
    shares = [weight * share for share in shares]
    v = start
    for _ in range(COARSE_SWEEPS - 1):
        terms = [share * rolled(v, *turn) for share, turn in zip(shares, turns)]
        v = (start + keep * v) + ((terms[0] + terms[1]) + (terms[2] + terms[3]) + (terms[4] + terms[5]))
    top = v[:SUB]
    top = jnp.where(even, rolled(top, -rows - 1, 0), rolled(top, -1, 0))

    wide = iota((nx, LANES), 1)
    first_lane, last_lane = wide == 0, wide == LANES - 1
    keep, lift = steps()[-1]

    def own(ref, z):
        return ref[z % nz * nx : (z % nz + 1) * nx]

    def long(ref, z):
        return ref[z % nz * ext : z % nz * ext + nx]

    copies = []
    size = COARSEN * nx
    for Z in range(nz // COARSEN):
        spread = jnp.take_along_axis(top, Z * SPREAD + RIM + part(lane, COARSEN)[0], axis=1)
        value = jnp.concatenate([jnp.broadcast_to(spread[X : X + 1], (COARSEN, LANES)) for X in range(rows)], axis=0)
        for z in range(Z * COARSEN, (Z + 1) * COARSEN):
            at = slice(z * ext, (z + 1) * ext)
            v, gx = v_ref[at], cx_ref[at]
            near = (gx * rolled(v, -1, 0) + rolled(gx * v, 1, 0))[:nx]
            v, gy, zi = v[:nx], own(cy_ref, z), z % zs
            edge = beside(w_ref[zi * ext : zi * ext + nx], z, zs, RIM - 1)
            near = near + gy * jnp.where(last_lane, edge, rolled(v, -1, 1))
            near = near + jnp.where(first_lane, edge, rolled(gy * v, 1, 1))
            near = near + own(cz_ref, z) * long(v_ref, z + 1) + own(cz_ref, z - 1) * long(v_ref, z - 1)
            scaled = long(q_ref, z) - v + near * long(inv_ref, z)
            here = slice(z * nx, (z + 1) * nx)
            out[here] = (own(sum_ref, z) + (keep * v + lift * scaled)) + value
        here = pl.ds(Z * size, size)
        copies.append(pltpu.make_async_copy(out.at[here], o_ref.at[here], sems.at[Z]))
        copies[-1].start()
    for copy in copies:
        copy.wait()


def finish(passed, cy, cz, m, r, nz, nx):
    shape = (nz * nx, LANES)
    return pl.pallas_call(
        functools.partial(finish_kernel, nz=nz, nx=nx),
        out_shape=jax.ShapeDtypeStruct(shape, f32),
        in_specs=[VMEM] * 10,
        out_specs=pl.BlockSpec(memory_space=pltpu.HBM),
        scratch_shapes=[pltpu.VMEM(shape, f32), pltpu.SemaphoreType.DMA((nz // COARSEN,))],
        compiler_params=SMALL,
        name="finish",
    )(*passed, cy, cz, m, r)


def moves():
    size_x, size_y = lax.axis_size("gx"), lax.axis_size("gy")

    def send(x, go):
        pairs = []
        for i in range(size_x):
            for j in range(size_y):
                k, l = go(i, j)
                pairs.append((i * size_y + j, (k % size_x) * size_y + l % size_y))
        return lax.ppermute(x, ("gx", "gy"), pairs)

    def mate(x):
        return send(x, lambda i, j: (i + 1 if i % 2 == 0 else i - 1, j))

    def shift(x, by):
        return send(x, lambda i, j: (i + by, j))

    def far(x):
        return send(x, lambda i, j: (i - 1 if i % 2 == 0 else i + 1, j))

    def beside_y(x):
        left = send(x, lambda i, j: (i, j + 1))
        if size_y == 2:
            return left, left
        return left, send(x, lambda i, j: (i, j - 1))

    return mate, far, shift, beside_y


def body(iterate, source, conduct):
    nz, nx, ny = iterate.shape
    if nz != ZS * 4 or ny != LANES or nx != 3 * SUB or lax.axis_size("gx") % 2:
        raise ValueError("shapes")
    mate, far, shift, beside_y = moves()
    u, s, c = (x.reshape(nz * nx, ny) for x in (iterate, source, conduct))
    q, f1, last, one, two, r, own = pack(u, s, c, nz, nx)
    ql, qr = beside_y(q)
    rf1 = mate(f1)
    before = shift(last, 1)
    b1, b2, strips, kept = join(q, ql, qr, rf1, own, nz, nx)
    rb2 = far(b2)
    rb1 = mate(b1)
    one, two, strips = lax.optimization_barrier((one, two, strips))
    after = shift(one, -1), shift(two, -1)
    begun = begin(strips, u, c, r, nz, nx)
    m = faces(own, kept, rb2, rb1, begun[0], nz, nx)
    rm = mate(m)
    passed = fine(strips, rb2, rb1, *after, before, u, c, begun, nz, nx)
    return finish(passed, begun[1], begun[2], m, rm, nz, nx).reshape(nz, nx, ny)


def solution(mesh):
    spec = P(None, "gx", "gy")
    return jax.shard_map(body, mesh=mesh, in_specs=(spec,) * 3, out_specs=spec, check_vma=False)
```

```python
import functools

import jax
import jax.numpy as jnp
from jax import lax
from jax.experimental import pallas as pl
from jax.experimental.pallas import tpu as pltpu
from jax.sharding import PartitionSpec as P

SWEEPS = 3
COARSE_SWEEPS = 4
COARSEN = 8

SHIFT = 0.1
LMIN = 0.3
LMAX = 2.0
OMEGA = 0.8

THETA = (LMAX + LMIN) / 2.0
DELTA = (LMAX - LMIN) / 2.0
SIGMA = THETA / DELTA

RIM = SWEEPS + 1
SUB = 8
LANES = 128
HALF = LANES // 2
GROUP = 4 * RIM
ZS = LANES // GROUP
WIDTH = LANES // COARSEN
SPREAD = 2 * WIDTH
REACH = (COARSE_SWEEPS - 1) * COARSEN
SPARE = 2 * REACH // WIDTH
CELLS = COARSEN**3

f32 = jnp.float32
VMEM = pl.BlockSpec(memory_space=pltpu.VMEM)
SMALL = pltpu.CompilerParams(vmem_limit_bytes=12 * 1024 * 1024)


def steps():
    rho, listed = 1.0 / SIGMA, []
    for _ in range(SWEEPS):
        nxt = 1.0 / (2.0 * SIGMA - rho)
        listed.append((nxt * rho, 2.0 * nxt / DELTA))
        rho = nxt
    return listed


def iota(shape, dim):
    return lax.broadcasted_iota(jnp.int32, shape, dim)


def part(index, size):
    return lax.shift_right_logical(index, size.bit_length() - 1), lax.bitwise_and(index, size - 1)


def rolled(x, by, dim):
    return pltpu.roll(x, by % x.shape[dim], dim)


def is_even():
    return lax.axis_index("gx") % 2 == 0


def tiles(count):
    return jax.ShapeDtypeStruct((count * SUB, LANES), f32)


def tile(ref, index):
    return ref[index * SUB : (index + 1) * SUB]


def picked(ref, start, stride):
    return ref[pl.ds(start, SUB, stride=stride), :]


def gathered(rows, source):
    parts = [jnp.take_along_axis(rows, source + k, axis=1) for k in range(COARSEN)]
    while len(parts) > 1:
        parts = [a + b for a, b in zip(parts[::2], parts[1::2])]
    return parts[0]


def compact(rows, place):
    plane, column = part(iota(rows.shape, 1), SPREAD)
    column = column - RIM
    source = jnp.clip(column * COARSEN, 0, LANES - COARSEN)
    here = (plane == place) & (column >= 0) & (column < WIDTH)
    return jnp.where(here, gathered(rows, source), 0.0)


def block_rows(values):
    sub = iota((SUB, LANES), 0)
    out = jnp.zeros((SUB, LANES), f32)
    for block in range(values.shape[0] // COARSEN):
        part = values[block * COARSEN : (block + 1) * COARSEN]
        out = jnp.where(sub == block, jnp.sum(part, axis=0, keepdims=True), out)
    return out


def all_rows(values):
    return jnp.sum(values, axis=0, keepdims=True)


def pack_kernel(
    u_hbm, s_hbm, c_hbm, q_ref, f1_ref, last_ref, one_ref, two_ref, r_ref, own_ref, u_ref, s_ref, c_ref, sums_ref, sems, *, nz, nx
):
    pieces = sems.shape[1]
    size = nz * nx // pieces
    copies = []
    for k, (source, target) in enumerate(((c_hbm, c_ref), (u_hbm, u_ref), (s_hbm, s_ref))):
        for piece in range(pieces):
            at = pl.ds(piece * size, size)
            copies.append(pltpu.make_async_copy(source.at[at], target.at[at], sems.at[k, piece]))
    for copy in copies:
        copy.start()
    for copy in copies[: 2 * pieces]:
        copy.wait()

    even = is_even()
    sub, lane = iota((SUB, LANES), 0), iota((SUB, LANES), 1)
    low = sub < RIM
    row, wide = iota((nx, LANES), 0), iota((nx, LANES), 1)
    slot, spot = part(wide, 2 * RIM)

    def plane(ref, z):
        return ref[z % nz * nx : (z % nz + 1) * nx]

    def up(z):
        return 0.5 * (plane(c_ref, z) + plane(c_ref, z + 1)) * (plane(u_ref, z) - plane(u_ref, z + 1))

    for z in range(nz):
        u, c = plane(u_ref, z), plane(c_ref, z)
        fy = 0.5 * (c + rolled(c, -1, 1)) * (u - rolled(u, -1, 1))
        r_ref[z * nx : (z + 1) * nx] = jnp.where(wide == LANES - 1, 0.0, fy)
    for copy in copies[2 * pieces :]:
        copy.wait()
    below = up(nz - 1)
    for Z in range(nz // COARSEN):
        sum_r = sum_c = jnp.zeros((nx, LANES), f32)
        for z in range(Z * COARSEN, (Z + 1) * COARSEN):
            u, c = plane(u_ref, z), plane(c_ref, z)
            above = up(z)
            fx = 0.5 * (c + rolled(c, -1, 0)) * (u - rolled(u, -1, 0))
            fy = plane(r_ref, z)
            fx = jnp.where(row == nx - 1, 0.0, fx)
            r = plane(s_ref, z) - SHIFT * u - (fx - rolled(fx, 1, 0)) - (fy - rolled(fy, 1, 1)) - (above - below)
            below = above
            r_ref[z * nx : (z + 1) * nx] = r
            sum_r = sum_r + r
            sum_c = sum_c + c
            u0, u2, c0, c2 = u[:SUB], u[nx - SUB :], c[:SUB], c[nx - SUB :]
            first = jnp.where(low, c0, jnp.where(sub == SUB - 1, rolled(u0, -1, 0), rolled(r[:SUB], RIM, 0)))
            last = jnp.where(low, jnp.where(sub == 0, rolled(u2, 1, 0), rolled(r[nx - SUB :], RIM, 0)), c2)
            last_ref[z * SUB : (z + 1) * SUB] = last
            to = z % (nz // 2) * SUB
            (one_ref if z < nz // 2 else two_ref)[to : to + SUB] = first
        sums_ref[Z * nx : (Z + 1) * nx] = sum_r
        sums_ref[(Z + nz // COARSEN) * nx : (Z + nz // COARSEN + 1) * nx] = sum_c

    zs = nz // ZS
    half = zs // 2
    def strips():
        for zi in range(zs):
            strip = jnp.zeros((nx, LANES), f32)
            for g in range(ZS):
                z, at = g * zs + zi, g * GROUP + RIM
                outer = jnp.where(spot < 2, rolled(plane(u_ref, z), at + RIM + 1, 1), rolled(plane(r_ref, z), at + 2 * RIM + 1, 1))
                strip = jnp.where(slot == 2 * g + 1, outer, strip)
                strip = jnp.where(slot == 2 * g, rolled(plane(c_ref, z), at, 1), strip)
            q_ref[zi * nx : (zi + 1) * nx] = strip

    def finish():
        coarse = jnp.zeros((SUB, LANES), f32)
        planes = nz // COARSEN
        for Z in range(planes):
            sum_r, sum_c = (sums_ref[(Z + k * planes) * nx : (Z + k * planes + 1) * nx] for k in range(2))
            coarse = coarse + compact(block_rows(sum_r) + rolled(block_rows(sum_c), RIM, 0), Z)
        coarse = coarse * (1.0 / CELLS)
        strips()

        base = zs * nx + SUB
        within = part(lane, HALF)[1]
        for a, ref in enumerate((u_ref, c_ref)):
            outer = []
            for Z in range(nz // SUB):
                at = Z * SUB * nx
                first, last = picked(ref, at, nx), picked(ref, at + nx - 1, nx)
                to = a * nz + Z * SUB
                own_ref[to : to + SUB] = first
                own_ref[2 * nz + to : 2 * nz + to + SUB] = last
                f1_ref[to : to + SUB] = jnp.where(even, last, first)
                outer.append(jnp.where(lane < HALF, rolled(first, REACH, 1), rolled(last, REACH + HALF, 1)))
            kept = outer.pop()
            for k, tile_k in enumerate(outer):
                to = base + (a * SPARE + k) * SUB
                q_ref[to : to + SUB] = jnp.where(within < 2 * REACH, tile_k, rolled(kept, (SPARE - k) * WIDTH, 1))
        q_ref[base + 2 * SPARE * SUB :] = coarse
        f1_ref[2 * nz :] = coarse
        corners = jnp.zeros((SUB, LANES), f32)
        group = part(lane, GROUP)[0]
        for Z in range(nz // SUB):
            at = Z * SUB * nx
            first, last = picked(u_ref, at, nx), picked(u_ref, at + nx - 1, nx)
            both = jnp.where(low, first, rolled(last, RIM, 0)), jnp.where(low, rolled(first, RIM, 0), last)
            for second in range(2):
                g = 2 * Z + second
                corners = jnp.where(group == g, rolled(both[second], g * GROUP + RIM, 1), corners)
        q_ref[zs * nx : base] = corners

    finish()


def pack(u, s, c, nz, nx):
    pieces = 1
    return pl.pallas_call(
        functools.partial(pack_kernel, nz=nz, nx=nx),
        out_shape=(
            tiles(nz // ZS * nx // SUB + 2 * SPARE + 2),
            tiles(2 * nz // SUB + 1),
            tiles(nz),
            tiles(nz // 2),
            tiles(nz // 2),
            jax.ShapeDtypeStruct(u.shape, f32),
            tiles(4 * nz // SUB),
        ),
        in_specs=[pl.BlockSpec(memory_space=pltpu.HBM)] * 3,
        out_specs=(VMEM,) * 7,
        scratch_shapes=[pltpu.VMEM(u.shape, f32)] * 3
        + [pltpu.VMEM((2 * nz // COARSEN * nx, LANES), f32), pltpu.SemaphoreType.DMA((3, pieces))],
        compiler_params=SMALL,
        name="pack",
    )(*(pltpu.with_memory_space_constraint(x, pltpu.HBM) for x in (u, s, c)))


def facing(own_ref, a, z, nz, last):
    first, second = own_ref[a * nz + z : a * nz + z + SUB], own_ref[(2 + a) * nz + z : (2 + a) * nz + z + SUB]
    return jnp.where(last, second, first)


def join_kernel(q_ref, ql_ref, qr_ref, f1_ref, own_ref, b1_ref, b2_ref, strip_ref, kept_ref, *, nz, nx):
    zs = nz // ZS
    half = zs // 2
    even = is_even()
    sub, lane = iota((SUB, LANES), 0), iota((SUB, LANES), 1)
    low = sub < RIM
    spot = part(iota((nx, LANES), 1), GROUP)[1]
    thin, row = part(lane, GROUP)[1], iota((nx, LANES), 0)

    def before(spot, left, own, right):
        moved = rolled(jnp.where(spot < RIM, own, right), 2 * RIM, 1)
        return jnp.where(spot < 2 * RIM, jnp.where(spot < RIM, left, own), moved)

    def behind(spot, left, own, right):
        lower, at = spot < 2 * RIM, 2 * RIM
        split = spot < at + 2 + SWEEPS
        residual = jnp.where(
            lower,
            rolled(jnp.where(split, left, own), -(at + 1), 1),
            rolled(jnp.where(split, own, right), -1, 1),
        )
        split = spot == at
        u = jnp.where(
            lower,
            rolled(jnp.where(split, left, own), RIM - 1 - at, 1),
            rolled(jnp.where(split, own, right), RIM - 1, 1),
        )
        return residual, u

    at = slice(zs * nx, zs * nx + SUB)
    corners = before(thin, ql_ref[at], q_ref[at], qr_ref[at])
    joined = [], [], []
    for zi in range(zs):
        at = slice(zi * nx, (zi + 1) * nx)
        parts = ql_ref[at], q_ref[at], qr_ref[at]
        residual, u = behind(spot, *parts)
        u = jnp.where(row == 0, corners[zi : zi + 1], u)
        u = jnp.where(row == nx - 1, corners[RIM + zi : RIM + zi + 1], u)
        for group, strip in zip(joined, (u, before(spot, *parts), residual)):
            group.append(strip)
    for a, group in enumerate(joined):
        for zi in range(zs):
            strip_ref[(a * zs + zi) * nx : (a * zs + zi + 1) * nx] = group[zi]
        for pair in range(half):
            one, two = group[pair], group[pair + half]
            first = jnp.where(low, one[:SUB], rolled(two[:SUB], RIM, 0))
            last = jnp.where(low, rolled(two[nx - SUB :], RIM, 0), one[nx - SUB :])
            to = slice((a * half + pair) * SUB, (a * half + pair + 1) * SUB)
            b1_ref[to] = jnp.where(even, last, first)
            b2_ref[to] = jnp.where(even, first, last)

    source, target = zs * nx + SUB, 3 * half * SUB
    lower, outer = lane < HALF, part(lane, HALF)[1] < REACH
    within = part(lane, HALF)[1]

    def outer_columns(a, Z):
        def sent(ref, k):
            at = source + (a * SPARE + k) * SUB
            return ref[at : at + SUB]

        if Z < SPARE:
            return jnp.where(outer, sent(ql_ref, Z), sent(qr_ref, Z))
        out = rolled(sent(qr_ref, SPARE - 1), -WIDTH, 1)
        for k in reversed(range(SPARE - 1)):
            for ref, end in ((qr_ref, (k + 1) * WIDTH), (ql_ref, min(REACH, (k + 1) * WIDTH))):
                if (ref is ql_ref or end > REACH) and k * WIDTH < REACH:
                    out = jnp.where(within < end, rolled(sent(ref, k), (k - SPARE) * WIDTH, 1), out)
        return out

    for Z in range(nz // SUB):
        u, c = outer_columns(0, Z), outer_columns(1, Z)
        kept_ref[Z * SUB : (Z + 1) * SUB] = u
        kept_ref[nz + Z * SUB : nz + (Z + 1) * SUB] = c
        first, last = jnp.where(lower, u, rolled(c, HALF, 1)), jnp.where(lower, rolled(u, HALF, 1), c)
        to = slice(target + Z * SUB, target + (Z + 1) * SUB)
        b1_ref[to] = jnp.where(even, last, first)
        b2_ref[to] = jnp.where(even, first, last)

    at = slice(source + 2 * SPARE * SUB, source + (2 * SPARE + 1) * SUB)
    place = part(lane, SPREAD)[1]
    window = jnp.where(
        place < RIM,
        rolled(ql_ref[at], -WIDTH, 1),
        jnp.where(place < RIM + WIDTH, q_ref[at], rolled(qr_ref[at], WIDTH, 1)),
    )
    flux = jnp.zeros((nx, LANES), f32)
    for u, c in zip(joined[0], joined[1]):
        flux = flux + (c + rolled(c, -1, 1)) * (u - rolled(u, -1, 1))
    flux = block_rows((0.5 / CELLS) * flux)
    plane = part(lane, SPREAD)[0] * SPREAD
    at_left, after = (place == RIM - 1) | (place == RIM), (place == RIM) | (place == RIM + WIDTH)
    at_face = at_left | (place == RIM + WIDTH - 1) | (place == RIM + WIDTH)
    face = plane + jnp.where(at_left, RIM - 1, 3 * RIM - 1)
    flux = jnp.take_along_axis(flux, face, axis=1) + jnp.take_along_axis(flux, face + GROUP, axis=1)
    change = jnp.where(at_face, jnp.where(after, flux, -flux), 0.0)
    rows = nx // COARSEN
    nearest = jnp.where(even, rows - 1, 0)
    for Z in range(nz // COARSEN):
        u, c = facing(own_ref, 0, Z * SUB, nz, even) - tile(f1_ref, Z), facing(own_ref, 1, Z * SUB, nz, even)
        across = all_rows((0.5 / CELLS) * (c + tile(f1_ref, nz // SUB + Z)) * u)
        change = change - compact(jnp.where(sub == nearest, across, 0.0), Z)
    mate = f1_ref[2 * nz : 2 * nz + SUB]
    mate = jnp.where(even, rolled(mate, rows - RIM, 0), rolled(mate, 1 - RIM, 0))
    cond = jnp.where(sub == rows, mate, rolled(window, -RIM, 0))
    coarse = jnp.where(sub < RIM, window + change, rolled(cond, RIM, 0))
    kept_ref[2 * nz :] = coarse
    to = target + nz
    b1_ref[to:] = coarse
    b2_ref[to : to + SUB] = coarse
    to = to + SUB
    for a in range(2):
        for Z in range(nz // SUB):
            at = to + a * nz + Z * SUB
            b2_ref[at : at + SUB] = facing(own_ref, a, Z * SUB, nz, jnp.logical_not(even))


def join(q, ql, qr, f1, own, nz, nx):
    zs = nz // ZS
    size = 3 * (zs // 2) + nz // SUB + 1
    return pl.pallas_call(
        functools.partial(join_kernel, nz=nz, nx=nx),
        out_shape=(
            tiles(size),
            tiles(size + 2 * nz // SUB),
            jax.ShapeDtypeStruct((3 * zs * nx, LANES), f32),
            tiles(2 * nz // SUB + 1),
        ),
        in_specs=[VMEM] * 5,
        out_specs=(VMEM,) * 4,
        compiler_params=SMALL,
        name="join",
    )(q, ql, qr, f1, own)


def faces_kernel(own_ref, kept_ref, r2_ref, r1_ref, after_ref, o_ref, *, nz, nx):
    del after_ref
    half = nz // ZS // 2
    even = is_even()
    sub, lane = iota((SUB, LANES), 0), iota((SUB, LANES), 1)
    plane, place = part(lane, SPREAD)
    rows = nx // COARSEN
    base = 3 * half * SUB

    outer = REACH // COARSEN
    is_left, is_right = (place >= RIM - outer) & (place < RIM), (place >= RIM + WIDTH) & (place < RIM + WIDTH + outer)
    is_own = (place >= RIM) & (place < RIM + WIDTH)
    source = jnp.where(is_left, place - (RIM - outer), place - (RIM + WIDTH - outer))
    source = jnp.where(sub == 0, place - RIM, source) * COARSEN
    source = jnp.clip(source, 0, LANES - COARSEN)
    valid = ((sub == 0) & is_own) | ((sub > 0) & (is_left | is_right))

    def outside(r_ref, Z, upper):
        def mine(at):
            tile_at = kept_ref[at + Z * SUB : at + (Z + 1) * SUB]
            return jnp.where(upper, rolled(tile_at, HALF, 1), tile_at)

        other = r_ref[base + Z * SUB : base + (Z + 1) * SUB]
        return all_rows(0.5 * (mine(nz) + rolled(other, HALF, 1)) * (mine(0) - other))

    odd = jnp.logical_not(even)
    far_rows = base + nz + SUB
    flux = jnp.zeros((SUB, LANES), f32)
    for Z in range(nz // COARSEN):
        u, c = (
            (facing(own_ref, a, Z * SUB, nz, odd), r2_ref[at : at + SUB])
            for a, at in ((0, far_rows + Z * SUB), (1, far_rows + nz + Z * SUB))
        )
        one = all_rows(0.5 * (c[0] + c[1]) * (u[0] - u[1]))
        two = outside(r2_ref, Z, odd)
        three = outside(r1_ref, Z, even)
        sums = jnp.where(sub == 0, one, jnp.where(sub == 1, two, jnp.where(sub == 2, three, 0.0)))
        here = valid & (plane == Z)
        flux = flux + jnp.where(here, gathered(sums, source), 0.0)
    flux = flux * (1.0 / CELLS)
    far, mate = flux[0:1] + flux[1:2], flux[2:3]

    def stacked(own, other):
        before, after = jnp.where(even, other, own), jnp.where(even, own, other)
        return jnp.where(sub <= rows, rolled(before, 1, 0), rolled(after, rows + 1, 0))

    at = base + nz
    coarse, near_c, far_c = kept_ref[2 * nz :], r1_ref[at : at + SUB], r2_ref[at : at + SUB]
    rhs = stacked(coarse, far_c)
    sign = jnp.where(even, 1.0, -1.0)
    rhs = rhs + jnp.where(sub == rows, sign * far, jnp.where(sub == rows + 1, -sign * far, 0.0))
    rhs = rhs - jnp.where(sub == jnp.where(even, 2 * rows, 1), mate, 0.0)
    coarse, near_c, far_c = (rolled(x, -RIM, 0) for x in (coarse, near_c, far_c))
    cond = stacked(coarse, far_c)
    before = jnp.where(even, rolled(far_c, -rows, 0), rolled(near_c, 1 - rows, 0))
    after = jnp.where(even, rolled(near_c, 2 * rows + 1, 0), rolled(far_c, rows + 1, 0))
    cond = jnp.where(sub == 0, before, jnp.where(sub == 2 * rows + 1, after, cond))
    around = rolled(cond, -1, 0) + rolled(cond, 1, 0) + rolled(cond, -1, 1) + rolled(cond, 1, 1)
    around = around + rolled(cond, -SPREAD, 1) + rolled(cond, SPREAD, 1)
    weight = OMEGA / (SHIFT + (0.5 / COARSEN**2) * (6.0 * cond + around))
    o_ref[0:SUB] = weight * rhs
    o_ref[SUB : 2 * SUB] = weight
    o_ref[2 * SUB :] = cond


def faces(own, kept, r2, r1, after, nz, nx):
    return pl.pallas_call(
        functools.partial(faces_kernel, nz=nz, nx=nx),
        out_shape=tiles(3),
        in_specs=[VMEM] * 4 + [pl.BlockSpec(memory_space=pl.ANY)],
        out_specs=VMEM,
        compiler_params=SMALL,
        name="faces",
    )(own, kept, r2, r1, after)


def sides(even, one, two):
    return jnp.where(even, one, two), jnp.where(even, two, one)


def rim_of(low, after, before):
    return jnp.where(low, after, before), rolled(jnp.where(low, before, after), RIM, 0)


def rims_of(low, one_ref, two_ref, last_ref, nz):
    half = nz // 2
    for z in range(nz):
        yield rim_of(low, tile(one_ref if z < half else two_ref, z % half), tile(last_ref, z))


def rim_faces(sub, face, rim_face, u_first, u_last, rim):
    u_rim = jnp.where(sub == 0, rolled(rim, 1 - RIM, 0), rolled(rim, RIM - 1, 0))
    end = sub == SUB - 1
    after = jnp.where(end, face * (u_last - rolled(u_rim, -1, 0)), 0.0)
    before = jnp.where(end, rim_face * (u_rim - rolled(u_first, -1, 0)), 0.0)
    return after, before


def beside(w, z, zs, column):
    return rolled(w, -column - z // zs * GROUP, 1)


def window(spot, left, right, column):
    return jnp.where(spot == RIM - 1, left, rolled(right, RIM - 2 - column, 1))


def begin_kernel(
    strip_ref, u_ref, c_ref, r_ref, cx_ref, cy_ref, cz_ref, diag_ref, inv_ref, q_ref, v_ref, *, nz, nx
):
    zs = nz // ZS
    spot = part(iota((nx, LANES), 1), GROUP)[1]
    row, lane = iota((nx, LANES), 0), iota((nx, LANES), 1)
    first_lane, last_lane = lane == 0, lane == LANES - 1

    def strip(a, zi):
        return strip_ref[(a * zs + zi) * nx : (a * zs + zi + 1) * nx]

    edge_c, edge_f = [], []
    for zi in range(zs):
        u, c = strip(0, zi), strip(1, zi)
        flux = 0.5 * (c + rolled(c, -1, 1)) * (u - rolled(u, -1, 1))
        edge_c.append(window(spot, c, c, 3 * RIM))
        edge_f.append(window(spot, flux, flux, 3 * RIM - 1))

    def own(ref, z):
        return ref[z % nz * nx : (z % nz + 1) * nx]

    below = 0.5 * (own(c_ref, -1) + own(c_ref, 0))
    for z in range(nz):
        at = slice(z * nx, (z + 1) * nx)
        c = own(c_ref, z)
        gx = jnp.where(row == nx - 1, 0.0, 0.5 * (c + rolled(c, -1, 0)))
        edge = beside(edge_c[z % zs], z, zs, RIM - 1)
        gy = 0.5 * (c + jnp.where(last_lane, edge, rolled(c, -1, 1)))
        gyl = 0.5 * (c + jnp.where(first_lane, edge, rolled(c, 1, 1)))
        above = 0.5 * (c + own(c_ref, z + 1))
        diag = SHIFT + (gx + rolled(gx, 1, 0)) + (gy + gyl) + (above + below)
        edge = beside(edge_f[z % zs], z, zs, RIM - 1)
        r = own(r_ref, z) + jnp.where(first_lane, edge, jnp.where(last_lane, -edge, 0.0))
        inner = slice(SUB, nx - SUB)
        inverse = 1.0 / diag[inner]
        scaled = r[inner] * inverse
        cx_ref[at] = gx
        cy_ref[at] = gy
        cz_ref[at] = above
        diag_ref[at] = diag
        q_ref[at] = jnp.concatenate([r[:SUB], scaled, r[nx - SUB :]], axis=0)
        to = slice(z * (nx - 2 * SUB), (z + 1) * (nx - 2 * SUB))
        inv_ref[to] = inverse
        v_ref[to] = scaled * (1.0 / THETA)
        below = above


def begin(strips, u, c, r, nz, nx):
    inner = jax.ShapeDtypeStruct((nz * (nx - 2 * SUB), LANES), f32)
    return pl.pallas_call(
        functools.partial(begin_kernel, nz=nz, nx=nx),
        out_shape=(jax.ShapeDtypeStruct(u.shape, f32),) * 4 + (inner, jax.ShapeDtypeStruct(u.shape, f32), inner),
        in_specs=[VMEM] * 4,
        out_specs=(VMEM,) * 7,
        compiler_params=SMALL,
        cost_estimate=pl.CostEstimate(flops=40 * u.size, bytes_accessed=40 * u.size, transcendentals=0),
        name="begin",
    )(strips, u, c, r)


def fine_kernel(
    strip_ref, b2_ref, b1_ref, one_ref, two_ref, last_ref, u_ref, c_ref, cx_ref, cy_ref, cz_ref, diag_ref, inv_ref, q_ref, v_ref,
    cx, inv, q, va, acc, w2,
    ch, cyh, czh, vb, wr, w0, w1,
    *, nz, nx,
):
    zs = nz // ZS
    half = zs // 2
    ext = nx + SUB
    even = is_even()
    sub = iota((SUB, LANES), 0)
    low, end = sub < RIM, sub == SUB - 1
    table = steps()

    rims = []
    for z, (cond, rim) in enumerate(rims_of(low, one_ref, two_ref, last_ref, nz)):
        ch[z * SUB : (z + 1) * SUB] = cond
        rims.append(rim)

    row, spot = iota((ext, LANES), 0), part(iota((ext, LANES), 1), GROUP)[1]

    def strips_of(a):
        ends = [None] * zs
        for pair in range(half):
            index = a * half + pair
            ends[pair], ends[pair + half] = rim_of(low, *sides(even, tile(b1_ref, index), tile(b2_ref, index)))
        return [
            jnp.concatenate([strip_ref[(a * zs + zi) * nx : (a * zs + zi + 1) * nx], ends[zi]], axis=0)
            for zi in range(zs)
        ]

    def z_up(x):
        return x[1:] + [rolled(x[0], -GROUP, 1)]

    def z_down(x):
        return [rolled(x[-1], GROUP, 1)] + x[:-1]

    us, cs, rs = strips_of(0), strips_of(1), strips_of(2)
    cxs = [0.5 * (c + rolled(c, -1, 0)) for c in cs]
    cys = [0.5 * (c + rolled(c, -1, 1)) for c in cs]
    czs = [0.5 * (c + d) for c, d in zip(cs, z_up(cs))]
    czds = z_down(czs)
    invs, qs, vs = [], [], []
    for zi in range(zs):
        u = us[zi]
        fx = jnp.where((row == nx - 1) | (row == ext - 1), cxs[zi] * (u - rolled(u, -1, 0)), 0.0)
        fy = jnp.where((spot == RIM - 1) | (spot == 3 * RIM - 1), cys[zi] * (u - rolled(u, -1, 1)), 0.0)
        r = rs[zi] - (fx - rolled(fx, 1, 0)) - (fy - rolled(fy, 1, 1))
        wr[zi * SUB : (zi + 1) * SUB] = jnp.where(spot == RIM, r, rolled(r, -2 * RIM, 1))[nx:]
        diag = SHIFT + (cxs[zi] + rolled(cxs[zi], 1, 0)) + (cys[zi] + rolled(cys[zi], 1, 1)) + (czs[zi] + czds[zi])
        invs.append(1.0 / diag)
        qs.append(r * invs[zi])
        vs.append(qs[zi] * (1.0 / THETA))
    for k, w in enumerate((w0, w1, w2)):
        prod = [cys[zi] * vs[zi] for zi in range(zs)]
        for zi in range(zs):
            w[zi * ext : (zi + 1) * ext] = window(spot, prod[zi], vs[zi], 3 * RIM)
        if k == SWEEPS - 1:
            break
        keep, lift = table[k]
        v_up, v_down = z_up(vs), z_down(vs)
        fresh = []
        for zi in range(zs):
            v = vs[zi]
            near = cxs[zi] * rolled(v, -1, 0) + rolled(cxs[zi] * v, 1, 0)
            near = near + cys[zi] * rolled(v, -1, 1) + rolled(prod[zi], 1, 1)
            near = near + czs[zi] * v_up[zi] + czds[zi] * v_down[zi]
            qs[zi] = qs[zi] - v + near * invs[zi]
            fresh.append(keep * v + lift * qs[zi])
        vs = fresh
    edge_c = [window(spot, c, c, 3 * RIM)[nx:] for c in cs]

    lane = iota((SUB, LANES), 1)
    first_lane, last_lane = lane == 0, lane == LANES - 1

    def own(ref, z):
        return ref[z % nz * nx : (z % nz + 1) * nx]

    def rim_at(ref, z):
        return tile(ref, z % nz)

    below = 0.5 * (rim_at(ch, -1) + rim_at(ch, 0))
    for z in range(nz):
        at = slice(z * SUB, (z + 1) * SUB)
        u, c = own(u_ref, z), tile(ch, z)
        c_first, c_last = own(c_ref, z)[:SUB], own(c_ref, z)[nx - SUB :]
        zi = z % zs
        face = jnp.where(end, 0.5 * (c_last + rolled(c, -1, 0)), 0.0)
        gx = 0.5 * (c + jnp.where(end, rolled(c_first, -1, 0), rolled(c, -1, 0)))
        gxl = rolled(gx, 1, 0)
        edge = beside(edge_c[zi], z, zs, RIM - 1)
        gy = 0.5 * (c + jnp.where(last_lane, edge, rolled(c, -1, 1)))
        gyl = 0.5 * (c + jnp.where(first_lane, edge, rolled(c, 1, 1)))
        above = 0.5 * (c + rim_at(ch, z + 1))
        diag = SHIFT + (gx + jnp.where(sub == 0, rolled(face, 1, 0), gxl)) + (gy + gyl) + (above + below)
        after, before = rim_faces(sub, face, gx, u[:SUB], u[nx - SUB :], rims[z])
        r = rims[z] + rolled(after, 1, 0) - before
        r = jnp.where(first_lane | last_lane, beside(wr[zi * SUB : (zi + 1) * SUB], z, zs, RIM), r)
        own_diag, own_q = own(diag_ref, z), own(q_ref, z)
        long_at = slice(z * ext, (z + 1) * ext)
        parts = []
        for this_diag, this_r in (
            (own_diag[:SUB] + jnp.where(sub == 0, gxl, 0.0), own_q[:SUB] + rolled(before, 1, 0)),
            (own_diag[nx - SUB :] + face, own_q[nx - SUB :] - after),
            (diag, r),
        ):
            inverse = 1.0 / this_diag
            scaled = this_r * inverse
            parts.append((inverse, scaled, scaled * (1.0 / THETA)))
        inner = slice(z * (nx - 2 * SUB), (z + 1) * (nx - 2 * SUB))
        middle = (inv_ref[inner], own_q[SUB : nx - SUB], v_ref[inner])
        for ref, one, two, three, four in zip((inv, q, va), parts[0], middle, parts[1], parts[2]):
            ref[long_at] = jnp.concatenate([one, two, three, four], axis=0)
        own_cx = own(cx_ref, z)
        cx[long_at] = jnp.concatenate([own_cx[: nx - SUB], own_cx[nx - SUB :] + face, gx], axis=0)
        cyh[at] = gy
        czh[at] = above
        below = above

    lane = iota((ext, LANES), 1)
    first_lane, last_lane = lane == 0, lane == LANES - 1

    def whole(ref, rim, z):
        return jnp.concatenate([own(ref, z), rim_at(rim, z)], axis=0)

    def long(ref, z):
        return ref[z % nz * ext : (z % nz + 1) * ext]

    for k, w in enumerate((w0, w1)):
        old, new = (va, vb) if k % 2 == 0 else (vb, va)
        keep, lift = table[k]
        for z in range(nz):
            at, here = slice(z * ext, (z + 1) * ext), slice(z * nx, (z + 1) * nx)
            zi = z % zs
            v, gx, gy = old[at], cx[at], whole(cy_ref, cyh, z)
            edge = beside(w[zi * ext : (zi + 1) * ext], z, zs, RIM - 1)
            near = gx * rolled(v, -1, 0) + rolled(gx * v, 1, 0)
            near = near + gy * jnp.where(last_lane, edge, rolled(v, -1, 1))
            near = near + jnp.where(first_lane, edge, rolled(gy * v, 1, 1))
            near = near + whole(cz_ref, czh, z) * long(old, z + 1) + whole(cz_ref, czh, z - 1) * long(old, z - 1)
            scaled = q[at] - v + near * inv[at]
            fresh = keep * v + lift * scaled
            q[at] = scaled
            new[at] = fresh
            acc[here] = (own(u_ref, z) + v[:nx] if k == 0 else acc[here]) + fresh[:nx]


def fine(strips, b2, b1, one, two, last, u, c, begun, nz, nx):
    zs = nz // ZS
    ext = nx + SUB
    rim = pltpu.VMEM((nz * SUB, LANES), f32)
    full = jax.ShapeDtypeStruct((nz * ext, LANES), f32)
    strip = pltpu.VMEM((zs * ext, LANES), f32)
    return pl.pallas_call(
        functools.partial(fine_kernel, nz=nz, nx=nx),
        out_shape=(full,) * 4 + (jax.ShapeDtypeStruct(u.shape, f32), jax.ShapeDtypeStruct((zs * ext, LANES), f32)),
        in_specs=[VMEM] * 15,
        out_specs=(VMEM,) * 6,
        scratch_shapes=[rim] * 3 + [pltpu.VMEM((nz * ext, LANES), f32), pltpu.VMEM((zs * SUB, LANES), f32)] + [strip] * 2,
        compiler_params=SMALL,
        cost_estimate=pl.CostEstimate(flops=100 * u.size, bytes_accessed=40 * u.size, transcendentals=0),
        name="fine",
    )(strips, b2, b1, one, two, last, u, c, *begun)


def finish_kernel(
    cx_ref, inv_ref, q_ref, v_ref, sum_ref, w_ref, cy_ref, cz_ref, m_ref, r_ref, o_ref, out, sems, *, nz, nx
):
    zs = nz // ZS
    ext = nx + SUB
    rows = nx // COARSEN
    even = is_even()
    sub, lane = iota((SUB, LANES), 0), iota((SUB, LANES), 1)
    beyond = sub == jnp.where(even, 2 * rows + 1, 0)
    fields = []
    for a in range(3):
        mine, mate = tile(m_ref, a), tile(r_ref, a)
        mate = jnp.where(even, rolled(mate, 2 * rows, 0), rolled(mate, -2 * rows, 0))
        fields.append(jnp.concatenate([jnp.where(beyond, mate, mine), mate], axis=0))
    start, weight, cond = fields
    scale = 0.5 / COARSEN**2
    turns = (-1, 0), (1, 0), (-1, 1), (1, 1), (-SPREAD, 1), (SPREAD, 1)
    shares = [scale * (cond + rolled(cond, *turn)) for turn in turns]
    keep = 1.0 - weight * (SHIFT + sum(shares))
    shares = [weight * share for share in shares]
    v = start
    for _ in range(COARSE_SWEEPS - 1):
        terms = [share * rolled(v, *turn) for share, turn in zip(shares, turns)]
        v = (start + keep * v) + ((terms[0] + terms[1]) + (terms[2] + terms[3]) + (terms[4] + terms[5]))
    top = v[:SUB]
    top = jnp.where(even, rolled(top, -rows - 1, 0), rolled(top, -1, 0))

    wide = iota((nx, LANES), 1)
    first_lane, last_lane = wide == 0, wide == LANES - 1
    keep, lift = steps()[-1]

    def own(ref, z):
        return ref[z % nz * nx : (z % nz + 1) * nx]

    def long(ref, z):
        return ref[z % nz * ext : z % nz * ext + nx]

    copies = []
    size = COARSEN * nx
    for Z in range(nz // COARSEN):
        spread = jnp.take_along_axis(top, Z * SPREAD + RIM + part(lane, COARSEN)[0], axis=1)
        value = jnp.concatenate([jnp.broadcast_to(spread[X : X + 1], (COARSEN, LANES)) for X in range(rows)], axis=0)
        for z in range(Z * COARSEN, (Z + 1) * COARSEN):
            at = slice(z * ext, (z + 1) * ext)
            v, gx = v_ref[at], cx_ref[at]
            near = (gx * rolled(v, -1, 0) + rolled(gx * v, 1, 0))[:nx]
            v, gy, zi = v[:nx], own(cy_ref, z), z % zs
            edge = beside(w_ref[zi * ext : zi * ext + nx], z, zs, RIM - 1)
            near = near + gy * jnp.where(last_lane, edge, rolled(v, -1, 1))
            near = near + jnp.where(first_lane, edge, rolled(gy * v, 1, 1))
            near = near + own(cz_ref, z) * long(v_ref, z + 1) + own(cz_ref, z - 1) * long(v_ref, z - 1)
            scaled = long(q_ref, z) - v + near * long(inv_ref, z)
            here = slice(z * nx, (z + 1) * nx)
            out[here] = (own(sum_ref, z) + (keep * v + lift * scaled)) + value
        here = pl.ds(Z * size, size)
        copies.append(pltpu.make_async_copy(out.at[here], o_ref.at[here], sems.at[Z]))
        copies[-1].start()
    for copy in copies:
        copy.wait()


def finish(passed, cy, cz, m, r, nz, nx):
    shape = (nz * nx, LANES)
    return pl.pallas_call(
        functools.partial(finish_kernel, nz=nz, nx=nx),
        out_shape=jax.ShapeDtypeStruct(shape, f32),
        in_specs=[VMEM] * 10,
        out_specs=pl.BlockSpec(memory_space=pltpu.HBM),
        scratch_shapes=[pltpu.VMEM(shape, f32), pltpu.SemaphoreType.DMA((nz // COARSEN,))],
        compiler_params=SMALL,
        name="finish",
    )(*passed, cy, cz, m, r)


def moves():
    size_x, size_y = lax.axis_size("gx"), lax.axis_size("gy")

    def send(x, go):
        pairs = []
        for i in range(size_x):
            for j in range(size_y):
                k, l = go(i, j)
                pairs.append((i * size_y + j, (k % size_x) * size_y + l % size_y))
        return lax.ppermute(x, ("gx", "gy"), pairs)

    def mate(x):
        return send(x, lambda i, j: (i + 1 if i % 2 == 0 else i - 1, j))

    def shift(x, by):
        return send(x, lambda i, j: (i + by, j))

    def far(x):
        return send(x, lambda i, j: (i - 1 if i % 2 == 0 else i + 1, j))

    def beside_y(x):
        left = send(x, lambda i, j: (i, j + 1))
        if size_y == 2:
            return left, left
        return left, send(x, lambda i, j: (i, j - 1))

    return mate, far, shift, beside_y


def body(iterate, source, conduct):
    nz, nx, ny = iterate.shape
    if nz != ZS * 4 or ny != LANES or nx != 3 * SUB or lax.axis_size("gx") % 2:
        raise ValueError("shapes")
    mate, far, shift, beside_y = moves()
    u, s, c = (x.reshape(nz * nx, ny) for x in (iterate, source, conduct))
    q, f1, last, one, two, r, own = pack(u, s, c, nz, nx)
    ql, qr = beside_y(q)
    rf1 = mate(f1)
    before = shift(last, 1)
    b1, b2, strips, kept = join(q, ql, qr, rf1, own, nz, nx)
    rb2 = far(b2)
    rb1 = mate(b1)
    one, two, strips = lax.optimization_barrier((one, two, strips))
    after = shift(one, -1), shift(two, -1)
    begun = begin(strips, u, c, r, nz, nx)
    m = faces(own, kept, rb2, rb1, begun[0], nz, nx)
    rm = mate(m)
    passed = fine(strips, rb2, rb1, *after, before, u, c, begun, nz, nx)
    return finish(passed, begun[1], begun[2], m, rm, nz, nx).reshape(nz, nx, ny)


def solution(mesh):
    spec = P(None, "gx", "gy")
    return jax.shard_map(body, mesh=mesh, in_specs=(spec,) * 3, out_specs=spec, check_vma=False)
```
